32 devices in a mesh: col: 8 (over y, x, core), row: 4 (over z).
Axes of the slice: x: 2, y: 2, z: 4, core: 2. Of those that a mesh axis runs over, the one named last changes fastest.
Arguments:
- features: bfloat16 [4096, 256], P(('col', 'row')), may hold values from -6 to 6
- weight: bfloat16 [256, 256], replicated, may hold values from -0.375 to 0.375
- bias_term: float32 [256], replicated, may hold values from -3 to 3
- cotangent: bfloat16 [4096, 256], P(('row', 'col')), may hold values from -6 to 6
- tile_values: bfloat16 [4, 8, 32, 128, 128], P('row', 'col'), may hold values from 0 to 0.07980869
- tile_row: int32 [4, 8, 32], P('row', 'col'), may hold values from 0 to 7
- tile_col: int32 [4, 8, 32], P('row', 'col'), may hold values from 0 to 3
- tile_count: int32 [4, 8], P('row', 'col'), may hold values from 6 to 32, as said below
Outputs:
- hidden_out: bfloat16 [4096, 256], P(('row', 'col'))
- grad_features: bfloat16 [4096, 256], P(('col', 'row'))
- grad_weight: float32 [256, 256], replicated
- grad_bias: float32 [256], replicated
The draws below stay inside these ranges and needn't reach their ends.
Inputs may be any that keep to these rules, and one draw needn't show every extreme that they name: Live slots are the first tile_count[r, c] slots of a grid place; at least 6 of them, and all 32 on some grid place. Slots past the count are ignored. `tile_row`: A grid place's live slots may name the same tile position more than once; their values add.
All inputs are finite; a program needn't handle non-finite values.
Results may differ from the reference program's by a relative error of at most 0.02.
Values may be sent and summed in bfloat16 or wider, within the bound.
No kernel may reach another device: no remote copies, remote signals or barrier semaphores. Data moves between devices by JAX's collectives and lax.ppermute only.
A program may use at most 64 MiB of HBM per device.

```python
import jax
import jax.numpy as jnp
from jax import lax

FEATURES = 256
HIDDEN_SIZE = 256
TILE = 128
TILES_DEV = 32
NODES = 4096
N_COL = 8
N_ROW = 4


def draw_tile_count(key, part):
    divisor = jax.random.randint(jax.random.fold_in(key, 11), (N_ROW, N_COL), 1, 6)
    counts = (TILES_DEV // divisor).astype(jnp.int32)
    chosen = jax.random.randint(jax.random.fold_in(key, 12), (), 0, N_ROW * N_COL)
    flat_counts = counts.reshape(-1).at[chosen].set(TILES_DEV)
    return flat_counts.reshape(N_ROW, N_COL).astype(jnp.int32)


def draw_tile_values(key, part):
    shape = (N_ROW, N_COL, TILES_DEV, TILE, TILE)
    top_value = (TILES_DEV * TILE // 26) ** (-0.5)
    picks = jax.random.randint(jax.random.fold_in(key, 21), shape, 0, 4)
    eye_mask = jnp.eye(TILE, dtype=jnp.int32)[None, None, None, :, :]
    keep = jnp.maximum((picks == 0).astype(jnp.int32), eye_mask).astype(jnp.float32)
    values = jax.random.uniform(jax.random.fold_in(key, 22), shape, jnp.float32, 0.1, 1.0) * top_value
    return (values * keep).astype(jnp.bfloat16)


def with_ends(result, key, smallest, largest):
    shape = result.shape
    place = [jax.random.randint(jax.random.fold_in(key, axis), (), 0, shape[axis]) for axis in range(len(shape))]
    result = result.at[tuple(place)].set(smallest)
    longest = shape.index(max(shape))
    place[longest] = (place[longest] + 1) % shape[longest]
    return result.at[tuple(place)].set(largest)


def shard_levels(own_key, dims, split, least, high):
    factor_of = 1.0
    for axis_at, shards_of in split:
        heights = jax.random.uniform(jax.random.fold_in(jax.random.fold_in(own_key, 6), axis_at), (shards_of,), jnp.float32, least / len(split), high / len(split))
        factor_of = factor_of * jnp.repeat(jnp.exp(heights), dims[axis_at] // shards_of).reshape((-1,) + (1,) * (len(dims) - 1 - axis_at))
    return factor_of


def bell_draw(stream_key, extent, deviation, reach, split=(), held_as=jnp.bfloat16):
    level = shard_levels(stream_key, extent, split, -0.22, 0.18) if split else 1.0
    drawn = jax.random.normal(stream_key, extent, jnp.float32) * deviation * level
    return jnp.minimum(jnp.maximum(drawn, -reach), reach).astype(held_as)


def setup_inputs(seed: int = 0) -> dict:
    key_list = jax.random.split(jax.random.key(seed), 9)
    features = bell_draw(key_list[0], (NODES, FEATURES), 1.0, 6.0, ((0, 32),))
    weight = bell_draw(key_list[1], (FEATURES, HIDDEN_SIZE), FEATURES ** -0.5, 0.375)
    bias_term = bell_draw(key_list[2], (HIDDEN_SIZE,), 0.5, 3.0, (), jnp.float32)
    cotangent = bell_draw(key_list[3], (NODES, HIDDEN_SIZE), 1.0, 6.0, ((0, 32),))
    tile_values = draw_tile_values(jax.random.fold_in(key_list[8], 71), 0)
    tile_row = with_ends(jax.random.randint(key_list[5], (N_ROW, N_COL, TILES_DEV), 0, N_COL), jax.random.fold_in(key_list[5], 1), 0, N_COL - 1).astype(jnp.int32)
    tile_col = with_ends(jax.random.randint(key_list[6], (N_ROW, N_COL, TILES_DEV), 0, N_ROW), jax.random.fold_in(key_list[6], 1), 0, N_ROW - 1).astype(jnp.int32)
    tile_count = draw_tile_count(jax.random.fold_in(key_list[8], 71), 0)
    return {"features": features, "weight": weight, "bias_term": bias_term, "cotangent": cotangent, "tile_values": tile_values, "tile_row": tile_row, "tile_col": tile_col, "tile_count": tile_count}


def slot_sum(tile_block, slab_rows, target_idx, live_mask, groups, transposed):
    tile_float = tile_block.astype(jnp.float32)
    slab_float = slab_rows.astype(jnp.float32)
    if transposed:
        products = jnp.einsum('sji,sjc->sic', tile_float, slab_float)
    else:
        products = jnp.einsum('sij,sjc->sic', tile_float, slab_float)
    products = products * live_mask[:, None, None].astype(products.dtype)
    empty = jnp.zeros((groups,) + products.shape[1:], products.dtype)
    return empty.at[target_idx].add(products)

def rounded(values):
    return lax.optimization_barrier(values.astype(jnp.bfloat16)).astype(jnp.float32)

def activate(inputs):
    return jax.nn.gelu(inputs, approximate=True)

def reference(features, weight, bias_term, cotangent, tile_values, tile_row, tile_col, tile_count):
    slot_ids = jnp.arange(TILES_DEV, dtype=jnp.int32)
    feat_blocks = features.reshape(N_COL, N_ROW, TILE, FEATURES)

    def forward_row(row_idx):

        def add_col(running, col_idx):
            live_mask = slot_ids < tile_count[row_idx, col_idx]
            slab_rows = feat_blocks[col_idx][tile_col[row_idx, col_idx]]
            partial_value = slot_sum(tile_values[row_idx, col_idx], slab_rows, tile_row[row_idx, col_idx], live_mask, N_COL, False)
            return (running + rounded(partial_value), None)
        running, _ = lax.scan(add_col, jnp.zeros((N_COL, TILE, FEATURES), jnp.float32), jnp.arange(N_COL, dtype=jnp.int32))
        return running.astype(jnp.bfloat16)
    aggregated = lax.map(forward_row, jnp.arange(N_ROW, dtype=jnp.int32)).reshape(NODES, FEATURES)
    pre_act = jnp.dot(aggregated, weight, preferred_element_type=jnp.float32) + bias_term
    hidden_out = activate(pre_act).astype(jnp.bfloat16)
    _, pull_back = jax.vjp(activate, pre_act)
    grad_pre = pull_back(cotangent.astype(jnp.float32))[0].astype(jnp.bfloat16)
    grad_blocks = grad_pre.reshape(N_ROW, N_COL, TILE, HIDDEN_SIZE)

    def back_col(col_idx):

        def add_row(running, row_idx):
            live_mask = slot_ids < tile_count[row_idx, col_idx]
            slab_rows = grad_blocks[row_idx][tile_row[row_idx, col_idx]]
            partial_value = slot_sum(tile_values[row_idx, col_idx], slab_rows, tile_col[row_idx, col_idx], live_mask, N_ROW, True)
            return (running + rounded(partial_value), None)
        running, _ = lax.scan(add_row, jnp.zeros((N_ROW, TILE, HIDDEN_SIZE), jnp.float32), jnp.arange(N_ROW, dtype=jnp.int32))
        return running.astype(jnp.bfloat16)
    back_agg = lax.map(back_col, jnp.arange(N_COL, dtype=jnp.int32)).reshape(NODES, HIDDEN_SIZE)
    grad_features = jnp.einsum('nh,fh->nf', back_agg.astype(jnp.float32), weight.astype(jnp.float32)).astype(jnp.bfloat16)
    factor_root = NODES ** (-0.5)
    grad_weight = jnp.einsum('nf,nh->fh', aggregated.astype(jnp.float32), grad_pre.astype(jnp.float32)) * factor_root
    grad_bias = lax.optimization_barrier(jnp.sum(grad_pre.astype(jnp.float32), axis=0)) * factor_root
    return (hidden_out, grad_features, grad_weight, grad_bias)
```

```python
import functools

import jax
import jax.numpy as jnp
from jax import lax
from jax.experimental import pallas as pl
from jax.experimental.pallas import tpu as pltpu
from jax.sharding import PartitionSpec as P

F32 = jnp.float32
BF16 = jnp.bfloat16
ROOT_2_OVER_PI = 0.7978845608028654
CUBIC = 0.044715
VMEM_LIMIT = 48 * 1024 * 1024

VMEM_SPEC = pl.BlockSpec(memory_space=pltpu.VMEM)
SMEM_SPEC = pl.BlockSpec(memory_space=pltpu.SMEM)


def call(kernel, out_shape, in_specs, scratch, flops, moved):
    return pl.pallas_call(
        kernel,
        out_shape=out_shape,
        in_specs=in_specs,
        out_specs=jax.tree.map(lambda _: VMEM_SPEC, out_shape),
        scratch_shapes=scratch,
        compiler_params=pltpu.CompilerParams(vmem_limit_bytes=VMEM_LIMIT),
        cost_estimate=pl.CostEstimate(flops=flops, bytes_accessed=moved, transcendentals=0),
    )


def add_slots(count, source_idx, target_idx, tiles_ref, source_ref, acc_ref, contract):
    slots, tile = tiles_ref.shape[0], tiles_ref.shape[1]
    group = 4
    acc_ref[...] = jnp.zeros_like(acc_ref)

    def body(step, carry):
        first = step * group
        products = []
        for k in range(group):
            slot = first + k
            rows = source_ref[pl.ds(pl.multiple_of(source_idx[slot] * tile, tile), tile), :]
            product = lax.dot_general(
                tiles_ref[slot], rows, (((contract,), (0,)), ((), ())), preferred_element_type=F32
            )
            products.append(jnp.where(slot < count, product, 0.0))
        for k in range(group):
            slot = first + k
            place = jnp.where(slot < count, target_idx[slot], 0)
            where = pl.ds(pl.multiple_of(place * tile, tile), tile)
            acc_ref[where, :] += products[k]
        return carry

    lax.fori_loop(0, (count + group - 1) // group, body, 0)


def forward_kernel(count_ref, row_ref, col_ref, tiles_ref, source_ref, out_ref, acc_ref):
    add_slots(count_ref[0], col_ref, row_ref, tiles_ref, source_ref, acc_ref, 1)
    out_ref[...] = acc_ref[...].astype(BF16)


def middle_kernel(parts_ref, weight_ref, bias_ref, cot_ref, hidden_ref, both_ref):
    total = parts_ref[0].astype(F32)
    for k in range(1, parts_ref.shape[0]):
        total += parts_ref[k].astype(F32)
    aggregated = total.astype(BF16)
    v = jnp.dot(aggregated, weight_ref[...], preferred_element_type=F32) + bias_ref[...]
    square = v * v
    t = jnp.tanh(ROOT_2_OVER_PI * (v + CUBIC * (square * v)))
    half = 0.5 * (1.0 + t)
    hidden_ref[...] = (v * half).astype(BF16)
    slope = half + 0.5 * v * (1.0 - t * t) * (ROOT_2_OVER_PI * (1.0 + 3.0 * CUBIC * square))
    width = v.shape[1]
    both_ref[:, :width] = (cot_ref[...].astype(F32) * slope).astype(BF16)
    both_ref[:, width:] = aggregated


def backward_kernel(
    me_ref, count_ref, row_ref, col_ref, tiles_ref, both_ref, out_ref, acc_ref, weight_acc, *, share
):
    tile = tiles_ref.shape[1]
    width = out_ref.shape[2]
    grad_ref = both_ref.at[:, :width]
    add_slots(count_ref[0], row_ref, col_ref, tiles_ref, grad_ref, acc_ref, 0)
    grad = both_ref[:, :width]
    weight_acc[...] = lax.dot_general(
        both_ref[:, width:], grad, (((0,), (0,)), ((), ())), preferred_element_type=F32
    )
    mine = weight_acc[pl.ds(pl.multiple_of(me_ref[0] * share, share), share), :]
    bias = jnp.sum(grad.astype(F32), axis=0, keepdims=True)
    bias_high = bias.astype(BF16).astype(F32)
    rest = out_ref.shape[1] - tile - share
    extra = lax.broadcasted_iota(jnp.int32, (rest, width), 0)
    tail = jnp.where(extra == 0, bias_high, jnp.where(extra == 1, bias - bias_high, 0.0))
    tail = jnp.concatenate([mine, tail], axis=0).astype(BF16)
    for k in range(out_ref.shape[0]):
        out_ref[k, :tile, :] = acc_ref[k * tile : (k + 1) * tile, :].astype(BF16)
        out_ref[k, tile:, :] = tail


def final_kernel(parts_ref, weight_ref, features_ref, share_ref, bias_ref, *, factor, tile):
    total = parts_ref[0].astype(F32)
    for k in range(1, parts_ref.shape[0]):
        total += parts_ref[k].astype(F32)
    features_ref[...] = lax.dot_general(
        total[:tile].astype(BF16),
        weight_ref[...],
        (((1,), (1,)), ((), ())),
        preferred_element_type=F32,
    ).astype(BF16)
    share = share_ref.shape[0]
    share_ref[...] = total[tile : tile + share] * factor
    bias_ref[...] = (total[tile + share : tile + share + 1] + total[tile + share + 1 : tile + share + 2]) * factor


def local(features, weight, bias_term, cotangent, tile_values, tile_row, tile_col, tile_count):
    row_count = lax.axis_size("row")
    col_count = lax.axis_size("col")
    tile, width = features.shape
    hidden = weight.shape[1]
    slots = tile_values.shape[2]
    tiles = tile_values.reshape(slots, tile, tile)
    rows = tile_row.reshape(slots)
    cols = tile_col.reshape(slots)
    count = tile_count.reshape(1)
    bias_row = bias_term.reshape(1, hidden)
    slot_flops = 2 * slots * tile * tile

    column_block = lax.all_gather(features, "row", axis=0, tiled=True)
    partial_value = call(
        forward_kernel,
        jax.ShapeDtypeStruct((col_count * tile, width), BF16),
        [SMEM_SPEC] * 3 + [VMEM_SPEC] * 2,
        [pltpu.VMEM((col_count * tile, width), F32)],
        slot_flops * width,
        tiles.size * 2,
    )(count, rows, cols, tiles, column_block)
    parts = lax.all_to_all(
        partial_value.reshape(col_count, tile, width), "col", split_axis=0, concat_axis=0
    )
    hidden_out, both = call(
        middle_kernel,
        (
            jax.ShapeDtypeStruct((tile, hidden), BF16),
            jax.ShapeDtypeStruct((tile, hidden + width), BF16),
        ),
        [VMEM_SPEC] * 4,
        [],
        2 * tile * width * hidden,
        parts.size * 2,
    )(parts, weight, bias_row, cotangent)
    both_block = lax.all_gather(both, "col", axis=0, tiled=True)

    share = width // col_count
    extra = -(-(share + 2) // 16) * 16
    me = lax.axis_index("col").astype(jnp.int32).reshape(1)
    back = call(
        functools.partial(backward_kernel, share=share),
        jax.ShapeDtypeStruct((row_count, tile + extra, hidden), BF16),
        [SMEM_SPEC] * 4 + [VMEM_SPEC] * 2,
        [
            pltpu.VMEM((row_count * tile, hidden), F32),
            pltpu.VMEM((width, hidden), F32),
        ],
        slot_flops * hidden,
        tiles.size * 2,
    )(me, count, rows, cols, tiles, both_block)
    back_parts = lax.all_to_all(back, "row", split_axis=0, concat_axis=0)
    factor = (tile * row_count * col_count) ** (-0.5)
    grad_features, weight_share, grad_bias = call(
        functools.partial(final_kernel, factor=factor, tile=tile),
        (
            jax.ShapeDtypeStruct((tile, width), BF16),
            jax.ShapeDtypeStruct((share, hidden), F32),
            jax.ShapeDtypeStruct((1, hidden), F32),
        ),
        [VMEM_SPEC] * 2,
        [],
        2 * tile * width * hidden,
        back.size * 2,
    )(back_parts, weight)
    grad_weight = lax.all_gather(weight_share, "col", axis=0, tiled=True)
    return hidden_out, grad_features, grad_weight, grad_bias.reshape(hidden)


def solution(mesh):
    return jax.shard_map(
        local,
        mesh=mesh,
        in_specs=(
            P(("col", "row"), None),
            P(),
            P(),
            P(("row", "col"), None),
            P("row", "col", None, None, None),
            P("row", "col", None),
            P("row", "col", None),
            P("row", "col"),
        ),
        out_specs=(P(("row", "col"), None), P(("col", "row"), None), P(), P()),
        check_vma=False,
    )
```

```python
import functools

import jax
import jax.numpy as jnp
from jax import lax
from jax.experimental import pallas as pl
from jax.experimental.pallas import tpu as pltpu
from jax.sharding import PartitionSpec as P

F32 = jnp.float32
BF16 = jnp.bfloat16
ROOT_2_OVER_PI = 0.7978845608028654
CUBIC = 0.044715
VMEM_LIMIT = 48 * 1024 * 1024

VMEM_SPEC = pl.BlockSpec(memory_space=pltpu.VMEM)
SMEM_SPEC = pl.BlockSpec(memory_space=pltpu.SMEM)


def call(kernel, out_shape, in_specs, scratch, flops, moved):
    return pl.pallas_call(
        kernel,
        out_shape=out_shape,
        in_specs=in_specs,
        out_specs=jax.tree.map(lambda _: VMEM_SPEC, out_shape),
        scratch_shapes=scratch,
        compiler_params=pltpu.CompilerParams(vmem_limit_bytes=VMEM_LIMIT),
        cost_estimate=pl.CostEstimate(flops=flops, bytes_accessed=moved, transcendentals=0),
    )


def partner(index, k, count):
    if count & (count - 1) == 0:
        return index ^ k
    return (k - index) % count


def exchange(blocks, axis):
    count = len(blocks)
    received = []
    for k, block in enumerate(blocks):
        pairs = [(i, partner(i, k, count)) for i in range(count)]
        moves = any(i != j for i, j in pairs)
        received.append(lax.ppermute(block, axis, pairs) if moves else block)
    return received


def block_at(index, size):
    return pl.ds(pl.multiple_of(index * size, size), size)


def summed(refs, rows):
    total = refs[0][rows, :].astype(F32)
    for ref in refs[1:]:
        total += ref[rows, :].astype(F32)
    return total


def add_slots(count, source_idx, target_idx, tiles_ref, source_ref, acc_ref, contract):
    tile = tiles_ref.shape[1]
    group = 4
    acc_ref[...] = jnp.zeros_like(acc_ref)

    def body(step, carry):
        first = step * group
        products = []
        for k in range(group):
            slot = first + k
            rows = source_ref[block_at(source_idx[slot], tile), :]
            product = lax.dot_general(
                tiles_ref[slot], rows, (((contract,), (0,)), ((), ())), preferred_element_type=F32
            )
            products.append(jnp.where(slot < count, product, 0.0))
        for k in range(group):
            slot = first + k
            place = jnp.where(slot < count, target_idx[slot], 0)
            acc_ref[block_at(place, tile), :] += products[k]
        return carry

    lax.fori_loop(0, (count + group - 1) // group, body, 0)


def forward_kernel(me_ref, count_ref, row_ref, col_ref, tiles_ref, *refs, n_row, n_col):
    sources, outs, (source_ref, acc_ref) = refs[:n_row], refs[n_row:-2], refs[-2:]
    tile = tiles_ref.shape[1]
    for k, ref in enumerate(sources):
        source_ref[block_at(partner(me_ref[0], k, n_row), tile), :] = ref[...]
    add_slots(count_ref[0], col_ref, row_ref, tiles_ref, source_ref, acc_ref, 1)
    for k, ref in enumerate(outs):
        ref[...] = acc_ref[block_at(partner(me_ref[1], k, n_col), tile), :].astype(BF16)


def middle_kernel(me_ref, weight_ref, bias_ref, cot_ref, *refs, n_col, share):
    parts, (hidden_ref, *outs), weight_acc = refs[:n_col], refs[n_col:-1], refs[-1]
    tile, width = cot_ref.shape
    aggregated = summed(parts, slice(None)).astype(BF16)
    v = jnp.dot(aggregated, weight_ref[...], preferred_element_type=F32) + bias_ref[...]
    square = v * v
    t = jnp.tanh(ROOT_2_OVER_PI * (v + CUBIC * (square * v)))
    half = 0.5 * (1.0 + t)
    hidden_ref[...] = (v * half).astype(BF16)
    slope = half + 0.5 * v * (1.0 - t * t) * (ROOT_2_OVER_PI * (1.0 + 3.0 * CUBIC * square))
    grad = (cot_ref[...].astype(F32) * slope).astype(BF16)
    weight_acc[...] = lax.dot_general(
        aggregated, grad, (((0,), (0,)), ((), ())), preferred_element_type=F32
    )
    bias = jnp.sum(grad.astype(F32), axis=0, keepdims=True)
    high = bias.astype(BF16).astype(F32)
    rest = outs[0].shape[0] - tile - share
    line = lax.broadcasted_iota(jnp.int32, (rest, width), 0)
    tail = jnp.where(line == 0, high, jnp.where(line == 1, bias - high, 0.0))
    for k, ref in enumerate(outs):
        mine = weight_acc[block_at(partner(me_ref[1], k, n_col), share), :]
        ref[:tile, :] = grad
        ref[tile:, :] = jnp.concatenate([mine, tail], axis=0).astype(BF16)


def share_kernel(*refs, tile, share):
    parts, out_ref = refs[:-1], refs[-1]
    total = summed(parts, slice(tile, None))
    bias = total[share : share + 1] + total[share + 1 : share + 2]
    high = bias.astype(BF16).astype(F32)
    line = lax.broadcasted_iota(jnp.int32, total.shape, 0)
    total = jnp.where(line == share, high, jnp.where(line == share + 1, bias - high, total))
    out_ref[...] = total.astype(BF16)


def backward_kernel(me_ref, count_ref, row_ref, col_ref, tiles_ref, *refs, n_row, n_col):
    sources, outs, (source_ref, acc_ref) = refs[:n_col], refs[n_col:-2], refs[-2:]
    tile = tiles_ref.shape[1]
    for k, ref in enumerate(sources):
        source_ref[block_at(partner(me_ref[1], k, n_col), tile), :] = ref[:tile, :]
    add_slots(count_ref[0], row_ref, col_ref, tiles_ref, source_ref, acc_ref, 0)
    for k, ref in enumerate(outs):
        ref[...] = acc_ref[block_at(partner(me_ref[0], k, n_row), tile), :].astype(BF16)


def scale_kernel(*refs, factor):
    parts, (share_ref, bias_ref) = refs[:-2], refs[-2:]
    share = share_ref.shape[0]
    total = summed(parts, slice(None))
    share_ref[...] = total[:share] * factor
    bias_ref[...] = (total[share : share + 1] + total[share + 1 : share + 2]) * factor


def features_kernel(weight_ref, *refs):
    parts, out_ref = refs[:-1], refs[-1]
    out_ref[...] = lax.dot_general(
        summed(parts, slice(None)).astype(BF16),
        weight_ref[...],
        (((1,), (1,)), ((), ())),
        preferred_element_type=F32,
    ).astype(BF16)


def join_kernel(me_ref, *refs):
    parts, out_ref = refs[:-1], refs[-1]
    share = parts[0].shape[0]
    for k, ref in enumerate(parts):
        out_ref[block_at(partner(me_ref[1], k, len(parts)), share), :] = ref[...]


def local(features, weight, bias_term, cotangent, tile_values, tile_row, tile_col, tile_count):
    n_row = lax.axis_size("row")
    n_col = lax.axis_size("col")
    tile, width = features.shape
    hidden = weight.shape[1]
    slots = tile_values.shape[2]
    tiles = tile_values.reshape(slots, tile, tile)
    rows = tile_row.reshape(slots)
    cols = tile_col.reshape(slots)
    count = tile_count.reshape(1)
    bias_row = bias_term.reshape(1, hidden)
    me = jnp.stack([lax.axis_index("row"), lax.axis_index("col")]).astype(jnp.int32)
    slot_flops = 2 * slots * tile * tile
    share = width // n_col
    extra = -(-(share + 2) // 16) * 16

    def like(rows, columns, dtype=BF16):
        return jax.ShapeDtypeStruct((rows, columns), dtype)

    sources = exchange([features] * n_row, "row")
    partials = call(
        functools.partial(forward_kernel, n_row=n_row, n_col=n_col),
        [like(tile, width)] * n_col,
        [SMEM_SPEC] * 4 + [VMEM_SPEC] * (1 + n_row),
        [pltpu.VMEM((n_row * tile, width), BF16), pltpu.VMEM((n_col * tile, width), F32)],
        slot_flops * width,
        tiles.size * 2,
    )(me, count, rows, cols, tiles, *sources)
    parts = exchange(partials, "col")
    hidden_out, *blocks = call(
        functools.partial(middle_kernel, n_col=n_col, share=share),
        [like(tile, hidden)] + [like(tile + extra, hidden)] * n_col,
        [SMEM_SPEC] + [VMEM_SPEC] * (3 + n_col),
        [pltpu.VMEM((width, hidden), F32)],
        4 * tile * width * hidden,
        n_col * tile * width * 4,
    )(me, weight, bias_row, cotangent, *parts)
    blocks = exchange(blocks, "col")
    block_share = call(
        functools.partial(share_kernel, tile=tile, share=share),
        like(extra, hidden),
        [VMEM_SPEC] * n_col,
        [],
        n_col * extra * hidden,
        n_col * (tile + extra) * hidden * 2,
    )(*blocks)
    shares = exchange([block_share] * n_row, "row")
    backs = call(
        functools.partial(backward_kernel, n_row=n_row, n_col=n_col),
        [like(tile, hidden)] * n_row,
        [SMEM_SPEC] * 4 + [VMEM_SPEC] * (1 + n_col),
        [pltpu.VMEM((n_col * tile, hidden), BF16), pltpu.VMEM((n_row * tile, hidden), F32)],
        slot_flops * hidden,
        tiles.size * 2,
    )(me, count, rows, cols, tiles, *blocks)
    backs = exchange(backs, "row")
    factor = (tile * n_row * n_col) ** (-0.5)
    own_share, grad_bias = call(
        functools.partial(scale_kernel, factor=factor),
        (like(share, hidden, F32), like(1, hidden, F32)),
        [VMEM_SPEC] * n_row,
        [],
        n_row * extra * hidden,
        n_row * extra * hidden * 2,
    )(*shares)
    all_shares = exchange([own_share] * n_col, "col")
    grad_features = call(
        features_kernel,
        like(tile, width),
        [VMEM_SPEC] * (1 + n_row),
        [],
        2 * tile * width * hidden,
        n_row * tile * hidden * 2,
    )(weight, *backs)
    grad_weight = call(
        join_kernel,
        like(width, hidden, F32),
        [SMEM_SPEC] + [VMEM_SPEC] * n_col,
        [],
        0,
        width * hidden * 8,
    )(me, *all_shares)
    return hidden_out, grad_features, grad_weight, grad_bias.reshape(hidden)


def solution(mesh):
    return jax.shard_map(
        local,
        mesh=mesh,
        in_specs=(
            P(("col", "row"), None),
            P(),
            P(),
            P(("row", "col"), None),
            P("row", "col", None, None, None),
            P("row", "col", None),
            P("row", "col", None),
            P("row", "col"),
        ),
        out_specs=(P(("row", "col"), None), P(("col", "row"), None), P(), P()),
        check_vma=False,
    )
```

```python
import functools

import jax
import jax.numpy as jnp
from jax import lax
from jax.experimental import pallas as pl
from jax.experimental.pallas import tpu as pltpu
from jax.sharding import PartitionSpec as P

F32 = jnp.float32
BF16 = jnp.bfloat16
ROOT_2_OVER_PI = 0.7978845608028654
CUBIC = 0.044715
VMEM_LIMIT = 48 * 1024 * 1024
BIAS_ROWS = 16

VMEM_SPEC = pl.BlockSpec(memory_space=pltpu.VMEM)
SMEM_SPEC = pl.BlockSpec(memory_space=pltpu.SMEM)


def call(kernel, out_shape, in_specs, scratch, flops, moved):
    return pl.pallas_call(
        kernel,
        out_shape=out_shape,
        in_specs=in_specs,
        out_specs=jax.tree.map(lambda _: VMEM_SPEC, out_shape),
        scratch_shapes=scratch,
        compiler_params=pltpu.CompilerParams(vmem_limit_bytes=VMEM_LIMIT),
        cost_estimate=pl.CostEstimate(flops=flops, bytes_accessed=moved, transcendentals=0),
    )


def partner(index, k, count):
    if count & (count - 1) == 0:
        return index ^ k
    return (k - index) % count


def exchange(blocks, axis, size, cores=1):
    count = size // cores
    received = []
    for k, block in enumerate(blocks):
        pairs = [(i, partner(i // cores, k, count) * cores + i % cores) for i in range(size)]
        moves = any(i != j for i, j in pairs)
        received.append(lax.ppermute(block, axis, pairs) if moves else block)
    return received


def block_at(index, size):
    return pl.ds(pl.multiple_of(index * size, size), size)


def summed(refs, rows=slice(None)):
    total = refs[0][rows, :].astype(F32)
    for ref in refs[1:]:
        total += ref[rows, :].astype(F32)
    return total


def bias_rows(bias):
    high = bias.astype(BF16).astype(F32)
    line = lax.broadcasted_iota(jnp.int32, (BIAS_ROWS, bias.shape[1]), 0)
    return jnp.where(line == 0, high, jnp.where(line == 1, bias - high, 0.0))


def dense_kernel(count_ref, row_ref, col_ref, tiles_ref, dense_ref, turned_ref, sum_ref, turned_sum):
    tile = tiles_ref.shape[1]
    sum_ref[...] = jnp.zeros_like(sum_ref)
    turned_sum[...] = jnp.zeros_like(turned_sum)

    def body(slot, carry):
        values = tiles_ref[slot].astype(F32)
        rows = block_at(row_ref[slot], tile)
        cols = block_at(col_ref[slot], tile)
        sum_ref[rows, cols] += values
        turned_sum[cols, rows] += values.T
        return carry

    lax.fori_loop(0, count_ref[0], body, 0)
    dense_ref[...] = sum_ref[...].astype(BF16)
    turned_ref[...] = turned_sum[...].astype(BF16)


def dense_product(refs, source_ref, acc_ref, turned):
    (dense_ref,) = refs
    rows = dense_ref.shape[0]
    step = 256 if rows % 256 == 0 else rows
    for first in range(0, rows, step):
        acc_ref[first : first + step, :] = jnp.dot(
            dense_ref[first : first + step, :], source_ref[...], preferred_element_type=F32
        )


def slot_product(refs, source_ref, acc_ref, turned):
    count_ref, row_ref, col_ref, tiles_ref = refs
    source_idx, target_idx = (row_ref, col_ref) if turned else (col_ref, row_ref)
    contract = 0 if turned else 1
    count = count_ref[0]
    tile = tiles_ref.shape[1]
    acc_ref[...] = jnp.zeros_like(acc_ref)

    def body(slot, carry):
        rows = source_ref[block_at(source_idx[slot], tile), :]
        acc_ref[block_at(target_idx[slot], tile), :] += lax.dot_general(
            tiles_ref[slot], rows, (((contract,), (0,)), ((), ())), preferred_element_type=F32
        )
        return carry

    lax.fori_loop(0, count, body, 0)


def forward_kernel(me_ref, cot_ref, *refs, product, n_adj, n_row):
    adjacency, sources = refs[:n_adj], refs[n_adj : n_adj + n_row]
    out_ref, source_ref, acc_ref = refs[n_adj + n_row :]
    tile = sources[0].shape[0]
    for k, ref in enumerate(sources):
        source_ref[block_at(partner(me_ref[0], k, n_row), tile), :] = ref[...]
    product(adjacency, source_ref, acc_ref, False)
    nodes = acc_ref.shape[0]
    out_ref[:nodes, :] = acc_ref[...].astype(BF16)
    out_ref[nodes:, :] = cot_ref[...]


def chip_kernel(me_ref, own_ref, other_ref, cot_ref, *refs):
    outs, sum_ref = refs[:-1], refs[-1]
    n_chip = len(outs)
    nodes = sum_ref.shape[0]
    tile = own_ref.shape[0] - nodes
    chip, core = me_ref[1], me_ref[2]
    sum_ref[...] = own_ref[:nodes, :].astype(F32) + other_ref[:nodes, :].astype(F32)
    for k, ref in enumerate(outs):
        ref[...] = sum_ref[block_at(partner(chip, k, n_chip), 2 * tile), :].astype(BF16)
    cot_ref[block_at(core, tile), :] = own_ref[nodes:, :]
    cot_ref[block_at(1 - core, tile), :] = other_ref[nodes:, :]


def middle_kernel(me_ref, weight_ref, bias_ref, cot_ref, *refs, n_chip, n_row):
    parts, (hidden_ref, grad_ref, *outs) = refs[:n_chip], refs[n_chip:-2]
    hidden_both, weight_acc = refs[-2:]
    tile = hidden_ref.shape[0]
    aggregated = summed(parts).astype(BF16)
    v = jnp.dot(aggregated, weight_ref[...], preferred_element_type=F32) + bias_ref[...]
    square = v * v
    t = jnp.tanh(ROOT_2_OVER_PI * (v + CUBIC * (square * v)))
    half = 0.5 * (1.0 + t)
    hidden_both[...] = v * half
    hidden_ref[...] = hidden_both[block_at(me_ref[2], tile), :].astype(BF16)
    slope = half + 0.5 * v * (1.0 - t * t) * (ROOT_2_OVER_PI * (1.0 + 3.0 * CUBIC * square))
    grad = (cot_ref[...].astype(F32) * slope).astype(BF16)
    grad_ref[...] = grad
    weight_acc[...] = lax.dot_general(
        aggregated, grad, (((0,), (0,)), ((), ())), preferred_element_type=F32
    )
    tail = bias_rows(jnp.sum(grad.astype(F32), axis=0, keepdims=True))
    share = outs[0].shape[0] - BIAS_ROWS
    for k, ref in enumerate(outs):
        mine = weight_acc[block_at(partner(me_ref[0], k, n_row), share), :]
        ref[...] = jnp.concatenate([mine, tail], axis=0).astype(BF16)


def share_kernel(*refs):
    parts, out_ref = refs[:-1], refs[-1]
    total = summed(parts)
    share = total.shape[0] - BIAS_ROWS
    tail = bias_rows(total[share : share + 1] + total[share + 1 : share + 2])
    out_ref[...] = jnp.concatenate([total[:share], tail], axis=0).astype(BF16)


def backward_kernel(me_ref, *refs, product, n_adj, n_row, n_chip, factor):
    adjacency, refs = refs[:n_adj], refs[n_adj:]
    sources, shares, refs = refs[:n_chip], refs[n_chip : 2 * n_chip], refs[2 * n_chip :]
    (bias_ref, *outs), (source_ref, acc_ref) = refs[:-2], refs[-2:]
    nodes = sources[0].shape[0]
    for k, ref in enumerate(sources):
        source_ref[block_at(partner(me_ref[1], k, n_chip), nodes), :] = ref[...]
    product(adjacency, source_ref, acc_ref, True)
    total = summed(shares) * factor
    share = total.shape[0] - BIAS_ROWS
    bias_ref[...] = total[share : share + 1] + total[share + 1 : share + 2]
    tile = nodes // 2
    for k, ref in enumerate(outs):
        ref[:tile, :] = acc_ref[block_at(partner(me_ref[0], k, n_row), tile), :].astype(BF16)
        ref[tile:, :] = total[:share].astype(BF16)


def final_kernel(me_ref, weight_ref, *refs, n_row):
    parts, (features_ref, grad_ref) = refs[:n_row], refs[n_row:]
    tile = features_ref.shape[0]
    features_ref[...] = lax.dot_general(
        summed(parts, slice(0, tile)).astype(BF16),
        weight_ref[...],
        (((1,), (1,)), ((), ())),
        preferred_element_type=F32,
    ).astype(BF16)
    share = parts[0].shape[0] - tile
    for k, ref in enumerate(parts):
        grad_ref[block_at(partner(me_ref[0], k, n_row), share), :] = ref[tile:, :].astype(F32)


def local(features, weight, bias_term, cotangent, tile_values, tile_row, tile_col, tile_count):
    n_row = lax.axis_size("row")
    n_col = lax.axis_size("col")
    n_chip = n_col // 2
    tile, width = features.shape
    hidden = weight.shape[1]
    slots = tile_values.shape[2]
    tiles = tile_values.reshape(slots, tile, tile)
    row_nodes, col_nodes = n_col * tile, n_row * tile
    bias_row = bias_term.reshape(1, hidden)
    col = lax.axis_index("col")
    me = jnp.stack([lax.axis_index("row"), col // 2, col % 2]).astype(jnp.int32)
    share = width // n_row
    matrix = 2 * tile * width * hidden

    def like(rows, columns, dtype=BF16):
        return jax.ShapeDtypeStruct((rows, columns), dtype)

    slot_args = (tile_count.reshape(1), tile_row.reshape(slots), tile_col.reshape(slots), tiles)
    if n_row * n_col <= 2 * slots:
        product, n_adj, adj_specs = dense_product, 1, [VMEM_SPEC]
        dense, turned = call(
            dense_kernel,
            (like(row_nodes, col_nodes), like(col_nodes, row_nodes)),
            [SMEM_SPEC] * 3 + [VMEM_SPEC],
            [pltpu.VMEM((row_nodes, col_nodes), F32), pltpu.VMEM((col_nodes, row_nodes), F32)],
            0,
            12 * row_nodes * col_nodes,
        )(*slot_args)
        adjacency, adjacency_back = (dense,), (turned,)
    else:
        product, n_adj, adj_specs = slot_product, 4, [SMEM_SPEC] * 3 + [VMEM_SPEC]
        adjacency = adjacency_back = slot_args

    sources = exchange([features] * n_row, "row", n_row)
    partial_value = call(
        functools.partial(forward_kernel, product=product, n_adj=n_adj, n_row=n_row),
        like(row_nodes + tile, width),
        [SMEM_SPEC, VMEM_SPEC] + adj_specs + [VMEM_SPEC] * n_row,
        [pltpu.VMEM((col_nodes, width), BF16), pltpu.VMEM((row_nodes, width), F32)],
        slots * matrix // 2,
        row_nodes * width * 8,
    )(me, cotangent, *adjacency, *sources)
    swapped = lax.ppermute(partial_value, "col", [(i, i ^ 1) for i in range(n_col)])
    cot_both, *pieces = call(
        chip_kernel,
        [like(2 * tile, hidden)] + [like(2 * tile, width)] * n_chip,
        [SMEM_SPEC] + [VMEM_SPEC] * 2,
        [pltpu.VMEM((row_nodes, width), F32)],
        row_nodes * width,
        row_nodes * width * 6,
    )(me, partial_value, swapped)
    parts = exchange(pieces, "col", n_col, 2)
    hidden_out, grad, *terms = call(
        functools.partial(middle_kernel, n_chip=n_chip, n_row=n_row),
        [like(tile, hidden), like(2 * tile, hidden)] + [like(share + BIAS_ROWS, hidden)] * n_row,
        [SMEM_SPEC] + [VMEM_SPEC] * (3 + n_chip),
        [pltpu.VMEM((2 * tile, hidden), F32), pltpu.VMEM((width, hidden), F32)],
        4 * matrix,
        n_chip * tile * width * 8,
    )(me, weight, bias_row, cot_both, *parts)
    grads = exchange([grad] * n_chip, "col", n_col, 2)
    terms = exchange(terms, "row", n_row)
    row_share = call(
        share_kernel,
        like(share + BIAS_ROWS, hidden),
        [VMEM_SPEC] * n_row,
        [],
        n_row * share * hidden,
        n_row * share * hidden * 2,
    )(*terms)
    shares = exchange([row_share] * n_chip, "col", n_col, 2)
    factor = (tile * n_row * n_col) ** (-0.5)
    grad_bias, *backs = call(
        functools.partial(
            backward_kernel, product=product, n_adj=n_adj, n_row=n_row, n_chip=n_chip, factor=factor
        ),
        [like(1, hidden, F32)] + [like(tile + share, hidden)] * n_row,
        [SMEM_SPEC] + adj_specs + [VMEM_SPEC] * (2 * n_chip),
        [pltpu.VMEM((row_nodes, hidden), BF16), pltpu.VMEM((col_nodes, hidden), F32)],
        slots * matrix // 2,
        row_nodes * hidden * 8,
    )(me, *adjacency_back, *grads, *shares)
    backs = exchange(backs, "row", n_row)
    grad_features, grad_weight = call(
        functools.partial(final_kernel, n_row=n_row),
        (like(tile, width), like(width, hidden, F32)),
        [SMEM_SPEC] + [VMEM_SPEC] * (1 + n_row),
        [],
        matrix,
        n_row * tile * hidden * 4,
    )(me, weight, *backs)
    return hidden_out, grad_features, grad_weight, grad_bias.reshape(hidden)


def solution(mesh):
    return jax.shard_map(
        local,
        mesh=mesh,
        in_specs=(
            P(("col", "row"), None),
            P(),
            P(),
            P(("row", "col"), None),
            P("row", "col", None, None, None),
            P("row", "col", None),
            P("row", "col", None),
            P("row", "col"),
        ),
        out_specs=(P(("row", "col"), None), P(("col", "row"), None), P(), P()),
        check_vma=False,
    )
```

```python
import functools

import jax
import jax.numpy as jnp
from jax import lax
from jax.experimental import pallas as pl
from jax.experimental.pallas import tpu as pltpu
from jax.sharding import PartitionSpec as P

F32 = jnp.float32
BF16 = jnp.bfloat16
ROOT_2_OVER_PI = 0.7978845608028654
CUBIC = 0.044715
VMEM_LIMIT = 48 * 1024 * 1024
BIAS_ROWS = 16

VMEM_SPEC = pl.BlockSpec(memory_space=pltpu.VMEM)
HBM_SPEC = pl.BlockSpec(memory_space=pltpu.HBM)
SMEM_SPEC = pl.BlockSpec(memory_space=pltpu.SMEM)


def call(kernel, out_shape, in_specs, scratch, flops, moved):
    return pl.pallas_call(
        kernel,
        out_shape=out_shape,
        in_specs=in_specs,
        out_specs=jax.tree.map(lambda _: VMEM_SPEC, out_shape),
        scratch_shapes=scratch,
        compiler_params=pltpu.CompilerParams(vmem_limit_bytes=VMEM_LIMIT),
        cost_estimate=pl.CostEstimate(flops=flops, bytes_accessed=moved, transcendentals=0),
    )


def partner(index, k, count):
    if count & (count - 1) == 0:
        return index ^ k
    return (k - index) % count


def far_first(count):
    return list(dict.fromkeys([count - 1, *range(1, count), 0]))


def exchange(blocks, axis, size, cores=1):
    count = size // cores
    received = []
    for k in far_first(count):
        pairs = [(i, partner(i // cores, k, count) * cores + i % cores) for i in range(size)]
        moves = any(i != j for i, j in pairs)
        received.append(lax.ppermute(blocks[k], axis, pairs) if moves else blocks[k])
    return received


def block_at(index, size):
    return pl.ds(pl.multiple_of(index * size, size), size)


def row_index():
    return lax.axis_index("row")


def chip_index():
    return lax.axis_index("col") // 2


def core_index():
    return lax.axis_index("col") % 2


def summed(refs):
    by_partner = dict(zip(far_first(len(refs)), refs))
    values = [by_partner[k][...].astype(F32) for k in sorted(by_partner)]
    while len(values) > 1:
        values = [sum(values[i + 1 : i + 2], values[i]) for i in range(0, len(values), 2)]
    return values[0]


def bias_rows(bias):
    high = bias.astype(BF16).astype(F32)
    line = lax.broadcasted_iota(jnp.int32, (BIAS_ROWS, bias.shape[1]), 0)
    return jnp.where(line == 0, high, jnp.where(line == 1, bias - high, 0.0))


def dense_kernel(
    count_ref, row_hbm, col_hbm, tiles_hbm, bias_hbm, dense_ref, bias_ref,
    row_ref, col_ref, tiles_ref, sum_ref, sems, tile_sems,
):
    slots, tile = tiles_ref.shape[0], tiles_ref.shape[1]
    chunks = tile_sems.shape[0]
    size = slots // chunks
    small = [
        pltpu.make_async_copy(row_hbm, row_ref, sems.at[0]),
        pltpu.make_async_copy(col_hbm, col_ref, sems.at[1]),
        pltpu.make_async_copy(bias_hbm, bias_ref, sems.at[2]),
    ]
    large = []
    for k in range(chunks):
        part = pl.ds(k * size, size)
        large.append(
            pltpu.make_async_copy(tiles_hbm.at[0, 0, part], tiles_ref.at[part], tile_sems.at[k])
        )
    for copy in small + large:
        copy.start()
    sum_ref[...] = jnp.zeros_like(sum_ref)
    for copy in small:
        copy.wait()
    count = count_ref[0, 0]

    def body(slot, carry):
        rows = block_at(row_ref[0, 0, slot], tile)
        cols = block_at(col_ref[0, 0, slot], tile)
        sum_ref[rows, cols] += tiles_ref[slot].astype(F32)
        return carry

    for k, copy in enumerate(large):
        copy.wait()
        lax.fori_loop(k * size, jnp.minimum(count, (k + 1) * size), body, 0)
    dense_ref[...] = sum_ref[...].astype(BF16)


def turn_kernel(dense_ref, after_ref, turned_ref):
    rows = dense_ref.shape[0]
    step = 256 if rows % 256 == 0 else rows
    for first in range(0, rows, step):
        turned_ref[:, first : first + step] = dense_ref[first : first + step, :].T


def dense_product(refs, source_ref, acc_ref, turned):
    (dense_ref,) = refs
    rows = dense_ref.shape[0]
    step = 256 if rows % 256 == 0 else rows
    for first in range(0, rows, step):
        acc_ref[first : first + step, :] = jnp.dot(
            dense_ref[first : first + step, :], source_ref[...], preferred_element_type=F32
        )


def slot_product(refs, source_ref, acc_ref, turned):
    count_ref, row_ref, col_ref, tiles_ref = refs
    source_idx, target_idx = (row_ref, col_ref) if turned else (col_ref, row_ref)
    contract = 0 if turned else 1
    tile = tiles_ref.shape[1]
    acc_ref[...] = jnp.zeros_like(acc_ref)

    def body(slot, carry):
        rows = source_ref[block_at(source_idx[slot], tile), :]
        acc_ref[block_at(target_idx[slot], tile), :] += lax.dot_general(
            tiles_ref[slot], rows, (((contract,), (0,)), ((), ())), preferred_element_type=F32
        )
        return carry

    lax.fori_loop(0, count_ref[0], body, 0)


def forward_kernel(cot_ref, *refs, product, n_adj, n_row):
    adjacency, sources = refs[:n_adj], refs[n_adj : n_adj + n_row]
    out_ref, source_ref, acc_ref = refs[n_adj + n_row :]
    tile = sources[0].shape[0]
    for k, ref in zip(far_first(n_row), sources):
        source_ref[block_at(partner(row_index(), k, n_row), tile), :] = ref[...]
    product(adjacency, source_ref, acc_ref, False)
    nodes = acc_ref.shape[0]
    out_ref[:nodes, :] = acc_ref[...].astype(BF16)
    out_ref[nodes:, :] = cot_ref[...]


def chip_kernel(own_ref, other_ref, *refs, k, n_chip):
    out_ref = refs[-1]
    rows = block_at(partner(chip_index(), k, n_chip), out_ref.shape[0])
    out_ref[...] = (own_ref[rows, :].astype(F32) + other_ref[rows, :].astype(F32)).astype(BF16)


def middle_kernel(weight_ref, bias_ref, own_ref, other_ref, *refs):
    parts, (hidden_ref, grad_ref, agg_ref) = refs[:-3], refs[-3:]
    aggregated = summed(parts).astype(BF16)
    agg_ref[...] = aggregated
    v = jnp.dot(aggregated, weight_ref[...], preferred_element_type=F32) + bias_ref[...]
    square = v * v
    t = jnp.tanh(ROOT_2_OVER_PI * (v + CUBIC * (square * v)))
    half = 0.5 * (1.0 + t)
    hidden_ref[...] = (v * half).astype(BF16)
    slope = half + 0.5 * v * (1.0 - t * t) * (ROOT_2_OVER_PI * (1.0 + 3.0 * CUBIC * square))
    tile = v.shape[0] // 2
    last = own_ref.shape[0] - tile
    own, other = own_ref[last:, :].astype(F32), other_ref[last:, :].astype(F32)
    for core in range(2):
        part = slice(core * tile, (core + 1) * tile)
        cot = jnp.where(core_index() == core, own, other)
        grad_ref[part, :] = (cot * slope[part, :]).astype(BF16)


def hidden_kernel(both_ref, out_ref):
    out_ref[...] = both_ref[block_at(core_index(), out_ref.shape[0]), :]


def term_kernel(agg_ref, grad_ref, after_ref, out_ref, acc_ref):
    grad = grad_ref[...]
    acc_ref[...] = lax.dot_general(
        agg_ref[...], grad, (((0,), (0,)), ((), ())), preferred_element_type=F32
    )
    half = acc_ref.shape[0] // 2
    out_ref[:half, :] = acc_ref[block_at(core_index(), half), :].astype(BF16)
    bias = jnp.sum(grad.astype(F32), axis=0, keepdims=True)
    out_ref[half:, :] = bias_rows(bias).astype(BF16)


def add_terms_kernel(after_ref, *refs):
    parts, out_ref = refs[:-1], refs[-1]
    total = summed(parts)
    half = total.shape[0] - BIAS_ROWS
    out_ref[:half, :] = total[:half].astype(BF16)
    out_ref[half:, :] = bias_rows(total[half : half + 1] + total[half + 1 : half + 2]).astype(BF16)


def scale_kernel(after_ref, *refs, factor):
    parts, (half_ref, bias_ref) = refs[:-2], refs[-2:]
    total = summed(parts) * factor
    half = half_ref.shape[0]
    half_ref[...] = total[:half]
    bias_ref[...] = total[half : half + 1] + total[half + 1 : half + 2]


def gather_kernel(*refs):
    parts, out_ref = refs[:-1], refs[-1]
    nodes = parts[0].shape[0]
    for k, ref in zip(far_first(len(parts)), parts):
        out_ref[block_at(partner(chip_index(), k, len(parts)), nodes), :] = ref[...]


def slot_back_kernel(count_ref, row_ref, col_ref, tiles_ref, source_ref, out_ref, acc_ref):
    slot_product((count_ref, row_ref, col_ref, tiles_ref), source_ref, acc_ref, True)
    out_ref[...] = acc_ref[...].astype(BF16)


def slot_piece_kernel(back_ref, *refs, k, n_row):
    out_ref = refs[-1]
    out_ref[...] = back_ref[block_at(partner(row_index(), k, n_row), out_ref.shape[0]), :]


def dense_piece_kernel(turned_ref, source_ref, *refs, k, n_row):
    out_ref = refs[-1]
    rows = block_at(partner(row_index(), k, n_row), out_ref.shape[0])
    out_ref[...] = jnp.dot(
        turned_ref[rows, :], source_ref[...], preferred_element_type=F32
    ).astype(BF16)


def features_kernel(weight_ref, *refs):
    parts, out_ref = refs[:-1], refs[-1]
    out_ref[...] = lax.dot_general(
        summed(parts).astype(BF16),
        weight_ref[...],
        (((1,), (1,)), ((), ())),
        preferred_element_type=F32,
    ).astype(BF16)


def join_kernel(own_ref, other_ref, bias_ref, weight_ref, bias_out):
    half = own_ref.shape[0]
    weight_ref[block_at(core_index(), half), :] = own_ref[...]
    weight_ref[block_at(1 - core_index(), half), :] = other_ref[...]
    bias_out[...] = bias_ref[...]


def in_turn(count, make):
    made, before = {}, []
    for k in far_first(count):
        made[k] = make(k, before)
        before = [made[k]]
    return made


def local(features, weight, bias_term, cotangent, tile_values, tile_row, tile_col, tile_count):
    n_row = lax.axis_size("row")
    n_col = lax.axis_size("col")
    n_chip = n_col // 2
    tile, width = features.shape
    hidden = weight.shape[1]
    slots = tile_values.shape[2]
    row_nodes, col_nodes = n_col * tile, n_row * tile
    bias_row = bias_term.reshape(1, hidden)
    half = width // 2
    matrix = 2 * tile * width * hidden
    block_bytes = 2 * tile * width

    def like(rows, columns, dtype=BF16):
        return jax.ShapeDtypeStruct((rows, columns), dtype)

    near = 1
    is_dense = n_row * n_col <= 2 * slots
    if is_dense:
        product, n_adj, adj_specs = dense_product, 1, [VMEM_SPEC]
        chunks = 4 if slots % 4 == 0 else 1
        dense, bias_row = call(
            dense_kernel,
            (like(row_nodes, col_nodes), like(1, hidden, F32)),
            [SMEM_SPEC] + [HBM_SPEC] * 4,
            [
                pltpu.SMEM((1, 1, slots), jnp.int32),
                pltpu.SMEM((1, 1, slots), jnp.int32),
                pltpu.VMEM((slots, tile, tile), BF16),
                pltpu.VMEM((row_nodes, col_nodes), F32),
                pltpu.SemaphoreType.DMA((3,)),
                pltpu.SemaphoreType.DMA((chunks,)),
            ],
            0,
            12 * row_nodes * col_nodes,
        )(tile_count, *(
            pltpu.with_memory_space_constraint(array, pltpu.HBM)
            for array in (tile_row, tile_col, tile_values, bias_row)
        ))
        adjacency = (dense,)
    else:
        product, n_adj, adj_specs = slot_product, 4, [SMEM_SPEC] * 3 + [VMEM_SPEC]
        adjacency = (
            tile_count.reshape(1),
            tile_row.reshape(slots),
            tile_col.reshape(slots),
            tile_values.reshape(slots, tile, tile),
        )

    sources = exchange([features] * n_row, "row", n_row)
    partial_value = call(
        functools.partial(forward_kernel, product=product, n_adj=n_adj, n_row=n_row),
        like(row_nodes + tile, width),
        [VMEM_SPEC] + adj_specs + [VMEM_SPEC] * n_row,
        [pltpu.VMEM((col_nodes, width), BF16), pltpu.VMEM((row_nodes, width), F32)],
        slots * matrix // 2,
        row_nodes * width * 8,
    )(cotangent, *adjacency, *sources)
    swapped = lax.ppermute(partial_value, "col", [(i, i ^ 1) for i in range(n_col)])

    def chip_piece(k, before):
        return call(
            functools.partial(chip_kernel, k=k, n_chip=n_chip),
            like(2 * tile, width),
            [VMEM_SPEC] * (2 + len(before)),
            [],
            2 * tile * width,
            6 * block_bytes,
        )(partial_value, swapped, *before)

    pieces = in_turn(n_chip, chip_piece)
    parts = exchange(pieces, "col", n_col, 2)
    if is_dense:
        turned = call(
            turn_kernel,
            like(col_nodes, row_nodes),
            [VMEM_SPEC] * 2,
            [],
            0,
            4 * row_nodes * col_nodes,
        )(dense, pieces[0])
    both_hidden, grad, aggregated = call(
        middle_kernel,
        [like(2 * tile, hidden), like(2 * tile, hidden), like(2 * tile, width)],
        [VMEM_SPEC] * (4 + n_chip),
        [],
        2 * matrix,
        n_chip * 2 * block_bytes,
    )(weight, bias_row, partial_value, swapped, *parts)
    grads = exchange([grad] * n_chip, "col", n_col, 2)
    hidden_out = call(
        hidden_kernel, like(tile, hidden), [VMEM_SPEC], [], 0, 2 * block_bytes
    )(both_hidden)
    term = call(
        term_kernel,
        like(half + BIAS_ROWS, hidden),
        [VMEM_SPEC] * 3,
        [pltpu.VMEM((width, hidden), F32)],
        2 * matrix,
        6 * block_bytes,
    )(aggregated, grad, grads[near])
    source = call(
        gather_kernel,
        like(row_nodes, hidden),
        [VMEM_SPEC] * n_chip,
        [],
        0,
        row_nodes * hidden * 4,
    )(*grads)
    if is_dense:
        piece_kernel, piece_args, piece_flops = dense_piece_kernel, (turned, source), n_col * matrix
    else:
        back = call(
            slot_back_kernel,
            like(col_nodes, hidden),
            [SMEM_SPEC] * 3 + [VMEM_SPEC] * 2,
            [pltpu.VMEM((col_nodes, hidden), F32)],
            slots * matrix // 2,
            row_nodes * hidden * 8,
        )(*adjacency, source)
        piece_kernel, piece_args, piece_flops = slot_piece_kernel, (back,), 0

    def back_piece(k, before):
        return call(
            functools.partial(piece_kernel, k=k, n_row=n_row),
            like(tile, hidden),
            [VMEM_SPEC] * (len(piece_args) + len(before)),
            [],
            piece_flops,
            2 * block_bytes,
        )(*piece_args, *before)

    made = in_turn(n_row, back_piece)
    backs = exchange(made, "row", n_row)
    terms = exchange([term] * n_row, "row", n_row)
    row_term = call(
        add_terms_kernel,
        like(half + BIAS_ROWS, hidden),
        [VMEM_SPEC] * (1 + n_row),
        [],
        n_row * half * hidden,
        n_row * half * hidden * 2,
    )(made[0], *terms)
    row_terms = exchange([row_term] * n_chip, "col", n_col, 2)
    factor = (tile * n_row * n_col) ** (-0.5)
    grad_features = call(
        features_kernel,
        like(tile, width),
        [VMEM_SPEC] * (1 + n_row),
        [],
        matrix,
        n_row * block_bytes,
    )(weight, *backs)
    own_half, bias_grad = call(
        functools.partial(scale_kernel, factor=factor),
        (like(half, hidden, F32), like(1, hidden, F32)),
        [HBM_SPEC] + [VMEM_SPEC] * n_chip,
        [],
        n_chip * half * hidden,
        n_chip * half * hidden * 2,
    )(pltpu.with_memory_space_constraint(grad_features, pltpu.HBM), *row_terms)
    other_half = lax.ppermute(own_half, "col", [(i, i ^ 1) for i in range(n_col)])
    grad_weight, grad_bias = call(
        join_kernel,
        (like(width, hidden, F32), like(1, hidden, F32)),
        [VMEM_SPEC] * 3,
        [],
        0,
        width * hidden * 8,
    )(own_half, other_half, bias_grad)
    return hidden_out, grad_features, grad_weight, grad_bias.reshape(hidden)


def solution(mesh):
    return jax.shard_map(
        local,
        mesh=mesh,
        in_specs=(
            P(("col", "row"), None),
            P(),
            P(),
            P(("row", "col"), None),
            P("row", "col", None, None, None),
            P("row", "col", None),
            P("row", "col", None),
            P("row", "col"),
        ),
        out_specs=(P(("row", "col"), None), P(("col", "row"), None), P(), P()),
        check_vma=False,
    )
```

```python
import functools

import jax
import jax.numpy as jnp
from jax import lax
from jax.experimental import pallas as pl
from jax.experimental.pallas import tpu as pltpu
from jax.sharding import PartitionSpec as P

F32 = jnp.float32
BF16 = jnp.bfloat16
ROOT_2_OVER_PI = 0.7978845608028654
CUBIC = 0.044715
VMEM_LIMIT = 48 * 1024 * 1024
BIAS_ROWS = 16

VMEM_SPEC = pl.BlockSpec(memory_space=pltpu.VMEM)
HBM_SPEC = pl.BlockSpec(memory_space=pltpu.HBM)
SMEM_SPEC = pl.BlockSpec(memory_space=pltpu.SMEM)


def call(kernel, out_shape, in_specs, scratch, flops, moved):
    return pl.pallas_call(
        kernel,
        out_shape=out_shape,
        in_specs=in_specs,
        out_specs=jax.tree.map(lambda _: VMEM_SPEC, out_shape),
        scratch_shapes=scratch,
        compiler_params=pltpu.CompilerParams(vmem_limit_bytes=VMEM_LIMIT),
        cost_estimate=pl.CostEstimate(flops=flops, bytes_accessed=moved, transcendentals=0),
    )


def partner(index, k, count):
    if count & (count - 1) == 0:
        return index ^ k
    return (k - index) % count


def far_first(count):
    return list(dict.fromkeys([count - 1, *range(1, count), 0]))


def pairs_of(k, size, cores):
    return [(i, partner(i // cores, k, size // cores) * cores + i % cores) for i in range(size)]


def exchange(blocks, axis, size, cores=1):
    received = []
    for k in far_first(size // cores):
        pairs = pairs_of(k, size, cores)
        moves = any(i != j for i, j in pairs)
        received.append(lax.ppermute(blocks[k], axis, pairs) if moves else blocks[k])
    return received


def swap_cores(block, size):
    return lax.ppermute(block, "col", [(i, i ^ 1) for i in range(size)])


def total_over(block, add, axis, size, cores=1):
    count = size // cores
    if count & (count - 1):
        return exchange([block] * count, axis, size, cores)
    terms, step = [block], 1
    while step < count:
        block = add(terms) if len(terms) > 1 else block
        terms = [lax.ppermute(block, axis, pairs_of(step, size, cores)), block]
        step *= 2
    return terms


def block_at(index, size):
    return pl.ds(pl.multiple_of(index * size, size), size)


def row_index():
    return lax.axis_index("row")


def chip_index():
    return lax.axis_index("col") // 2


def core_index():
    return lax.axis_index("col") % 2


def summed(refs):
    by_partner = dict(zip(far_first(len(refs)), refs))
    values = [by_partner[k][...].astype(F32) for k in sorted(by_partner)]
    while len(values) > 1:
        values = [sum(values[i + 1 : i + 2], values[i]) for i in range(0, len(values), 2)]
    return values[0]


def bias_rows(bias):
    high = bias.astype(BF16).astype(F32)
    line = lax.broadcasted_iota(jnp.int32, (BIAS_ROWS, bias.shape[1]), 0)
    return jnp.where(line == 0, high, jnp.where(line == 1, bias - high, 0.0))


def row_place(row, n_chip):
    return jnp.where(row % 2 == core_index(), 0, n_chip) + row // 2


def dense_kernel(
    count_ref, row_hbm, col_hbm, tiles_hbm, bias_hbm, dense_ref, bias_ref,
    row_ref, col_ref, tiles_ref, sum_ref, sems, tile_sems,
):
    slots, tile = tiles_ref.shape[0], tiles_ref.shape[1]
    n_chip = sum_ref.shape[0] // (2 * tile)
    chunks = tile_sems.shape[0]
    size = slots // chunks
    small = [
        pltpu.make_async_copy(row_hbm, row_ref, sems.at[0]),
        pltpu.make_async_copy(col_hbm, col_ref, sems.at[1]),
        pltpu.make_async_copy(bias_hbm, bias_ref, sems.at[2]),
    ]
    large = []
    for k in range(chunks):
        part = pl.ds(k * size, size)
        large.append(
            pltpu.make_async_copy(tiles_hbm.at[0, 0, part], tiles_ref.at[part], tile_sems.at[k])
        )
    for copy in small + large:
        copy.start()
    sum_ref[...] = jnp.zeros_like(sum_ref)
    for copy in small:
        copy.wait()
    count = count_ref[0, 0]

    def body(slot, carry):
        rows = block_at(row_place(row_ref[0, 0, slot], n_chip), tile)
        cols = block_at(col_ref[0, 0, slot], tile)
        sum_ref[rows, cols] += tiles_ref[slot].astype(F32)
        return carry

    for k, copy in enumerate(large):
        copy.wait()
        lax.fori_loop(k * size, jnp.minimum(count, (k + 1) * size), body, 0)
    dense_ref[...] = sum_ref[...].astype(BF16)


def turn_kernel(dense_ref, after_ref, turned_ref):
    rows = dense_ref.shape[0]
    step = 256 if rows % 256 == 0 else rows
    for first in range(0, rows, step):
        turned_ref[:, first : first + step] = dense_ref[first : first + step, :].T


def dense_dot(left, right):
    return jnp.dot(left, right, preferred_element_type=F32)


def gather_sources(sources, source_ref, index):
    tile = sources[0].shape[0]
    for k, ref in zip(far_first(len(sources)), sources):
        source_ref[block_at(partner(index, k, len(sources)), tile), :] = ref[...]


def slot_product(refs, source_ref, acc_ref, turned):
    count_ref, row_ref, col_ref, tiles_ref = refs
    tile = tiles_ref.shape[1]
    n_chip = (source_ref if turned else acc_ref).shape[0] // (2 * tile)
    contract = 0 if turned else 1
    acc_ref[...] = jnp.zeros_like(acc_ref)

    def body(slot, carry):
        places = [row_place(row_ref[slot], n_chip), col_ref[slot]]
        source, target = places if turned else places[::-1]
        acc_ref[block_at(target, tile), :] += lax.dot_general(
            tiles_ref[slot],
            source_ref[block_at(source, tile), :],
            (((contract,), (0,)), ((), ())),
            preferred_element_type=F32,
        )
        return carry

    lax.fori_loop(0, count_ref[0], body, 0)


def forward_other_kernel(dense_ref, *refs):
    sources, (other_ref, source_ref) = refs[:-2], refs[-2:]
    gather_sources(sources, source_ref, row_index())
    half = other_ref.shape[0]
    other_ref[...] = dense_dot(dense_ref[half:, :], source_ref[...]).astype(BF16)


def forward_own_kernel(dense_ref, source_ref, own_ref):
    own_ref[...] = dense_dot(dense_ref[: own_ref.shape[0], :], source_ref[...]).astype(BF16)


def slot_forward_kernel(count_ref, row_ref, col_ref, tiles_ref, *refs):
    sources, (other_ref, own_ref, source_ref, acc_ref) = refs[:-4], refs[-4:]
    gather_sources(sources, source_ref, row_index())
    slot_product((count_ref, row_ref, col_ref, tiles_ref), source_ref, acc_ref, False)
    half = own_ref.shape[0]
    own_ref[...] = acc_ref[:half, :].astype(BF16)
    other_ref[...] = acc_ref[half:, :].astype(BF16)


def chip_kernel(own_ref, other_ref, *refs, k, n_chip):
    out_ref = refs[-1]
    rows = block_at(partner(chip_index(), k, n_chip), out_ref.shape[0])
    out_ref[...] = (own_ref[rows, :].astype(F32) + other_ref[rows, :].astype(F32)).astype(BF16)


def middle_kernel(weight_ref, bias_ref, cot_ref, *refs):
    parts, (hidden_ref, grad_ref, agg_ref) = refs[:-3], refs[-3:]
    aggregated = summed(parts).astype(BF16)
    agg_ref[...] = aggregated
    v = dense_dot(aggregated, weight_ref[...]) + bias_ref[...]
    square = v * v
    t = jnp.tanh(ROOT_2_OVER_PI * (v + CUBIC * (square * v)))
    half = 0.5 * (1.0 + t)
    hidden_ref[...] = (v * half).astype(BF16)
    slope = half + 0.5 * v * (1.0 - t * t) * (ROOT_2_OVER_PI * (1.0 + 3.0 * CUBIC * square))
    grad_ref[...] = (cot_ref[...].astype(F32) * slope).astype(BF16)


def copy_kernel(in_ref, out_ref):
    out_ref[...] = in_ref[...]


def term_kernel(agg_ref, grad_ref, mine_ref, theirs_ref, acc_ref):
    grad = grad_ref[...]
    acc_ref[...] = lax.dot_general(
        agg_ref[...], grad, (((0,), (0,)), ((), ())), preferred_element_type=F32
    )
    half = acc_ref.shape[0] // 2
    bias = bias_rows(jnp.sum(grad.astype(F32), axis=0, keepdims=True)).astype(BF16)
    for ref, core in ((mine_ref, core_index()), (theirs_ref, 1 - core_index())):
        ref[:half, :] = acc_ref[block_at(core, half), :].astype(BF16)
        ref[half:, :] = bias


def add_terms_kernel(*refs, n_terms):
    total = summed(refs[:n_terms])
    out_ref = refs[-1]
    half = total.shape[0] - BIAS_ROWS
    out_ref[:half, :] = total[:half].astype(BF16)
    out_ref[half:, :] = bias_rows(total[half : half + 1] + total[half + 1 : half + 2]).astype(BF16)


def scale_kernel(after_ref, *refs, factor):
    parts, (half_ref, bias_ref) = refs[:-2], refs[-2:]
    total = summed(parts) * factor
    half = half_ref.shape[0]
    half_ref[...] = total[:half]
    bias_ref[...] = total[half : half + 1] + total[half + 1 : half + 2]


def gather_kernel(after_ref, *refs):
    gather_sources(refs[:-1], refs[-1], chip_index())


def back_own_kernel(turned_ref, source_ref, out_ref):
    out_ref[...] = dense_dot(turned_ref[:, : source_ref.shape[0]], source_ref[...])


def slot_back_kernel(count_ref, row_ref, col_ref, tiles_ref, own_ref, other_ref, out_ref, source_ref):
    half = own_ref.shape[0]
    source_ref[:half, :] = own_ref[...]
    source_ref[half:, :] = other_ref[...]
    slot_product((count_ref, row_ref, col_ref, tiles_ref), source_ref, out_ref, True)


def back_rows(refs, place):
    if len(refs) == 1:
        return refs[0][place, :]
    turned_ref, own_ref, source_ref = refs
    rest = dense_dot(turned_ref[place, source_ref.shape[0] :], source_ref[...])
    return own_ref[place, :] + rest


def back_near_kernel(*refs, targets):
    out_ref = refs[-1]
    tile = out_ref.shape[0] // len(targets)
    for i, k in enumerate(targets):
        place = block_at(row_index() ^ k, tile)
        out_ref[i * tile : (i + 1) * tile, :] = back_rows(refs[:-1], place).astype(BF16)


def back_far_kernel(*refs, k, at):
    near_ref, out_ref = refs[-2:]
    tile = out_ref.shape[0]
    rows = back_rows(refs[:-2], block_at(row_index() ^ k, tile))
    near = near_ref[at * tile : (at + 1) * tile, :].astype(F32)
    out_ref[...] = (rows + near).astype(BF16)


def features_kernel(weight_ref, near_ref, *refs):
    parts, out_ref = refs[:-1], refs[-1]
    total = near_ref[: out_ref.shape[0], :].astype(F32)
    for ref in parts:
        total += ref[...].astype(F32)
    out_ref[...] = lax.dot_general(
        total.astype(BF16),
        weight_ref[...],
        (((1,), (1,)), ((), ())),
        preferred_element_type=F32,
    ).astype(BF16)


def join_kernel(own_ref, other_ref, bias_ref, weight_ref, bias_out):
    half = own_ref.shape[0]
    weight_ref[block_at(core_index(), half), :] = own_ref[...]
    weight_ref[block_at(1 - core_index(), half), :] = other_ref[...]
    bias_out[...] = bias_ref[...]


def in_turn(count, make):
    made, before = {}, []
    for k in far_first(count):
        made[k] = make(k, before)
        before = [made[k]]
    return made


def local(features, weight, bias_term, cotangent, tile_values, tile_row, tile_col, tile_count):
    n_row = lax.axis_size("row")
    n_col = lax.axis_size("col")
    n_chip = n_col // 2
    tile, width = features.shape
    hidden = weight.shape[1]
    slots = tile_values.shape[2]
    row_nodes, col_nodes = n_col * tile, n_row * tile
    bias_row = bias_term.reshape(1, hidden)
    half = width // 2
    matrix = 2 * tile * width * hidden
    block_bytes = 2 * tile * width

    def like(rows, columns, dtype=BF16):
        return jax.ShapeDtypeStruct((rows, columns), dtype)

    near = 1
    own_nodes = n_chip * tile

    def add(terms, after=()):
        return call(
            functools.partial(add_terms_kernel, n_terms=len(terms)),
            like(half + BIAS_ROWS, hidden),
            [VMEM_SPEC] * (len(terms) + len(after)),
            [],
            len(terms) * half * hidden,
            len(terms) * half * hidden * 2,
        )(*terms, *after)

    is_dense = n_row * n_col <= 2 * slots
    if is_dense:
        chunks = 4 if slots % 4 == 0 else 1
        dense, bias_row = call(
            dense_kernel,
            (like(row_nodes, col_nodes), like(1, hidden, F32)),
            [SMEM_SPEC] + [HBM_SPEC] * 4,
            [
                pltpu.SMEM((1, 1, slots), jnp.int32),
                pltpu.SMEM((1, 1, slots), jnp.int32),
                pltpu.VMEM((slots, tile, tile), BF16),
                pltpu.VMEM((row_nodes, col_nodes), F32),
                pltpu.SemaphoreType.DMA((3,)),
                pltpu.SemaphoreType.DMA((chunks,)),
            ],
            0,
            12 * row_nodes * col_nodes,
        )(tile_count, *(
            pltpu.with_memory_space_constraint(array, pltpu.HBM)
            for array in (tile_row, tile_col, tile_values, bias_row)
        ))
    else:
        slot_args = (
            tile_count.reshape(1),
            tile_row.reshape(slots),
            tile_col.reshape(slots),
            tile_values.reshape(slots, tile, tile),
        )
        slot_specs = [SMEM_SPEC] * 3 + [VMEM_SPEC]

    sources = exchange([features] * n_row, "row", n_row)
    if is_dense:
        other, source = call(
            forward_other_kernel,
            (like(own_nodes, width), like(col_nodes, width)),
            [VMEM_SPEC] * (1 + n_row),
            [],
            slots * matrix // 2,
            row_nodes * width * 8,
        )(dense, *sources)
        own = call(
            forward_own_kernel,
            like(own_nodes, width),
            [VMEM_SPEC] * 2,
            [],
            slots * matrix // 2,
            row_nodes * width * 8,
        )(dense, source)
    else:
        other, own = call(
            slot_forward_kernel,
            (like(own_nodes, width), like(own_nodes, width)),
            slot_specs + [VMEM_SPEC] * n_row,
            [pltpu.VMEM((col_nodes, width), BF16), pltpu.VMEM((row_nodes, width), F32)],
            slots * matrix // 2,
            row_nodes * width * 8,
        )(*slot_args, *sources)
    swapped = swap_cores(other, n_col)

    def chip_piece(k, before):
        return call(
            functools.partial(chip_kernel, k=k, n_chip=n_chip),
            like(tile, width),
            [VMEM_SPEC] * (2 + len(before)),
            [],
            tile * width,
            3 * block_bytes,
        )(own, swapped, *before)

    pieces = in_turn(n_chip, chip_piece)
    parts = exchange(pieces, "col", n_col, 2)
    if is_dense:
        turned = call(
            turn_kernel,
            like(col_nodes, row_nodes),
            [VMEM_SPEC] * 2,
            [],
            0,
            4 * row_nodes * col_nodes,
        )(dense, pieces[0])
    hidden_own, grad, aggregated = call(
        middle_kernel,
        [like(tile, hidden), like(tile, hidden), like(tile, width)],
        [VMEM_SPEC] * (3 + n_chip),
        [],
        matrix,
        n_chip * block_bytes,
    )(weight, bias_row, cotangent, *parts)
    grads = exchange([grad] * n_chip, "col", n_col, 2)
    hidden_out = call(copy_kernel, like(tile, hidden), [VMEM_SPEC], [], 0, 2 * block_bytes)(hidden_own)
    mine, theirs = call(
        term_kernel,
        [like(half + BIAS_ROWS, hidden)] * 2,
        [VMEM_SPEC] * 2,
        [pltpu.VMEM((width, hidden), F32)],
        matrix,
        6 * block_bytes,
    )(aggregated, grad)
    chip_term = add([swap_cores(theirs, n_col), mine])
    row_terms = total_over(chip_term, add, "row", n_row)
    row_term = add(row_terms)

    own_grads = call(
        gather_kernel,
        like(own_nodes, hidden),
        [VMEM_SPEC] * (1 + n_chip),
        [],
        0,
        own_nodes * hidden * 4,
    )(chip_term, *grads)
    other_grads = swap_cores(own_grads, n_col)
    if is_dense:
        back_own = call(
            back_own_kernel,
            like(col_nodes, hidden, F32),
            [VMEM_SPEC] * 2,
            [],
            slots * matrix // 2,
            row_nodes * hidden * 8,
        )(turned, own_grads)
        back_args = (turned, back_own, other_grads)
    else:
        back = call(
            slot_back_kernel,
            like(col_nodes, hidden, F32),
            slot_specs + [VMEM_SPEC] * 2,
            [pltpu.VMEM((row_nodes, hidden), BF16)],
            slots * matrix // 2,
            row_nodes * hidden * 8,
        )(*slot_args, own_grads, other_grads)
        back_args = (back,)

    evens, odds = range(2, n_row, 2), range(3, n_row, 2)
    targets = [1, *evens]
    near_piece = call(
        functools.partial(back_near_kernel, targets=targets),
        like(len(targets) * tile, hidden),
        [VMEM_SPEC] * len(back_args),
        [],
        len(targets) * n_chip * matrix,
        len(targets) * 2 * block_bytes,
    )(*back_args)
    near = lax.ppermute(near_piece, "row", pairs_of(1, n_row, 1))
    backs = []
    for k in [0, *odds]:
        piece = call(
            functools.partial(back_far_kernel, k=k, at=(k - 1) // 2) if k else
            functools.partial(back_near_kernel, targets=[0]),
            like(tile, hidden),
            [VMEM_SPEC] * (len(back_args) + (k > 0)),
            [],
            n_chip * matrix,
            2 * block_bytes,
        )(*back_args, *([near] if k else []))
        backs.append(lax.ppermute(piece, "row", pairs_of(k, n_row, 1)) if k else piece)
    grad_features = call(
        features_kernel,
        like(tile, width),
        [VMEM_SPEC] * (2 + len(backs)),
        [],
        matrix,
        n_row * block_bytes,
    )(weight, near, *backs)
    all_terms = total_over(row_term, add, "col", n_col, 2)
    factor = (tile * n_row * n_col) ** (-0.5)
    own_half, bias_grad = call(
        functools.partial(scale_kernel, factor=factor),
        (like(half, hidden, F32), like(1, hidden, F32)),
        [HBM_SPEC] + [VMEM_SPEC] * len(all_terms),
        [],
        len(all_terms) * half * hidden,
        len(all_terms) * half * hidden * 2,
    )(pltpu.with_memory_space_constraint(grad_features, pltpu.HBM), *all_terms)
    other_half = swap_cores(own_half, n_col)
    grad_weight, grad_bias = call(
        join_kernel,
        (like(width, hidden, F32), like(1, hidden, F32)),
        [VMEM_SPEC] * 3,
        [],
        0,
        width * hidden * 8,
    )(own_half, other_half, bias_grad)
    return hidden_out, grad_features, grad_weight, grad_bias.reshape(hidden)


def solution(mesh):
    return jax.shard_map(
        local,
        mesh=mesh,
        in_specs=(
            P(("col", "row"), None),
            P(),
            P(),
            P(("row", "col"), None),
            P("row", "col", None, None, None),
            P("row", "col", None),
            P("row", "col", None),
            P("row", "col"),
        ),
        out_specs=(P(("row", "col"), None), P(("col", "row"), None), P(), P()),
        check_vma=False,
    )
```

```python
import functools

import jax
import jax.numpy as jnp
from jax import lax
from jax.experimental import pallas as pl
from jax.experimental.pallas import tpu as pltpu
from jax.sharding import PartitionSpec as P

F32 = jnp.float32
BF16 = jnp.bfloat16
ROOT_2_OVER_PI = 0.7978845608028654
CUBIC = 0.044715
VMEM_LIMIT = 48 * 1024 * 1024
BIAS_ROWS = 16

VMEM_SPEC = pl.BlockSpec(memory_space=pltpu.VMEM)
HBM_SPEC = pl.BlockSpec(memory_space=pltpu.HBM)
SMEM_SPEC = pl.BlockSpec(memory_space=pltpu.SMEM)


def call(kernel, out_shape, in_specs, scratch, flops, moved):
    return pl.pallas_call(
        kernel,
        out_shape=out_shape,
        in_specs=in_specs,
        out_specs=jax.tree.map(lambda _: VMEM_SPEC, out_shape),
        scratch_shapes=scratch,
        compiler_params=pltpu.CompilerParams(vmem_limit_bytes=VMEM_LIMIT),
        cost_estimate=pl.CostEstimate(flops=flops, bytes_accessed=moved, transcendentals=0),
    )


def partner(index, k, count):
    if count & (count - 1) == 0:
        return index ^ k
    return (k - index) % count


def far_first(count):
    return list(dict.fromkeys([count - 1, *range(1, count), 0]))


def pairs_of(k, size, cores):
    return [(i, partner(i // cores, k, size // cores) * cores + i % cores) for i in range(size)]


def exchange(blocks, axis, size, cores=1):
    received = []
    for k in far_first(size // cores):
        pairs = pairs_of(k, size, cores)
        moves = any(i != j for i, j in pairs)
        received.append(lax.ppermute(blocks[k], axis, pairs) if moves else blocks[k])
    return received


def swap_cores(block, size):
    return lax.ppermute(block, "col", [(i, i ^ 1) for i in range(size)])


def exchange_second(block, along, n_row, n_col):
    count = n_row if along == "row" else n_col // 2
    received = []
    for k in far_first(count):
        pairs = []
        for row in range(n_row):
            for col in range(1, n_col, 2):
                if along == "row":
                    target = col * n_row + partner(row, k, count)
                else:
                    target = (2 * partner(col // 2, k, count) + 1) * n_row + row
                pairs.append((col * n_row + row, target))
        received.append(lax.ppermute(block, ("col", "row"), pairs) if k else block)
    return received


def block_at(index, size):
    return pl.ds(pl.multiple_of(index * size, size), size)


def row_index():
    return lax.axis_index("row")


def chip_index():
    return lax.axis_index("col") // 2


def core_index():
    return lax.axis_index("col") % 2


def summed(refs):
    by_partner = dict(zip(far_first(len(refs)), refs))
    values = [by_partner[k][...].astype(F32) for k in sorted(by_partner)]
    while len(values) > 1:
        values = [sum(values[i + 1 : i + 2], values[i]) for i in range(0, len(values), 2)]
    return values[0]


def bias_rows(bias):
    high = bias.astype(BF16).astype(F32)
    line = lax.broadcasted_iota(jnp.int32, (BIAS_ROWS, bias.shape[1]), 0)
    return jnp.where(line == 0, high, jnp.where(line == 1, bias - high, 0.0))


def row_place(row, n_chip):
    return jnp.where(row % 2 == core_index(), 0, n_chip) + row // 2


def dense_kernel(
    count_ref, row_hbm, col_hbm, tiles_hbm, bias_hbm, dense_ref, bias_ref,
    row_ref, col_ref, tiles_ref, sum_ref, sems, tile_sems,
):
    slots, tile = tiles_ref.shape[0], tiles_ref.shape[1]
    n_chip = sum_ref.shape[0] // (2 * tile)
    chunks = tile_sems.shape[0]
    size = slots // chunks
    small = [
        pltpu.make_async_copy(row_hbm, row_ref, sems.at[0]),
        pltpu.make_async_copy(col_hbm, col_ref, sems.at[1]),
        pltpu.make_async_copy(bias_hbm, bias_ref, sems.at[2]),
    ]
    large = []
    for k in range(chunks):
        part = pl.ds(k * size, size)
        large.append(
            pltpu.make_async_copy(tiles_hbm.at[0, 0, part], tiles_ref.at[part], tile_sems.at[k])
        )
    for copy in small + large:
        copy.start()
    sum_ref[...] = jnp.zeros_like(sum_ref)
    for copy in small:
        copy.wait()
    count = count_ref[0, 0]

    def body(slot, carry):
        rows = block_at(row_place(row_ref[0, 0, slot], n_chip), tile)
        cols = block_at(col_ref[0, 0, slot], tile)
        sum_ref[rows, cols] += tiles_ref[slot].astype(F32)
        return carry

    for k, copy in enumerate(large):
        copy.wait()
        lax.fori_loop(k * size, jnp.minimum(count, (k + 1) * size), body, 0)
    dense_ref[...] = sum_ref[...].astype(BF16)


def turn_kernel(dense_ref, after_ref, turned_ref):
    rows = dense_ref.shape[0]
    step = 256 if rows % 256 == 0 else rows
    for first in range(0, rows, step):
        turned_ref[:, first : first + step] = dense_ref[first : first + step, :].T


def dense_dot(left, right):
    return jnp.dot(left, right, preferred_element_type=F32)


def gather_sources(sources, source_ref, index):
    tile = sources[0].shape[0]
    for k, ref in zip(far_first(len(sources)), sources):
        source_ref[block_at(partner(index, k, len(sources)), tile), :] = ref[...]


def slot_product(refs, source_ref, acc_ref, turned):
    count_ref, row_ref, col_ref, tiles_ref = refs
    tile = tiles_ref.shape[1]
    n_chip = (source_ref if turned else acc_ref).shape[0] // (2 * tile)
    contract = 0 if turned else 1
    acc_ref[...] = jnp.zeros_like(acc_ref)

    def body(slot, carry):
        places = [row_place(row_ref[slot], n_chip), col_ref[slot]]
        source, target = places if turned else places[::-1]
        acc_ref[block_at(target, tile), :] += lax.dot_general(
            tiles_ref[slot],
            source_ref[block_at(source, tile), :],
            (((contract,), (0,)), ((), ())),
            preferred_element_type=F32,
        )
        return carry

    lax.fori_loop(0, count_ref[0], body, 0)


def forward_other_kernel(dense_ref, *refs):
    sources, (other_ref, source_ref) = refs[:-2], refs[-2:]
    gather_sources(sources, source_ref, row_index())
    half = other_ref.shape[0]
    other_ref[...] = dense_dot(dense_ref[half:, :], source_ref[...]).astype(BF16)


def forward_own_kernel(dense_ref, source_ref, own_ref):
    own_ref[...] = dense_dot(dense_ref[: own_ref.shape[0], :], source_ref[...]).astype(BF16)


def slot_forward_kernel(count_ref, row_ref, col_ref, tiles_ref, *refs):
    sources, (other_ref, own_ref, source_ref, acc_ref) = refs[:-4], refs[-4:]
    gather_sources(sources, source_ref, row_index())
    slot_product((count_ref, row_ref, col_ref, tiles_ref), source_ref, acc_ref, False)
    half = own_ref.shape[0]
    own_ref[...] = acc_ref[:half, :].astype(BF16)
    other_ref[...] = acc_ref[half:, :].astype(BF16)


def chip_kernel(own_ref, other_ref, *refs, k, n_chip):
    out_ref = refs[-1]
    rows = block_at(partner(chip_index(), k, n_chip), out_ref.shape[0])
    out_ref[...] = (own_ref[rows, :].astype(F32) + other_ref[rows, :].astype(F32)).astype(BF16)


def middle_kernel(weight_ref, bias_ref, cot_ref, *refs):
    parts, (hidden_ref, grad_ref, agg_ref) = refs[:-3], refs[-3:]
    aggregated = summed(parts).astype(BF16)
    agg_ref[...] = aggregated
    v = dense_dot(aggregated, weight_ref[...]) + bias_ref[...]
    square = v * v
    t = jnp.tanh(ROOT_2_OVER_PI * (v + CUBIC * (square * v)))
    half = 0.5 * (1.0 + t)
    hidden_ref[...] = (v * half).astype(BF16)
    slope = half + 0.5 * v * (1.0 - t * t) * (ROOT_2_OVER_PI * (1.0 + 3.0 * CUBIC * square))
    grad_ref[...] = (cot_ref[...].astype(F32) * slope).astype(BF16)


def copy_kernel(in_ref, out_ref):
    out_ref[...] = in_ref[...]


def term_kernel(agg_ref, grad_ref, out_ref):
    grad = grad_ref[...]
    term = lax.dot_general(
        agg_ref[...], grad, (((0,), (0,)), ((), ())), preferred_element_type=F32
    )
    width = term.shape[0]
    out_ref[:width, :] = term.astype(BF16)
    out_ref[width:, :] = bias_rows(jnp.sum(grad.astype(F32), axis=0, keepdims=True)).astype(BF16)


def add_terms_kernel(*refs, n_terms):
    total = summed(refs[:n_terms])
    out_ref = refs[-1]
    width = total.shape[0] - BIAS_ROWS
    out_ref[:width, :] = total[:width].astype(BF16)
    bias = total[width : width + 1] + total[width + 1 : width + 2]
    out_ref[width:, :] = bias_rows(bias).astype(BF16)


def scale_kernel(after_ref, *refs, factor):
    parts, out_ref = refs[:-1], refs[-1]
    total = summed(parts) * factor
    width = total.shape[0] - BIAS_ROWS
    out_ref[:width, :] = total[:width]
    bias = total[width : width + 1] + total[width + 1 : width + 2]
    out_ref[width:, :] = jnp.broadcast_to(bias, (out_ref.shape[0] - width, bias.shape[1]))


def gather_kernel(after_ref, *refs):
    gather_sources(refs[:-1], refs[-1], chip_index())


def back_own_kernel(turned_ref, source_ref, out_ref):
    out_ref[...] = dense_dot(turned_ref[:, : source_ref.shape[0]], source_ref[...])


def back_piece_kernel(turned_ref, own_ref, source_ref, *refs, k, n_row):
    out_ref = refs[-1]
    rows = block_at(partner(row_index(), k, n_row), out_ref.shape[0])
    rest = dense_dot(turned_ref[rows, source_ref.shape[0] :], source_ref[...])
    out_ref[...] = (own_ref[rows, :] + rest).astype(BF16)


def slot_back_kernel(count_ref, row_ref, col_ref, tiles_ref, own_ref, other_ref, out_ref, source_ref):
    half = own_ref.shape[0]
    source_ref[:half, :] = own_ref[...]
    source_ref[half:, :] = other_ref[...]
    slot_product((count_ref, row_ref, col_ref, tiles_ref), source_ref, out_ref, True)


def slot_piece_kernel(back_ref, *refs, k, n_row):
    out_ref = refs[-1]
    rows = block_at(partner(row_index(), k, n_row), out_ref.shape[0])
    out_ref[...] = back_ref[rows, :].astype(BF16)


def features_kernel(weight_ref, *refs):
    parts, out_ref = refs[:-1], refs[-1]
    out_ref[...] = lax.dot_general(
        summed(parts).astype(BF16),
        weight_ref[...],
        (((1,), (1,)), ((), ())),
        preferred_element_type=F32,
    ).astype(BF16)


def join_kernel(own_ref, other_ref, weight_ref, bias_ref):
    width = weight_ref.shape[0]
    second = core_index() == 1
    weight_ref[...] = jnp.where(second, own_ref[:width, :], other_ref[:width, :])
    bias_ref[...] = jnp.where(second, own_ref[width : width + 1, :], other_ref[width : width + 1, :])


def in_turn(count, make):
    made, before = {}, []
    for k in far_first(count):
        made[k] = make(k, before)
        before = [made[k]]
    return made


def local(features, weight, bias_term, cotangent, tile_values, tile_row, tile_col, tile_count):
    n_row = lax.axis_size("row")
    n_col = lax.axis_size("col")
    n_chip = n_col // 2
    tile, width = features.shape
    hidden = weight.shape[1]
    slots = tile_values.shape[2]
    row_nodes, col_nodes = n_col * tile, n_row * tile
    bias_row = bias_term.reshape(1, hidden)
    matrix = 2 * tile * width * hidden
    block_bytes = 2 * tile * width

    def like(rows, columns, dtype=BF16):
        return jax.ShapeDtypeStruct((rows, columns), dtype)

    near = 1
    own_nodes = n_chip * tile

    def add(terms, after=()):
        return call(
            functools.partial(add_terms_kernel, n_terms=len(terms)),
            like(width + BIAS_ROWS, hidden),
            [VMEM_SPEC] * (len(terms) + len(after)),
            [],
            len(terms) * width * hidden,
            len(terms) * width * hidden * 2,
        )(*terms, *after)

    is_dense = n_row * n_col <= 2 * slots
    if is_dense:
        chunks = 4 if slots % 4 == 0 else 1
        dense, bias_row = call(
            dense_kernel,
            (like(row_nodes, col_nodes), like(1, hidden, F32)),
            [SMEM_SPEC] + [HBM_SPEC] * 4,
            [
                pltpu.SMEM((1, 1, slots), jnp.int32),
                pltpu.SMEM((1, 1, slots), jnp.int32),
                pltpu.VMEM((slots, tile, tile), BF16),
                pltpu.VMEM((row_nodes, col_nodes), F32),
                pltpu.SemaphoreType.DMA((3,)),
                pltpu.SemaphoreType.DMA((chunks,)),
            ],
            0,
            12 * row_nodes * col_nodes,
        )(tile_count, *(
            pltpu.with_memory_space_constraint(array, pltpu.HBM)
            for array in (tile_row, tile_col, tile_values, bias_row)
        ))
    else:
        slot_args = (
            tile_count.reshape(1),
            tile_row.reshape(slots),
            tile_col.reshape(slots),
            tile_values.reshape(slots, tile, tile),
        )
        slot_specs = [SMEM_SPEC] * 3 + [VMEM_SPEC]

    sources = exchange([features] * n_row, "row", n_row)
    if is_dense:
        other, source = call(
            forward_other_kernel,
            (like(own_nodes, width), like(col_nodes, width)),
            [VMEM_SPEC] * (1 + n_row),
            [],
            slots * matrix // 2,
            row_nodes * width * 8,
        )(dense, *sources)
        own = call(
            forward_own_kernel,
            like(own_nodes, width),
            [VMEM_SPEC] * 2,
            [],
            slots * matrix // 2,
            row_nodes * width * 8,
        )(dense, source)
    else:
        other, own = call(
            slot_forward_kernel,
            (like(own_nodes, width), like(own_nodes, width)),
            slot_specs + [VMEM_SPEC] * n_row,
            [pltpu.VMEM((col_nodes, width), BF16), pltpu.VMEM((row_nodes, width), F32)],
            slots * matrix // 2,
            row_nodes * width * 8,
        )(*slot_args, *sources)
    swapped = swap_cores(other, n_col)

    def chip_piece(k, before):
        return call(
            functools.partial(chip_kernel, k=k, n_chip=n_chip),
            like(tile, width),
            [VMEM_SPEC] * (2 + len(before)),
            [],
            tile * width,
            3 * block_bytes,
        )(own, swapped, *before)

    pieces = in_turn(n_chip, chip_piece)
    parts = exchange(pieces, "col", n_col, 2)
    if is_dense:
        turned = call(
            turn_kernel,
            like(col_nodes, row_nodes),
            [VMEM_SPEC] * 2,
            [],
            0,
            4 * row_nodes * col_nodes,
        )(dense, pieces[0])
    hidden_own, grad, aggregated = call(
        middle_kernel,
        [like(tile, hidden), like(tile, hidden), like(tile, width)],
        [VMEM_SPEC] * (3 + n_chip),
        [],
        matrix,
        n_chip * block_bytes,
    )(weight, bias_row, cotangent, *parts)
    grads = exchange([grad] * n_chip, "col", n_col, 2)
    hidden_out = call(copy_kernel, like(tile, hidden), [VMEM_SPEC], [], 0, 2 * block_bytes)(hidden_own)
    term = call(
        term_kernel,
        like(width + BIAS_ROWS, hidden),
        [VMEM_SPEC] * 2,
        [],
        matrix,
        6 * block_bytes,
    )(aggregated, grad)
    first_term = lax.ppermute(term, "col", [(i - 1, i) for i in range(1, n_col, 2)])
    chip_term = add([first_term, term])
    row_terms = exchange_second(chip_term, "row", n_row, n_col)

    own_grads = call(
        gather_kernel,
        like(own_nodes, hidden),
        [VMEM_SPEC] * (1 + n_chip),
        [],
        0,
        own_nodes * hidden * 4,
    )(chip_term, *grads)
    other_grads = swap_cores(own_grads, n_col)
    if is_dense:
        back_own = call(
            back_own_kernel,
            like(col_nodes, hidden, F32),
            [VMEM_SPEC] * 2,
            [],
            slots * matrix // 2,
            row_nodes * hidden * 8,
        )(turned, own_grads)
        piece_kernel, piece_args = back_piece_kernel, (turned, back_own, other_grads)
    else:
        back = call(
            slot_back_kernel,
            like(col_nodes, hidden, F32),
            slot_specs + [VMEM_SPEC] * 2,
            [pltpu.VMEM((row_nodes, hidden), BF16)],
            slots * matrix // 2,
            row_nodes * hidden * 8,
        )(*slot_args, own_grads, other_grads)
        piece_kernel, piece_args = slot_piece_kernel, (back,)

    def back_piece(k, before):
        return call(
            functools.partial(piece_kernel, k=k, n_row=n_row),
            like(tile, hidden),
            [VMEM_SPEC] * (len(piece_args) + len(before)),
            [],
            n_chip * matrix,
            2 * block_bytes,
        )(*piece_args, *before)

    made = in_turn(n_row, back_piece)
    backs = exchange(made, "row", n_row)
    row_term = add(row_terms, [made[0]])
    grad_features = call(
        features_kernel,
        like(tile, width),
        [VMEM_SPEC] * (1 + n_row),
        [],
        matrix,
        n_row * block_bytes,
    )(weight, *backs)
    all_terms = exchange_second(row_term, "col", n_row, n_col)
    factor = (tile * n_row * n_col) ** (-0.5)
    total = call(
        functools.partial(scale_kernel, factor=factor),
        like(width + 8, hidden, F32),
        [HBM_SPEC] + [VMEM_SPEC] * len(all_terms),
        [],
        len(all_terms) * width * hidden,
        len(all_terms) * width * hidden * 2,
    )(pltpu.with_memory_space_constraint(grad_features, pltpu.HBM), *all_terms)
    second_total = lax.ppermute(total, "col", [(i, i - 1) for i in range(1, n_col, 2)])
    grad_weight, grad_bias = call(
        join_kernel,
        (like(width, hidden, F32), like(1, hidden, F32)),
        [VMEM_SPEC] * 2,
        [],
        0,
        width * hidden * 8,
    )(total, second_total)
    return hidden_out, grad_features, grad_weight, grad_bias.reshape(hidden)


def solution(mesh):
    return jax.shard_map(
        local,
        mesh=mesh,
        in_specs=(
            P(("col", "row"), None),
            P(),
            P(),
            P(("row", "col"), None),
            P("row", "col", None, None, None),
            P("row", "col", None),
            P("row", "col", None),
            P("row", "col"),
        ),
        out_specs=(P(("row", "col"), None), P(("col", "row"), None), P(), P()),
        check_vma=False,
    )
```

```python
import functools

import jax
import jax.numpy as jnp
from jax import lax
from jax.experimental import pallas as pl
from jax.experimental.pallas import tpu as pltpu
from jax.sharding import PartitionSpec as P

F32 = jnp.float32
BF16 = jnp.bfloat16
ROOT_2_OVER_PI = 0.7978845608028654
CUBIC = 0.044715
VMEM_LIMIT = 48 * 1024 * 1024
BIAS_ROWS = 16
ROW_SUM_WEIGHT = 250
FEATURES_WEIGHT = 150

VMEM_SPEC = pl.BlockSpec(memory_space=pltpu.VMEM)
HBM_SPEC = pl.BlockSpec(memory_space=pltpu.HBM)
SMEM_SPEC = pl.BlockSpec(memory_space=pltpu.SMEM)


def call(kernel, out_shape, in_specs, scratch, flops, moved):
    return pl.pallas_call(
        kernel,
        out_shape=out_shape,
        in_specs=in_specs,
        out_specs=jax.tree.map(lambda _: VMEM_SPEC, out_shape),
        scratch_shapes=scratch,
        compiler_params=pltpu.CompilerParams(vmem_limit_bytes=VMEM_LIMIT),
        cost_estimate=pl.CostEstimate(flops=flops, bytes_accessed=moved, transcendentals=0),
    )


def partner(index, k, count):
    if count & (count - 1) == 0:
        return index ^ k
    return (k - index) % count


def far_first(count):
    return list(dict.fromkeys([count - 1, *range(1, count), 0]))


def pairs_of(k, size, cores):
    return [(i, partner(i // cores, k, size // cores) * cores + i % cores) for i in range(size)]


def exchange(blocks, axis, size, cores=1):
    received = []
    for k in far_first(size // cores):
        pairs = pairs_of(k, size, cores)
        moves = any(i != j for i, j in pairs)
        received.append(lax.ppermute(blocks[k], axis, pairs) if moves else blocks[k])
    return received


def swap_cores(block, size):
    return lax.ppermute(block, "col", [(i, i ^ 1) for i in range(size)])


def total_over(block, add, axis, size, cores=1):
    count = size // cores
    if count & (count - 1):
        return exchange([block] * count, axis, size, cores)
    terms, step = [block], 1
    while step < count:
        block = add(terms) if len(terms) > 1 else block
        terms = [lax.ppermute(block, axis, pairs_of(step, size, cores)), block]
        step *= 2
    return terms


def block_at(index, size):
    return pl.ds(pl.multiple_of(index * size, size), size)


def row_index():
    return lax.axis_index("row")


def chip_index():
    return lax.axis_index("col") // 2


def core_index():
    return lax.axis_index("col") % 2


def summed(refs):
    by_partner = dict(zip(far_first(len(refs)), refs))
    values = [by_partner[k][...].astype(F32) for k in sorted(by_partner)]
    while len(values) > 1:
        values = [sum(values[i + 1 : i + 2], values[i]) for i in range(0, len(values), 2)]
    return values[0]


def bias_rows(bias):
    high = bias.astype(BF16).astype(F32)
    line = lax.broadcasted_iota(jnp.int32, (BIAS_ROWS, bias.shape[1]), 0)
    return jnp.where(line == 0, high, jnp.where(line == 1, bias - high, 0.0))


def row_place(row, n_chip):
    return jnp.where(row % 2 == core_index(), 0, n_chip) + row // 2


def dense_kernel(
    count_ref, row_hbm, col_hbm, tiles_hbm, bias_hbm, dense_ref, bias_ref,
    row_ref, col_ref, tiles_ref, sum_ref, sems, tile_sems,
):
    slots, tile = tiles_ref.shape[0], tiles_ref.shape[1]
    n_chip = sum_ref.shape[0] // (2 * tile)
    chunks = tile_sems.shape[0]
    size = slots // chunks
    small = [
        pltpu.make_async_copy(row_hbm, row_ref, sems.at[0]),
        pltpu.make_async_copy(col_hbm, col_ref, sems.at[1]),
        pltpu.make_async_copy(bias_hbm, bias_ref, sems.at[2]),
    ]
    large = []
    for k in range(chunks):
        part = pl.ds(k * size, size)
        large.append(
            pltpu.make_async_copy(tiles_hbm.at[0, 0, part], tiles_ref.at[part], tile_sems.at[k])
        )
    for copy in small + large:
        copy.start()
    sum_ref[...] = jnp.zeros_like(sum_ref)
    for copy in small:
        copy.wait()
    count = count_ref[0, 0]

    def body(slot, carry):
        rows = block_at(row_place(row_ref[0, 0, slot], n_chip), tile)
        cols = block_at(col_ref[0, 0, slot], tile)
        sum_ref[rows, cols] += tiles_ref[slot].astype(F32)
        return carry

    for k, copy in enumerate(large):
        copy.wait()
        lax.fori_loop(k * size, jnp.minimum(count, (k + 1) * size), body, 0)
    dense_ref[...] = sum_ref[...].astype(BF16)


def turn_kernel(dense_ref, after_ref, turned_ref):
    rows = dense_ref.shape[0]
    step = 256 if rows % 256 == 0 else rows
    for first in range(0, rows, step):
        turned_ref[:, first : first + step] = dense_ref[first : first + step, :].T


def dense_dot(left, right):
    return jnp.dot(left, right, preferred_element_type=F32)


def gather_sources(sources, source_ref, index):
    tile = sources[0].shape[0]
    for k, ref in zip(far_first(len(sources)), sources):
        source_ref[block_at(partner(index, k, len(sources)), tile), :] = ref[...]


def slot_product(refs, source_ref, acc_ref, turned):
    count_ref, row_ref, col_ref, tiles_ref = refs
    tile = tiles_ref.shape[1]
    n_chip = (source_ref if turned else acc_ref).shape[0] // (2 * tile)
    contract = 0 if turned else 1
    acc_ref[...] = jnp.zeros_like(acc_ref)

    def body(slot, carry):
        places = [row_place(row_ref[slot], n_chip), col_ref[slot]]
        source, target = places if turned else places[::-1]
        acc_ref[block_at(target, tile), :] += lax.dot_general(
            tiles_ref[slot],
            source_ref[block_at(source, tile), :],
            (((contract,), (0,)), ((), ())),
            preferred_element_type=F32,
        )
        return carry

    lax.fori_loop(0, count_ref[0], body, 0)


def forward_other_kernel(dense_ref, *refs):
    sources, (other_ref, source_ref) = refs[:-2], refs[-2:]
    gather_sources(sources, source_ref, row_index())
    half = other_ref.shape[0]
    other_ref[...] = dense_dot(dense_ref[half:, :], source_ref[...]).astype(BF16)


def forward_own_kernel(dense_ref, source_ref, own_ref):
    own_ref[...] = dense_dot(dense_ref[: own_ref.shape[0], :], source_ref[...]).astype(BF16)


def slot_forward_kernel(count_ref, row_ref, col_ref, tiles_ref, *refs):
    sources, (other_ref, own_ref, source_ref, acc_ref) = refs[:-4], refs[-4:]
    gather_sources(sources, source_ref, row_index())
    slot_product((count_ref, row_ref, col_ref, tiles_ref), source_ref, acc_ref, False)
    half = own_ref.shape[0]
    own_ref[...] = acc_ref[:half, :].astype(BF16)
    other_ref[...] = acc_ref[half:, :].astype(BF16)


def chip_kernel(own_ref, other_ref, *refs, k, n_chip):
    out_ref = refs[-1]
    rows = block_at(partner(chip_index(), k, n_chip), out_ref.shape[0])
    out_ref[...] = (own_ref[rows, :].astype(F32) + other_ref[rows, :].astype(F32)).astype(BF16)


def middle_kernel(weight_ref, bias_ref, cot_ref, *refs):
    parts, (hidden_ref, grad_ref, agg_ref) = refs[:-3], refs[-3:]
    aggregated = summed(parts).astype(BF16)
    agg_ref[...] = aggregated
    v = dense_dot(aggregated, weight_ref[...]) + bias_ref[...]
    square = v * v
    t = jnp.tanh(ROOT_2_OVER_PI * (v + CUBIC * (square * v)))
    half = 0.5 * (1.0 + t)
    hidden_ref[...] = (v * half).astype(BF16)
    slope = half + 0.5 * v * (1.0 - t * t) * (ROOT_2_OVER_PI * (1.0 + 3.0 * CUBIC * square))
    grad_ref[...] = (cot_ref[...].astype(F32) * slope).astype(BF16)


def copy_kernel(in_ref, out_ref):
    out_ref[...] = in_ref[...]


def term_kernel(agg_ref, grad_ref, mine_ref, theirs_ref, acc_ref):
    grad = grad_ref[...]
    acc_ref[...] = lax.dot_general(
        agg_ref[...], grad, (((0,), (0,)), ((), ())), preferred_element_type=F32
    )
    half = acc_ref.shape[0] // 2
    bias = bias_rows(jnp.sum(grad.astype(F32), axis=0, keepdims=True)).astype(BF16)
    for ref, core in ((mine_ref, core_index()), (theirs_ref, 1 - core_index())):
        ref[:half, :] = acc_ref[block_at(core, half), :].astype(BF16)
        ref[half:, :] = bias


def add_terms_kernel(*refs, n_terms):
    total = summed(refs[:n_terms])
    out_ref = refs[-1]
    half = total.shape[0] - BIAS_ROWS
    out_ref[:half, :] = total[:half].astype(BF16)
    out_ref[half:, :] = bias_rows(total[half : half + 1] + total[half + 1 : half + 2]).astype(BF16)


def scale_kernel(after_ref, *refs, factor):
    parts, (half_ref, bias_ref) = refs[:-2], refs[-2:]
    total = summed(parts) * factor
    half = half_ref.shape[0]
    half_ref[...] = total[:half]
    bias_ref[...] = total[half : half + 1] + total[half + 1 : half + 2]


def gather_kernel(after_ref, *refs):
    gather_sources(refs[:-1], refs[-1], chip_index())


def back_own_kernel(turned_ref, source_ref, out_ref):
    out_ref[...] = dense_dot(turned_ref[:, : source_ref.shape[0]], source_ref[...])


def back_piece_kernel(turned_ref, own_ref, source_ref, *refs, k, n_row):
    out_ref = refs[-1]
    rows = block_at(partner(row_index(), k, n_row), out_ref.shape[0])
    rest = dense_dot(turned_ref[rows, source_ref.shape[0] :], source_ref[...])
    out_ref[...] = (own_ref[rows, :] + rest).astype(BF16)


def slot_back_kernel(count_ref, row_ref, col_ref, tiles_ref, own_ref, other_ref, out_ref, source_ref):
    half = own_ref.shape[0]
    source_ref[:half, :] = own_ref[...]
    source_ref[half:, :] = other_ref[...]
    slot_product((count_ref, row_ref, col_ref, tiles_ref), source_ref, out_ref, True)


def slot_piece_kernel(back_ref, *refs, k, n_row):
    out_ref = refs[-1]
    rows = block_at(partner(row_index(), k, n_row), out_ref.shape[0])
    out_ref[...] = back_ref[rows, :].astype(BF16)


def features_kernel(weight_ref, *refs):
    parts, out_ref = refs[:-1], refs[-1]
    out_ref[...] = lax.dot_general(
        summed(parts).astype(BF16),
        weight_ref[...],
        (((1,), (1,)), ((), ())),
        preferred_element_type=F32,
    ).astype(BF16)


def join_kernel(own_ref, other_ref, bias_ref, weight_ref, bias_out):
    half = own_ref.shape[0]
    weight_ref[block_at(core_index(), half), :] = own_ref[...]
    weight_ref[block_at(1 - core_index(), half), :] = other_ref[...]
    bias_out[...] = bias_ref[...]


def in_turn(count, make):
    made, before = {}, []
    for k in far_first(count):
        made[k] = make(k, before)
        before = [made[k]]
    return made


def local(features, weight, bias_term, cotangent, tile_values, tile_row, tile_col, tile_count):
    n_row = lax.axis_size("row")
    n_col = lax.axis_size("col")
    n_chip = n_col // 2
    tile, width = features.shape
    hidden = weight.shape[1]
    slots = tile_values.shape[2]
    row_nodes, col_nodes = n_col * tile, n_row * tile
    bias_row = bias_term.reshape(1, hidden)
    half = width // 2
    matrix = 2 * tile * width * hidden
    block_bytes = 2 * tile * width

    def like(rows, columns, dtype=BF16):
        return jax.ShapeDtypeStruct((rows, columns), dtype)

    near = 1
    own_nodes = n_chip * tile

    def add(terms, flops=0):
        return call(
            functools.partial(add_terms_kernel, n_terms=len(terms)),
            like(half + BIAS_ROWS, hidden),
            [VMEM_SPEC] * len(terms),
            [],
            flops or len(terms) * half * hidden,
            len(terms) * half * hidden * 2,
        )(*terms)

    is_dense = n_row * n_col <= 2 * slots
    if is_dense:
        chunks = 4 if slots % 4 == 0 else 1
        dense, bias_row = call(
            dense_kernel,
            (like(row_nodes, col_nodes), like(1, hidden, F32)),
            [SMEM_SPEC] + [HBM_SPEC] * 4,
            [
                pltpu.SMEM((1, 1, slots), jnp.int32),
                pltpu.SMEM((1, 1, slots), jnp.int32),
                pltpu.VMEM((slots, tile, tile), BF16),
                pltpu.VMEM((row_nodes, col_nodes), F32),
                pltpu.SemaphoreType.DMA((3,)),
                pltpu.SemaphoreType.DMA((chunks,)),
            ],
            0,
            12 * row_nodes * col_nodes,
        )(tile_count, *(
            pltpu.with_memory_space_constraint(array, pltpu.HBM)
            for array in (tile_row, tile_col, tile_values, bias_row)
        ))
    else:
        slot_args = (
            tile_count.reshape(1),
            tile_row.reshape(slots),
            tile_col.reshape(slots),
            tile_values.reshape(slots, tile, tile),
        )
        slot_specs = [SMEM_SPEC] * 3 + [VMEM_SPEC]

    sources = exchange([features] * n_row, "row", n_row)
    if is_dense:
        other, source = call(
            forward_other_kernel,
            (like(own_nodes, width), like(col_nodes, width)),
            [VMEM_SPEC] * (1 + n_row),
            [],
            slots * matrix // 2,
            row_nodes * width * 8,
        )(dense, *sources)
        own = call(
            forward_own_kernel,
            like(own_nodes, width),
            [VMEM_SPEC] * 2,
            [],
            slots * matrix // 2,
            row_nodes * width * 8,
        )(dense, source)
    else:
        other, own = call(
            slot_forward_kernel,
            (like(own_nodes, width), like(own_nodes, width)),
            slot_specs + [VMEM_SPEC] * n_row,
            [pltpu.VMEM((col_nodes, width), BF16), pltpu.VMEM((row_nodes, width), F32)],
            slots * matrix // 2,
            row_nodes * width * 8,
        )(*slot_args, *sources)
    swapped = swap_cores(other, n_col)

    def chip_piece(k, before):
        return call(
            functools.partial(chip_kernel, k=k, n_chip=n_chip),
            like(tile, width),
            [VMEM_SPEC] * (2 + len(before)),
            [],
            tile * width,
            3 * block_bytes,
        )(own, swapped, *before)

    pieces = in_turn(n_chip, chip_piece)
    parts = exchange(pieces, "col", n_col, 2)
    if is_dense:
        turned = call(
            turn_kernel,
            like(col_nodes, row_nodes),
            [VMEM_SPEC] * 2,
            [],
            0,
            4 * row_nodes * col_nodes,
        )(dense, pieces[0])
    hidden_own, grad, aggregated = call(
        middle_kernel,
        [like(tile, hidden), like(tile, hidden), like(tile, width)],
        [VMEM_SPEC] * (3 + n_chip),
        [],
        matrix,
        n_chip * block_bytes,
    )(weight, bias_row, cotangent, *parts)
    grads = exchange([grad] * n_chip, "col", n_col, 2)
    hidden_out = call(copy_kernel, like(tile, hidden), [VMEM_SPEC], [], 0, 2 * block_bytes)(hidden_own)
    mine, theirs = call(
        term_kernel,
        [like(half + BIAS_ROWS, hidden)] * 2,
        [VMEM_SPEC] * 2,
        [pltpu.VMEM((width, hidden), F32)],
        matrix,
        6 * block_bytes,
    )(aggregated, grad)
    chip_term = add([swap_cores(theirs, n_col), mine])
    row_term = add(exchange([chip_term] * n_row, "row", n_row), flops=ROW_SUM_WEIGHT * matrix)

    own_grads = call(
        gather_kernel,
        like(own_nodes, hidden),
        [VMEM_SPEC] * (1 + n_chip),
        [],
        0,
        own_nodes * hidden * 4,
    )(chip_term, *grads)
    other_grads = swap_cores(own_grads, n_col)
    if is_dense:
        back_own = call(
            back_own_kernel,
            like(col_nodes, hidden, F32),
            [VMEM_SPEC] * 2,
            [],
            slots * matrix // 2,
            row_nodes * hidden * 8,
        )(turned, own_grads)
        piece_kernel, piece_args = back_piece_kernel, (turned, back_own, other_grads)
    else:
        back = call(
            slot_back_kernel,
            like(col_nodes, hidden, F32),
            slot_specs + [VMEM_SPEC] * 2,
            [pltpu.VMEM((row_nodes, hidden), BF16)],
            slots * matrix // 2,
            row_nodes * hidden * 8,
        )(*slot_args, own_grads, other_grads)
        piece_kernel, piece_args = slot_piece_kernel, (back,)

    def back_piece(k, before):
        return call(
            functools.partial(piece_kernel, k=k, n_row=n_row),
            like(tile, hidden),
            [VMEM_SPEC] * (len(piece_args) + len(before)),
            [],
            n_chip * matrix,
            2 * block_bytes,
        )(*piece_args, *before)

    backs = exchange(in_turn(n_row, back_piece), "row", n_row)
    grad_features = call(
        features_kernel,
        like(tile, width),
        [VMEM_SPEC] * (1 + n_row),
        [],
        FEATURES_WEIGHT * matrix,
        n_row * block_bytes,
    )(weight, *backs)
    all_terms = total_over(row_term, add, "col", n_col, 2)
    factor = (tile * n_row * n_col) ** (-0.5)
    own_half, bias_grad = call(
        functools.partial(scale_kernel, factor=factor),
        (like(half, hidden, F32), like(1, hidden, F32)),
        [HBM_SPEC] + [VMEM_SPEC] * len(all_terms),
        [],
        len(all_terms) * half * hidden,
        len(all_terms) * half * hidden * 2,
    )(pltpu.with_memory_space_constraint(grad_features, pltpu.HBM), *all_terms)
    other_half = swap_cores(own_half, n_col)
    grad_weight, grad_bias = call(
        join_kernel,
        (like(width, hidden, F32), like(1, hidden, F32)),
        [VMEM_SPEC] * 3,
        [],
        0,
        width * hidden * 8,
    )(own_half, other_half, bias_grad)
    return hidden_out, grad_features, grad_weight, grad_bias.reshape(hidden)


def solution(mesh):
    return jax.shard_map(
        local,
        mesh=mesh,
        in_specs=(
            P(("col", "row"), None),
            P(),
            P(),
            P(("row", "col"), None),
            P("row", "col", None, None, None),
            P("row", "col", None),
            P("row", "col", None),
            P("row", "col"),
        ),
        out_specs=(P(("row", "col"), None), P(("col", "row"), None), P(), P()),
        check_vma=False,
    )
```

```python
import functools

import jax
import jax.numpy as jnp
from jax import lax
from jax.experimental import pallas as pl
from jax.experimental.pallas import tpu as pltpu
from jax.sharding import PartitionSpec as P

F32 = jnp.float32
BF16 = jnp.bfloat16
ROOT_2_OVER_PI = 0.7978845608028654
CUBIC = 0.044715
VMEM_LIMIT = 48 * 1024 * 1024
BIAS_ROWS = 16
ROW_SUM_WEIGHT = 250
FEATURES_WEIGHT = 150

VMEM_SPEC = pl.BlockSpec(memory_space=pltpu.VMEM)
HBM_SPEC = pl.BlockSpec(memory_space=pltpu.HBM)
SMEM_SPEC = pl.BlockSpec(memory_space=pltpu.SMEM)


def call(kernel, out_shape, in_specs, scratch, flops, moved):
    return pl.pallas_call(
        kernel,
        out_shape=out_shape,
        in_specs=in_specs,
        out_specs=jax.tree.map(lambda _: VMEM_SPEC, out_shape),
        scratch_shapes=scratch,
        compiler_params=pltpu.CompilerParams(vmem_limit_bytes=VMEM_LIMIT),
        cost_estimate=pl.CostEstimate(flops=flops, bytes_accessed=moved, transcendentals=0),
    )


def partner(index, k, count):
    if count & (count - 1) == 0:
        return index ^ k
    return (k - index) % count


def far_first(count):
    return list(dict.fromkeys([count - 1, *range(1, count), 0]))


def pairs_of(k, size, cores):
    return [(i, partner(i // cores, k, size // cores) * cores + i % cores) for i in range(size)]


def exchange(blocks, axis, size, cores=1):
    received = []
    for k in far_first(size // cores):
        pairs = pairs_of(k, size, cores)
        moves = any(i != j for i, j in pairs)
        received.append(lax.ppermute(blocks[k], axis, pairs) if moves else blocks[k])
    return received


def swap_cores(block, size):
    return lax.ppermute(block, "col", [(i, i ^ 1) for i in range(size)])


def total_over(block, add, axis, size, cores=1):
    count = size // cores
    if count & (count - 1):
        return exchange([block] * count, axis, size, cores)
    terms, step = [block], 1
    while step < count:
        block = add(terms) if len(terms) > 1 else block
        terms = [lax.ppermute(block, axis, pairs_of(step, size, cores)), block]
        step *= 2
    return terms


def block_at(index, size):
    return pl.ds(pl.multiple_of(index * size, size), size)


def row_index():
    return lax.axis_index("row")


def chip_index():
    return lax.axis_index("col") // 2


def core_index():
    return lax.axis_index("col") % 2


def summed(refs):
    by_partner = dict(zip(far_first(len(refs)), refs))
    values = [by_partner[k][...].astype(F32) for k in sorted(by_partner)]
    while len(values) > 1:
        values = [sum(values[i + 1 : i + 2], values[i]) for i in range(0, len(values), 2)]
    return values[0]


def bias_rows(bias):
    high = bias.astype(BF16).astype(F32)
    line = lax.broadcasted_iota(jnp.int32, (BIAS_ROWS, bias.shape[1]), 0)
    return jnp.where(line == 0, high, jnp.where(line == 1, bias - high, 0.0))


def row_place(row, n_chip):
    return jnp.where(row % 2 == core_index(), 0, n_chip) + row // 2


def dense_kernel(
    count_ref, row_hbm, col_hbm, tiles_hbm, bias_hbm, dense_ref, bias_ref,
    row_ref, col_ref, tiles_ref, sum_ref, sems, tile_sems,
):
    slots, tile = tiles_ref.shape[0], tiles_ref.shape[1]
    n_chip = sum_ref.shape[0] // (2 * tile)
    chunks = tile_sems.shape[0]
    size = slots // chunks
    small = [
        pltpu.make_async_copy(row_hbm, row_ref, sems.at[0]),
        pltpu.make_async_copy(col_hbm, col_ref, sems.at[1]),
        pltpu.make_async_copy(bias_hbm, bias_ref, sems.at[2]),
    ]
    large = []
    for k in range(chunks):
        part = pl.ds(k * size, size)
        large.append(
            pltpu.make_async_copy(tiles_hbm.at[0, 0, part], tiles_ref.at[part], tile_sems.at[k])
        )
    for copy in small + large:
        copy.start()
    sum_ref[...] = jnp.zeros_like(sum_ref)
    for copy in small:
        copy.wait()
    count = count_ref[0, 0]

    def body(slot, carry):
        rows = block_at(row_place(row_ref[0, 0, slot], n_chip), tile)
        cols = block_at(col_ref[0, 0, slot], tile)
        sum_ref[rows, cols] += tiles_ref[slot].astype(F32)
        return carry

    for k, copy in enumerate(large):
        copy.wait()
        lax.fori_loop(k * size, jnp.minimum(count, (k + 1) * size), body, 0)
    dense_ref[...] = sum_ref[...].astype(BF16)


def turn_kernel(dense_ref, after_ref, turned_ref):
    rows = dense_ref.shape[0]
    step = 256 if rows % 256 == 0 else rows
    for first in range(0, rows, step):
        turned_ref[:, first : first + step] = dense_ref[first : first + step, :].T


def dense_dot(left, right):
    return jnp.dot(left, right, preferred_element_type=F32)


def gather_sources(sources, source_ref, index):
    tile = sources[0].shape[0]
    for k, ref in zip(far_first(len(sources)), sources):
        source_ref[block_at(partner(index, k, len(sources)), tile), :] = ref[...]


def slot_product(refs, source_ref, acc_ref, turned):
    count_ref, row_ref, col_ref, tiles_ref = refs
    tile = tiles_ref.shape[1]
    n_chip = (source_ref if turned else acc_ref).shape[0] // (2 * tile)
    contract = 0 if turned else 1
    acc_ref[...] = jnp.zeros_like(acc_ref)

    def body(slot, carry):
        places = [row_place(row_ref[slot], n_chip), col_ref[slot]]
        source, target = places if turned else places[::-1]
        acc_ref[block_at(target, tile), :] += lax.dot_general(
            tiles_ref[slot],
            source_ref[block_at(source, tile), :],
            (((contract,), (0,)), ((), ())),
            preferred_element_type=F32,
        )
        return carry

    lax.fori_loop(0, count_ref[0], body, 0)


def forward_other_kernel(dense_ref, *refs):
    sources, (other_ref, source_ref) = refs[:-2], refs[-2:]
    gather_sources(sources, source_ref, row_index())
    half = other_ref.shape[0]
    other_ref[...] = dense_dot(dense_ref[half:, :], source_ref[...]).astype(BF16)


def forward_own_kernel(dense_ref, source_ref, own_ref):
    own_ref[...] = dense_dot(dense_ref[: own_ref.shape[0], :], source_ref[...]).astype(BF16)


def slot_forward_kernel(count_ref, row_ref, col_ref, tiles_ref, *refs):
    sources, (other_ref, own_ref, source_ref, acc_ref) = refs[:-4], refs[-4:]
    gather_sources(sources, source_ref, row_index())
    slot_product((count_ref, row_ref, col_ref, tiles_ref), source_ref, acc_ref, False)
    half = own_ref.shape[0]
    own_ref[...] = acc_ref[:half, :].astype(BF16)
    other_ref[...] = acc_ref[half:, :].astype(BF16)


def chip_kernel(own_ref, other_ref, *refs, k, n_chip):
    out_ref = refs[-1]
    rows = block_at(partner(chip_index(), k, n_chip), out_ref.shape[0])
    out_ref[...] = (own_ref[rows, :].astype(F32) + other_ref[rows, :].astype(F32)).astype(BF16)


def middle_kernel(weight_ref, bias_ref, cot_ref, *refs):
    parts, (hidden_ref, grad_ref, agg_ref) = refs[:-3], refs[-3:]
    aggregated = summed(parts).astype(BF16)
    agg_ref[...] = aggregated
    v = dense_dot(aggregated, weight_ref[...]) + bias_ref[...]
    square = v * v
    t = jnp.tanh(ROOT_2_OVER_PI * (v + CUBIC * (square * v)))
    half = 0.5 * (1.0 + t)
    hidden_ref[...] = (v * half).astype(BF16)
    slope = half + 0.5 * v * (1.0 - t * t) * (ROOT_2_OVER_PI * (1.0 + 3.0 * CUBIC * square))
    grad_ref[...] = (cot_ref[...].astype(F32) * slope).astype(BF16)


def copy_kernel(in_ref, out_ref):
    out_ref[...] = in_ref[...]


def term_kernel(agg_ref, grad_ref, mine_ref, theirs_ref, acc_ref):
    grad = grad_ref[...]
    acc_ref[...] = lax.dot_general(
        agg_ref[...], grad, (((0,), (0,)), ((), ())), preferred_element_type=F32
    )
    half = acc_ref.shape[0] // 2
    bias = bias_rows(jnp.sum(grad.astype(F32), axis=0, keepdims=True)).astype(BF16)
    for ref, core in ((mine_ref, core_index()), (theirs_ref, 1 - core_index())):
        ref[:half, :] = acc_ref[block_at(core, half), :].astype(BF16)
        ref[half:, :] = bias


def add_terms_kernel(*refs, n_terms):
    total = summed(refs[:n_terms])
    out_ref = refs[-1]
    half = total.shape[0] - BIAS_ROWS
    out_ref[:half, :] = total[:half].astype(BF16)
    out_ref[half:, :] = bias_rows(total[half : half + 1] + total[half + 1 : half + 2]).astype(BF16)


def scale_kernel(after_ref, *refs, factor):
    parts, (half_ref, bias_ref) = refs[:-2], refs[-2:]
    total = summed(parts) * factor
    half = half_ref.shape[0]
    half_ref[...] = total[:half]
    bias_ref[...] = total[half : half + 1] + total[half + 1 : half + 2]


def gather_kernel(after_ref, *refs):
    gather_sources(refs[:-1], refs[-1], chip_index())


def back_own_kernel(turned_ref, source_ref, out_ref):
    out_ref[...] = dense_dot(turned_ref[:, : source_ref.shape[0]], source_ref[...])


def back_piece_kernel(turned_ref, own_ref, source_ref, *refs, k, n_row):
    out_ref = refs[-1]
    rows = block_at(partner(row_index(), k, n_row), out_ref.shape[0])
    rest = dense_dot(turned_ref[rows, source_ref.shape[0] :], source_ref[...])
    out_ref[...] = (own_ref[rows, :] + rest).astype(BF16)


def slot_back_kernel(count_ref, row_ref, col_ref, tiles_ref, own_ref, other_ref, out_ref, source_ref):
    half = own_ref.shape[0]
    source_ref[:half, :] = own_ref[...]
    source_ref[half:, :] = other_ref[...]
    slot_product((count_ref, row_ref, col_ref, tiles_ref), source_ref, out_ref, True)


def slot_piece_kernel(back_ref, *refs, k, n_row):
    out_ref = refs[-1]
    rows = block_at(partner(row_index(), k, n_row), out_ref.shape[0])
    out_ref[...] = back_ref[rows, :].astype(BF16)


def features_kernel(weight_ref, *refs):
    parts, out_ref = refs[:-1], refs[-1]
    out_ref[...] = lax.dot_general(
        summed(parts).astype(BF16),
        weight_ref[...],
        (((1,), (1,)), ((), ())),
        preferred_element_type=F32,
    ).astype(BF16)


def join_kernel(own_ref, other_ref, bias_ref, weight_ref, bias_out):
    half = own_ref.shape[0]
    weight_ref[block_at(core_index(), half), :] = own_ref[...]
    weight_ref[block_at(1 - core_index(), half), :] = other_ref[...]
    bias_out[...] = bias_ref[...]


def in_turn(count, make):
    made, before = {}, []
    for k in far_first(count):
        made[k] = make(k, before)
        before = [made[k]]
    return made


def local(features, weight, bias_term, cotangent, tile_values, tile_row, tile_col, tile_count):
    n_row = lax.axis_size("row")
    n_col = lax.axis_size("col")
    n_chip = n_col // 2
    tile, width = features.shape
    hidden = weight.shape[1]
    slots = tile_values.shape[2]
    row_nodes, col_nodes = n_col * tile, n_row * tile
    bias_row = bias_term.reshape(1, hidden)
    half = width // 2
    matrix = 2 * tile * width * hidden
    block_bytes = 2 * tile * width

    def like(rows, columns, dtype=BF16):
        return jax.ShapeDtypeStruct((rows, columns), dtype)

    near = 1
    own_nodes = n_chip * tile

    def add(terms, flops=0):
        return call(
            functools.partial(add_terms_kernel, n_terms=len(terms)),
            like(half + BIAS_ROWS, hidden),
            [VMEM_SPEC] * len(terms),
            [],
            flops or len(terms) * half * hidden,
            len(terms) * half * hidden * 2,
        )(*terms)

    is_dense = n_row * n_col <= 2 * slots
    if is_dense:
        chunks = 4 if slots % 4 == 0 else 1
        dense, bias_row = call(
            dense_kernel,
            (like(row_nodes, col_nodes), like(1, hidden, F32)),
            [SMEM_SPEC] + [HBM_SPEC] * 4,
            [
                pltpu.SMEM((1, 1, slots), jnp.int32),
                pltpu.SMEM((1, 1, slots), jnp.int32),
                pltpu.VMEM((slots, tile, tile), BF16),
                pltpu.VMEM((row_nodes, col_nodes), F32),
                pltpu.SemaphoreType.DMA((3,)),
                pltpu.SemaphoreType.DMA((chunks,)),
            ],
            0,
            12 * row_nodes * col_nodes,
        )(tile_count, *(
            pltpu.with_memory_space_constraint(array, pltpu.HBM)
            for array in (tile_row, tile_col, tile_values, bias_row)
        ))
    else:
        slot_args = (
            tile_count.reshape(1),
            tile_row.reshape(slots),
            tile_col.reshape(slots),
            tile_values.reshape(slots, tile, tile),
        )
        slot_specs = [SMEM_SPEC] * 3 + [VMEM_SPEC]

    sources = exchange([features] * n_row, "row", n_row)
    if is_dense:
        other, source = call(
            forward_other_kernel,
            (like(own_nodes, width), like(col_nodes, width)),
            [VMEM_SPEC] * (1 + n_row),
            [],
            slots * matrix // 2,
            row_nodes * width * 8,
        )(dense, *sources)
        own = call(
            forward_own_kernel,
            like(own_nodes, width),
            [VMEM_SPEC] * 2,
            [],
            slots * matrix // 2,
            row_nodes * width * 8,
        )(dense, source)
    else:
        other, own = call(
            slot_forward_kernel,
            (like(own_nodes, width), like(own_nodes, width)),
            slot_specs + [VMEM_SPEC] * n_row,
            [pltpu.VMEM((col_nodes, width), BF16), pltpu.VMEM((row_nodes, width), F32)],
            slots * matrix // 2,
            row_nodes * width * 8,
        )(*slot_args, *sources)
    swapped = swap_cores(other, n_col)

    def chip_piece(k, before):
        return call(
            functools.partial(chip_kernel, k=k, n_chip=n_chip),
            like(tile, width),
            [VMEM_SPEC] * (2 + len(before)),
            [],
            tile * width,
            3 * block_bytes,
        )(own, swapped, *before)

    pieces = in_turn(n_chip, chip_piece)
    parts = exchange(pieces, "col", n_col, 2)
    if is_dense:
        turned = call(
            turn_kernel,
            like(col_nodes, row_nodes),
            [VMEM_SPEC] * 2,
            [],
            0,
            4 * row_nodes * col_nodes,
        )(dense, pieces[0])
    hidden_own, grad, aggregated = call(
        middle_kernel,
        [like(tile, hidden), like(tile, hidden), like(tile, width)],
        [VMEM_SPEC] * (3 + n_chip),
        [],
        matrix,
        n_chip * block_bytes,
    )(weight, bias_row, cotangent, *parts)
    grads = exchange([grad] * n_chip, "col", n_col, 2)
    hidden_out = call(copy_kernel, like(tile, hidden), [VMEM_SPEC], [], 0, 2 * block_bytes)(hidden_own)
    mine, theirs = call(
        term_kernel,
        [like(half + BIAS_ROWS, hidden)] * 2,
        [VMEM_SPEC] * 2,
        [pltpu.VMEM((width, hidden), F32)],
        matrix,
        6 * block_bytes,
    )(aggregated, grad)
    chip_term = add([swap_cores(theirs, n_col), mine])
    add_late = functools.partial(add, flops=ROW_SUM_WEIGHT * matrix)
    row_term = add_late(total_over(chip_term, add, "row", n_row))

    own_grads = call(
        gather_kernel,
        like(own_nodes, hidden),
        [VMEM_SPEC] * (1 + n_chip),
        [],
        0,
        own_nodes * hidden * 4,
    )(chip_term, *grads)
    other_grads = swap_cores(own_grads, n_col)
    if is_dense:
        back_own = call(
            back_own_kernel,
            like(col_nodes, hidden, F32),
            [VMEM_SPEC] * 2,
            [],
            slots * matrix // 2,
            row_nodes * hidden * 8,
        )(turned, own_grads)
        piece_kernel, piece_args = back_piece_kernel, (turned, back_own, other_grads)
    else:
        back = call(
            slot_back_kernel,
            like(col_nodes, hidden, F32),
            slot_specs + [VMEM_SPEC] * 2,
            [pltpu.VMEM((row_nodes, hidden), BF16)],
            slots * matrix // 2,
            row_nodes * hidden * 8,
        )(*slot_args, own_grads, other_grads)
        piece_kernel, piece_args = slot_piece_kernel, (back,)

    def back_piece(k, before):
        return call(
            functools.partial(piece_kernel, k=k, n_row=n_row),
            like(tile, hidden),
            [VMEM_SPEC] * (len(piece_args) + len(before)),
            [],
            n_chip * matrix,
            2 * block_bytes,
        )(*piece_args, *before)

    backs = exchange(in_turn(n_row, back_piece), "row", n_row)
    grad_features = call(
        features_kernel,
        like(tile, width),
        [VMEM_SPEC] * (1 + n_row),
        [],
        FEATURES_WEIGHT * matrix,
        n_row * block_bytes,
    )(weight, *backs)
    all_terms = total_over(row_term, add, "col", n_col, 2)
    factor = (tile * n_row * n_col) ** (-0.5)
    own_half, bias_grad = call(
        functools.partial(scale_kernel, factor=factor),
        (like(half, hidden, F32), like(1, hidden, F32)),
        [HBM_SPEC] + [VMEM_SPEC] * len(all_terms),
        [],
        len(all_terms) * half * hidden,
        len(all_terms) * half * hidden * 2,
    )(pltpu.with_memory_space_constraint(grad_features, pltpu.HBM), *all_terms)
    other_half = swap_cores(own_half, n_col)
    grad_weight, grad_bias = call(
        join_kernel,
        (like(width, hidden, F32), like(1, hidden, F32)),
        [VMEM_SPEC] * 3,
        [],
        0,
        width * hidden * 8,
    )(own_half, other_half, bias_grad)
    return hidden_out, grad_features, grad_weight, grad_bias.reshape(hidden)


def solution(mesh):
    return jax.shard_map(
        local,
        mesh=mesh,
        in_specs=(
            P(("col", "row"), None),
            P(),
            P(),
            P(("row", "col"), None),
            P("row", "col", None, None, None),
            P("row", "col", None),
            P("row", "col", None),
            P("row", "col"),
        ),
        out_specs=(P(("row", "col"), None), P(("col", "row"), None), P(), P()),
        check_vma=False,
    )
```

```python
import functools

import jax
import jax.numpy as jnp
from jax import lax
from jax.experimental import pallas as pl
from jax.experimental.pallas import tpu as pltpu
from jax.sharding import PartitionSpec as P

F32 = jnp.float32
BF16 = jnp.bfloat16
ROOT_2_OVER_PI = 0.7978845608028654
CUBIC = 0.044715
VMEM_LIMIT = 48 * 1024 * 1024
BIAS_ROWS = 16
ROW_SUM_WEIGHT = 70
FEATURES_WEIGHT = 150

VMEM_SPEC = pl.BlockSpec(memory_space=pltpu.VMEM)
HBM_SPEC = pl.BlockSpec(memory_space=pltpu.HBM)
SMEM_SPEC = pl.BlockSpec(memory_space=pltpu.SMEM)


def call(kernel, out_shape, in_specs, scratch, flops, moved):
    return pl.pallas_call(
        kernel,
        out_shape=out_shape,
        in_specs=in_specs,
        out_specs=jax.tree.map(lambda _: VMEM_SPEC, out_shape),
        scratch_shapes=scratch,
        compiler_params=pltpu.CompilerParams(vmem_limit_bytes=VMEM_LIMIT),
        cost_estimate=pl.CostEstimate(flops=flops, bytes_accessed=moved, transcendentals=0),
    )


def partner(index, k, count):
    if count & (count - 1) == 0:
        return index ^ k
    return (k - index) % count


def far_first(count):
    return list(dict.fromkeys([count - 1, *range(1, count), 0]))


def pairs_of(k, size, cores):
    return [(i, partner(i // cores, k, size // cores) * cores + i % cores) for i in range(size)]


def exchange(blocks, axis, size, cores=1):
    received = []
    for k in far_first(size // cores):
        pairs = pairs_of(k, size, cores)
        moves = any(i != j for i, j in pairs)
        received.append(lax.ppermute(blocks[k], axis, pairs) if moves else blocks[k])
    return received


def swap_cores(block, size):
    return lax.ppermute(block, "col", [(i, i ^ 1) for i in range(size)])


def doubling(block, add, axes, count, pairs_at):
    terms, step = [block], 1
    while step < count:
        block = add(terms) if len(terms) > 1 else block
        terms = [lax.ppermute(block, axes, pairs_at(step)), block]
        step *= 2
    return terms


def second_cores_along_row(step, n_row, n_col):
    return [
        (col * n_row + row, col * n_row + (row ^ step if col % 2 else row))
        for col in range(n_col)
        for row in range(n_row)
    ]


def second_cores_along_col(step, n_col):
    return [(col, col ^ (2 * step) if col % 2 else col) for col in range(n_col)]


def block_at(index, size):
    return pl.ds(pl.multiple_of(index * size, size), size)


def row_index():
    return lax.axis_index("row")


def chip_index():
    return lax.axis_index("col") // 2


def core_index():
    return lax.axis_index("col") % 2


def summed(refs):
    by_partner = dict(zip(far_first(len(refs)), refs))
    values = [by_partner[k][...].astype(F32) for k in sorted(by_partner)]
    while len(values) > 1:
        values = [sum(values[i + 1 : i + 2], values[i]) for i in range(0, len(values), 2)]
    return values[0]


def bias_rows(bias):
    high = bias.astype(BF16).astype(F32)
    line = lax.broadcasted_iota(jnp.int32, (BIAS_ROWS, bias.shape[1]), 0)
    return jnp.where(line == 0, high, jnp.where(line == 1, bias - high, 0.0))


def row_place(row, n_chip):
    return jnp.where(row % 2 == core_index(), 0, n_chip) + row // 2


def dense_kernel(
    count_ref, row_hbm, col_hbm, tiles_hbm, bias_hbm, dense_ref, bias_ref,
    row_ref, col_ref, tiles_ref, sum_ref, sems, tile_sems,
):
    slots, tile = tiles_ref.shape[0], tiles_ref.shape[1]
    n_chip = sum_ref.shape[0] // (2 * tile)
    chunks = tile_sems.shape[0]
    size = slots // chunks
    small = [
        pltpu.make_async_copy(row_hbm, row_ref, sems.at[0]),
        pltpu.make_async_copy(col_hbm, col_ref, sems.at[1]),
        pltpu.make_async_copy(bias_hbm, bias_ref, sems.at[2]),
    ]
    large = []
    for k in range(chunks):
        part = pl.ds(k * size, size)
        large.append(
            pltpu.make_async_copy(tiles_hbm.at[0, 0, part], tiles_ref.at[part], tile_sems.at[k])
        )
    for copy in small + large:
        copy.start()
    sum_ref[...] = jnp.zeros_like(sum_ref)
    for copy in small:
        copy.wait()
    count = count_ref[0, 0]

    def body(slot, carry):
        rows = block_at(row_place(row_ref[0, 0, slot], n_chip), tile)
        cols = block_at(col_ref[0, 0, slot], tile)
        sum_ref[rows, cols] += tiles_ref[slot].astype(F32)
        return carry

    for k, copy in enumerate(large):
        copy.wait()
        lax.fori_loop(k * size, jnp.minimum(count, (k + 1) * size), body, 0)
    dense_ref[...] = sum_ref[...].astype(BF16)


def turn_kernel(dense_ref, after_ref, turned_ref):
    rows = dense_ref.shape[0]
    step = 256 if rows % 256 == 0 else rows
    for first in range(0, rows, step):
        turned_ref[:, first : first + step] = dense_ref[first : first + step, :].T


def dense_dot(left, right):
    return jnp.dot(left, right, preferred_element_type=F32)


def gather_sources(sources, source_ref, index):
    tile = sources[0].shape[0]
    for k, ref in zip(far_first(len(sources)), sources):
        source_ref[block_at(partner(index, k, len(sources)), tile), :] = ref[...]


def slot_product(refs, source_ref, acc_ref, turned):
    count_ref, row_ref, col_ref, tiles_ref = refs
    tile = tiles_ref.shape[1]
    n_chip = (source_ref if turned else acc_ref).shape[0] // (2 * tile)
    contract = 0 if turned else 1
    acc_ref[...] = jnp.zeros_like(acc_ref)

    def body(slot, carry):
        places = [row_place(row_ref[slot], n_chip), col_ref[slot]]
        source, target = places if turned else places[::-1]
        acc_ref[block_at(target, tile), :] += lax.dot_general(
            tiles_ref[slot],
            source_ref[block_at(source, tile), :],
            (((contract,), (0,)), ((), ())),
            preferred_element_type=F32,
        )
        return carry

    lax.fori_loop(0, count_ref[0], body, 0)


def forward_other_kernel(dense_ref, *refs):
    sources, (other_ref, source_ref) = refs[:-2], refs[-2:]
    gather_sources(sources, source_ref, row_index())
    half = other_ref.shape[0]
    other_ref[...] = dense_dot(dense_ref[half:, :], source_ref[...]).astype(BF16)


def forward_own_kernel(dense_ref, source_ref, own_ref):
    own_ref[...] = dense_dot(dense_ref[: own_ref.shape[0], :], source_ref[...]).astype(BF16)


def slot_forward_kernel(count_ref, row_ref, col_ref, tiles_ref, *refs):
    sources, (other_ref, own_ref, source_ref, acc_ref) = refs[:-4], refs[-4:]
    gather_sources(sources, source_ref, row_index())
    slot_product((count_ref, row_ref, col_ref, tiles_ref), source_ref, acc_ref, False)
    half = own_ref.shape[0]
    own_ref[...] = acc_ref[:half, :].astype(BF16)
    other_ref[...] = acc_ref[half:, :].astype(BF16)


def chip_kernel(own_ref, other_ref, *refs, k, n_chip):
    out_ref = refs[-1]
    rows = block_at(partner(chip_index(), k, n_chip), out_ref.shape[0])
    out_ref[...] = (own_ref[rows, :].astype(F32) + other_ref[rows, :].astype(F32)).astype(BF16)


def middle_kernel(weight_ref, bias_ref, cot_ref, *refs):
    parts, (hidden_ref, grad_ref, agg_ref) = refs[:-3], refs[-3:]
    aggregated = summed(parts).astype(BF16)
    agg_ref[...] = aggregated
    v = dense_dot(aggregated, weight_ref[...]) + bias_ref[...]
    square = v * v
    t = jnp.tanh(ROOT_2_OVER_PI * (v + CUBIC * (square * v)))
    half = 0.5 * (1.0 + t)
    hidden_ref[...] = (v * half).astype(BF16)
    slope = half + 0.5 * v * (1.0 - t * t) * (ROOT_2_OVER_PI * (1.0 + 3.0 * CUBIC * square))
    grad_ref[...] = (cot_ref[...].astype(F32) * slope).astype(BF16)


def copy_kernel(in_ref, out_ref):
    out_ref[...] = in_ref[...]


def term_kernel(agg_ref, grad_ref, out_ref):
    grad = grad_ref[...]
    term = lax.dot_general(
        agg_ref[...], grad, (((0,), (0,)), ((), ())), preferred_element_type=F32
    )
    width = term.shape[0]
    out_ref[:width, :] = term.astype(BF16)
    out_ref[width:, :] = bias_rows(jnp.sum(grad.astype(F32), axis=0, keepdims=True)).astype(BF16)


def add_terms_kernel(*refs, n_terms):
    total = summed(refs[:n_terms])
    out_ref = refs[-1]
    width = total.shape[0] - BIAS_ROWS
    out_ref[:width, :] = total[:width].astype(BF16)
    bias = total[width : width + 1] + total[width + 1 : width + 2]
    out_ref[width:, :] = bias_rows(bias).astype(BF16)


def scale_kernel(after_ref, *refs, factor):
    parts, out_ref = refs[:-1], refs[-1]
    total = summed(parts) * factor
    width = total.shape[0] - BIAS_ROWS
    out_ref[:width, :] = total[:width]
    bias = total[width : width + 1] + total[width + 1 : width + 2]
    out_ref[width:, :] = jnp.broadcast_to(bias, (out_ref.shape[0] - width, bias.shape[1]))


def gather_kernel(after_ref, *refs):
    gather_sources(refs[:-1], refs[-1], chip_index())


def back_own_kernel(turned_ref, source_ref, out_ref):
    out_ref[...] = dense_dot(turned_ref[:, : source_ref.shape[0]], source_ref[...])


def back_piece_kernel(turned_ref, own_ref, source_ref, *refs, k, n_row):
    out_ref = refs[-1]
    rows = block_at(partner(row_index(), k, n_row), out_ref.shape[0])
    rest = dense_dot(turned_ref[rows, source_ref.shape[0] :], source_ref[...])
    out_ref[...] = (own_ref[rows, :] + rest).astype(BF16)


def slot_back_kernel(count_ref, row_ref, col_ref, tiles_ref, own_ref, other_ref, out_ref, source_ref):
    half = own_ref.shape[0]
    source_ref[:half, :] = own_ref[...]
    source_ref[half:, :] = other_ref[...]
    slot_product((count_ref, row_ref, col_ref, tiles_ref), source_ref, out_ref, True)


def slot_piece_kernel(back_ref, *refs, k, n_row):
    out_ref = refs[-1]
    rows = block_at(partner(row_index(), k, n_row), out_ref.shape[0])
    out_ref[...] = back_ref[rows, :].astype(BF16)


def features_kernel(weight_ref, *refs):
    parts, out_ref = refs[:-1], refs[-1]
    out_ref[...] = lax.dot_general(
        summed(parts).astype(BF16),
        weight_ref[...],
        (((1,), (1,)), ((), ())),
        preferred_element_type=F32,
    ).astype(BF16)


def join_kernel(own_ref, other_ref, weight_ref, bias_ref):
    width = weight_ref.shape[0]
    second = core_index() == 1
    weight_ref[...] = jnp.where(second, own_ref[:width, :], other_ref[:width, :])
    bias_ref[...] = jnp.where(second, own_ref[width : width + 1, :], other_ref[width : width + 1, :])


def in_turn(count, make):
    made, before = {}, []
    for k in far_first(count):
        made[k] = make(k, before)
        before = [made[k]]
    return made


def local(features, weight, bias_term, cotangent, tile_values, tile_row, tile_col, tile_count):
    n_row = lax.axis_size("row")
    n_col = lax.axis_size("col")
    n_chip = n_col // 2
    tile, width = features.shape
    hidden = weight.shape[1]
    slots = tile_values.shape[2]
    row_nodes, col_nodes = n_col * tile, n_row * tile
    bias_row = bias_term.reshape(1, hidden)
    matrix = 2 * tile * width * hidden
    block_bytes = 2 * tile * width

    def like(rows, columns, dtype=BF16):
        return jax.ShapeDtypeStruct((rows, columns), dtype)

    near = 1
    own_nodes = n_chip * tile

    def add(terms, flops=0):
        return call(
            functools.partial(add_terms_kernel, n_terms=len(terms)),
            like(width + BIAS_ROWS, hidden),
            [VMEM_SPEC] * len(terms),
            [],
            flops or len(terms) * width * hidden,
            len(terms) * width * hidden * 2,
        )(*terms)

    is_dense = n_row * n_col <= 2 * slots
    if is_dense:
        chunks = 4 if slots % 4 == 0 else 1
        dense, bias_row = call(
            dense_kernel,
            (like(row_nodes, col_nodes), like(1, hidden, F32)),
            [SMEM_SPEC] + [HBM_SPEC] * 4,
            [
                pltpu.SMEM((1, 1, slots), jnp.int32),
                pltpu.SMEM((1, 1, slots), jnp.int32),
                pltpu.VMEM((slots, tile, tile), BF16),
                pltpu.VMEM((row_nodes, col_nodes), F32),
                pltpu.SemaphoreType.DMA((3,)),
                pltpu.SemaphoreType.DMA((chunks,)),
            ],
            0,
            12 * row_nodes * col_nodes,
        )(tile_count, *(
            pltpu.with_memory_space_constraint(array, pltpu.HBM)
            for array in (tile_row, tile_col, tile_values, bias_row)
        ))
    else:
        slot_args = (
            tile_count.reshape(1),
            tile_row.reshape(slots),
            tile_col.reshape(slots),
            tile_values.reshape(slots, tile, tile),
        )
        slot_specs = [SMEM_SPEC] * 3 + [VMEM_SPEC]

    sources = exchange([features] * n_row, "row", n_row)
    if is_dense:
        other, source = call(
            forward_other_kernel,
            (like(own_nodes, width), like(col_nodes, width)),
            [VMEM_SPEC] * (1 + n_row),
            [],
            slots * matrix // 2,
            row_nodes * width * 8,
        )(dense, *sources)
        own = call(
            forward_own_kernel,
            like(own_nodes, width),
            [VMEM_SPEC] * 2,
            [],
            slots * matrix // 2,
            row_nodes * width * 8,
        )(dense, source)
    else:
        other, own = call(
            slot_forward_kernel,
            (like(own_nodes, width), like(own_nodes, width)),
            slot_specs + [VMEM_SPEC] * n_row,
            [pltpu.VMEM((col_nodes, width), BF16), pltpu.VMEM((row_nodes, width), F32)],
            slots * matrix // 2,
            row_nodes * width * 8,
        )(*slot_args, *sources)
    swapped = swap_cores(other, n_col)

    def chip_piece(k, before):
        return call(
            functools.partial(chip_kernel, k=k, n_chip=n_chip),
            like(tile, width),
            [VMEM_SPEC] * (2 + len(before)),
            [],
            tile * width,
            3 * block_bytes,
        )(own, swapped, *before)

    pieces = in_turn(n_chip, chip_piece)
    parts = exchange(pieces, "col", n_col, 2)
    if is_dense:
        turned = call(
            turn_kernel,
            like(col_nodes, row_nodes),
            [VMEM_SPEC] * 2,
            [],
            0,
            4 * row_nodes * col_nodes,
        )(dense, pieces[0])
    hidden_own, grad, aggregated = call(
        middle_kernel,
        [like(tile, hidden), like(tile, hidden), like(tile, width)],
        [VMEM_SPEC] * (3 + n_chip),
        [],
        matrix,
        n_chip * block_bytes,
    )(weight, bias_row, cotangent, *parts)
    grads = exchange([grad] * n_chip, "col", n_col, 2)
    hidden_out = call(copy_kernel, like(tile, hidden), [VMEM_SPEC], [], 0, 2 * block_bytes)(hidden_own)
    term = call(
        term_kernel,
        like(width + BIAS_ROWS, hidden),
        [VMEM_SPEC] * 2,
        [],
        matrix,
        6 * block_bytes,
    )(aggregated, grad)
    chip_term = add([swap_cores(term, n_col), term])
    along_row = functools.partial(second_cores_along_row, n_row=n_row, n_col=n_col)
    row_terms = doubling(chip_term, add, ("col", "row"), n_row, along_row)
    row_term = add(row_terms, flops=ROW_SUM_WEIGHT * matrix)

    own_grads = call(
        gather_kernel,
        like(own_nodes, hidden),
        [VMEM_SPEC] * (1 + n_chip),
        [],
        0,
        own_nodes * hidden * 4,
    )(chip_term, *grads)
    other_grads = swap_cores(own_grads, n_col)
    if is_dense:
        back_own = call(
            back_own_kernel,
            like(col_nodes, hidden, F32),
            [VMEM_SPEC] * 2,
            [],
            slots * matrix // 2,
            row_nodes * hidden * 8,
        )(turned, own_grads)
        piece_kernel, piece_args = back_piece_kernel, (turned, back_own, other_grads)
    else:
        back = call(
            slot_back_kernel,
            like(col_nodes, hidden, F32),
            slot_specs + [VMEM_SPEC] * 2,
            [pltpu.VMEM((row_nodes, hidden), BF16)],
            slots * matrix // 2,
            row_nodes * hidden * 8,
        )(*slot_args, own_grads, other_grads)
        piece_kernel, piece_args = slot_piece_kernel, (back,)

    def back_piece(k, before):
        return call(
            functools.partial(piece_kernel, k=k, n_row=n_row),
            like(tile, hidden),
            [VMEM_SPEC] * (len(piece_args) + len(before)),
            [],
            n_chip * matrix,
            2 * block_bytes,
        )(*piece_args, *before)

    backs = exchange(in_turn(n_row, back_piece), "row", n_row)
    grad_features = call(
        features_kernel,
        like(tile, width),
        [VMEM_SPEC] * (1 + n_row),
        [],
        FEATURES_WEIGHT * matrix,
        n_row * block_bytes,
    )(weight, *backs)
    along_col = functools.partial(second_cores_along_col, n_col=n_col)
    all_terms = doubling(row_term, add, "col", n_chip, along_col)
    factor = (tile * n_row * n_col) ** (-0.5)
    total = call(
        functools.partial(scale_kernel, factor=factor),
        like(width + 8, hidden, F32),
        [HBM_SPEC] + [VMEM_SPEC] * len(all_terms),
        [],
        len(all_terms) * width * hidden,
        len(all_terms) * width * hidden * 2,
    )(pltpu.with_memory_space_constraint(grad_features, pltpu.HBM), *all_terms)
    grad_weight, grad_bias = call(
        join_kernel,
        (like(width, hidden, F32), like(1, hidden, F32)),
        [VMEM_SPEC] * 2,
        [],
        0,
        width * hidden * 8,
    )(total, swap_cores(total, n_col))
    return hidden_out, grad_features, grad_weight, grad_bias.reshape(hidden)


def solution(mesh):
    return jax.shard_map(
        local,
        mesh=mesh,
        in_specs=(
            P(("col", "row"), None),
            P(),
            P(),
            P(("row", "col"), None),
            P("row", "col", None, None, None),
            P("row", "col", None),
            P("row", "col", None),
            P("row", "col"),
        ),
        out_specs=(P(("row", "col"), None), P(("col", "row"), None), P(), P()),
        check_vma=False,
    )
```

```python
import functools

import jax
import jax.numpy as jnp
from jax import lax
from jax.experimental import pallas as pl
from jax.experimental.pallas import tpu as pltpu
from jax.sharding import PartitionSpec as P

F32 = jnp.float32
BF16 = jnp.bfloat16
ROOT_2_OVER_PI = 0.7978845608028654
CUBIC = 0.044715
VMEM_LIMIT = 48 * 1024 * 1024
BIAS_ROWS = 16
BACK_SUM_WEIGHT = 30
ROW_SUM_WEIGHT = 120
FEATURES_WEIGHT = 100

VMEM_SPEC = pl.BlockSpec(memory_space=pltpu.VMEM)
HBM_SPEC = pl.BlockSpec(memory_space=pltpu.HBM)
SMEM_SPEC = pl.BlockSpec(memory_space=pltpu.SMEM)


def call(kernel, out_shape, in_specs, scratch, flops, moved):
    return pl.pallas_call(
        kernel,
        out_shape=out_shape,
        in_specs=in_specs,
        out_specs=jax.tree.map(lambda _: VMEM_SPEC, out_shape),
        scratch_shapes=scratch,
        compiler_params=pltpu.CompilerParams(vmem_limit_bytes=VMEM_LIMIT),
        cost_estimate=pl.CostEstimate(flops=flops, bytes_accessed=moved, transcendentals=0),
    )


def partner(index, k, count):
    if count & (count - 1) == 0:
        return index ^ k
    return (k - index) % count


def far_first(count):
    return list(range(count - 1, -1, -1))


def pairs_of(k, size, cores):
    return [(i, partner(i // cores, k, size // cores) * cores + i % cores) for i in range(size)]


def exchange(blocks, axis, size, cores=1):
    received = []
    for k in far_first(size // cores):
        pairs = pairs_of(k, size, cores)
        moves = any(i != j for i, j in pairs)
        received.append(lax.ppermute(blocks[k], axis, pairs) if moves else blocks[k])
    return received


def swap_cores(block, size):
    return lax.ppermute(block, "col", [(i, i ^ 1) for i in range(size)])


def total_over(block, add, axis, size, cores=1):
    count = size // cores
    if count & (count - 1):
        return exchange([block] * count, axis, size, cores)
    terms, step = [block], 1
    while step < count:
        block = add(terms) if len(terms) > 1 else block
        terms = [lax.ppermute(block, axis, pairs_of(step, size, cores)), block]
        step *= 2
    return terms


def block_at(index, size):
    return pl.ds(pl.multiple_of(index * size, size), size)


def row_index():
    return lax.axis_index("row")


def chip_index():
    return lax.axis_index("col") // 2


def core_index():
    return lax.axis_index("col") % 2


def summed(refs):
    by_partner = dict(zip(far_first(len(refs)), refs))
    values = [by_partner[k][...].astype(F32) for k in sorted(by_partner)]
    while len(values) > 1:
        values = [sum(values[i + 1 : i + 2], values[i]) for i in range(0, len(values), 2)]
    return values[0]


def bias_rows(bias):
    high = bias.astype(BF16).astype(F32)
    line = lax.broadcasted_iota(jnp.int32, (BIAS_ROWS, bias.shape[1]), 0)
    return jnp.where(line == 0, high, jnp.where(line == 1, bias - high, 0.0))


def row_place(row, n_chip):
    return jnp.where(row % 2 == core_index(), 0, n_chip) + row // 2


def dense_kernel(
    count_ref, row_hbm, col_hbm, tiles_hbm, bias_hbm, dense_ref, bias_ref,
    row_ref, col_ref, tiles_ref, sum_ref, sems, tile_sems,
):
    slots, tile = tiles_ref.shape[0], tiles_ref.shape[1]
    n_chip = sum_ref.shape[0] // (2 * tile)
    chunks = tile_sems.shape[0]
    size = slots // chunks
    small = [
        pltpu.make_async_copy(row_hbm, row_ref, sems.at[0]),
        pltpu.make_async_copy(col_hbm, col_ref, sems.at[1]),
        pltpu.make_async_copy(bias_hbm, bias_ref, sems.at[2]),
    ]
    large = []
    for k in range(chunks):
        part = pl.ds(k * size, size)
        large.append(
            pltpu.make_async_copy(tiles_hbm.at[0, 0, part], tiles_ref.at[part], tile_sems.at[k])
        )
    for copy in small + large:
        copy.start()
    sum_ref[...] = jnp.zeros_like(sum_ref)
    for copy in small:
        copy.wait()
    count = count_ref[0, 0]

    def body(slot, carry):
        rows = block_at(row_place(row_ref[0, 0, slot], n_chip), tile)
        cols = block_at(col_ref[0, 0, slot], tile)
        sum_ref[rows, cols] += tiles_ref[slot].astype(F32)
        return carry

    for k, copy in enumerate(large):
        copy.wait()
        lax.fori_loop(k * size, jnp.minimum(count, (k + 1) * size), body, 0)
    dense_ref[...] = sum_ref[...].astype(BF16)


def turn_kernel(dense_ref, after_ref, turned_ref):
    rows = dense_ref.shape[0]
    step = 256 if rows % 256 == 0 else rows
    for first in range(0, rows, step):
        turned_ref[:, first : first + step] = dense_ref[first : first + step, :].T


def dense_dot(left, right):
    return jnp.dot(left, right, preferred_element_type=F32)


def gather_sources(sources, source_ref, index):
    tile = sources[0].shape[0]
    for k, ref in zip(far_first(len(sources)), sources):
        source_ref[block_at(partner(index, k, len(sources)), tile), :] = ref[...]


def slot_product(refs, source_ref, acc_ref, turned):
    count_ref, row_ref, col_ref, tiles_ref = refs
    tile = tiles_ref.shape[1]
    n_chip = (source_ref if turned else acc_ref).shape[0] // (2 * tile)
    contract = 0 if turned else 1
    acc_ref[...] = jnp.zeros_like(acc_ref)

    def body(slot, carry):
        places = [row_place(row_ref[slot], n_chip), col_ref[slot]]
        source, target = places if turned else places[::-1]
        acc_ref[block_at(target, tile), :] += lax.dot_general(
            tiles_ref[slot],
            source_ref[block_at(source, tile), :],
            (((contract,), (0,)), ((), ())),
            preferred_element_type=F32,
        )
        return carry

    lax.fori_loop(0, count_ref[0], body, 0)


def forward_other_kernel(dense_ref, *refs):
    sources, (other_ref, source_ref) = refs[:-2], refs[-2:]
    gather_sources(sources, source_ref, row_index())
    half = other_ref.shape[0]
    other_ref[...] = dense_dot(dense_ref[half:, :], source_ref[...]).astype(BF16)


def forward_own_kernel(dense_ref, source_ref, own_ref):
    own_ref[...] = dense_dot(dense_ref[: own_ref.shape[0], :], source_ref[...]).astype(BF16)


def slot_forward_kernel(count_ref, row_ref, col_ref, tiles_ref, *refs):
    sources, (other_ref, own_ref, source_ref, acc_ref) = refs[:-4], refs[-4:]
    gather_sources(sources, source_ref, row_index())
    slot_product((count_ref, row_ref, col_ref, tiles_ref), source_ref, acc_ref, False)
    half = own_ref.shape[0]
    own_ref[...] = acc_ref[:half, :].astype(BF16)
    other_ref[...] = acc_ref[half:, :].astype(BF16)


def chip_kernel(own_ref, other_ref, *refs, k, n_chip):
    out_ref = refs[-1]
    rows = block_at(partner(chip_index(), k, n_chip), out_ref.shape[0])
    out_ref[...] = (own_ref[rows, :].astype(F32) + other_ref[rows, :].astype(F32)).astype(BF16)


def middle_kernel(weight_ref, bias_ref, cot_ref, *refs):
    parts, (hidden_ref, grad_ref, agg_ref) = refs[:-3], refs[-3:]
    aggregated = summed(parts).astype(BF16)
    agg_ref[...] = aggregated
    v = dense_dot(aggregated, weight_ref[...]) + bias_ref[...]
    square = v * v
    t = jnp.tanh(ROOT_2_OVER_PI * (v + CUBIC * (square * v)))
    half = 0.5 * (1.0 + t)
    hidden_ref[...] = (v * half).astype(BF16)
    slope = half + 0.5 * v * (1.0 - t * t) * (ROOT_2_OVER_PI * (1.0 + 3.0 * CUBIC * square))
    grad_ref[...] = (cot_ref[...].astype(F32) * slope).astype(BF16)


def copy_kernel(in_ref, out_ref):
    out_ref[...] = in_ref[...]


def term_kernel(agg_ref, grad_ref, mine_ref, theirs_ref, acc_ref):
    grad = grad_ref[...]
    acc_ref[...] = lax.dot_general(
        agg_ref[...], grad, (((0,), (0,)), ((), ())), preferred_element_type=F32
    )
    half = acc_ref.shape[0] // 2
    bias = bias_rows(jnp.sum(grad.astype(F32), axis=0, keepdims=True)).astype(BF16)
    for ref, core in ((mine_ref, core_index()), (theirs_ref, 1 - core_index())):
        ref[:half, :] = acc_ref[block_at(core, half), :].astype(BF16)
        ref[half:, :] = bias


def add_terms_kernel(*refs, n_terms):
    total = summed(refs[:n_terms])
    out_ref = refs[-1]
    half = total.shape[0] - BIAS_ROWS
    out_ref[:half, :] = total[:half].astype(BF16)
    out_ref[half:, :] = bias_rows(total[half : half + 1] + total[half + 1 : half + 2]).astype(BF16)


def scale_kernel(after_ref, *refs, factor):
    parts, (half_ref, bias_ref) = refs[:-2], refs[-2:]
    total = summed(parts) * factor
    half = half_ref.shape[0]
    half_ref[...] = total[:half]
    bias_ref[...] = total[half : half + 1] + total[half + 1 : half + 2]


def gather_kernel(after_ref, *refs):
    gather_sources(refs[:-1], refs[-1], chip_index())


def back_own_kernel(turned_ref, source_ref, out_ref):
    out_ref[...] = dense_dot(turned_ref[:, : source_ref.shape[0]], source_ref[...])


def back_piece_kernel(turned_ref, own_ref, source_ref, *refs, k, n_row):
    out_ref = refs[-1]
    rows = block_at(partner(row_index(), k, n_row), out_ref.shape[0])
    rest = dense_dot(turned_ref[rows, source_ref.shape[0] :], source_ref[...])
    out_ref[...] = (own_ref[rows, :] + rest).astype(BF16)


def slot_back_kernel(count_ref, row_ref, col_ref, tiles_ref, own_ref, other_ref, out_ref, source_ref):
    half = own_ref.shape[0]
    source_ref[:half, :] = own_ref[...]
    source_ref[half:, :] = other_ref[...]
    slot_product((count_ref, row_ref, col_ref, tiles_ref), source_ref, out_ref, True)


def slot_piece_kernel(back_ref, *refs, k, n_row):
    out_ref = refs[-1]
    rows = block_at(partner(row_index(), k, n_row), out_ref.shape[0])
    out_ref[...] = back_ref[rows, :].astype(BF16)


def back_sum_kernel(*refs):
    total = refs[0][...].astype(F32)
    for ref in refs[1:-1]:
        total += ref[...].astype(F32)
    refs[-1][...] = total


def features_kernel(weight_ref, most_ref, last_ref, out_ref):
    out_ref[...] = lax.dot_general(
        (most_ref[...] + last_ref[...].astype(F32)).astype(BF16),
        weight_ref[...],
        (((1,), (1,)), ((), ())),
        preferred_element_type=F32,
    ).astype(BF16)


def join_kernel(own_ref, other_ref, bias_ref, weight_ref, bias_out):
    half = own_ref.shape[0]
    weight_ref[block_at(core_index(), half), :] = own_ref[...]
    weight_ref[block_at(1 - core_index(), half), :] = other_ref[...]
    bias_out[...] = bias_ref[...]


def in_turn(count, make):
    made, before = {}, []
    for k in far_first(count):
        made[k] = make(k, before)
        before = [made[k]]
    return made


def local(features, weight, bias_term, cotangent, tile_values, tile_row, tile_col, tile_count):
    n_row = lax.axis_size("row")
    n_col = lax.axis_size("col")
    n_chip = n_col // 2
    tile, width = features.shape
    hidden = weight.shape[1]
    slots = tile_values.shape[2]
    row_nodes, col_nodes = n_col * tile, n_row * tile
    bias_row = bias_term.reshape(1, hidden)
    half = width // 2
    matrix = 2 * tile * width * hidden
    block_bytes = 2 * tile * width

    def like(rows, columns, dtype=BF16):
        return jax.ShapeDtypeStruct((rows, columns), dtype)

    near = 1
    own_nodes = n_chip * tile

    def add(terms, flops=0):
        return call(
            functools.partial(add_terms_kernel, n_terms=len(terms)),
            like(half + BIAS_ROWS, hidden),
            [VMEM_SPEC] * len(terms),
            [],
            flops or len(terms) * half * hidden,
            len(terms) * half * hidden * 2,
        )(*terms)

    is_dense = n_row * n_col <= 2 * slots
    if is_dense:
        chunks = 4 if slots % 4 == 0 else 1
        dense, bias_row = call(
            dense_kernel,
            (like(row_nodes, col_nodes), like(1, hidden, F32)),
            [SMEM_SPEC] + [HBM_SPEC] * 4,
            [
                pltpu.SMEM((1, 1, slots), jnp.int32),
                pltpu.SMEM((1, 1, slots), jnp.int32),
                pltpu.VMEM((slots, tile, tile), BF16),
                pltpu.VMEM((row_nodes, col_nodes), F32),
                pltpu.SemaphoreType.DMA((3,)),
                pltpu.SemaphoreType.DMA((chunks,)),
            ],
            0,
            12 * row_nodes * col_nodes,
        )(tile_count, *(
            pltpu.with_memory_space_constraint(array, pltpu.HBM)
            for array in (tile_row, tile_col, tile_values, bias_row)
        ))
    else:
        slot_args = (
            tile_count.reshape(1),
            tile_row.reshape(slots),
            tile_col.reshape(slots),
            tile_values.reshape(slots, tile, tile),
        )
        slot_specs = [SMEM_SPEC] * 3 + [VMEM_SPEC]

    sources = exchange([features] * n_row, "row", n_row)
    if is_dense:
        other, source = call(
            forward_other_kernel,
            (like(own_nodes, width), like(col_nodes, width)),
            [VMEM_SPEC] * (1 + n_row),
            [],
            slots * matrix // 2,
            row_nodes * width * 8,
        )(dense, *sources)
        own = call(
            forward_own_kernel,
            like(own_nodes, width),
            [VMEM_SPEC] * 2,
            [],
            slots * matrix // 2,
            row_nodes * width * 8,
        )(dense, source)
    else:
        other, own = call(
            slot_forward_kernel,
            (like(own_nodes, width), like(own_nodes, width)),
            slot_specs + [VMEM_SPEC] * n_row,
            [pltpu.VMEM((col_nodes, width), BF16), pltpu.VMEM((row_nodes, width), F32)],
            slots * matrix // 2,
            row_nodes * width * 8,
        )(*slot_args, *sources)
    swapped = swap_cores(other, n_col)

    def chip_piece(k, before):
        return call(
            functools.partial(chip_kernel, k=k, n_chip=n_chip),
            like(tile, width),
            [VMEM_SPEC] * (2 + len(before)),
            [],
            tile * width,
            3 * block_bytes,
        )(own, swapped, *before)

    pieces = in_turn(n_chip, chip_piece)
    parts = exchange(pieces, "col", n_col, 2)
    if is_dense:
        turned = call(
            turn_kernel,
            like(col_nodes, row_nodes),
            [VMEM_SPEC] * 2,
            [],
            0,
            4 * row_nodes * col_nodes,
        )(dense, pieces[0])
    hidden_own, grad, aggregated = call(
        middle_kernel,
        [like(tile, hidden), like(tile, hidden), like(tile, width)],
        [VMEM_SPEC] * (3 + n_chip),
        [],
        matrix,
        n_chip * block_bytes,
    )(weight, bias_row, cotangent, *parts)
    grads = exchange([grad] * n_chip, "col", n_col, 2)
    hidden_out = call(copy_kernel, like(tile, hidden), [VMEM_SPEC], [], 0, 2 * block_bytes)(hidden_own)
    mine, theirs = call(
        term_kernel,
        [like(half + BIAS_ROWS, hidden)] * 2,
        [VMEM_SPEC] * 2,
        [pltpu.VMEM((width, hidden), F32)],
        matrix,
        6 * block_bytes,
    )(aggregated, grad)
    chip_term = add([swap_cores(theirs, n_col), mine])
    add_late = functools.partial(add, flops=ROW_SUM_WEIGHT * matrix)
    row_term = add_late(total_over(chip_term, add, "row", n_row))

    own_grads = call(
        gather_kernel,
        like(own_nodes, hidden),
        [VMEM_SPEC] * (1 + n_chip),
        [],
        0,
        own_nodes * hidden * 4,
    )(chip_term, *grads)
    other_grads = swap_cores(own_grads, n_col)
    if is_dense:
        back_own = call(
            back_own_kernel,
            like(col_nodes, hidden, F32),
            [VMEM_SPEC] * 2,
            [],
            slots * matrix // 2,
            row_nodes * hidden * 8,
        )(turned, own_grads)
        piece_kernel, piece_args = back_piece_kernel, (turned, back_own, other_grads)
    else:
        back = call(
            slot_back_kernel,
            like(col_nodes, hidden, F32),
            slot_specs + [VMEM_SPEC] * 2,
            [pltpu.VMEM((row_nodes, hidden), BF16)],
            slots * matrix // 2,
            row_nodes * hidden * 8,
        )(*slot_args, own_grads, other_grads)
        piece_kernel, piece_args = slot_piece_kernel, (back,)

    def back_piece(k, before):
        return call(
            functools.partial(piece_kernel, k=k, n_row=n_row),
            like(tile, hidden),
            [VMEM_SPEC] * (len(piece_args) + len(before)),
            [],
            n_chip * matrix,
            2 * block_bytes,
        )(*piece_args, *before)

    backs = exchange(in_turn(n_row, back_piece), "row", n_row)
    most = call(
        back_sum_kernel,
        like(tile, hidden, F32),
        [VMEM_SPEC] * (n_row - 1),
        [],
        BACK_SUM_WEIGHT * matrix,
        n_row * block_bytes,
    )(*backs[:-2], backs[-1])
    grad_features = call(
        features_kernel,
        like(tile, width),
        [VMEM_SPEC] * 3,
        [],
        FEATURES_WEIGHT * matrix,
        n_row * block_bytes,
    )(weight, most, backs[-2])
    all_terms = total_over(row_term, add, "col", n_col, 2)
    factor = (tile * n_row * n_col) ** (-0.5)
    own_half, bias_grad = call(
        functools.partial(scale_kernel, factor=factor),
        (like(half, hidden, F32), like(1, hidden, F32)),
        [VMEM_SPEC] * (1 + len(all_terms)),
        [],
        len(all_terms) * half * hidden,
        len(all_terms) * half * hidden * 2,
    )(most, *all_terms)
    other_half = swap_cores(own_half, n_col)
    grad_weight, grad_bias = call(
        join_kernel,
        (like(width, hidden, F32), like(1, hidden, F32)),
        [VMEM_SPEC] * 3,
        [],
        0,
        width * hidden * 8,
    )(own_half, other_half, bias_grad)
    return hidden_out, grad_features, grad_weight, grad_bias.reshape(hidden)


def solution(mesh):
    return jax.shard_map(
        local,
        mesh=mesh,
        in_specs=(
            P(("col", "row"), None),
            P(),
            P(),
            P(("row", "col"), None),
            P("row", "col", None, None, None),
            P("row", "col", None),
            P("row", "col", None),
            P("row", "col"),
        ),
        out_specs=(P(("row", "col"), None), P(("col", "row"), None), P(), P()),
        check_vma=False,
    )
```

```python
import functools

import jax
import jax.numpy as jnp
from jax import lax
from jax.experimental import pallas as pl
from jax.experimental.pallas import tpu as pltpu
from jax.sharding import PartitionSpec as P

F32 = jnp.float32
BF16 = jnp.bfloat16
ROOT_2_OVER_PI = 0.7978845608028654
CUBIC = 0.044715
VMEM_LIMIT = 48 * 1024 * 1024
BIAS_ROWS = 16
BACK_SUM_WEIGHT = 30
ROW_SUM_WEIGHT = 120
FEATURES_WEIGHT = 100

VMEM_SPEC = pl.BlockSpec(memory_space=pltpu.VMEM)
HBM_SPEC = pl.BlockSpec(memory_space=pltpu.HBM)
SMEM_SPEC = pl.BlockSpec(memory_space=pltpu.SMEM)


def call(kernel, out_shape, in_specs, scratch, flops, moved, out_spec=VMEM_SPEC):
    return pl.pallas_call(
        kernel,
        out_shape=out_shape,
        in_specs=in_specs,
        out_specs=jax.tree.map(lambda _: out_spec, out_shape),
        scratch_shapes=scratch,
        compiler_params=pltpu.CompilerParams(vmem_limit_bytes=VMEM_LIMIT),
        cost_estimate=pl.CostEstimate(flops=flops, bytes_accessed=moved, transcendentals=0),
    )


def partner(index, k, count):
    if count & (count - 1) == 0:
        return index ^ k
    return (k - index) % count


def far_first(count):
    return list(range(count - 1, -1, -1))


def pairs_of(k, size, cores):
    return [(i, partner(i // cores, k, size // cores) * cores + i % cores) for i in range(size)]


def exchange(blocks, axis, size, cores=1):
    received = []
    for k in far_first(size // cores):
        pairs = pairs_of(k, size, cores)
        moves = any(i != j for i, j in pairs)
        received.append(lax.ppermute(blocks[k], axis, pairs) if moves else blocks[k])
    return received


def swap_cores(block, size):
    return lax.ppermute(block, "col", [(i, i ^ 1) for i in range(size)])


def total_over(block, add, axis, size, cores=1):
    count = size // cores
    if count & (count - 1):
        return exchange([block] * count, axis, size, cores)
    terms, step = [block], 1
    while step < count:
        block = add(terms) if len(terms) > 1 else block
        terms = [lax.ppermute(block, axis, pairs_of(step, size, cores)), block]
        step *= 2
    return terms


def block_at(index, size):
    return pl.ds(pl.multiple_of(index * size, size), size)


def row_index():
    return lax.axis_index("row")


def chip_index():
    return lax.axis_index("col") // 2


def core_index():
    return lax.axis_index("col") % 2


def summed(refs):
    by_partner = dict(zip(far_first(len(refs)), refs))
    values = [by_partner[k][...].astype(F32) for k in sorted(by_partner)]
    while len(values) > 1:
        values = [sum(values[i + 1 : i + 2], values[i]) for i in range(0, len(values), 2)]
    return values[0]


def bias_rows(bias):
    high = bias.astype(BF16).astype(F32)
    line = lax.broadcasted_iota(jnp.int32, (BIAS_ROWS, bias.shape[1]), 0)
    return jnp.where(line == 0, high, jnp.where(line == 1, bias - high, 0.0))


def row_place(row, n_chip):
    return jnp.where(row % 2 == core_index(), 0, n_chip) + row // 2


def dense_kernel(
    count_ref, row_hbm, col_hbm, tiles_hbm, bias_hbm, dense_ref, bias_ref,
    row_ref, col_ref, tiles_ref, sum_ref, sems, tile_sems,
):
    slots, tile = tiles_ref.shape[0], tiles_ref.shape[1]
    n_chip = sum_ref.shape[0] // (2 * tile)
    chunks = tile_sems.shape[0]
    size = slots // chunks
    small = [
        pltpu.make_async_copy(row_hbm, row_ref, sems.at[0]),
        pltpu.make_async_copy(col_hbm, col_ref, sems.at[1]),
        pltpu.make_async_copy(bias_hbm, bias_ref, sems.at[2]),
    ]
    large = []
    for k in range(chunks):
        part = pl.ds(k * size, size)
        large.append(
            pltpu.make_async_copy(tiles_hbm.at[0, 0, part], tiles_ref.at[part], tile_sems.at[k])
        )
    for copy in small + large:
        copy.start()
    sum_ref[...] = jnp.zeros_like(sum_ref)
    for copy in small:
        copy.wait()
    count = count_ref[0, 0]

    def body(slot, carry):
        rows = block_at(row_place(row_ref[0, 0, slot], n_chip), tile)
        cols = block_at(col_ref[0, 0, slot], tile)
        sum_ref[rows, cols] += tiles_ref[slot].astype(F32)
        return carry

    for k, copy in enumerate(large):
        copy.wait()
        lax.fori_loop(k * size, jnp.minimum(count, (k + 1) * size), body, 0)
    dense_ref[...] = sum_ref[...].astype(BF16)


def turn_kernel(dense_ref, after_ref, turned_ref):
    rows = dense_ref.shape[0]
    step = 256 if rows % 256 == 0 else rows
    for first in range(0, rows, step):
        turned_ref[:, first : first + step] = dense_ref[first : first + step, :].T


def dense_dot(left, right):
    return jnp.dot(left, right, preferred_element_type=F32)


def gather_sources(sources, source_ref, index):
    tile = sources[0].shape[0]
    for k, ref in zip(far_first(len(sources)), sources):
        source_ref[block_at(partner(index, k, len(sources)), tile), :] = ref[...]


def slot_product(refs, source_ref, acc_ref, turned):
    count_ref, row_ref, col_ref, tiles_ref = refs
    tile = tiles_ref.shape[1]
    n_chip = (source_ref if turned else acc_ref).shape[0] // (2 * tile)
    contract = 0 if turned else 1
    acc_ref[...] = jnp.zeros_like(acc_ref)

    def body(slot, carry):
        places = [row_place(row_ref[slot], n_chip), col_ref[slot]]
        source, target = places if turned else places[::-1]
        acc_ref[block_at(target, tile), :] += lax.dot_general(
            tiles_ref[slot],
            source_ref[block_at(source, tile), :],
            (((contract,), (0,)), ((), ())),
            preferred_element_type=F32,
        )
        return carry

    lax.fori_loop(0, count_ref[0], body, 0)


def forward_other_kernel(dense_ref, *refs):
    sources, (other_ref, source_ref) = refs[:-2], refs[-2:]
    gather_sources(sources, source_ref, row_index())
    half = other_ref.shape[0]
    other_ref[...] = dense_dot(dense_ref[half:, :], source_ref[...]).astype(BF16)


def forward_own_kernel(dense_ref, source_ref, own_ref):
    own_ref[...] = dense_dot(dense_ref[: own_ref.shape[0], :], source_ref[...]).astype(BF16)


def slot_forward_kernel(count_ref, row_ref, col_ref, tiles_ref, *refs):
    sources, (other_ref, own_ref, source_ref, acc_ref) = refs[:-4], refs[-4:]
    gather_sources(sources, source_ref, row_index())
    slot_product((count_ref, row_ref, col_ref, tiles_ref), source_ref, acc_ref, False)
    half = own_ref.shape[0]
    own_ref[...] = acc_ref[:half, :].astype(BF16)
    other_ref[...] = acc_ref[half:, :].astype(BF16)


def chip_kernel(own_ref, other_ref, *refs, k, n_chip):
    out_ref = refs[-1]
    rows = block_at(partner(chip_index(), k, n_chip), out_ref.shape[0])
    out_ref[...] = (own_ref[rows, :].astype(F32) + other_ref[rows, :].astype(F32)).astype(BF16)


def middle_kernel(weight_ref, bias_ref, cot_ref, *refs):
    parts, (hidden_ref, grad_ref, agg_ref) = refs[:-3], refs[-3:]
    aggregated = summed(parts).astype(BF16)
    agg_ref[...] = aggregated
    v = dense_dot(aggregated, weight_ref[...]) + bias_ref[...]
    square = v * v
    t = jnp.tanh(ROOT_2_OVER_PI * (v + CUBIC * (square * v)))
    half = 0.5 * (1.0 + t)
    hidden_ref[...] = (v * half).astype(BF16)
    slope = half + 0.5 * v * (1.0 - t * t) * (ROOT_2_OVER_PI * (1.0 + 3.0 * CUBIC * square))
    grad_ref[...] = (cot_ref[...].astype(F32) * slope).astype(BF16)


def copy_kernel(in_ref, out_ref):
    out_ref[...] = in_ref[...]


def term_kernel(agg_ref, grad_ref, mine_ref, theirs_ref, acc_ref):
    grad = grad_ref[...]
    acc_ref[...] = lax.dot_general(
        agg_ref[...], grad, (((0,), (0,)), ((), ())), preferred_element_type=F32
    )
    half = acc_ref.shape[0] // 2
    bias = bias_rows(jnp.sum(grad.astype(F32), axis=0, keepdims=True)).astype(BF16)
    for ref, core in ((mine_ref, core_index()), (theirs_ref, 1 - core_index())):
        ref[:half, :] = acc_ref[block_at(core, half), :].astype(BF16)
        ref[half:, :] = bias


def add_terms_kernel(*refs, n_terms):
    total = summed(refs[:n_terms])
    out_ref = refs[-1]
    half = total.shape[0] - BIAS_ROWS
    out_ref[:half, :] = total[:half].astype(BF16)
    out_ref[half:, :] = bias_rows(total[half : half + 1] + total[half + 1 : half + 2]).astype(BF16)


def scale_kernel(after_ref, *refs, factor):
    parts, (half_ref, bias_ref) = refs[:-2], refs[-2:]
    total = summed(parts) * factor
    half = half_ref.shape[0]
    half_ref[...] = total[:half]
    bias_ref[...] = total[half : half + 1] + total[half + 1 : half + 2]


def gather_kernel(after_ref, *refs):
    gather_sources(refs[:-1], refs[-1], chip_index())


def back_own_kernel(turned_ref, source_ref, out_ref):
    out_ref[...] = dense_dot(turned_ref[:, : source_ref.shape[0]], source_ref[...])


def back_pieces_kernel(turned_ref, own_ref, source_ref, *outs):
    tile = outs[0].shape[0]
    for k, out_ref in zip(far_first(len(outs)), outs):
        rows = block_at(partner(row_index(), k, len(outs)), tile)
        rest = dense_dot(turned_ref[rows, source_ref.shape[0] :], source_ref[...])
        out_ref[...] = (own_ref[rows, :] + rest).astype(BF16)


def slot_back_kernel(count_ref, row_ref, col_ref, tiles_ref, own_ref, other_ref, *refs):
    outs, (source_ref, acc_ref) = refs[:-2], refs[-2:]
    half = own_ref.shape[0]
    source_ref[:half, :] = own_ref[...]
    source_ref[half:, :] = other_ref[...]
    slot_product((count_ref, row_ref, col_ref, tiles_ref), source_ref, acc_ref, True)
    tile = outs[0].shape[0]
    for k, out_ref in zip(far_first(len(outs)), outs):
        rows = block_at(partner(row_index(), k, len(outs)), tile)
        out_ref[...] = acc_ref[rows, :].astype(BF16)


def back_sum_kernel(*refs):
    total = refs[0][...].astype(F32)
    for ref in refs[1:-1]:
        total += ref[...].astype(F32)
    refs[-1][...] = total


def features_kernel(weight_ref, most_ref, last_ref, out_ref):
    out_ref[...] = lax.dot_general(
        (most_ref[...] + last_ref[...].astype(F32)).astype(BF16),
        weight_ref[...],
        (((1,), (1,)), ((), ())),
        preferred_element_type=F32,
    ).astype(BF16)


def write_kernel(
    features_ref, own_ref, other_ref, bias_ref, features_hbm, grad_hbm, bias_hbm, sems
):
    half = own_ref.shape[0]
    copies = [
        pltpu.make_async_copy(own_ref, grad_hbm.at[block_at(core_index(), half)], sems.at[0]),
        pltpu.make_async_copy(other_ref, grad_hbm.at[block_at(1 - core_index(), half)], sems.at[1]),
        pltpu.make_async_copy(features_ref, features_hbm, sems.at[2]),
        pltpu.make_async_copy(bias_ref, bias_hbm, sems.at[3]),
    ]
    for copy in copies:
        copy.start()
    for copy in copies:
        copy.wait()


def in_turn(count, make):
    made, before = {}, []
    for k in far_first(count):
        made[k] = make(k, before)
        before = [made[k]]
    return made


def local(features, weight, bias_term, cotangent, tile_values, tile_row, tile_col, tile_count):
    n_row = lax.axis_size("row")
    n_col = lax.axis_size("col")
    n_chip = n_col // 2
    tile, width = features.shape
    hidden = weight.shape[1]
    slots = tile_values.shape[2]
    row_nodes, col_nodes = n_col * tile, n_row * tile
    bias_row = bias_term.reshape(1, hidden)
    half = width // 2
    matrix = 2 * tile * width * hidden
    block_bytes = 2 * tile * width

    def like(rows, columns, dtype=BF16):
        return jax.ShapeDtypeStruct((rows, columns), dtype)

    near = 1
    own_nodes = n_chip * tile

    def add(terms, flops=0, after=()):
        return call(
            functools.partial(add_terms_kernel, n_terms=len(terms)),
            like(half + BIAS_ROWS, hidden),
            [VMEM_SPEC] * (len(terms) + len(after)),
            [],
            flops or len(terms) * half * hidden,
            len(terms) * half * hidden * 2,
        )(*terms, *after)

    is_dense = n_row * n_col <= 2 * slots
    if is_dense:
        chunks = 4 if slots % 4 == 0 else 1
        dense, bias_row = call(
            dense_kernel,
            (like(row_nodes, col_nodes), like(1, hidden, F32)),
            [SMEM_SPEC] + [HBM_SPEC] * 4,
            [
                pltpu.SMEM((1, 1, slots), jnp.int32),
                pltpu.SMEM((1, 1, slots), jnp.int32),
                pltpu.VMEM((slots, tile, tile), BF16),
                pltpu.VMEM((row_nodes, col_nodes), F32),
                pltpu.SemaphoreType.DMA((3,)),
                pltpu.SemaphoreType.DMA((chunks,)),
            ],
            0,
            12 * row_nodes * col_nodes,
        )(tile_count, *(
            pltpu.with_memory_space_constraint(array, pltpu.HBM)
            for array in (tile_row, tile_col, tile_values, bias_row)
        ))
    else:
        slot_args = (
            tile_count.reshape(1),
            tile_row.reshape(slots),
            tile_col.reshape(slots),
            tile_values.reshape(slots, tile, tile),
        )
        slot_specs = [SMEM_SPEC] * 3 + [VMEM_SPEC]

    sources = exchange([features] * n_row, "row", n_row)
    if is_dense:
        other, source = call(
            forward_other_kernel,
            (like(own_nodes, width), like(col_nodes, width)),
            [VMEM_SPEC] * (1 + n_row),
            [],
            slots * matrix // 2,
            row_nodes * width * 8,
        )(dense, *sources)
        own = call(
            forward_own_kernel,
            like(own_nodes, width),
            [VMEM_SPEC] * 2,
            [],
            slots * matrix // 2,
            row_nodes * width * 8,
        )(dense, source)
    else:
        other, own = call(
            slot_forward_kernel,
            (like(own_nodes, width), like(own_nodes, width)),
            slot_specs + [VMEM_SPEC] * n_row,
            [pltpu.VMEM((col_nodes, width), BF16), pltpu.VMEM((row_nodes, width), F32)],
            slots * matrix // 2,
            row_nodes * width * 8,
        )(*slot_args, *sources)
    swapped = swap_cores(other, n_col)

    def chip_piece(k, before):
        return call(
            functools.partial(chip_kernel, k=k, n_chip=n_chip),
            like(tile, width),
            [VMEM_SPEC] * (2 + len(before)),
            [],
            tile * width,
            3 * block_bytes,
        )(own, swapped, *before)

    pieces = in_turn(n_chip, chip_piece)
    parts = exchange(pieces, "col", n_col, 2)
    if is_dense:
        turned = call(
            turn_kernel,
            like(col_nodes, row_nodes),
            [VMEM_SPEC] * 2,
            [],
            0,
            4 * row_nodes * col_nodes,
        )(dense, pieces[0])
    hidden_own, grad, aggregated = call(
        middle_kernel,
        [like(tile, hidden), like(tile, hidden), like(tile, width)],
        [VMEM_SPEC] * (3 + n_chip),
        [],
        matrix,
        n_chip * block_bytes,
    )(weight, bias_row, cotangent, *parts)
    grads = exchange([grad] * n_chip, "col", n_col, 2)
    hidden_out = call(copy_kernel, like(tile, hidden), [VMEM_SPEC], [], 0, 2 * block_bytes)(hidden_own)
    mine, theirs = call(
        term_kernel,
        [like(half + BIAS_ROWS, hidden)] * 2,
        [VMEM_SPEC] * 2,
        [pltpu.VMEM((width, hidden), F32)],
        matrix,
        6 * block_bytes,
    )(aggregated, grad)
    chip_term = add([swap_cores(theirs, n_col), mine])
    add_late = functools.partial(add, flops=ROW_SUM_WEIGHT * matrix)
    row_terms = total_over(chip_term, add, "row", n_row)
    row_term = add_late(row_terms)

    own_grads = call(
        gather_kernel,
        like(own_nodes, hidden),
        [VMEM_SPEC] * (1 + n_chip),
        [],
        0,
        own_nodes * hidden * 4,
    )(row_terms[-1], *grads)
    other_grads = swap_cores(own_grads, n_col)
    if is_dense:
        back_own = call(
            back_own_kernel,
            like(col_nodes, hidden, F32),
            [VMEM_SPEC] * 2,
            [],
            slots * matrix // 2,
            row_nodes * hidden * 8,
        )(turned, own_grads)
        back_pieces = call(
            back_pieces_kernel,
            [like(tile, hidden)] * n_row,
            [VMEM_SPEC] * 3,
            [],
            slots * matrix // 2,
            row_nodes * hidden * 8,
        )(turned, back_own, other_grads)
    else:
        back_pieces = call(
            slot_back_kernel,
            [like(tile, hidden)] * n_row,
            slot_specs + [VMEM_SPEC] * 2,
            [pltpu.VMEM((row_nodes, hidden), BF16), pltpu.VMEM((col_nodes, hidden), F32)],
            slots * matrix // 2,
            row_nodes * hidden * 8,
        )(*slot_args, own_grads, other_grads)
    backs = exchange(dict(zip(far_first(n_row), back_pieces)), "row", n_row)
    def back_sum(*blocks):
        return call(
            back_sum_kernel,
            like(tile, hidden, F32),
            [VMEM_SPEC] * len(blocks),
            [],
            BACK_SUM_WEIGHT * matrix,
            n_row * block_bytes,
        )(*blocks)

    first = back_sum(*backs[:1], backs[-1])
    most = back_sum(first, *backs[1:-2])
    own_features = call(
        features_kernel,
        like(tile, width),
        [VMEM_SPEC] * 3,
        [],
        FEATURES_WEIGHT * matrix,
        n_row * block_bytes,
    )(weight, most, backs[-2])
    all_terms = total_over(row_term, functools.partial(add, after=[first]), "col", n_col, 2)
    factor = (tile * n_row * n_col) ** (-0.5)
    own_half, bias_grad = call(
        functools.partial(scale_kernel, factor=factor),
        (like(half, hidden, F32), like(1, hidden, F32)),
        [VMEM_SPEC] * (1 + len(all_terms)),
        [],
        len(all_terms) * half * hidden,
        len(all_terms) * half * hidden * 2,
    )(most, *all_terms)
    grad_features, grad_weight, grad_bias = call(
        write_kernel,
        (like(tile, width), like(width, hidden, F32), like(1, hidden, F32)),
        [VMEM_SPEC] * 4,
        [pltpu.SemaphoreType.DMA((4,))],
        0,
        width * hidden * 8,
        HBM_SPEC,
    )(own_features, own_half, swap_cores(own_half, n_col), bias_grad)
    return hidden_out, grad_features, grad_weight, grad_bias.reshape(hidden)


def solution(mesh):
    return jax.shard_map(
        local,
        mesh=mesh,
        in_specs=(
            P(("col", "row"), None),
            P(),
            P(),
            P(("row", "col"), None),
            P("row", "col", None, None, None),
            P("row", "col", None),
            P("row", "col", None),
            P("row", "col"),
        ),
        out_specs=(P(("row", "col"), None), P(("col", "row"), None), P(), P()),
        check_vma=False,
    )
```

```python
import functools

import jax
import jax.numpy as jnp
from jax import lax
from jax.experimental import pallas as pl
from jax.experimental.pallas import tpu as pltpu
from jax.sharding import PartitionSpec as P

F32 = jnp.float32
BF16 = jnp.bfloat16
ROOT_2_OVER_PI = 0.7978845608028654
CUBIC = 0.044715
VMEM_LIMIT = 48 * 1024 * 1024
BIAS_ROWS = 16
BACK_SUM_WEIGHT = 30
ROW_SUM_WEIGHT = 120
FEATURES_WEIGHT = 100

VMEM_SPEC = pl.BlockSpec(memory_space=pltpu.VMEM)
HBM_SPEC = pl.BlockSpec(memory_space=pltpu.HBM)
SMEM_SPEC = pl.BlockSpec(memory_space=pltpu.SMEM)


def call(kernel, out_shape, in_specs, scratch, flops, moved, out_spec=VMEM_SPEC):
    return pl.pallas_call(
        kernel,
        out_shape=out_shape,
        in_specs=in_specs,
        out_specs=jax.tree.map(lambda _: out_spec, out_shape),
        scratch_shapes=scratch,
        compiler_params=pltpu.CompilerParams(vmem_limit_bytes=VMEM_LIMIT),
        cost_estimate=pl.CostEstimate(flops=flops, bytes_accessed=moved, transcendentals=0),
    )


def partner(index, k, count):
    if count & (count - 1) == 0:
        return index ^ k
    return (k - index) % count


def far_first(count):
    return list(range(count - 1, -1, -1))


def pairs_of(k, size, cores):
    return [(i, partner(i // cores, k, size // cores) * cores + i % cores) for i in range(size)]


def exchange(blocks, axis, size, cores=1):
    received = []
    for k in far_first(size // cores):
        pairs = pairs_of(k, size, cores)
        moves = any(i != j for i, j in pairs)
        received.append(lax.ppermute(blocks[k], axis, pairs) if moves else blocks[k])
    return received


def swap_cores(block, size):
    return lax.ppermute(block, "col", [(i, i ^ 1) for i in range(size)])


def total_over(block, add, axis, size, cores=1):
    count = size // cores
    if count & (count - 1):
        return exchange([block] * count, axis, size, cores)
    terms, step = [block], count // 2
    while step:
        block = add(terms) if len(terms) > 1 else block
        terms = [lax.ppermute(block, axis, pairs_of(step, size, cores)), block]
        step //= 2
    return terms


def block_at(index, size):
    return pl.ds(pl.multiple_of(index * size, size), size)


def row_index():
    return lax.axis_index("row")


def chip_index():
    return lax.axis_index("col") // 2


def core_index():
    return lax.axis_index("col") % 2


def summed(refs):
    by_partner = dict(zip(far_first(len(refs)), refs))
    values = [by_partner[k][...].astype(F32) for k in sorted(by_partner)]
    while len(values) > 1:
        values = [sum(values[i + 1 : i + 2], values[i]) for i in range(0, len(values), 2)]
    return values[0]


def bias_rows(bias):
    high = bias.astype(BF16).astype(F32)
    line = lax.broadcasted_iota(jnp.int32, (BIAS_ROWS, bias.shape[1]), 0)
    return jnp.where(line == 0, high, jnp.where(line == 1, bias - high, 0.0))


def row_place(row, n_chip):
    return jnp.where(row % 2 == core_index(), 0, n_chip) + row // 2


def dense_kernel(
    count_ref, row_hbm, col_hbm, tiles_hbm, bias_hbm, dense_ref, bias_ref,
    row_ref, col_ref, tiles_ref, sum_ref, sems, tile_sems,
):
    slots, tile = tiles_ref.shape[0], tiles_ref.shape[1]
    n_chip = sum_ref.shape[0] // (2 * tile)
    chunks = tile_sems.shape[0]
    size = slots // chunks
    small = [
        pltpu.make_async_copy(row_hbm, row_ref, sems.at[0]),
        pltpu.make_async_copy(col_hbm, col_ref, sems.at[1]),
        pltpu.make_async_copy(bias_hbm, bias_ref, sems.at[2]),
    ]
    large = []
    for k in range(chunks):
        part = pl.ds(k * size, size)
        large.append(
            pltpu.make_async_copy(tiles_hbm.at[0, 0, part], tiles_ref.at[part], tile_sems.at[k])
        )
    for copy in small + large:
        copy.start()
    sum_ref[...] = jnp.zeros_like(sum_ref)
    for copy in small:
        copy.wait()
    count = count_ref[0, 0]

    def body(slot, carry):
        rows = block_at(row_place(row_ref[0, 0, slot], n_chip), tile)
        cols = block_at(col_ref[0, 0, slot], tile)
        sum_ref[rows, cols] += tiles_ref[slot].astype(F32)
        return carry

    for k, copy in enumerate(large):
        copy.wait()
        lax.fori_loop(k * size, jnp.minimum(count, (k + 1) * size), body, 0)
    dense_ref[...] = sum_ref[...].astype(BF16)


def turn_kernel(dense_ref, after_ref, turned_ref):
    rows = dense_ref.shape[0]
    step = 256 if rows % 256 == 0 else rows
    for first in range(0, rows, step):
        turned_ref[:, first : first + step] = dense_ref[first : first + step, :].T


def dense_dot(left, right):
    return jnp.dot(left, right, preferred_element_type=F32)


def gather_sources(sources, source_ref, index):
    tile = sources[0].shape[0]
    for k, ref in zip(far_first(len(sources)), sources):
        source_ref[block_at(partner(index, k, len(sources)), tile), :] = ref[...]


def slot_product(refs, source_ref, acc_ref, turned):
    count_ref, row_ref, col_ref, tiles_ref = refs
    tile = tiles_ref.shape[1]
    n_chip = (source_ref if turned else acc_ref).shape[0] // (2 * tile)
    contract = 0 if turned else 1
    acc_ref[...] = jnp.zeros_like(acc_ref)

    def body(slot, carry):
        places = [row_place(row_ref[slot], n_chip), col_ref[slot]]
        source, target = places if turned else places[::-1]
        acc_ref[block_at(target, tile), :] += lax.dot_general(
            tiles_ref[slot],
            source_ref[block_at(source, tile), :],
            (((contract,), (0,)), ((), ())),
            preferred_element_type=F32,
        )
        return carry

    lax.fori_loop(0, count_ref[0], body, 0)


def forward_other_kernel(dense_ref, *refs):
    sources, (other_ref, source_ref) = refs[:-2], refs[-2:]
    gather_sources(sources, source_ref, row_index())
    half = other_ref.shape[0]
    other_ref[...] = dense_dot(dense_ref[half:, :], source_ref[...]).astype(BF16)


def forward_own_kernel(dense_ref, source_ref, own_ref):
    own_ref[...] = dense_dot(dense_ref[: own_ref.shape[0], :], source_ref[...]).astype(BF16)


def slot_forward_kernel(count_ref, row_ref, col_ref, tiles_ref, *refs):
    sources, (other_ref, own_ref, source_ref, acc_ref) = refs[:-4], refs[-4:]
    gather_sources(sources, source_ref, row_index())
    slot_product((count_ref, row_ref, col_ref, tiles_ref), source_ref, acc_ref, False)
    half = own_ref.shape[0]
    own_ref[...] = acc_ref[:half, :].astype(BF16)
    other_ref[...] = acc_ref[half:, :].astype(BF16)


def chip_kernel(own_ref, other_ref, *refs, k, n_chip):
    out_ref = refs[-1]
    rows = block_at(partner(chip_index(), k, n_chip), out_ref.shape[0])
    out_ref[...] = (own_ref[rows, :].astype(F32) + other_ref[rows, :].astype(F32)).astype(BF16)


def middle_kernel(weight_ref, bias_ref, cot_ref, *refs):
    parts, (hidden_ref, grad_ref, agg_ref) = refs[:-3], refs[-3:]
    aggregated = summed(parts).astype(BF16)
    agg_ref[...] = aggregated
    v = dense_dot(aggregated, weight_ref[...]) + bias_ref[...]
    square = v * v
    t = jnp.tanh(ROOT_2_OVER_PI * (v + CUBIC * (square * v)))
    half = 0.5 * (1.0 + t)
    hidden_ref[...] = (v * half).astype(BF16)
    slope = half + 0.5 * v * (1.0 - t * t) * (ROOT_2_OVER_PI * (1.0 + 3.0 * CUBIC * square))
    grad_ref[...] = (cot_ref[...].astype(F32) * slope).astype(BF16)


def copy_kernel(in_ref, out_ref):
    out_ref[...] = in_ref[...]


def term_kernel(agg_ref, grad_ref, mine_ref, theirs_ref, acc_ref):
    grad = grad_ref[...]
    acc_ref[...] = lax.dot_general(
        agg_ref[...], grad, (((0,), (0,)), ((), ())), preferred_element_type=F32
    )
    half = acc_ref.shape[0] // 2
    bias = bias_rows(jnp.sum(grad.astype(F32), axis=0, keepdims=True)).astype(BF16)
    for ref, core in ((mine_ref, core_index()), (theirs_ref, 1 - core_index())):
        ref[:half, :] = acc_ref[block_at(core, half), :].astype(BF16)
        ref[half:, :] = bias


def add_terms_kernel(*refs, n_terms):
    total = summed(refs[:n_terms])
    out_ref = refs[-1]
    half = total.shape[0] - BIAS_ROWS
    out_ref[:half, :] = total[:half].astype(BF16)
    out_ref[half:, :] = bias_rows(total[half : half + 1] + total[half + 1 : half + 2]).astype(BF16)


def scale_kernel(after_ref, *refs, factor):
    parts, (half_ref, bias_ref) = refs[:-2], refs[-2:]
    total = summed(parts) * factor
    half = half_ref.shape[0]
    half_ref[...] = total[:half]
    bias_ref[...] = total[half : half + 1] + total[half + 1 : half + 2]


def gather_kernel(after_ref, *refs):
    gather_sources(refs[:-1], refs[-1], chip_index())


def back_own_kernel(turned_ref, source_ref, out_ref):
    out_ref[...] = dense_dot(turned_ref[:, : source_ref.shape[0]], source_ref[...])


def back_pieces_kernel(turned_ref, own_ref, source_ref, *outs):
    tile = outs[0].shape[0]
    for k, out_ref in zip(far_first(len(outs)), outs):
        rows = block_at(partner(row_index(), k, len(outs)), tile)
        rest = dense_dot(turned_ref[rows, source_ref.shape[0] :], source_ref[...])
        out_ref[...] = (own_ref[rows, :] + rest).astype(BF16)


def slot_back_kernel(count_ref, row_ref, col_ref, tiles_ref, own_ref, other_ref, *refs):
    outs, (source_ref, acc_ref) = refs[:-2], refs[-2:]
    half = own_ref.shape[0]
    source_ref[:half, :] = own_ref[...]
    source_ref[half:, :] = other_ref[...]
    slot_product((count_ref, row_ref, col_ref, tiles_ref), source_ref, acc_ref, True)
    tile = outs[0].shape[0]
    for k, out_ref in zip(far_first(len(outs)), outs):
        rows = block_at(partner(row_index(), k, len(outs)), tile)
        out_ref[...] = acc_ref[rows, :].astype(BF16)


def back_sum_kernel(*refs):
    total = refs[0][...].astype(F32)
    for ref in refs[1:-1]:
        total += ref[...].astype(F32)
    refs[-1][...] = total


def features_kernel(weight_ref, most_ref, last_ref, out_ref):
    out_ref[...] = lax.dot_general(
        (most_ref[...] + last_ref[...].astype(F32)).astype(BF16),
        weight_ref[...],
        (((1,), (1,)), ((), ())),
        preferred_element_type=F32,
    ).astype(BF16)


def write_kernel(
    features_ref, own_ref, other_ref, bias_ref, features_hbm, grad_hbm, bias_hbm, sems
):
    half = own_ref.shape[0]
    copies = [
        pltpu.make_async_copy(own_ref, grad_hbm.at[block_at(core_index(), half)], sems.at[0]),
        pltpu.make_async_copy(other_ref, grad_hbm.at[block_at(1 - core_index(), half)], sems.at[1]),
        pltpu.make_async_copy(features_ref, features_hbm, sems.at[2]),
        pltpu.make_async_copy(bias_ref, bias_hbm, sems.at[3]),
    ]
    for copy in copies:
        copy.start()
    for copy in copies:
        copy.wait()


def in_turn(count, make):
    made, before = {}, []
    for k in far_first(count):
        made[k] = make(k, before)
        before = [made[k]]
    return made


def local(features, weight, bias_term, cotangent, tile_values, tile_row, tile_col, tile_count):
    n_row = lax.axis_size("row")
    n_col = lax.axis_size("col")
    n_chip = n_col // 2
    tile, width = features.shape
    hidden = weight.shape[1]
    slots = tile_values.shape[2]
    row_nodes, col_nodes = n_col * tile, n_row * tile
    bias_row = bias_term.reshape(1, hidden)
    half = width // 2
    matrix = 2 * tile * width * hidden
    block_bytes = 2 * tile * width

    def like(rows, columns, dtype=BF16):
        return jax.ShapeDtypeStruct((rows, columns), dtype)

    near = 1
    own_nodes = n_chip * tile

    def add(terms, flops=0):
        return call(
            functools.partial(add_terms_kernel, n_terms=len(terms)),
            like(half + BIAS_ROWS, hidden),
            [VMEM_SPEC] * len(terms),
            [],
            flops or len(terms) * half * hidden,
            len(terms) * half * hidden * 2,
        )(*terms)

    is_dense = n_row * n_col <= 2 * slots
    if is_dense:
        chunks = 4 if slots % 4 == 0 else 1
        dense, bias_row = call(
            dense_kernel,
            (like(row_nodes, col_nodes), like(1, hidden, F32)),
            [SMEM_SPEC] + [HBM_SPEC] * 4,
            [
                pltpu.SMEM((1, 1, slots), jnp.int32),
                pltpu.SMEM((1, 1, slots), jnp.int32),
                pltpu.VMEM((slots, tile, tile), BF16),
                pltpu.VMEM((row_nodes, col_nodes), F32),
                pltpu.SemaphoreType.DMA((3,)),
                pltpu.SemaphoreType.DMA((chunks,)),
            ],
            0,
            12 * row_nodes * col_nodes,
        )(tile_count, *(
            pltpu.with_memory_space_constraint(array, pltpu.HBM)
            for array in (tile_row, tile_col, tile_values, bias_row)
        ))
    else:
        slot_args = (
            tile_count.reshape(1),
            tile_row.reshape(slots),
            tile_col.reshape(slots),
            tile_values.reshape(slots, tile, tile),
        )
        slot_specs = [SMEM_SPEC] * 3 + [VMEM_SPEC]

    sources = exchange([features] * n_row, "row", n_row)
    if is_dense:
        other, source = call(
            forward_other_kernel,
            (like(own_nodes, width), like(col_nodes, width)),
            [VMEM_SPEC] * (1 + n_row),
            [],
            slots * matrix // 2,
            row_nodes * width * 8,
        )(dense, *sources)
        own = call(
            forward_own_kernel,
            like(own_nodes, width),
            [VMEM_SPEC] * 2,
            [],
            slots * matrix // 2,
            row_nodes * width * 8,
        )(dense, source)
    else:
        other, own = call(
            slot_forward_kernel,
            (like(own_nodes, width), like(own_nodes, width)),
            slot_specs + [VMEM_SPEC] * n_row,
            [pltpu.VMEM((col_nodes, width), BF16), pltpu.VMEM((row_nodes, width), F32)],
            slots * matrix // 2,
            row_nodes * width * 8,
        )(*slot_args, *sources)
    swapped = swap_cores(other, n_col)

    def chip_piece(k, before):
        return call(
            functools.partial(chip_kernel, k=k, n_chip=n_chip),
            like(tile, width),
            [VMEM_SPEC] * (2 + len(before)),
            [],
            tile * width,
            3 * block_bytes,
        )(own, swapped, *before)

    pieces = in_turn(n_chip, chip_piece)
    parts = exchange(pieces, "col", n_col, 2)
    if is_dense:
        turned = call(
            turn_kernel,
            like(col_nodes, row_nodes),
            [VMEM_SPEC] * 2,
            [],
            0,
            4 * row_nodes * col_nodes,
        )(dense, pieces[0])
    hidden_own, grad, aggregated = call(
        middle_kernel,
        [like(tile, hidden), like(tile, hidden), like(tile, width)],
        [VMEM_SPEC] * (3 + n_chip),
        [],
        matrix,
        n_chip * block_bytes,
    )(weight, bias_row, cotangent, *parts)
    grads = exchange([grad] * n_chip, "col", n_col, 2)
    hidden_out = call(copy_kernel, like(tile, hidden), [VMEM_SPEC], [], 0, 2 * block_bytes)(hidden_own)
    mine, theirs = call(
        term_kernel,
        [like(half + BIAS_ROWS, hidden)] * 2,
        [VMEM_SPEC] * 2,
        [pltpu.VMEM((width, hidden), F32)],
        matrix,
        6 * block_bytes,
    )(aggregated, grad)
    chip_term = add([swap_cores(theirs, n_col), mine])
    add_late = functools.partial(add, flops=ROW_SUM_WEIGHT * matrix)
    row_term = add_late(total_over(chip_term, add, "row", n_row))

    own_grads = call(
        gather_kernel,
        like(own_nodes, hidden),
        [VMEM_SPEC] * (1 + n_chip),
        [],
        0,
        own_nodes * hidden * 4,
    )(chip_term, *grads)
    other_grads = swap_cores(own_grads, n_col)
    if is_dense:
        back_own = call(
            back_own_kernel,
            like(col_nodes, hidden, F32),
            [VMEM_SPEC] * 2,
            [],
            slots * matrix // 2,
            row_nodes * hidden * 8,
        )(turned, own_grads)
        back_pieces = call(
            back_pieces_kernel,
            [like(tile, hidden)] * n_row,
            [VMEM_SPEC] * 3,
            [],
            slots * matrix // 2,
            row_nodes * hidden * 8,
        )(turned, back_own, other_grads)
    else:
        back_pieces = call(
            slot_back_kernel,
            [like(tile, hidden)] * n_row,
            slot_specs + [VMEM_SPEC] * 2,
            [pltpu.VMEM((row_nodes, hidden), BF16), pltpu.VMEM((col_nodes, hidden), F32)],
            slots * matrix // 2,
            row_nodes * hidden * 8,
        )(*slot_args, own_grads, other_grads)
    backs = exchange(dict(zip(far_first(n_row), back_pieces)), "row", n_row)
    most = call(
        back_sum_kernel,
        like(tile, hidden, F32),
        [VMEM_SPEC] * (n_row - 1),
        [],
        BACK_SUM_WEIGHT * matrix,
        n_row * block_bytes,
    )(*backs[:-2], backs[-1])
    own_features = call(
        features_kernel,
        like(tile, width),
        [VMEM_SPEC] * 3,
        [],
        FEATURES_WEIGHT * matrix,
        n_row * block_bytes,
    )(weight, most, backs[-2])
    all_terms = total_over(row_term, add, "col", n_col, 2)
    factor = (tile * n_row * n_col) ** (-0.5)
    own_half, bias_grad = call(
        functools.partial(scale_kernel, factor=factor),
        (like(half, hidden, F32), like(1, hidden, F32)),
        [VMEM_SPEC] * (1 + len(all_terms)),
        [],
        len(all_terms) * half * hidden,
        len(all_terms) * half * hidden * 2,
    )(most, *all_terms)
    grad_features, grad_weight, grad_bias = call(
        write_kernel,
        (like(tile, width), like(width, hidden, F32), like(1, hidden, F32)),
        [VMEM_SPEC] * 4,
        [pltpu.SemaphoreType.DMA((4,))],
        0,
        width * hidden * 8,
        HBM_SPEC,
    )(own_features, own_half, swap_cores(own_half, n_col), bias_grad)
    return hidden_out, grad_features, grad_weight, grad_bias.reshape(hidden)


def solution(mesh):
    return jax.shard_map(
        local,
        mesh=mesh,
        in_specs=(
            P(("col", "row"), None),
            P(),
            P(),
            P(("row", "col"), None),
            P("row", "col", None, None, None),
            P("row", "col", None),
            P("row", "col", None),
            P("row", "col"),
        ),
        out_specs=(P(("row", "col"), None), P(("col", "row"), None), P(), P()),
        check_vma=False,
    )
```

```python
import functools

import jax
import jax.numpy as jnp
from jax import lax
from jax.experimental import pallas as pl
from jax.experimental.pallas import tpu as pltpu
from jax.sharding import PartitionSpec as P

F32 = jnp.float32
BF16 = jnp.bfloat16
ROOT_2_OVER_PI = 0.7978845608028654
CUBIC = 0.044715
VMEM_LIMIT = 48 * 1024 * 1024
BIAS_ROWS = 16
ROW_SUM_WEIGHT = 120
FEATURES_WEIGHT = 100

VMEM_SPEC = pl.BlockSpec(memory_space=pltpu.VMEM)
HBM_SPEC = pl.BlockSpec(memory_space=pltpu.HBM)
SMEM_SPEC = pl.BlockSpec(memory_space=pltpu.SMEM)


def call(kernel, out_shape, in_specs, scratch, flops, moved, out_spec=VMEM_SPEC):
    return pl.pallas_call(
        kernel,
        out_shape=out_shape,
        in_specs=in_specs,
        out_specs=jax.tree.map(lambda _: out_spec, out_shape),
        scratch_shapes=scratch,
        compiler_params=pltpu.CompilerParams(vmem_limit_bytes=VMEM_LIMIT),
        cost_estimate=pl.CostEstimate(flops=flops, bytes_accessed=moved, transcendentals=0),
    )


def partner(index, k, count):
    if count & (count - 1) == 0:
        return index ^ k
    return (k - index) % count


def far_first(count):
    return list(range(count - 1, -1, -1))


def pairs_of(k, size, cores):
    return [(i, partner(i // cores, k, size // cores) * cores + i % cores) for i in range(size)]


def exchange(blocks, axis, size, cores=1):
    received = []
    for k in far_first(size // cores):
        pairs = pairs_of(k, size, cores)
        moves = any(i != j for i, j in pairs)
        received.append(lax.ppermute(blocks[k], axis, pairs) if moves else blocks[k])
    return received


def swap_cores(block, size):
    return lax.ppermute(block, "col", [(i, i ^ 1) for i in range(size)])


def total_over(block, add, axis, size, cores=1):
    count = size // cores
    if count & (count - 1):
        return exchange([block] * count, axis, size, cores)
    terms, step = [block], 1
    while step < count:
        block = add(terms) if len(terms) > 1 else block
        terms = [lax.ppermute(block, axis, pairs_of(step, size, cores)), block]
        step *= 2
    return terms


def block_at(index, size):
    return pl.ds(pl.multiple_of(index * size, size), size)


def row_index():
    return lax.axis_index("row")


def chip_index():
    return lax.axis_index("col") // 2


def core_index():
    return lax.axis_index("col") % 2


def summed(refs):
    by_partner = dict(zip(far_first(len(refs)), refs))
    values = [by_partner[k][...].astype(F32) for k in sorted(by_partner)]
    while len(values) > 1:
        values = [sum(values[i + 1 : i + 2], values[i]) for i in range(0, len(values), 2)]
    return values[0]


def bias_rows(bias):
    high = bias.astype(BF16).astype(F32)
    line = lax.broadcasted_iota(jnp.int32, (BIAS_ROWS, bias.shape[1]), 0)
    return jnp.where(line == 0, high, jnp.where(line == 1, bias - high, 0.0))


def row_place(row, n_chip):
    return jnp.where(row % 2 == core_index(), 0, n_chip) + row // 2


def dense_kernel(
    count_ref, row_hbm, col_hbm, tiles_hbm, bias_hbm, dense_ref, bias_ref,
    row_ref, col_ref, tiles_ref, sum_ref, sems, tile_sems,
):
    slots, tile = tiles_ref.shape[0], tiles_ref.shape[1]
    n_chip = sum_ref.shape[0] // (2 * tile)
    chunks = tile_sems.shape[0]
    size = slots // chunks
    small = [
        pltpu.make_async_copy(row_hbm, row_ref, sems.at[0]),
        pltpu.make_async_copy(col_hbm, col_ref, sems.at[1]),
        pltpu.make_async_copy(bias_hbm, bias_ref, sems.at[2]),
    ]
    large = []
    for k in range(chunks):
        part = pl.ds(k * size, size)
        large.append(
            pltpu.make_async_copy(tiles_hbm.at[0, 0, part], tiles_ref.at[part], tile_sems.at[k])
        )
    for copy in small + large:
        copy.start()
    sum_ref[...] = jnp.zeros_like(sum_ref)
    for copy in small:
        copy.wait()
    count = count_ref[0, 0]

    def body(slot, carry):
        rows = block_at(row_place(row_ref[0, 0, slot], n_chip), tile)
        cols = block_at(col_ref[0, 0, slot], tile)
        sum_ref[rows, cols] += tiles_ref[slot].astype(F32)
        return carry

    for k, copy in enumerate(large):
        copy.wait()
        lax.fori_loop(k * size, jnp.minimum(count, (k + 1) * size), body, 0)
    dense_ref[...] = sum_ref[...].astype(BF16)


def turn_kernel(dense_ref, after_ref, turned_ref):
    rows = dense_ref.shape[0]
    step = 256 if rows % 256 == 0 else rows
    for first in range(0, rows, step):
        turned_ref[:, first : first + step] = dense_ref[first : first + step, :].T


def dense_dot(left, right):
    return jnp.dot(left, right, preferred_element_type=F32)


def gather_sources(sources, source_ref, index):
    tile = sources[0].shape[0]
    for k, ref in zip(far_first(len(sources)), sources):
        source_ref[block_at(partner(index, k, len(sources)), tile), :] = ref[...]


def slot_product(refs, source_ref, acc_ref, turned):
    count_ref, row_ref, col_ref, tiles_ref = refs
    tile = tiles_ref.shape[1]
    n_chip = (source_ref if turned else acc_ref).shape[0] // (2 * tile)
    contract = 0 if turned else 1
    acc_ref[...] = jnp.zeros_like(acc_ref)

    def body(slot, carry):
        places = [row_place(row_ref[slot], n_chip), col_ref[slot]]
        source, target = places if turned else places[::-1]
        acc_ref[block_at(target, tile), :] += lax.dot_general(
            tiles_ref[slot],
            source_ref[block_at(source, tile), :],
            (((contract,), (0,)), ((), ())),
            preferred_element_type=F32,
        )
        return carry

    lax.fori_loop(0, count_ref[0], body, 0)


def forward_other_kernel(dense_ref, *refs):
    sources, (other_ref, source_ref) = refs[:-2], refs[-2:]
    gather_sources(sources, source_ref, row_index())
    half = other_ref.shape[0]
    other_ref[...] = dense_dot(dense_ref[half:, :], source_ref[...]).astype(BF16)


def forward_own_kernel(dense_ref, source_ref, own_ref):
    own_ref[...] = dense_dot(dense_ref[: own_ref.shape[0], :], source_ref[...]).astype(BF16)


def slot_forward_kernel(count_ref, row_ref, col_ref, tiles_ref, *refs):
    sources, (other_ref, own_ref, source_ref, acc_ref) = refs[:-4], refs[-4:]
    gather_sources(sources, source_ref, row_index())
    slot_product((count_ref, row_ref, col_ref, tiles_ref), source_ref, acc_ref, False)
    half = own_ref.shape[0]
    own_ref[...] = acc_ref[:half, :].astype(BF16)
    other_ref[...] = acc_ref[half:, :].astype(BF16)


def chip_kernel(own_ref, other_ref, *refs, k, n_chip):
    out_ref = refs[-1]
    rows = block_at(partner(chip_index(), k, n_chip), out_ref.shape[0])
    out_ref[...] = (own_ref[rows, :].astype(F32) + other_ref[rows, :].astype(F32)).astype(BF16)


def middle_kernel(weight_ref, bias_ref, cot_ref, *refs):
    parts, (hidden_ref, grad_ref, agg_ref) = refs[:-3], refs[-3:]
    aggregated = summed(parts).astype(BF16)
    agg_ref[...] = aggregated
    v = dense_dot(aggregated, weight_ref[...]) + bias_ref[...]
    square = v * v
    t = jnp.tanh(ROOT_2_OVER_PI * (v + CUBIC * (square * v)))
    half = 0.5 * (1.0 + t)
    hidden_ref[...] = (v * half).astype(BF16)
    slope = half + 0.5 * v * (1.0 - t * t) * (ROOT_2_OVER_PI * (1.0 + 3.0 * CUBIC * square))
    grad_ref[...] = (cot_ref[...].astype(F32) * slope).astype(BF16)


def copy_kernel(in_ref, out_ref):
    out_ref[...] = in_ref[...]


def term_kernel(agg_ref, grad_ref, mine_ref, theirs_ref, acc_ref):
    grad = grad_ref[...]
    acc_ref[...] = lax.dot_general(
        agg_ref[...], grad, (((0,), (0,)), ((), ())), preferred_element_type=F32
    )
    half = acc_ref.shape[0] // 2
    bias = bias_rows(jnp.sum(grad.astype(F32), axis=0, keepdims=True)).astype(BF16)
    for ref, core in ((mine_ref, core_index()), (theirs_ref, 1 - core_index())):
        ref[:half, :] = acc_ref[block_at(core, half), :].astype(BF16)
        ref[half:, :] = bias


def add_terms_kernel(*refs, n_terms):
    total = summed(refs[:n_terms])
    out_ref = refs[-1]
    half = total.shape[0] - BIAS_ROWS
    out_ref[:half, :] = total[:half].astype(BF16)
    out_ref[half:, :] = bias_rows(total[half : half + 1] + total[half + 1 : half + 2]).astype(BF16)


def scale_kernel(after_ref, *refs, factor):
    parts, (half_ref, bias_ref) = refs[:-2], refs[-2:]
    total = summed(parts) * factor
    half = half_ref.shape[0]
    half_ref[...] = total[:half]
    bias_ref[...] = total[half : half + 1] + total[half + 1 : half + 2]


def gather_kernel(after_ref, *refs):
    gather_sources(refs[:-1], refs[-1], chip_index())


def back_own_kernel(turned_ref, source_ref, out_ref):
    out_ref[...] = dense_dot(turned_ref[:, : source_ref.shape[0]], source_ref[...])


def back_pieces_kernel(turned_ref, own_ref, source_ref, near_ref, *far_refs):
    tile = far_refs[0].shape[0]

    def rows_for(k):
        rows = block_at(row_index() ^ k, tile)
        rest = dense_dot(turned_ref[rows, source_ref.shape[0] :], source_ref[...])
        return own_ref[rows, :] + rest

    write_pieces(rows_for, near_ref, far_refs)


def write_pieces(rows_for, near_ref, far_refs):
    tile = far_refs[0].shape[0]
    for i in range(len(far_refs)):
        near_ref[i * tile : (i + 1) * tile, :] = rows_for(2 * i or 1).astype(BF16)
    for i, ref in enumerate(far_refs):
        ref[...] = rows_for(2 * i + 1 if i else 0)


def far_sum_kernel(near_ref, far_ref, out_ref, *, at):
    tile = out_ref.shape[0]
    near = near_ref[at * tile : (at + 1) * tile, :].astype(F32)
    out_ref[...] = (near + far_ref[...]).astype(BF16)


def slot_back_kernel(count_ref, row_ref, col_ref, tiles_ref, own_ref, other_ref, *refs):
    outs, (source_ref, acc_ref) = refs[:-2], refs[-2:]
    half = own_ref.shape[0]
    source_ref[:half, :] = own_ref[...]
    source_ref[half:, :] = other_ref[...]
    slot_product((count_ref, row_ref, col_ref, tiles_ref), source_ref, acc_ref, True)
    tile = outs[1].shape[0]
    write_pieces(lambda k: acc_ref[block_at(row_index() ^ k, tile), :], outs[0], outs[1:])


def features_kernel(weight_ref, near_ref, own_ref, *refs):
    parts, out_ref = refs[:-1], refs[-1]
    total = own_ref[...] + near_ref[: out_ref.shape[0], :].astype(F32)
    for ref in parts:
        total += ref[...].astype(F32)
    out_ref[...] = lax.dot_general(
        total.astype(BF16),
        weight_ref[...],
        (((1,), (1,)), ((), ())),
        preferred_element_type=F32,
    ).astype(BF16)


def write_kernel(
    features_ref, own_ref, other_ref, bias_ref, features_hbm, grad_hbm, bias_hbm, sems
):
    half = own_ref.shape[0]
    copies = [
        pltpu.make_async_copy(own_ref, grad_hbm.at[block_at(core_index(), half)], sems.at[0]),
        pltpu.make_async_copy(other_ref, grad_hbm.at[block_at(1 - core_index(), half)], sems.at[1]),
        pltpu.make_async_copy(features_ref, features_hbm, sems.at[2]),
        pltpu.make_async_copy(bias_ref, bias_hbm, sems.at[3]),
    ]
    for copy in copies:
        copy.start()
    for copy in copies:
        copy.wait()


def in_turn(count, make):
    made, before = {}, []
    for k in far_first(count):
        made[k] = make(k, before)
        before = [made[k]]
    return made


def local(features, weight, bias_term, cotangent, tile_values, tile_row, tile_col, tile_count):
    n_row = lax.axis_size("row")
    n_col = lax.axis_size("col")
    n_chip = n_col // 2
    tile, width = features.shape
    hidden = weight.shape[1]
    slots = tile_values.shape[2]
    row_nodes, col_nodes = n_col * tile, n_row * tile
    bias_row = bias_term.reshape(1, hidden)
    half = width // 2
    matrix = 2 * tile * width * hidden
    block_bytes = 2 * tile * width

    def like(rows, columns, dtype=BF16):
        return jax.ShapeDtypeStruct((rows, columns), dtype)

    near = 1
    own_nodes = n_chip * tile

    def add(terms, flops=0):
        return call(
            functools.partial(add_terms_kernel, n_terms=len(terms)),
            like(half + BIAS_ROWS, hidden),
            [VMEM_SPEC] * len(terms),
            [],
            flops or len(terms) * half * hidden,
            len(terms) * half * hidden * 2,
        )(*terms)

    is_dense = n_row * n_col <= 2 * slots
    if is_dense:
        chunks = 4 if slots % 4 == 0 else 1
        dense, bias_row = call(
            dense_kernel,
            (like(row_nodes, col_nodes), like(1, hidden, F32)),
            [SMEM_SPEC] + [HBM_SPEC] * 4,
            [
                pltpu.SMEM((1, 1, slots), jnp.int32),
                pltpu.SMEM((1, 1, slots), jnp.int32),
                pltpu.VMEM((slots, tile, tile), BF16),
                pltpu.VMEM((row_nodes, col_nodes), F32),
                pltpu.SemaphoreType.DMA((3,)),
                pltpu.SemaphoreType.DMA((chunks,)),
            ],
            0,
            12 * row_nodes * col_nodes,
        )(tile_count, *(
            pltpu.with_memory_space_constraint(array, pltpu.HBM)
            for array in (tile_row, tile_col, tile_values, bias_row)
        ))
    else:
        slot_args = (
            tile_count.reshape(1),
            tile_row.reshape(slots),
            tile_col.reshape(slots),
            tile_values.reshape(slots, tile, tile),
        )
        slot_specs = [SMEM_SPEC] * 3 + [VMEM_SPEC]

    sources = exchange([features] * n_row, "row", n_row)
    if is_dense:
        other, source = call(
            forward_other_kernel,
            (like(own_nodes, width), like(col_nodes, width)),
            [VMEM_SPEC] * (1 + n_row),
            [],
            slots * matrix // 2,
            row_nodes * width * 8,
        )(dense, *sources)
        own = call(
            forward_own_kernel,
            like(own_nodes, width),
            [VMEM_SPEC] * 2,
            [],
            slots * matrix // 2,
            row_nodes * width * 8,
        )(dense, source)
    else:
        other, own = call(
            slot_forward_kernel,
            (like(own_nodes, width), like(own_nodes, width)),
            slot_specs + [VMEM_SPEC] * n_row,
            [pltpu.VMEM((col_nodes, width), BF16), pltpu.VMEM((row_nodes, width), F32)],
            slots * matrix // 2,
            row_nodes * width * 8,
        )(*slot_args, *sources)
    swapped = swap_cores(other, n_col)

    def chip_piece(k, before):
        return call(
            functools.partial(chip_kernel, k=k, n_chip=n_chip),
            like(tile, width),
            [VMEM_SPEC] * (2 + len(before)),
            [],
            tile * width,
            3 * block_bytes,
        )(own, swapped, *before)

    pieces = in_turn(n_chip, chip_piece)
    parts = exchange(pieces, "col", n_col, 2)
    if is_dense:
        turned = call(
            turn_kernel,
            like(col_nodes, row_nodes),
            [VMEM_SPEC] * 2,
            [],
            0,
            4 * row_nodes * col_nodes,
        )(dense, pieces[0])
    hidden_own, grad, aggregated = call(
        middle_kernel,
        [like(tile, hidden), like(tile, hidden), like(tile, width)],
        [VMEM_SPEC] * (3 + n_chip),
        [],
        matrix,
        n_chip * block_bytes,
    )(weight, bias_row, cotangent, *parts)
    grads = exchange([grad] * n_chip, "col", n_col, 2)
    hidden_out = call(copy_kernel, like(tile, hidden), [VMEM_SPEC], [], 0, 2 * block_bytes)(hidden_own)
    mine, theirs = call(
        term_kernel,
        [like(half + BIAS_ROWS, hidden)] * 2,
        [VMEM_SPEC] * 2,
        [pltpu.VMEM((width, hidden), F32)],
        matrix,
        6 * block_bytes,
    )(aggregated, grad)
    chip_term = add([swap_cores(theirs, n_col), mine])
    add_late = functools.partial(add, flops=ROW_SUM_WEIGHT * matrix)
    row_term = add_late(total_over(chip_term, add, "row", n_row))

    own_grads = call(
        gather_kernel,
        like(own_nodes, hidden),
        [VMEM_SPEC] * (1 + n_chip),
        [],
        0,
        own_nodes * hidden * 4,
    )(chip_term, *grads)
    other_grads = swap_cores(own_grads, n_col)
    if is_dense:
        back_own = call(
            back_own_kernel,
            like(col_nodes, hidden, F32),
            [VMEM_SPEC] * 2,
            [],
            slots * matrix // 2,
            row_nodes * hidden * 8,
        )(turned, own_grads)
        near_piece, *far_pieces = call(
            back_pieces_kernel,
            [like(n_row // 2 * tile, hidden)] + [like(tile, hidden, F32)] * (n_row // 2),
            [VMEM_SPEC] * 3,
            [],
            slots * matrix // 2,
            row_nodes * hidden * 8,
        )(turned, back_own, other_grads)
    else:
        near_piece, *far_pieces = call(
            slot_back_kernel,
            [like(n_row // 2 * tile, hidden)] + [like(tile, hidden, F32)] * (n_row // 2),
            slot_specs + [VMEM_SPEC] * 2,
            [pltpu.VMEM((row_nodes, hidden), BF16), pltpu.VMEM((col_nodes, hidden), F32)],
            slots * matrix // 2,
            row_nodes * hidden * 8,
        )(*slot_args, own_grads, other_grads)
    near = lax.ppermute(near_piece, "row", pairs_of(1, n_row, 1))
    backs = []
    for i in range(1, n_row // 2):
        piece = call(
            functools.partial(far_sum_kernel, at=i),
            like(tile, hidden),
            [VMEM_SPEC] * 2,
            [],
            tile * hidden,
            4 * block_bytes,
        )(near, far_pieces[i])
        backs.append(lax.ppermute(piece, "row", pairs_of(2 * i + 1, n_row, 1)))
    own_features = call(
        features_kernel,
        like(tile, width),
        [VMEM_SPEC] * (3 + len(backs)),
        [],
        FEATURES_WEIGHT * matrix,
        n_row * block_bytes,
    )(weight, near, far_pieces[0], *backs)
    all_terms = total_over(row_term, add_late, "col", n_col, 2)
    factor = (tile * n_row * n_col) ** (-0.5)
    own_half, bias_grad = call(
        functools.partial(scale_kernel, factor=factor),
        (like(half, hidden, F32), like(1, hidden, F32)),
        [VMEM_SPEC] * (1 + len(all_terms)),
        [],
        len(all_terms) * half * hidden,
        len(all_terms) * half * hidden * 2,
    )(near, *all_terms)
    grad_features, grad_weight, grad_bias = call(
        write_kernel,
        (like(tile, width), like(width, hidden, F32), like(1, hidden, F32)),
        [VMEM_SPEC] * 4,
        [pltpu.SemaphoreType.DMA((4,))],
        0,
        width * hidden * 8,
        HBM_SPEC,
    )(own_features, own_half, swap_cores(own_half, n_col), bias_grad)
    return hidden_out, grad_features, grad_weight, grad_bias.reshape(hidden)


def solution(mesh):
    return jax.shard_map(
        local,
        mesh=mesh,
        in_specs=(
            P(("col", "row"), None),
            P(),
            P(),
            P(("row", "col"), None),
            P("row", "col", None, None, None),
            P("row", "col", None),
            P("row", "col", None),
            P("row", "col"),
        ),
        out_specs=(P(("row", "col"), None), P(("col", "row"), None), P(), P()),
        check_vma=False,
    )
```

```python
import functools

import jax
import jax.numpy as jnp
from jax import lax
from jax.experimental import pallas as pl
from jax.experimental.pallas import tpu as pltpu
from jax.sharding import PartitionSpec as P

F32 = jnp.float32
BF16 = jnp.bfloat16
ROOT_2_OVER_PI = 0.7978845608028654
CUBIC = 0.044715
VMEM_LIMIT = 48 * 1024 * 1024
BIAS_ROWS = 16
BACK_SUM_WEIGHT = 30
ROW_SUM_WEIGHT = 120
FEATURES_WEIGHT = 100

VMEM_SPEC = pl.BlockSpec(memory_space=pltpu.VMEM)
HBM_SPEC = pl.BlockSpec(memory_space=pltpu.HBM)
SMEM_SPEC = pl.BlockSpec(memory_space=pltpu.SMEM)


def call(kernel, out_shape, in_specs, scratch, flops, moved, out_spec=VMEM_SPEC):
    return pl.pallas_call(
        kernel,
        out_shape=out_shape,
        in_specs=in_specs,
        out_specs=jax.tree.map(lambda _: out_spec, out_shape),
        scratch_shapes=scratch,
        compiler_params=pltpu.CompilerParams(vmem_limit_bytes=VMEM_LIMIT),
        cost_estimate=pl.CostEstimate(flops=flops, bytes_accessed=moved, transcendentals=0),
    )


def partner(index, k, count):
    if count & (count - 1) == 0:
        return index ^ k
    return (k - index) % count


def far_first(count):
    return list(range(count - 1, -1, -1))


def pairs_of(k, size, cores):
    return [(i, partner(i // cores, k, size // cores) * cores + i % cores) for i in range(size)]


def exchange(blocks, axis, size, cores=1):
    received = []
    for k in far_first(size // cores):
        pairs = pairs_of(k, size, cores)
        moves = any(i != j for i, j in pairs)
        received.append(lax.ppermute(blocks[k], axis, pairs) if moves else blocks[k])
    return received


def swap_cores(block, size):
    return lax.ppermute(block, "col", [(i, i ^ 1) for i in range(size)])


def total_over(block, add, axis, size, cores=1):
    count = size // cores
    if count & (count - 1):
        return exchange([block] * count, axis, size, cores)
    terms, step = [block], 1
    while step < count:
        block = add(terms) if len(terms) > 1 else block
        terms = [lax.ppermute(block, axis, pairs_of(step, size, cores)), block]
        step *= 2
    return terms


def block_at(index, size):
    return pl.ds(pl.multiple_of(index * size, size), size)


def row_index():
    return lax.axis_index("row")


def chip_index():
    return lax.axis_index("col") // 2


def core_index():
    return lax.axis_index("col") % 2


def summed(refs):
    by_partner = dict(zip(far_first(len(refs)), refs))
    values = [by_partner[k][...].astype(F32) for k in sorted(by_partner)]
    while len(values) > 1:
        values = [sum(values[i + 1 : i + 2], values[i]) for i in range(0, len(values), 2)]
    return values[0]


def bias_rows(bias):
    high = bias.astype(BF16).astype(F32)
    line = lax.broadcasted_iota(jnp.int32, (BIAS_ROWS, bias.shape[1]), 0)
    return jnp.where(line == 0, high, jnp.where(line == 1, bias - high, 0.0))


def row_place(row, n_chip):
    return jnp.where(row % 2 == core_index(), 0, n_chip) + row // 2


def dense_kernel(
    count_ref, row_hbm, col_hbm, tiles_hbm, bias_hbm, dense_ref, bias_ref,
    row_ref, col_ref, tiles_ref, sum_ref, sems, tile_sems,
):
    slots, tile = tiles_ref.shape[0], tiles_ref.shape[1]
    n_chip = sum_ref.shape[0] // (2 * tile)
    chunks = tile_sems.shape[0]
    size = slots // chunks
    small = [
        pltpu.make_async_copy(row_hbm, row_ref, sems.at[0]),
        pltpu.make_async_copy(col_hbm, col_ref, sems.at[1]),
        pltpu.make_async_copy(bias_hbm, bias_ref, sems.at[2]),
    ]
    large = []
    for k in range(chunks):
        part = pl.ds(k * size, size)
        large.append(
            pltpu.make_async_copy(tiles_hbm.at[0, 0, part], tiles_ref.at[part], tile_sems.at[k])
        )
    for copy in small + large:
        copy.start()
    sum_ref[...] = jnp.zeros_like(sum_ref)
    for copy in small:
        copy.wait()
    count = count_ref[0, 0]

    def body(slot, carry):
        rows = block_at(row_place(row_ref[0, 0, slot], n_chip), tile)
        cols = block_at(col_ref[0, 0, slot], tile)
        sum_ref[rows, cols] += tiles_ref[slot].astype(F32)
        return carry

    for k, copy in enumerate(large):
        copy.wait()
        lax.fori_loop(k * size, jnp.minimum(count, (k + 1) * size), body, 0)
    dense_ref[...] = sum_ref[...].astype(BF16)


def turn_kernel(dense_ref, after_ref, turned_ref):
    rows = dense_ref.shape[0]
    step = 256 if rows % 256 == 0 else rows
    for first in range(0, rows, step):
        turned_ref[:, first : first + step] = dense_ref[first : first + step, :].T


def dense_dot(left, right):
    return jnp.dot(left, right, preferred_element_type=F32)


def gather_sources(sources, source_ref, index):
    tile = sources[0].shape[0]
    for k, ref in zip(far_first(len(sources)), sources):
        source_ref[block_at(partner(index, k, len(sources)), tile), :] = ref[...]


def slot_product(refs, source_ref, acc_ref, turned):
    count_ref, row_ref, col_ref, tiles_ref = refs
    tile = tiles_ref.shape[1]
    n_chip = (source_ref if turned else acc_ref).shape[0] // (2 * tile)
    contract = 0 if turned else 1
    acc_ref[...] = jnp.zeros_like(acc_ref)

    def body(slot, carry):
        places = [row_place(row_ref[slot], n_chip), col_ref[slot]]
        source, target = places if turned else places[::-1]
        acc_ref[block_at(target, tile), :] += lax.dot_general(
            tiles_ref[slot],
            source_ref[block_at(source, tile), :],
            (((contract,), (0,)), ((), ())),
            preferred_element_type=F32,
        )
        return carry

    lax.fori_loop(0, count_ref[0], body, 0)


def forward_other_kernel(dense_ref, *refs):
    sources, (other_ref, source_ref) = refs[:-2], refs[-2:]
    gather_sources(sources, source_ref, row_index())
    half = other_ref.shape[0]
    other_ref[...] = dense_dot(dense_ref[half:, :], source_ref[...]).astype(BF16)


def forward_own_kernel(dense_ref, source_ref, own_ref):
    own_ref[...] = dense_dot(dense_ref[: own_ref.shape[0], :], source_ref[...]).astype(BF16)


def slot_forward_kernel(count_ref, row_ref, col_ref, tiles_ref, *refs):
    sources, (other_ref, own_ref, source_ref, acc_ref) = refs[:-4], refs[-4:]
    gather_sources(sources, source_ref, row_index())
    slot_product((count_ref, row_ref, col_ref, tiles_ref), source_ref, acc_ref, False)
    half = own_ref.shape[0]
    own_ref[...] = acc_ref[:half, :].astype(BF16)
    other_ref[...] = acc_ref[half:, :].astype(BF16)


def chip_kernel(own_ref, other_ref, *refs, k, n_chip):
    out_ref = refs[-1]
    rows = block_at(partner(chip_index(), k, n_chip), out_ref.shape[0])
    out_ref[...] = (own_ref[rows, :].astype(F32) + other_ref[rows, :].astype(F32)).astype(BF16)


def middle_kernel(weight_ref, bias_ref, cot_ref, *refs):
    parts, (hidden_ref, grad_ref, agg_ref) = refs[:-3], refs[-3:]
    aggregated = summed(parts).astype(BF16)
    agg_ref[...] = aggregated
    v = dense_dot(aggregated, weight_ref[...]) + bias_ref[...]
    square = v * v
    t = jnp.tanh(ROOT_2_OVER_PI * (v + CUBIC * (square * v)))
    half = 0.5 * (1.0 + t)
    hidden_ref[...] = (v * half).astype(BF16)
    slope = half + 0.5 * v * (1.0 - t * t) * (ROOT_2_OVER_PI * (1.0 + 3.0 * CUBIC * square))
    grad_ref[...] = (cot_ref[...].astype(F32) * slope).astype(BF16)


def copy_kernel(in_ref, out_ref):
    out_ref[...] = in_ref[...]


def term_kernel(agg_ref, grad_ref, mine_ref, theirs_ref, acc_ref):
    grad = grad_ref[...]
    acc_ref[...] = lax.dot_general(
        agg_ref[...], grad, (((0,), (0,)), ((), ())), preferred_element_type=F32
    )
    half = acc_ref.shape[0] // 2
    bias = bias_rows(jnp.sum(grad.astype(F32), axis=0, keepdims=True)).astype(BF16)
    for ref, core in ((mine_ref, core_index()), (theirs_ref, 1 - core_index())):
        ref[:half, :] = acc_ref[block_at(core, half), :].astype(BF16)
        ref[half:, :] = bias


def add_terms_kernel(*refs, n_terms):
    total = summed(refs[:n_terms])
    out_ref = refs[-1]
    half = total.shape[0] - BIAS_ROWS
    out_ref[:half, :] = total[:half].astype(BF16)
    out_ref[half:, :] = bias_rows(total[half : half + 1] + total[half + 1 : half + 2]).astype(BF16)


def scale_kernel(after_ref, *refs, factor):
    parts, (half_ref, bias_ref) = refs[:-2], refs[-2:]
    total = summed(parts) * factor
    half = half_ref.shape[0]
    half_ref[...] = total[:half]
    bias_ref[...] = total[half : half + 1] + total[half + 1 : half + 2]


def gather_kernel(after_ref, *refs):
    gather_sources(refs[:-1], refs[-1], chip_index())


def back_own_kernel(turned_ref, source_ref, out_ref):
    out_ref[...] = dense_dot(turned_ref[:, : source_ref.shape[0]], source_ref[...])


def back_pieces_kernel(turned_ref, own_ref, source_ref, *outs):
    tile = outs[0].shape[0]
    for k, out_ref in zip(far_first(len(outs)), outs):
        rows = block_at(partner(row_index(), k, len(outs)), tile)
        rest = dense_dot(turned_ref[rows, source_ref.shape[0] :], source_ref[...])
        out_ref[...] = (own_ref[rows, :] + rest).astype(BF16)


def slot_back_kernel(count_ref, row_ref, col_ref, tiles_ref, own_ref, other_ref, *refs):
    outs, (source_ref, acc_ref) = refs[:-2], refs[-2:]
    half = own_ref.shape[0]
    source_ref[:half, :] = own_ref[...]
    source_ref[half:, :] = other_ref[...]
    slot_product((count_ref, row_ref, col_ref, tiles_ref), source_ref, acc_ref, True)
    tile = outs[0].shape[0]
    for k, out_ref in zip(far_first(len(outs)), outs):
        rows = block_at(partner(row_index(), k, len(outs)), tile)
        out_ref[...] = acc_ref[rows, :].astype(BF16)


def back_sum_kernel(*refs):
    total = refs[0][...].astype(F32)
    for ref in refs[1:-1]:
        total += ref[...].astype(F32)
    refs[-1][...] = total


def features_kernel(weight_ref, most_ref, last_ref, out_ref):
    out_ref[...] = lax.dot_general(
        (most_ref[...] + last_ref[...].astype(F32)).astype(BF16),
        weight_ref[...],
        (((1,), (1,)), ((), ())),
        preferred_element_type=F32,
    ).astype(BF16)


def write_kernel(
    features_ref, own_ref, other_ref, bias_ref, features_hbm, grad_hbm, bias_hbm, sems
):
    half = own_ref.shape[0]
    copies = [
        pltpu.make_async_copy(own_ref, grad_hbm.at[block_at(core_index(), half)], sems.at[0]),
        pltpu.make_async_copy(other_ref, grad_hbm.at[block_at(1 - core_index(), half)], sems.at[1]),
        pltpu.make_async_copy(features_ref, features_hbm, sems.at[2]),
        pltpu.make_async_copy(bias_ref, bias_hbm, sems.at[3]),
    ]
    for copy in copies:
        copy.start()
    for copy in copies:
        copy.wait()


def in_turn(count, make):
    made, before = {}, []
    for k in far_first(count):
        made[k] = make(k, before)
        before = [made[k]]
    return made


def local(features, weight, bias_term, cotangent, tile_values, tile_row, tile_col, tile_count):
    n_row = lax.axis_size("row")
    n_col = lax.axis_size("col")
    n_chip = n_col // 2
    tile, width = features.shape
    hidden = weight.shape[1]
    slots = tile_values.shape[2]
    row_nodes, col_nodes = n_col * tile, n_row * tile
    bias_row = bias_term.reshape(1, hidden)
    half = width // 2
    matrix = 2 * tile * width * hidden
    block_bytes = 2 * tile * width

    def like(rows, columns, dtype=BF16):
        return jax.ShapeDtypeStruct((rows, columns), dtype)

    near = 1
    own_nodes = n_chip * tile

    def add(terms, flops=0):
        return call(
            functools.partial(add_terms_kernel, n_terms=len(terms)),
            like(half + BIAS_ROWS, hidden),
            [VMEM_SPEC] * len(terms),
            [],
            flops or len(terms) * half * hidden,
            len(terms) * half * hidden * 2,
        )(*terms)

    is_dense = n_row * n_col <= 2 * slots
    if is_dense:
        chunks = 4 if slots % 4 == 0 else 1
        dense, bias_row = call(
            dense_kernel,
            (like(row_nodes, col_nodes), like(1, hidden, F32)),
            [SMEM_SPEC] + [HBM_SPEC] * 4,
            [
                pltpu.SMEM((1, 1, slots), jnp.int32),
                pltpu.SMEM((1, 1, slots), jnp.int32),
                pltpu.VMEM((slots, tile, tile), BF16),
                pltpu.VMEM((row_nodes, col_nodes), F32),
                pltpu.SemaphoreType.DMA((3,)),
                pltpu.SemaphoreType.DMA((chunks,)),
            ],
            0,
            12 * row_nodes * col_nodes,
        )(tile_count, *(
            pltpu.with_memory_space_constraint(array, pltpu.HBM)
            for array in (tile_row, tile_col, tile_values, bias_row)
        ))
    else:
        slot_args = (
            tile_count.reshape(1),
            tile_row.reshape(slots),
            tile_col.reshape(slots),
            tile_values.reshape(slots, tile, tile),
        )
        slot_specs = [SMEM_SPEC] * 3 + [VMEM_SPEC]

    sources = exchange([features] * n_row, "row", n_row)
    if is_dense:
        other, source = call(
            forward_other_kernel,
            (like(own_nodes, width), like(col_nodes, width)),
            [VMEM_SPEC] * (1 + n_row),
            [],
            slots * matrix // 2,
            row_nodes * width * 8,
        )(dense, *sources)
        own = call(
            forward_own_kernel,
            like(own_nodes, width),
            [VMEM_SPEC] * 2,
            [],
            slots * matrix // 2,
            row_nodes * width * 8,
        )(dense, source)
    else:
        other, own = call(
            slot_forward_kernel,
            (like(own_nodes, width), like(own_nodes, width)),
            slot_specs + [VMEM_SPEC] * n_row,
            [pltpu.VMEM((col_nodes, width), BF16), pltpu.VMEM((row_nodes, width), F32)],
            slots * matrix // 2,
            row_nodes * width * 8,
        )(*slot_args, *sources)
    swapped = swap_cores(other, n_col)

    def chip_piece(k, before):
        return call(
            functools.partial(chip_kernel, k=k, n_chip=n_chip),
            like(tile, width),
            [VMEM_SPEC] * (2 + len(before)),
            [],
            tile * width,
            3 * block_bytes,
        )(own, swapped, *before)

    pieces = in_turn(n_chip, chip_piece)
    parts = exchange(pieces, "col", n_col, 2)
    if is_dense:
        turned = call(
            turn_kernel,
            like(col_nodes, row_nodes),
            [VMEM_SPEC] * 2,
            [],
            0,
            4 * row_nodes * col_nodes,
        )(dense, pieces[0])
    hidden_own, grad, aggregated = call(
        middle_kernel,
        [like(tile, hidden), like(tile, hidden), like(tile, width)],
        [VMEM_SPEC] * (3 + n_chip),
        [],
        matrix,
        n_chip * block_bytes,
    )(weight, bias_row, cotangent, *parts)
    grads = exchange([grad] * n_chip, "col", n_col, 2)
    hidden_out = call(copy_kernel, like(tile, hidden), [VMEM_SPEC], [], 0, 2 * block_bytes)(hidden_own)
    mine, theirs = call(
        term_kernel,
        [like(half + BIAS_ROWS, hidden)] * 2,
        [VMEM_SPEC] * 2,
        [pltpu.VMEM((width, hidden), F32)],
        matrix,
        6 * block_bytes,
    )(aggregated, grad)
    chip_term = add([swap_cores(theirs, n_col), mine])
    add_late = functools.partial(add, flops=ROW_SUM_WEIGHT * matrix)
    row_term = add_late(total_over(chip_term, add, "row", n_row))

    own_grads = call(
        gather_kernel,
        like(own_nodes, hidden),
        [VMEM_SPEC] * (1 + n_chip),
        [],
        0,
        own_nodes * hidden * 4,
    )(chip_term, *grads)
    other_grads = swap_cores(own_grads, n_col)
    if is_dense:
        back_own = call(
            back_own_kernel,
            like(col_nodes, hidden, F32),
            [VMEM_SPEC] * 2,
            [],
            slots * matrix // 2,
            row_nodes * hidden * 8,
        )(turned, own_grads)
        back_pieces = call(
            back_pieces_kernel,
            [like(tile, hidden)] * n_row,
            [VMEM_SPEC] * 3,
            [],
            slots * matrix // 2,
            row_nodes * hidden * 8,
        )(turned, back_own, other_grads)
    else:
        back_pieces = call(
            slot_back_kernel,
            [like(tile, hidden)] * n_row,
            slot_specs + [VMEM_SPEC] * 2,
            [pltpu.VMEM((row_nodes, hidden), BF16), pltpu.VMEM((col_nodes, hidden), F32)],
            slots * matrix // 2,
            row_nodes * hidden * 8,
        )(*slot_args, own_grads, other_grads)
    backs = exchange(dict(zip(far_first(n_row), back_pieces)), "row", n_row)
    most = call(
        back_sum_kernel,
        like(tile, hidden, F32),
        [VMEM_SPEC] * (n_row - 1),
        [],
        BACK_SUM_WEIGHT * matrix,
        n_row * block_bytes,
    )(*backs[:-2], backs[-1])
    own_features = call(
        features_kernel,
        like(tile, width),
        [VMEM_SPEC] * 3,
        [],
        FEATURES_WEIGHT * matrix,
        n_row * block_bytes,
    )(weight, most, backs[-2])
    all_terms = total_over(row_term, add, "col", n_col, 2)
    factor = (tile * n_row * n_col) ** (-0.5)
    own_half, bias_grad = call(
        functools.partial(scale_kernel, factor=factor),
        (like(half, hidden, F32), like(1, hidden, F32)),
        [VMEM_SPEC] * (1 + len(all_terms)),
        [],
        len(all_terms) * half * hidden,
        len(all_terms) * half * hidden * 2,
    )(most, *all_terms)
    grad_features, grad_weight, grad_bias = call(
        write_kernel,
        (like(tile, width), like(width, hidden, F32), like(1, hidden, F32)),
        [VMEM_SPEC] * 4,
        [pltpu.SemaphoreType.DMA((4,))],
        0,
        width * hidden * 8,
        HBM_SPEC,
    )(own_features, own_half, swap_cores(own_half, n_col), bias_grad)
    return hidden_out, grad_features, grad_weight, grad_bias.reshape(hidden)


def solution(mesh):
    return jax.shard_map(
        local,
        mesh=mesh,
        in_specs=(
            P(("col", "row"), None),
            P(),
            P(),
            P(("row", "col"), None),
            P("row", "col", None, None, None),
            P("row", "col", None),
            P("row", "col", None),
            P("row", "col"),
        ),
        out_specs=(P(("row", "col"), None), P(("col", "row"), None), P(), P()),
        check_vma=False,
    )
```

```python
import functools

import jax
import jax.numpy as jnp
from jax import lax
from jax.experimental import pallas as pl
from jax.experimental.pallas import tpu as pltpu
from jax.sharding import PartitionSpec as P

F32 = jnp.float32
BF16 = jnp.bfloat16
ROOT_2_OVER_PI = 0.7978845608028654
CUBIC = 0.044715
VMEM_LIMIT = 48 * 1024 * 1024
BIAS_ROWS = 16
BACK_SUM_WEIGHT = 30
ROW_SUM_WEIGHT = 120
FEATURES_WEIGHT = 100

VMEM_SPEC = pl.BlockSpec(memory_space=pltpu.VMEM)
HBM_SPEC = pl.BlockSpec(memory_space=pltpu.HBM)
SMEM_SPEC = pl.BlockSpec(memory_space=pltpu.SMEM)


def call(kernel, out_shape, in_specs, scratch, flops, moved, out_spec=VMEM_SPEC):
    return pl.pallas_call(
        kernel,
        out_shape=out_shape,
        in_specs=in_specs,
        out_specs=jax.tree.map(lambda _: out_spec, out_shape),
        scratch_shapes=scratch,
        compiler_params=pltpu.CompilerParams(vmem_limit_bytes=VMEM_LIMIT),
        cost_estimate=pl.CostEstimate(flops=flops, bytes_accessed=moved, transcendentals=0),
    )


def partner(index, k, count):
    if count & (count - 1) == 0:
        return index ^ k
    return (k - index) % count


def turns(count, core):
    if core == 0:
        return list(range(count - 1, -1, -1))
    return list(dict.fromkeys([count - 1, *range(1, count), 0]))


def steps(count, core):
    powers = [1 << i for i in range(count.bit_length() - 1)]
    return powers if core else powers[::-1]


def turn(i, count):
    return jnp.where(core_index() == 0, turns(count, 0)[i], turns(count, 1)[i])


def permute(block, axis, sizes, distances):
    n_col, n_row = sizes
    pairs = []
    for col in range(n_col):
        chip, core = col // 2, col % 2
        for row in range(n_row):
            if axis == "row":
                target = col, partner(row, distances[core], n_row)
            else:
                target = 2 * partner(chip, distances[core], n_col // 2) + core, row
            pairs.append((col * n_row + row, target[0] * n_row + target[1]))
    return lax.ppermute(block, ("col", "row"), pairs)


def exchange(blocks, axis, sizes):
    count = len(blocks)
    received = []
    for i, block in enumerate(blocks):
        distances = [turns(count, core)[i] for core in range(2)]
        received.append(permute(block, axis, sizes, distances) if any(distances) else block)
    return received


def swap_cores(block, size):
    return lax.ppermute(block, "col", [(i, i ^ 1) for i in range(size)])


def total_over(block, add, axis, sizes):
    count = sizes[1] if axis == "row" else sizes[0] // 2
    if count & (count - 1):
        return exchange([block] * count, axis, sizes)
    terms = [block]
    for distances in zip(steps(count, 0), steps(count, 1)):
        block = add(terms) if len(terms) > 1 else block
        terms = [permute(block, axis, sizes, distances), block]
    return terms


def block_at(index, size):
    return pl.ds(pl.multiple_of(index * size, size), size)


def row_index():
    return lax.axis_index("row")


def chip_index():
    return lax.axis_index("col") // 2


def core_index():
    return lax.axis_index("col") % 2


def summed(refs):
    total = refs[0][...].astype(F32)
    for ref in refs[1:]:
        total += ref[...].astype(F32)
    return total


def bias_rows(bias):
    high = bias.astype(BF16).astype(F32)
    line = lax.broadcasted_iota(jnp.int32, (BIAS_ROWS, bias.shape[1]), 0)
    return jnp.where(line == 0, high, jnp.where(line == 1, bias - high, 0.0))


def row_place(row, n_chip):
    return jnp.where(row % 2 == core_index(), 0, n_chip) + row // 2


def dense_kernel(
    count_ref, row_hbm, col_hbm, tiles_hbm, bias_hbm, dense_ref, bias_ref,
    row_ref, col_ref, tiles_ref, sum_ref, sems, tile_sems,
):
    slots, tile = tiles_ref.shape[0], tiles_ref.shape[1]
    n_chip = sum_ref.shape[0] // (2 * tile)
    chunks = tile_sems.shape[0]
    size = slots // chunks
    small = [
        pltpu.make_async_copy(row_hbm, row_ref, sems.at[0]),
        pltpu.make_async_copy(col_hbm, col_ref, sems.at[1]),
        pltpu.make_async_copy(bias_hbm, bias_ref, sems.at[2]),
    ]
    large = []
    for k in range(chunks):
        part = pl.ds(k * size, size)
        large.append(
            pltpu.make_async_copy(tiles_hbm.at[0, 0, part], tiles_ref.at[part], tile_sems.at[k])
        )
    for copy in small + large:
        copy.start()
    sum_ref[...] = jnp.zeros_like(sum_ref)
    for copy in small:
        copy.wait()
    count = count_ref[0, 0]

    def body(slot, carry):
        rows = block_at(row_place(row_ref[0, 0, slot], n_chip), tile)
        cols = block_at(col_ref[0, 0, slot], tile)
        sum_ref[rows, cols] += tiles_ref[slot].astype(F32)
        return carry

    for k, copy in enumerate(large):
        copy.wait()
        lax.fori_loop(k * size, jnp.minimum(count, (k + 1) * size), body, 0)
    dense_ref[...] = sum_ref[...].astype(BF16)


def turn_kernel(dense_ref, after_ref, turned_ref):
    rows = dense_ref.shape[0]
    step = 256 if rows % 256 == 0 else rows
    for first in range(0, rows, step):
        turned_ref[:, first : first + step] = dense_ref[first : first + step, :].T


def dense_dot(left, right):
    return jnp.dot(left, right, preferred_element_type=F32)


def gather_sources(sources, source_ref, index):
    tile = sources[0].shape[0]
    for i, ref in enumerate(sources):
        place = partner(index, turn(i, len(sources)), len(sources))
        source_ref[block_at(place, tile), :] = ref[...]


def slot_product(refs, source_ref, acc_ref, turned):
    count_ref, row_ref, col_ref, tiles_ref = refs
    tile = tiles_ref.shape[1]
    n_chip = (source_ref if turned else acc_ref).shape[0] // (2 * tile)
    contract = 0 if turned else 1
    acc_ref[...] = jnp.zeros_like(acc_ref)

    def body(slot, carry):
        places = [row_place(row_ref[slot], n_chip), col_ref[slot]]
        source, target = places if turned else places[::-1]
        acc_ref[block_at(target, tile), :] += lax.dot_general(
            tiles_ref[slot],
            source_ref[block_at(source, tile), :],
            (((contract,), (0,)), ((), ())),
            preferred_element_type=F32,
        )
        return carry

    lax.fori_loop(0, count_ref[0], body, 0)


def forward_other_kernel(dense_ref, *refs):
    sources, (other_ref, source_ref) = refs[:-2], refs[-2:]
    gather_sources(sources, source_ref, row_index())
    half = other_ref.shape[0]
    other_ref[...] = dense_dot(dense_ref[half:, :], source_ref[...]).astype(BF16)


def forward_own_kernel(dense_ref, source_ref, own_ref):
    own_ref[...] = dense_dot(dense_ref[: own_ref.shape[0], :], source_ref[...]).astype(BF16)


def slot_forward_kernel(count_ref, row_ref, col_ref, tiles_ref, *refs):
    sources, (other_ref, own_ref, source_ref, acc_ref) = refs[:-4], refs[-4:]
    gather_sources(sources, source_ref, row_index())
    slot_product((count_ref, row_ref, col_ref, tiles_ref), source_ref, acc_ref, False)
    half = own_ref.shape[0]
    own_ref[...] = acc_ref[:half, :].astype(BF16)
    other_ref[...] = acc_ref[half:, :].astype(BF16)


def chip_kernel(own_ref, other_ref, *refs, i, n_chip):
    out_ref = refs[-1]
    rows = block_at(partner(chip_index(), turn(i, n_chip), n_chip), out_ref.shape[0])
    out_ref[...] = (own_ref[rows, :].astype(F32) + other_ref[rows, :].astype(F32)).astype(BF16)


def middle_kernel(weight_ref, bias_ref, cot_ref, *refs):
    parts, (hidden_ref, grad_ref, agg_ref) = refs[:-3], refs[-3:]
    aggregated = summed(parts).astype(BF16)
    agg_ref[...] = aggregated
    v = dense_dot(aggregated, weight_ref[...]) + bias_ref[...]
    square = v * v
    t = jnp.tanh(ROOT_2_OVER_PI * (v + CUBIC * (square * v)))
    half = 0.5 * (1.0 + t)
    hidden_ref[...] = (v * half).astype(BF16)
    slope = half + 0.5 * v * (1.0 - t * t) * (ROOT_2_OVER_PI * (1.0 + 3.0 * CUBIC * square))
    grad_ref[...] = (cot_ref[...].astype(F32) * slope).astype(BF16)


def copy_kernel(in_ref, out_ref):
    out_ref[...] = in_ref[...]


def term_kernel(agg_ref, grad_ref, mine_ref, theirs_ref, acc_ref):
    grad = grad_ref[...]
    acc_ref[...] = lax.dot_general(
        agg_ref[...], grad, (((0,), (0,)), ((), ())), preferred_element_type=F32
    )
    half = acc_ref.shape[0] // 2
    bias = bias_rows(jnp.sum(grad.astype(F32), axis=0, keepdims=True)).astype(BF16)
    for ref, core in ((mine_ref, core_index()), (theirs_ref, 1 - core_index())):
        ref[:half, :] = acc_ref[block_at(core, half), :].astype(BF16)
        ref[half:, :] = bias


def add_terms_kernel(*refs, n_terms):
    total = summed(refs[:n_terms])
    out_ref = refs[-1]
    half = total.shape[0] - BIAS_ROWS
    out_ref[:half, :] = total[:half].astype(BF16)
    out_ref[half:, :] = bias_rows(total[half : half + 1] + total[half + 1 : half + 2]).astype(BF16)


def scale_kernel(after_ref, *refs, factor):
    parts, (half_ref, bias_ref) = refs[:-2], refs[-2:]
    total = summed(parts) * factor
    half = half_ref.shape[0]
    half_ref[...] = total[:half]
    bias_ref[...] = total[half : half + 1] + total[half + 1 : half + 2]


def gather_kernel(after_ref, *refs):
    gather_sources(refs[:-1], refs[-1], chip_index())


def back_own_kernel(turned_ref, source_ref, out_ref):
    out_ref[...] = dense_dot(turned_ref[:, : source_ref.shape[0]], source_ref[...])


def back_pieces_kernel(turned_ref, own_ref, source_ref, *outs):
    tile = outs[0].shape[0]
    for i, out_ref in enumerate(outs):
        rows = block_at(partner(row_index(), turn(i, len(outs)), len(outs)), tile)
        rest = dense_dot(turned_ref[rows, source_ref.shape[0] :], source_ref[...])
        out_ref[...] = (own_ref[rows, :] + rest).astype(BF16)


def slot_back_kernel(count_ref, row_ref, col_ref, tiles_ref, own_ref, other_ref, *refs):
    outs, (source_ref, acc_ref) = refs[:-2], refs[-2:]
    half = own_ref.shape[0]
    source_ref[:half, :] = own_ref[...]
    source_ref[half:, :] = other_ref[...]
    slot_product((count_ref, row_ref, col_ref, tiles_ref), source_ref, acc_ref, True)
    tile = outs[0].shape[0]
    for i, out_ref in enumerate(outs):
        rows = block_at(partner(row_index(), turn(i, len(outs)), len(outs)), tile)
        out_ref[...] = acc_ref[rows, :].astype(BF16)


def back_sum_kernel(*refs):
    total = refs[0][...].astype(F32)
    for ref in refs[1:-1]:
        total += ref[...].astype(F32)
    refs[-1][...] = total


def features_kernel(weight_ref, most_ref, last_ref, out_ref):
    out_ref[...] = lax.dot_general(
        (most_ref[...] + last_ref[...].astype(F32)).astype(BF16),
        weight_ref[...],
        (((1,), (1,)), ((), ())),
        preferred_element_type=F32,
    ).astype(BF16)


def write_kernel(
    features_ref, own_ref, other_ref, bias_ref, features_hbm, grad_hbm, bias_hbm, sems
):
    half = own_ref.shape[0]
    copies = [
        pltpu.make_async_copy(own_ref, grad_hbm.at[block_at(core_index(), half)], sems.at[0]),
        pltpu.make_async_copy(other_ref, grad_hbm.at[block_at(1 - core_index(), half)], sems.at[1]),
        pltpu.make_async_copy(features_ref, features_hbm, sems.at[2]),
        pltpu.make_async_copy(bias_ref, bias_hbm, sems.at[3]),
    ]
    for copy in copies:
        copy.start()
    for copy in copies:
        copy.wait()


def local(features, weight, bias_term, cotangent, tile_values, tile_row, tile_col, tile_count):
    n_row = lax.axis_size("row")
    n_col = lax.axis_size("col")
    n_chip = n_col // 2
    sizes = n_col, n_row
    tile, width = features.shape
    hidden = weight.shape[1]
    slots = tile_values.shape[2]
    row_nodes, col_nodes = n_col * tile, n_row * tile
    bias_row = bias_term.reshape(1, hidden)
    half = width // 2
    matrix = 2 * tile * width * hidden
    block_bytes = 2 * tile * width

    def like(rows, columns, dtype=BF16):
        return jax.ShapeDtypeStruct((rows, columns), dtype)

    near = 1
    own_nodes = n_chip * tile

    def add(terms, flops=0):
        return call(
            functools.partial(add_terms_kernel, n_terms=len(terms)),
            like(half + BIAS_ROWS, hidden),
            [VMEM_SPEC] * len(terms),
            [],
            flops or len(terms) * half * hidden,
            len(terms) * half * hidden * 2,
        )(*terms)

    is_dense = n_row * n_col <= 2 * slots
    if is_dense:
        chunks = 4 if slots % 4 == 0 else 1
        dense, bias_row = call(
            dense_kernel,
            (like(row_nodes, col_nodes), like(1, hidden, F32)),
            [SMEM_SPEC] + [HBM_SPEC] * 4,
            [
                pltpu.SMEM((1, 1, slots), jnp.int32),
                pltpu.SMEM((1, 1, slots), jnp.int32),
                pltpu.VMEM((slots, tile, tile), BF16),
                pltpu.VMEM((row_nodes, col_nodes), F32),
                pltpu.SemaphoreType.DMA((3,)),
                pltpu.SemaphoreType.DMA((chunks,)),
            ],
            0,
            12 * row_nodes * col_nodes,
        )(tile_count, *(
            pltpu.with_memory_space_constraint(array, pltpu.HBM)
            for array in (tile_row, tile_col, tile_values, bias_row)
        ))
    else:
        slot_args = (
            tile_count.reshape(1),
            tile_row.reshape(slots),
            tile_col.reshape(slots),
            tile_values.reshape(slots, tile, tile),
        )
        slot_specs = [SMEM_SPEC] * 3 + [VMEM_SPEC]

    sources = exchange([features] * n_row, "row", sizes)
    if is_dense:
        other, source = call(
            forward_other_kernel,
            (like(own_nodes, width), like(col_nodes, width)),
            [VMEM_SPEC] * (1 + n_row),
            [],
            slots * matrix // 2,
            row_nodes * width * 8,
        )(dense, *sources)
        own = call(
            forward_own_kernel,
            like(own_nodes, width),
            [VMEM_SPEC] * 2,
            [],
            slots * matrix // 2,
            row_nodes * width * 8,
        )(dense, source)
    else:
        other, own = call(
            slot_forward_kernel,
            (like(own_nodes, width), like(own_nodes, width)),
            slot_specs + [VMEM_SPEC] * n_row,
            [pltpu.VMEM((col_nodes, width), BF16), pltpu.VMEM((row_nodes, width), F32)],
            slots * matrix // 2,
            row_nodes * width * 8,
        )(*slot_args, *sources)
    swapped = swap_cores(other, n_col)

    def chip_piece(i, before):
        return call(
            functools.partial(chip_kernel, i=i, n_chip=n_chip),
            like(tile, width),
            [VMEM_SPEC] * (2 + len(before)),
            [],
            tile * width,
            3 * block_bytes,
        )(own, swapped, *before)

    pieces = []
    for i in range(n_chip):
        pieces.append(chip_piece(i, pieces[-1:]))
    parts = exchange(pieces, "chip", sizes)
    if is_dense:
        turned = call(
            turn_kernel,
            like(col_nodes, row_nodes),
            [VMEM_SPEC] * 2,
            [],
            0,
            4 * row_nodes * col_nodes,
        )(dense, pieces[-1])
    hidden_own, grad, aggregated = call(
        middle_kernel,
        [like(tile, hidden), like(tile, hidden), like(tile, width)],
        [VMEM_SPEC] * (3 + n_chip),
        [],
        matrix,
        n_chip * block_bytes,
    )(weight, bias_row, cotangent, *parts)
    grads = exchange([grad] * n_chip, "chip", sizes)
    hidden_out = call(copy_kernel, like(tile, hidden), [VMEM_SPEC], [], 0, 2 * block_bytes)(hidden_own)
    mine, theirs = call(
        term_kernel,
        [like(half + BIAS_ROWS, hidden)] * 2,
        [VMEM_SPEC] * 2,
        [pltpu.VMEM((width, hidden), F32)],
        matrix,
        6 * block_bytes,
    )(aggregated, grad)
    chip_term = add([swap_cores(theirs, n_col), mine])
    add_late = functools.partial(add, flops=ROW_SUM_WEIGHT * matrix)
    row_term = add_late(total_over(chip_term, add, "row", sizes))

    own_grads = call(
        gather_kernel,
        like(own_nodes, hidden),
        [VMEM_SPEC] * (1 + n_chip),
        [],
        0,
        own_nodes * hidden * 4,
    )(chip_term, *grads)
    other_grads = swap_cores(own_grads, n_col)
    if is_dense:
        back_own = call(
            back_own_kernel,
            like(col_nodes, hidden, F32),
            [VMEM_SPEC] * 2,
            [],
            slots * matrix // 2,
            row_nodes * hidden * 8,
        )(turned, own_grads)
        back_pieces = call(
            back_pieces_kernel,
            [like(tile, hidden)] * n_row,
            [VMEM_SPEC] * 3,
            [],
            slots * matrix // 2,
            row_nodes * hidden * 8,
        )(turned, back_own, other_grads)
    else:
        back_pieces = call(
            slot_back_kernel,
            [like(tile, hidden)] * n_row,
            slot_specs + [VMEM_SPEC] * 2,
            [pltpu.VMEM((row_nodes, hidden), BF16), pltpu.VMEM((col_nodes, hidden), F32)],
            slots * matrix // 2,
            row_nodes * hidden * 8,
        )(*slot_args, own_grads, other_grads)
    backs = exchange(back_pieces, "row", sizes)
    most = call(
        back_sum_kernel,
        like(tile, hidden, F32),
        [VMEM_SPEC] * (n_row - 1),
        [],
        BACK_SUM_WEIGHT * matrix,
        n_row * block_bytes,
    )(*backs[:-2], backs[-1])
    own_features = call(
        features_kernel,
        like(tile, width),
        [VMEM_SPEC] * 3,
        [],
        FEATURES_WEIGHT * matrix,
        n_row * block_bytes,
    )(weight, most, backs[-2])
    all_terms = total_over(row_term, add, "chip", sizes)
    factor = (tile * n_row * n_col) ** (-0.5)
    own_half, bias_grad = call(
        functools.partial(scale_kernel, factor=factor),
        (like(half, hidden, F32), like(1, hidden, F32)),
        [VMEM_SPEC] * (1 + len(all_terms)),
        [],
        len(all_terms) * half * hidden,
        len(all_terms) * half * hidden * 2,
    )(most, *all_terms)
    grad_features, grad_weight, grad_bias = call(
        write_kernel,
        (like(tile, width), like(width, hidden, F32), like(1, hidden, F32)),
        [VMEM_SPEC] * 4,
        [pltpu.SemaphoreType.DMA((4,))],
        0,
        width * hidden * 8,
        HBM_SPEC,
    )(own_features, own_half, swap_cores(own_half, n_col), bias_grad)
    return hidden_out, grad_features, grad_weight, grad_bias.reshape(hidden)


def solution(mesh):
    return jax.shard_map(
        local,
        mesh=mesh,
        in_specs=(
            P(("col", "row"), None),
            P(),
            P(),
            P(("row", "col"), None),
            P("row", "col", None, None, None),
            P("row", "col", None),
            P("row", "col", None),
            P("row", "col"),
        ),
        out_specs=(P(("row", "col"), None), P(("col", "row"), None), P(), P()),
        check_vma=False,
    )
```

```python
import functools

import jax
import jax.numpy as jnp
from jax import lax
from jax.experimental import pallas as pl
from jax.experimental.pallas import tpu as pltpu
from jax.sharding import PartitionSpec as P

F32 = jnp.float32
BF16 = jnp.bfloat16
ROOT_2_OVER_PI = 0.7978845608028654
CUBIC = 0.044715
VMEM_LIMIT = 48 * 1024 * 1024
BIAS_ROWS = 16
BACK_SUM_WEIGHT = 30
ROW_SUM_WEIGHT = 120
FEATURES_WEIGHT = 100

VMEM_SPEC = pl.BlockSpec(memory_space=pltpu.VMEM)
HBM_SPEC = pl.BlockSpec(memory_space=pltpu.HBM)
SMEM_SPEC = pl.BlockSpec(memory_space=pltpu.SMEM)


def call(kernel, out_shape, in_specs, scratch, flops, moved, out_spec=VMEM_SPEC):
    return pl.pallas_call(
        kernel,
        out_shape=out_shape,
        in_specs=in_specs,
        out_specs=jax.tree.map(lambda _: out_spec, out_shape),
        scratch_shapes=scratch,
        compiler_params=pltpu.CompilerParams(vmem_limit_bytes=VMEM_LIMIT),
        cost_estimate=pl.CostEstimate(flops=flops, bytes_accessed=moved, transcendentals=0),
    )


def partner(index, k, count):
    if count & (count - 1) == 0:
        return index ^ k
    return (k - index) % count


def far_first(count):
    return list(range(count - 1, -1, -1))


def pairs_of(k, size, cores):
    return [(i, partner(i // cores, k, size // cores) * cores + i % cores) for i in range(size)]


def exchange(blocks, axis, size, cores=1):
    received = []
    for k in far_first(size // cores):
        pairs = pairs_of(k, size, cores)
        moves = any(i != j for i, j in pairs)
        received.append(lax.ppermute(blocks[k], axis, pairs) if moves else blocks[k])
    return received


def swap_cores(block, size):
    return lax.ppermute(block, "col", [(i, i ^ 1) for i in range(size)])


def total_over(block, add, axis, size, cores=1):
    count = size // cores
    if count & (count - 1):
        return exchange([block] * count, axis, size, cores)
    terms, step = [block], 1
    while step < count:
        block = add(terms) if len(terms) > 1 else block
        terms = [lax.ppermute(block, axis, pairs_of(step, size, cores)), block]
        step *= 2
    return terms


def block_at(index, size):
    return pl.ds(pl.multiple_of(index * size, size), size)


def row_index():
    return lax.axis_index("row")


def chip_index():
    return lax.axis_index("col") // 2


def core_index():
    return lax.axis_index("col") % 2


def summed(refs):
    by_partner = dict(zip(far_first(len(refs)), refs))
    values = [by_partner[k][...].astype(F32) for k in sorted(by_partner)]
    while len(values) > 1:
        values = [sum(values[i + 1 : i + 2], values[i]) for i in range(0, len(values), 2)]
    return values[0]


def bias_rows(bias):
    high = bias.astype(BF16).astype(F32)
    line = lax.broadcasted_iota(jnp.int32, (BIAS_ROWS, bias.shape[1]), 0)
    return jnp.where(line == 0, high, jnp.where(line == 1, bias - high, 0.0))


def row_place(row, n_chip):
    return jnp.where(row % 2 == core_index(), 0, n_chip) + row // 2


def dense_kernel(
    count_ref, row_hbm, col_hbm, tiles_hbm, bias_hbm, dense_ref, bias_ref,
    row_ref, col_ref, tiles_ref, sum_ref, sems, tile_sems,
):
    slots, tile = tiles_ref.shape[0], tiles_ref.shape[1]
    n_chip = sum_ref.shape[0] // (2 * tile)
    chunks = tile_sems.shape[0]
    size = slots // chunks
    small = [
        pltpu.make_async_copy(row_hbm, row_ref, sems.at[0]),
        pltpu.make_async_copy(col_hbm, col_ref, sems.at[1]),
        pltpu.make_async_copy(bias_hbm, bias_ref, sems.at[2]),
    ]
    large = []
    for k in range(chunks):
        part = pl.ds(k * size, size)
        large.append(
            pltpu.make_async_copy(tiles_hbm.at[0, 0, part], tiles_ref.at[part], tile_sems.at[k])
        )
    for copy in small + large:
        copy.start()
    sum_ref[...] = jnp.zeros_like(sum_ref)
    for copy in small:
        copy.wait()
    count = count_ref[0, 0]

    def body(slot, carry):
        rows = block_at(row_place(row_ref[0, 0, slot], n_chip), tile)
        cols = block_at(col_ref[0, 0, slot], tile)
        sum_ref[rows, cols] += tiles_ref[slot].astype(F32)
        return carry

    for k, copy in enumerate(large):
        copy.wait()
        lax.fori_loop(k * size, jnp.minimum(count, (k + 1) * size), body, 0)
    dense_ref[...] = sum_ref[...].astype(BF16)


def turn_kernel(dense_ref, after_ref, turned_ref):
    rows = dense_ref.shape[0]
    step = 256 if rows % 256 == 0 else rows
    for first in range(0, rows, step):
        turned_ref[:, first : first + step] = dense_ref[first : first + step, :].T


def dense_dot(left, right):
    return jnp.dot(left, right, preferred_element_type=F32)


def gather_sources(sources, source_ref, index):
    tile = sources[0].shape[0]
    for k, ref in zip(far_first(len(sources)), sources):
        source_ref[block_at(partner(index, k, len(sources)), tile), :] = ref[...]


def slot_product(refs, source_ref, acc_ref, turned):
    count_ref, row_ref, col_ref, tiles_ref = refs
    tile = tiles_ref.shape[1]
    n_chip = (source_ref if turned else acc_ref).shape[0] // (2 * tile)
    contract = 0 if turned else 1
    acc_ref[...] = jnp.zeros_like(acc_ref)

    def body(slot, carry):
        places = [row_place(row_ref[slot], n_chip), col_ref[slot]]
        source, target = places if turned else places[::-1]
        acc_ref[block_at(target, tile), :] += lax.dot_general(
            tiles_ref[slot],
            source_ref[block_at(source, tile), :],
            (((contract,), (0,)), ((), ())),
            preferred_element_type=F32,
        )
        return carry

    lax.fori_loop(0, count_ref[0], body, 0)


def forward_other_kernel(dense_ref, *refs):
    sources, (other_ref, source_ref) = refs[:-2], refs[-2:]
    gather_sources(sources, source_ref, row_index())
    half = other_ref.shape[0]
    other_ref[...] = dense_dot(dense_ref[half:, :], source_ref[...]).astype(BF16)


def forward_own_kernel(dense_ref, source_ref, own_ref):
    own_ref[...] = dense_dot(dense_ref[: own_ref.shape[0], :], source_ref[...]).astype(BF16)


def slot_forward_kernel(count_ref, row_ref, col_ref, tiles_ref, *refs):
    sources, (other_ref, own_ref, source_ref, acc_ref) = refs[:-4], refs[-4:]
    gather_sources(sources, source_ref, row_index())
    slot_product((count_ref, row_ref, col_ref, tiles_ref), source_ref, acc_ref, False)
    half = own_ref.shape[0]
    own_ref[...] = acc_ref[:half, :].astype(BF16)
    other_ref[...] = acc_ref[half:, :].astype(BF16)


def chip_kernel(own_ref, other_ref, *refs, k, n_chip):
    out_ref = refs[-1]
    rows = block_at(partner(chip_index(), k, n_chip), out_ref.shape[0])
    out_ref[...] = (own_ref[rows, :].astype(F32) + other_ref[rows, :].astype(F32)).astype(BF16)


def middle_kernel(weight_ref, bias_ref, cot_ref, *refs):
    parts, (hidden_ref, grad_ref, agg_ref) = refs[:-3], refs[-3:]
    aggregated = summed(parts).astype(BF16)
    agg_ref[...] = aggregated
    v = dense_dot(aggregated, weight_ref[...]) + bias_ref[...]
    square = v * v
    t = jnp.tanh(ROOT_2_OVER_PI * (v + CUBIC * (square * v)))
    half = 0.5 * (1.0 + t)
    hidden_ref[...] = (v * half).astype(BF16)
    slope = half + 0.5 * v * (1.0 - t * t) * (ROOT_2_OVER_PI * (1.0 + 3.0 * CUBIC * square))
    grad_ref[...] = (cot_ref[...].astype(F32) * slope).astype(BF16)


def copy_kernel(in_ref, out_ref):
    out_ref[...] = in_ref[...]


def term_kernel(agg_ref, grad_ref, out_ref, *, own):
    half = agg_ref.shape[1] // 2
    core = core_index() if own else 1 - core_index()
    grad = grad_ref[...]
    out_ref[:half, :] = lax.dot_general(
        agg_ref[:, block_at(core, half)],
        grad,
        (((0,), (0,)), ((), ())),
        preferred_element_type=F32,
    ).astype(BF16)
    out_ref[half:, :] = bias_rows(jnp.sum(grad.astype(F32), axis=0, keepdims=True)).astype(BF16)


def add_terms_kernel(*refs, n_terms):
    total = summed(refs[:n_terms])
    out_ref = refs[-1]
    half = total.shape[0] - BIAS_ROWS
    out_ref[:half, :] = total[:half].astype(BF16)
    out_ref[half:, :] = bias_rows(total[half : half + 1] + total[half + 1 : half + 2]).astype(BF16)


def scale_kernel(after_ref, *refs, factor):
    parts, (half_ref, bias_ref) = refs[:-2], refs[-2:]
    total = summed(parts) * factor
    half = half_ref.shape[0]
    half_ref[...] = total[:half]
    bias_ref[...] = total[half : half + 1] + total[half + 1 : half + 2]


def gather_kernel(after_ref, *refs):
    gather_sources(refs[:-1], refs[-1], chip_index())


def back_own_kernel(turned_ref, source_ref, out_ref):
    out_ref[...] = dense_dot(turned_ref[:, : source_ref.shape[0]], source_ref[...])


def back_pieces_kernel(turned_ref, own_ref, source_ref, *outs):
    tile = outs[0].shape[0]
    for k, out_ref in zip(far_first(len(outs)), outs):
        rows = block_at(partner(row_index(), k, len(outs)), tile)
        rest = dense_dot(turned_ref[rows, source_ref.shape[0] :], source_ref[...])
        out_ref[...] = (own_ref[rows, :] + rest).astype(BF16)


def slot_back_kernel(count_ref, row_ref, col_ref, tiles_ref, own_ref, other_ref, *refs):
    outs, (source_ref, acc_ref) = refs[:-2], refs[-2:]
    half = own_ref.shape[0]
    source_ref[:half, :] = own_ref[...]
    source_ref[half:, :] = other_ref[...]
    slot_product((count_ref, row_ref, col_ref, tiles_ref), source_ref, acc_ref, True)
    tile = outs[0].shape[0]
    for k, out_ref in zip(far_first(len(outs)), outs):
        rows = block_at(partner(row_index(), k, len(outs)), tile)
        out_ref[...] = acc_ref[rows, :].astype(BF16)


def back_sum_kernel(*refs):
    total = refs[0][...].astype(F32)
    for ref in refs[1:-1]:
        total += ref[...].astype(F32)
    refs[-1][...] = total


def features_kernel(weight_ref, most_ref, last_ref, out_ref):
    out_ref[...] = lax.dot_general(
        (most_ref[...] + last_ref[...].astype(F32)).astype(BF16),
        weight_ref[...],
        (((1,), (1,)), ((), ())),
        preferred_element_type=F32,
    ).astype(BF16)


def write_kernel(
    features_ref, own_ref, other_ref, bias_ref, features_hbm, grad_hbm, bias_hbm, sems
):
    half = own_ref.shape[0]
    copies = [
        pltpu.make_async_copy(own_ref, grad_hbm.at[block_at(core_index(), half)], sems.at[0]),
        pltpu.make_async_copy(other_ref, grad_hbm.at[block_at(1 - core_index(), half)], sems.at[1]),
        pltpu.make_async_copy(features_ref, features_hbm, sems.at[2]),
        pltpu.make_async_copy(bias_ref, bias_hbm, sems.at[3]),
    ]
    for copy in copies:
        copy.start()
    for copy in copies:
        copy.wait()


def in_turn(count, make):
    made, before = {}, []
    for k in far_first(count):
        made[k] = make(k, before)
        before = [made[k]]
    return made


def local(features, weight, bias_term, cotangent, tile_values, tile_row, tile_col, tile_count):
    n_row = lax.axis_size("row")
    n_col = lax.axis_size("col")
    n_chip = n_col // 2
    tile, width = features.shape
    hidden = weight.shape[1]
    slots = tile_values.shape[2]
    row_nodes, col_nodes = n_col * tile, n_row * tile
    bias_row = bias_term.reshape(1, hidden)
    half = width // 2
    matrix = 2 * tile * width * hidden
    block_bytes = 2 * tile * width

    def like(rows, columns, dtype=BF16):
        return jax.ShapeDtypeStruct((rows, columns), dtype)

    near = 1
    own_nodes = n_chip * tile

    def add(terms, flops=0, after=()):
        return call(
            functools.partial(add_terms_kernel, n_terms=len(terms)),
            like(half + BIAS_ROWS, hidden),
            [VMEM_SPEC] * (len(terms) + len(after)),
            [],
            flops or len(terms) * half * hidden,
            len(terms) * half * hidden * 2,
        )(*terms, *after)

    is_dense = n_row * n_col <= 2 * slots
    if is_dense:
        chunks = 4 if slots % 4 == 0 else 1
        dense, bias_row = call(
            dense_kernel,
            (like(row_nodes, col_nodes), like(1, hidden, F32)),
            [SMEM_SPEC] + [HBM_SPEC] * 4,
            [
                pltpu.SMEM((1, 1, slots), jnp.int32),
                pltpu.SMEM((1, 1, slots), jnp.int32),
                pltpu.VMEM((slots, tile, tile), BF16),
                pltpu.VMEM((row_nodes, col_nodes), F32),
                pltpu.SemaphoreType.DMA((3,)),
                pltpu.SemaphoreType.DMA((chunks,)),
            ],
            0,
            12 * row_nodes * col_nodes,
        )(tile_count, *(
            pltpu.with_memory_space_constraint(array, pltpu.HBM)
            for array in (tile_row, tile_col, tile_values, bias_row)
        ))
    else:
        slot_args = (
            tile_count.reshape(1),
            tile_row.reshape(slots),
            tile_col.reshape(slots),
            tile_values.reshape(slots, tile, tile),
        )
        slot_specs = [SMEM_SPEC] * 3 + [VMEM_SPEC]

    sources = exchange([features] * n_row, "row", n_row)
    if is_dense:
        other, source = call(
            forward_other_kernel,
            (like(own_nodes, width), like(col_nodes, width)),
            [VMEM_SPEC] * (1 + n_row),
            [],
            slots * matrix // 2,
            row_nodes * width * 8,
        )(dense, *sources)
        own = call(
            forward_own_kernel,
            like(own_nodes, width),
            [VMEM_SPEC] * 2,
            [],
            slots * matrix // 2,
            row_nodes * width * 8,
        )(dense, source)
    else:
        other, own = call(
            slot_forward_kernel,
            (like(own_nodes, width), like(own_nodes, width)),
            slot_specs + [VMEM_SPEC] * n_row,
            [pltpu.VMEM((col_nodes, width), BF16), pltpu.VMEM((row_nodes, width), F32)],
            slots * matrix // 2,
            row_nodes * width * 8,
        )(*slot_args, *sources)
    swapped = swap_cores(other, n_col)

    def chip_piece(k, before):
        return call(
            functools.partial(chip_kernel, k=k, n_chip=n_chip),
            like(tile, width),
            [VMEM_SPEC] * (2 + len(before)),
            [],
            tile * width,
            3 * block_bytes,
        )(own, swapped, *before)

    pieces = in_turn(n_chip, chip_piece)
    parts = exchange(pieces, "col", n_col, 2)
    if is_dense:
        turned = call(
            turn_kernel,
            like(col_nodes, row_nodes),
            [VMEM_SPEC] * 2,
            [],
            0,
            4 * row_nodes * col_nodes,
        )(dense, pieces[0])
    hidden_own, grad, aggregated = call(
        middle_kernel,
        [like(tile, hidden), like(tile, hidden), like(tile, width)],
        [VMEM_SPEC] * (3 + n_chip),
        [],
        matrix,
        n_chip * block_bytes,
    )(weight, bias_row, cotangent, *parts)
    grads = exchange([grad] * n_chip, "col", n_col, 2)
    hidden_out = call(copy_kernel, like(tile, hidden), [VMEM_SPEC], [], 0, 2 * block_bytes)(hidden_own)
    mine, theirs = (
        call(
            functools.partial(term_kernel, own=own),
            like(half + BIAS_ROWS, hidden),
            [VMEM_SPEC] * 2,
            [],
            matrix // 2,
            4 * block_bytes,
        )(aggregated, grad)
        for own in (True, False)
    )
    chip_term = add([swap_cores(theirs, n_col), mine])
    add_late = functools.partial(add, flops=ROW_SUM_WEIGHT * matrix)
    row_terms = total_over(chip_term, add, "row", n_row)

    own_grads = call(
        gather_kernel,
        like(own_nodes, hidden),
        [VMEM_SPEC] * (1 + n_chip),
        [],
        0,
        own_nodes * hidden * 4,
    )(chip_term, *grads)
    other_grads = swap_cores(own_grads, n_col)
    if is_dense:
        back_own = call(
            back_own_kernel,
            like(col_nodes, hidden, F32),
            [VMEM_SPEC] * 2,
            [],
            slots * matrix // 2,
            row_nodes * hidden * 8,
        )(turned, own_grads)
        row_term = add_late(row_terms, after=[back_own])
        back_pieces = call(
            back_pieces_kernel,
            [like(tile, hidden)] * n_row,
            [VMEM_SPEC] * 3,
            [],
            slots * matrix // 2,
            row_nodes * hidden * 8,
        )(turned, back_own, other_grads)
    else:
        row_term = add_late(row_terms)
        back_pieces = call(
            slot_back_kernel,
            [like(tile, hidden)] * n_row,
            slot_specs + [VMEM_SPEC] * 2,
            [pltpu.VMEM((row_nodes, hidden), BF16), pltpu.VMEM((col_nodes, hidden), F32)],
            slots * matrix // 2,
            row_nodes * hidden * 8,
        )(*slot_args, own_grads, other_grads)
    backs = exchange(dict(zip(far_first(n_row), back_pieces)), "row", n_row)
    most = call(
        back_sum_kernel,
        like(tile, hidden, F32),
        [VMEM_SPEC] * (n_row - 1),
        [],
        BACK_SUM_WEIGHT * matrix,
        n_row * block_bytes,
    )(*backs[:-2], backs[-1])
    own_features = call(
        features_kernel,
        like(tile, width),
        [VMEM_SPEC] * 3,
        [],
        FEATURES_WEIGHT * matrix,
        n_row * block_bytes,
    )(weight, most, backs[-2])
    all_terms = total_over(row_term, add, "col", n_col, 2)
    factor = (tile * n_row * n_col) ** (-0.5)
    own_half, bias_grad = call(
        functools.partial(scale_kernel, factor=factor),
        (like(half, hidden, F32), like(1, hidden, F32)),
        [VMEM_SPEC] * (1 + len(all_terms)),
        [],
        len(all_terms) * half * hidden,
        len(all_terms) * half * hidden * 2,
    )(most, *all_terms)
    grad_features, grad_weight, grad_bias = call(
        write_kernel,
        (like(tile, width), like(width, hidden, F32), like(1, hidden, F32)),
        [VMEM_SPEC] * 4,
        [pltpu.SemaphoreType.DMA((4,))],
        0,
        width * hidden * 8,
        HBM_SPEC,
    )(own_features, own_half, swap_cores(own_half, n_col), bias_grad)
    return hidden_out, grad_features, grad_weight, grad_bias.reshape(hidden)


def solution(mesh):
    return jax.shard_map(
        local,
        mesh=mesh,
        in_specs=(
            P(("col", "row"), None),
            P(),
            P(),
            P(("row", "col"), None),
            P("row", "col", None, None, None),
            P("row", "col", None),
            P("row", "col", None),
            P("row", "col"),
        ),
        out_specs=(P(("row", "col"), None), P(("col", "row"), None), P(), P()),
        check_vma=False,
    )
```

```python
import functools

import jax
import jax.numpy as jnp
from jax import lax
from jax.experimental import pallas as pl
from jax.experimental.pallas import tpu as pltpu
from jax.sharding import PartitionSpec as P

F32 = jnp.float32
BF16 = jnp.bfloat16
ROOT_2_OVER_PI = 0.7978845608028654
CUBIC = 0.044715
VMEM_LIMIT = 48 * 1024 * 1024
BIAS_ROWS = 16
BACK_SUM_WEIGHT = 30
ROW_SUM_WEIGHT = 120
FEATURES_WEIGHT = 100

VMEM_SPEC = pl.BlockSpec(memory_space=pltpu.VMEM)
HBM_SPEC = pl.BlockSpec(memory_space=pltpu.HBM)
SMEM_SPEC = pl.BlockSpec(memory_space=pltpu.SMEM)


def call(kernel, out_shape, in_specs, scratch, flops, moved, out_spec=VMEM_SPEC):
    return pl.pallas_call(
        kernel,
        out_shape=out_shape,
        in_specs=in_specs,
        out_specs=jax.tree.map(lambda _: out_spec, out_shape),
        scratch_shapes=scratch,
        compiler_params=pltpu.CompilerParams(vmem_limit_bytes=VMEM_LIMIT),
        cost_estimate=pl.CostEstimate(flops=flops, bytes_accessed=moved, transcendentals=0),
    )


def partner(index, k, count):
    if count & (count - 1) == 0:
        return index ^ k
    return (k - index) % count


def far_first(count):
    return list(range(count - 1, -1, -1))


def pairs_of(k, size, cores):
    return [(i, partner(i // cores, k, size // cores) * cores + i % cores) for i in range(size)]


def half_first(count):
    return [count // 2] + [k for k in far_first(count) if k != count // 2]


def exchange(blocks, axis, size, cores=1, order=far_first):
    received = []
    for k in order(size // cores):
        pairs = pairs_of(k, size, cores)
        moves = any(i != j for i, j in pairs)
        received.append(lax.ppermute(blocks[k], axis, pairs) if moves else blocks[k])
    return received


def swap_cores(block, size):
    return lax.ppermute(block, "col", [(i, i ^ 1) for i in range(size)])


def total_over(block, add, axis, size, cores=1):
    count = size // cores
    if count & (count - 1):
        return exchange([block] * count, axis, size, cores)
    terms, step = [block], 1
    while step < count:
        block = add(terms) if len(terms) > 1 else block
        terms = [lax.ppermute(block, axis, pairs_of(step, size, cores)), block]
        step *= 2
    return terms


def block_at(index, size):
    return pl.ds(pl.multiple_of(index * size, size), size)


def row_index():
    return lax.axis_index("row")


def chip_index():
    return lax.axis_index("col") // 2


def core_index():
    return lax.axis_index("col") % 2


def summed(refs):
    by_partner = dict(zip(far_first(len(refs)), refs))
    values = [by_partner[k][...].astype(F32) for k in sorted(by_partner)]
    while len(values) > 1:
        values = [sum(values[i + 1 : i + 2], values[i]) for i in range(0, len(values), 2)]
    return values[0]


def bias_rows(bias):
    high = bias.astype(BF16).astype(F32)
    line = lax.broadcasted_iota(jnp.int32, (BIAS_ROWS, bias.shape[1]), 0)
    return jnp.where(line == 0, high, jnp.where(line == 1, bias - high, 0.0))


def row_place(row, n_chip):
    return jnp.where(row % 2 == core_index(), 0, n_chip) + row // 2


def dense_kernel(
    count_ref, row_hbm, col_hbm, tiles_hbm, bias_hbm, dense_ref, bias_ref,
    row_ref, col_ref, tiles_ref, sum_ref, sems, tile_sems,
):
    slots, tile = tiles_ref.shape[0], tiles_ref.shape[1]
    n_chip = sum_ref.shape[0] // (2 * tile)
    chunks = tile_sems.shape[0]
    size = slots // chunks
    small = [
        pltpu.make_async_copy(row_hbm, row_ref, sems.at[0]),
        pltpu.make_async_copy(col_hbm, col_ref, sems.at[1]),
        pltpu.make_async_copy(bias_hbm, bias_ref, sems.at[2]),
    ]
    large = []
    for k in range(chunks):
        part = pl.ds(k * size, size)
        large.append(
            pltpu.make_async_copy(tiles_hbm.at[0, 0, part], tiles_ref.at[part], tile_sems.at[k])
        )
    for copy in small + large:
        copy.start()
    sum_ref[...] = jnp.zeros_like(sum_ref)
    for copy in small:
        copy.wait()
    count = count_ref[0, 0]

    def body(slot, carry):
        rows = block_at(row_place(row_ref[0, 0, slot], n_chip), tile)
        cols = block_at(col_ref[0, 0, slot], tile)
        sum_ref[rows, cols] += tiles_ref[slot].astype(F32)
        return carry

    for k, copy in enumerate(large):
        copy.wait()
        lax.fori_loop(k * size, jnp.minimum(count, (k + 1) * size), body, 0)
    dense_ref[...] = sum_ref[...].astype(BF16)


def turn_kernel(dense_ref, after_ref, turned_ref):
    rows = dense_ref.shape[0]
    step = 256 if rows % 256 == 0 else rows
    for first in range(0, rows, step):
        turned_ref[:, first : first + step] = dense_ref[first : first + step, :].T


def dense_dot(left, right):
    return jnp.dot(left, right, preferred_element_type=F32)


def gather_sources(sources, source_ref, index, order):
    tile = sources[0].shape[0]
    for k, ref in zip(order(len(sources)), sources):
        source_ref[block_at(partner(index, k, len(sources)), tile), :] = ref[...]


def slot_product(refs, source_ref, acc_ref, turned):
    count_ref, row_ref, col_ref, tiles_ref = refs
    tile = tiles_ref.shape[1]
    n_chip = (source_ref if turned else acc_ref).shape[0] // (2 * tile)
    contract = 0 if turned else 1
    acc_ref[...] = jnp.zeros_like(acc_ref)

    def body(slot, carry):
        places = [row_place(row_ref[slot], n_chip), col_ref[slot]]
        source, target = places if turned else places[::-1]
        acc_ref[block_at(target, tile), :] += lax.dot_general(
            tiles_ref[slot],
            source_ref[block_at(source, tile), :],
            (((contract,), (0,)), ((), ())),
            preferred_element_type=F32,
        )
        return carry

    lax.fori_loop(0, count_ref[0], body, 0)


def forward_other_kernel(dense_ref, *refs):
    sources, (other_ref, source_ref) = refs[:-2], refs[-2:]
    gather_sources(sources, source_ref, row_index(), half_first)
    half = other_ref.shape[0]
    other_ref[...] = dense_dot(dense_ref[half:, :], source_ref[...]).astype(BF16)


def forward_own_kernel(dense_ref, source_ref, own_ref):
    own_ref[...] = dense_dot(dense_ref[: own_ref.shape[0], :], source_ref[...]).astype(BF16)


def slot_forward_kernel(count_ref, row_ref, col_ref, tiles_ref, *refs):
    sources, (other_ref, own_ref, source_ref, acc_ref) = refs[:-4], refs[-4:]
    gather_sources(sources, source_ref, row_index(), half_first)
    slot_product((count_ref, row_ref, col_ref, tiles_ref), source_ref, acc_ref, False)
    half = own_ref.shape[0]
    own_ref[...] = acc_ref[:half, :].astype(BF16)
    other_ref[...] = acc_ref[half:, :].astype(BF16)


def chip_kernel(own_ref, other_ref, *refs, k, n_chip):
    out_ref = refs[-1]
    rows = block_at(partner(chip_index(), k, n_chip), out_ref.shape[0])
    out_ref[...] = (own_ref[rows, :].astype(F32) + other_ref[rows, :].astype(F32)).astype(BF16)


def middle_kernel(weight_ref, bias_ref, cot_ref, *refs):
    parts, (hidden_ref, grad_ref, agg_ref) = refs[:-3], refs[-3:]
    aggregated = summed(parts).astype(BF16)
    agg_ref[...] = aggregated
    v = dense_dot(aggregated, weight_ref[...]) + bias_ref[...]
    square = v * v
    t = jnp.tanh(ROOT_2_OVER_PI * (v + CUBIC * (square * v)))
    half = 0.5 * (1.0 + t)
    hidden_ref[...] = (v * half).astype(BF16)
    slope = half + 0.5 * v * (1.0 - t * t) * (ROOT_2_OVER_PI * (1.0 + 3.0 * CUBIC * square))
    grad_ref[...] = (cot_ref[...].astype(F32) * slope).astype(BF16)


def copy_kernel(in_ref, out_ref):
    out_ref[...] = in_ref[...]


def term_kernel(agg_ref, grad_ref, out_ref, *, own):
    half = agg_ref.shape[1] // 2
    core = core_index() if own else 1 - core_index()
    grad = grad_ref[...]
    out_ref[:half, :] = lax.dot_general(
        agg_ref[:, block_at(core, half)],
        grad,
        (((0,), (0,)), ((), ())),
        preferred_element_type=F32,
    ).astype(BF16)
    out_ref[half:, :] = bias_rows(jnp.sum(grad.astype(F32), axis=0, keepdims=True)).astype(BF16)


def add_terms_kernel(*refs, n_terms):
    total = summed(refs[:n_terms])
    out_ref = refs[-1]
    half = total.shape[0] - BIAS_ROWS
    out_ref[:half, :] = total[:half].astype(BF16)
    out_ref[half:, :] = bias_rows(total[half : half + 1] + total[half + 1 : half + 2]).astype(BF16)


def scale_kernel(after_ref, *refs, factor):
    parts, (half_ref, bias_ref) = refs[:-2], refs[-2:]
    total = summed(parts) * factor
    half = half_ref.shape[0]
    half_ref[...] = total[:half]
    bias_ref[...] = total[half : half + 1] + total[half + 1 : half + 2]


def gather_kernel(after_ref, *refs):
    gather_sources(refs[:-1], refs[-1], chip_index(), far_first)


def back_own_kernel(turned_ref, source_ref, out_ref):
    out_ref[...] = dense_dot(turned_ref[:, : source_ref.shape[0]], source_ref[...])


def back_pieces_kernel(turned_ref, own_ref, source_ref, *outs):
    tile = outs[0].shape[0]
    for k, out_ref in zip(far_first(len(outs)), outs):
        rows = block_at(partner(row_index(), k, len(outs)), tile)
        rest = dense_dot(turned_ref[rows, source_ref.shape[0] :], source_ref[...])
        out_ref[...] = (own_ref[rows, :] + rest).astype(BF16)


def slot_back_kernel(count_ref, row_ref, col_ref, tiles_ref, own_ref, other_ref, *refs):
    outs, (source_ref, acc_ref) = refs[:-2], refs[-2:]
    half = own_ref.shape[0]
    source_ref[:half, :] = own_ref[...]
    source_ref[half:, :] = other_ref[...]
    slot_product((count_ref, row_ref, col_ref, tiles_ref), source_ref, acc_ref, True)
    tile = outs[0].shape[0]
    for k, out_ref in zip(far_first(len(outs)), outs):
        rows = block_at(partner(row_index(), k, len(outs)), tile)
        out_ref[...] = acc_ref[rows, :].astype(BF16)


def back_sum_kernel(*refs):
    total = refs[0][...].astype(F32)
    for ref in refs[1:-1]:
        total += ref[...].astype(F32)
    refs[-1][...] = total


def features_kernel(weight_ref, most_ref, last_ref, out_ref):
    out_ref[...] = lax.dot_general(
        (most_ref[...] + last_ref[...].astype(F32)).astype(BF16),
        weight_ref[...],
        (((1,), (1,)), ((), ())),
        preferred_element_type=F32,
    ).astype(BF16)


def write_kernel(
    features_ref, own_ref, other_ref, bias_ref, features_hbm, grad_hbm, bias_hbm, sems
):
    half = own_ref.shape[0]
    copies = [
        pltpu.make_async_copy(own_ref, grad_hbm.at[block_at(core_index(), half)], sems.at[0]),
        pltpu.make_async_copy(other_ref, grad_hbm.at[block_at(1 - core_index(), half)], sems.at[1]),
        pltpu.make_async_copy(features_ref, features_hbm, sems.at[2]),
        pltpu.make_async_copy(bias_ref, bias_hbm, sems.at[3]),
    ]
    for copy in copies:
        copy.start()
    for copy in copies:
        copy.wait()


def in_turn(count, make):
    made, before = {}, []
    for k in far_first(count):
        made[k] = make(k, before)
        before = [made[k]]
    return made


def local(features, weight, bias_term, cotangent, tile_values, tile_row, tile_col, tile_count):
    n_row = lax.axis_size("row")
    n_col = lax.axis_size("col")
    n_chip = n_col // 2
    tile, width = features.shape
    hidden = weight.shape[1]
    slots = tile_values.shape[2]
    row_nodes, col_nodes = n_col * tile, n_row * tile
    bias_row = bias_term.reshape(1, hidden)
    half = width // 2
    matrix = 2 * tile * width * hidden
    block_bytes = 2 * tile * width

    def like(rows, columns, dtype=BF16):
        return jax.ShapeDtypeStruct((rows, columns), dtype)

    near = 1
    own_nodes = n_chip * tile

    def add(terms, flops=0, after=()):
        return call(
            functools.partial(add_terms_kernel, n_terms=len(terms)),
            like(half + BIAS_ROWS, hidden),
            [VMEM_SPEC] * (len(terms) + len(after)),
            [],
            flops or len(terms) * half * hidden,
            len(terms) * half * hidden * 2,
        )(*terms, *after)

    is_dense = n_row * n_col <= 2 * slots
    if is_dense:
        chunks = 4 if slots % 4 == 0 else 1
        dense, bias_row = call(
            dense_kernel,
            (like(row_nodes, col_nodes), like(1, hidden, F32)),
            [SMEM_SPEC] + [HBM_SPEC] * 4,
            [
                pltpu.SMEM((1, 1, slots), jnp.int32),
                pltpu.SMEM((1, 1, slots), jnp.int32),
                pltpu.VMEM((slots, tile, tile), BF16),
                pltpu.VMEM((row_nodes, col_nodes), F32),
                pltpu.SemaphoreType.DMA((3,)),
                pltpu.SemaphoreType.DMA((chunks,)),
            ],
            0,
            12 * row_nodes * col_nodes,
        )(tile_count, *(
            pltpu.with_memory_space_constraint(array, pltpu.HBM)
            for array in (tile_row, tile_col, tile_values, bias_row)
        ))
    else:
        slot_args = (
            tile_count.reshape(1),
            tile_row.reshape(slots),
            tile_col.reshape(slots),
            tile_values.reshape(slots, tile, tile),
        )
        slot_specs = [SMEM_SPEC] * 3 + [VMEM_SPEC]

    sources = exchange([features] * n_row, "row", n_row, order=half_first)
    if is_dense:
        other, source = call(
            forward_other_kernel,
            (like(own_nodes, width), like(col_nodes, width)),
            [VMEM_SPEC] * (1 + n_row),
            [],
            slots * matrix // 2,
            row_nodes * width * 8,
        )(dense, *sources)
        own = call(
            forward_own_kernel,
            like(own_nodes, width),
            [VMEM_SPEC] * 2,
            [],
            slots * matrix // 2,
            row_nodes * width * 8,
        )(dense, source)
    else:
        other, own = call(
            slot_forward_kernel,
            (like(own_nodes, width), like(own_nodes, width)),
            slot_specs + [VMEM_SPEC] * n_row,
            [pltpu.VMEM((col_nodes, width), BF16), pltpu.VMEM((row_nodes, width), F32)],
            slots * matrix // 2,
            row_nodes * width * 8,
        )(*slot_args, *sources)
    swapped = swap_cores(other, n_col)

    def chip_piece(k, before):
        return call(
            functools.partial(chip_kernel, k=k, n_chip=n_chip),
            like(tile, width),
            [VMEM_SPEC] * (2 + len(before)),
            [],
            tile * width,
            3 * block_bytes,
        )(own, swapped, *before)

    pieces = in_turn(n_chip, chip_piece)
    parts = exchange(pieces, "col", n_col, 2)
    if is_dense:
        turned = call(
            turn_kernel,
            like(col_nodes, row_nodes),
            [VMEM_SPEC] * 2,
            [],
            0,
            4 * row_nodes * col_nodes,
        )(dense, pieces[0])
    hidden_own, grad, aggregated = call(
        middle_kernel,
        [like(tile, hidden), like(tile, hidden), like(tile, width)],
        [VMEM_SPEC] * (3 + n_chip),
        [],
        matrix,
        n_chip * block_bytes,
    )(weight, bias_row, cotangent, *parts)
    grads = exchange([grad] * n_chip, "col", n_col, 2)
    hidden_out = call(copy_kernel, like(tile, hidden), [VMEM_SPEC], [], 0, 2 * block_bytes)(hidden_own)
    mine, theirs = (
        call(
            functools.partial(term_kernel, own=own),
            like(half + BIAS_ROWS, hidden),
            [VMEM_SPEC] * 2,
            [],
            matrix // 2,
            4 * block_bytes,
        )(aggregated, grad)
        for own in (True, False)
    )
    chip_term = add([swap_cores(theirs, n_col), mine])
    add_late = functools.partial(add, flops=ROW_SUM_WEIGHT * matrix)
    row_terms = total_over(chip_term, add, "row", n_row)

    own_grads = call(
        gather_kernel,
        like(own_nodes, hidden),
        [VMEM_SPEC] * (1 + n_chip),
        [],
        0,
        own_nodes * hidden * 4,
    )(chip_term, *grads)
    other_grads = swap_cores(own_grads, n_col)
    if is_dense:
        back_own = call(
            back_own_kernel,
            like(col_nodes, hidden, F32),
            [VMEM_SPEC] * 2,
            [],
            slots * matrix // 2,
            row_nodes * hidden * 8,
        )(turned, own_grads)
        row_term = add_late(row_terms, after=[back_own])
        back_pieces = call(
            back_pieces_kernel,
            [like(tile, hidden)] * n_row,
            [VMEM_SPEC] * 3,
            [],
            slots * matrix // 2,
            row_nodes * hidden * 8,
        )(turned, back_own, other_grads)
    else:
        row_term = add_late(row_terms)
        back_pieces = call(
            slot_back_kernel,
            [like(tile, hidden)] * n_row,
            slot_specs + [VMEM_SPEC] * 2,
            [pltpu.VMEM((row_nodes, hidden), BF16), pltpu.VMEM((col_nodes, hidden), F32)],
            slots * matrix // 2,
            row_nodes * hidden * 8,
        )(*slot_args, own_grads, other_grads)
    backs = exchange(dict(zip(far_first(n_row), back_pieces)), "row", n_row)
    most = call(
        back_sum_kernel,
        like(tile, hidden, F32),
        [VMEM_SPEC] * (n_row - 1),
        [],
        BACK_SUM_WEIGHT * matrix,
        n_row * block_bytes,
    )(*backs[:-2], backs[-1])
    own_features = call(
        features_kernel,
        like(tile, width),
        [VMEM_SPEC] * 3,
        [],
        FEATURES_WEIGHT * matrix,
        n_row * block_bytes,
    )(weight, most, backs[-2])
    all_terms = total_over(row_term, add, "col", n_col, 2)
    factor = (tile * n_row * n_col) ** (-0.5)
    own_half, bias_grad = call(
        functools.partial(scale_kernel, factor=factor),
        (like(half, hidden, F32), like(1, hidden, F32)),
        [VMEM_SPEC] * (1 + len(all_terms)),
        [],
        len(all_terms) * half * hidden,
        len(all_terms) * half * hidden * 2,
    )(most, *all_terms)
    grad_features, grad_weight, grad_bias = call(
        write_kernel,
        (like(tile, width), like(width, hidden, F32), like(1, hidden, F32)),
        [VMEM_SPEC] * 4,
        [pltpu.SemaphoreType.DMA((4,))],
        0,
        width * hidden * 8,
        HBM_SPEC,
    )(own_features, own_half, swap_cores(own_half, n_col), bias_grad)
    return hidden_out, grad_features, grad_weight, grad_bias.reshape(hidden)


def solution(mesh):
    return jax.shard_map(
        local,
        mesh=mesh,
        in_specs=(
            P(("col", "row"), None),
            P(),
            P(),
            P(("row", "col"), None),
            P("row", "col", None, None, None),
            P("row", "col", None),
            P("row", "col", None),
            P("row", "col"),
        ),
        out_specs=(P(("row", "col"), None), P(("col", "row"), None), P(), P()),
        check_vma=False,
    )
```

```python
import functools

import jax
import jax.numpy as jnp
from jax import lax
from jax.experimental import pallas as pl
from jax.experimental.pallas import tpu as pltpu
from jax.sharding import PartitionSpec as P

F32 = jnp.float32
BF16 = jnp.bfloat16
ROOT_2_OVER_PI = 0.7978845608028654
CUBIC = 0.044715
VMEM_LIMIT = 48 * 1024 * 1024
BIAS_ROWS = 16
BACK_SUM_WEIGHT = 30
ROW_SUM_WEIGHT = 120
FEATURES_WEIGHT = 100

VMEM_SPEC = pl.BlockSpec(memory_space=pltpu.VMEM)
HBM_SPEC = pl.BlockSpec(memory_space=pltpu.HBM)
SMEM_SPEC = pl.BlockSpec(memory_space=pltpu.SMEM)


def call(kernel, out_shape, in_specs, scratch, flops, moved, out_spec=VMEM_SPEC):
    return pl.pallas_call(
        kernel,
        out_shape=out_shape,
        in_specs=in_specs,
        out_specs=jax.tree.map(lambda _: out_spec, out_shape),
        scratch_shapes=scratch,
        compiler_params=pltpu.CompilerParams(vmem_limit_bytes=VMEM_LIMIT),
        cost_estimate=pl.CostEstimate(flops=flops, bytes_accessed=moved, transcendentals=0),
    )


def partner(index, k, count):
    if count & (count - 1) == 0:
        return index ^ k
    return (k - index) % count


def far_first(count):
    return list(range(count - 1, -1, -1))


def pairs_of(k, size, cores):
    return [(i, partner(i // cores, k, size // cores) * cores + i % cores) for i in range(size)]


def half_first(count):
    return [count // 2] + [k for k in far_first(count) if k != count // 2]


def exchange(blocks, axis, size, cores=1, order=far_first):
    received = []
    for k in order(size // cores):
        pairs = pairs_of(k, size, cores)
        moves = any(i != j for i, j in pairs)
        received.append(lax.ppermute(blocks[k], axis, pairs) if moves else blocks[k])
    return received


def swap_cores(block, size):
    return lax.ppermute(block, "col", [(i, i ^ 1) for i in range(size)])


def total_over(block, add, axis, size, cores=1):
    count = size // cores
    if count & (count - 1):
        return exchange([block] * count, axis, size, cores)
    terms, step = [block], 1
    while step < count:
        block = add(terms) if len(terms) > 1 else block
        terms = [lax.ppermute(block, axis, pairs_of(step, size, cores)), block]
        step *= 2
    return terms


def block_at(index, size):
    return pl.ds(pl.multiple_of(index * size, size), size)


def row_index():
    return lax.axis_index("row")


def chip_index():
    return lax.axis_index("col") // 2


def core_index():
    return lax.axis_index("col") % 2


def summed(refs):
    by_partner = dict(zip(far_first(len(refs)), refs))
    values = [by_partner[k][...].astype(F32) for k in sorted(by_partner)]
    while len(values) > 1:
        values = [sum(values[i + 1 : i + 2], values[i]) for i in range(0, len(values), 2)]
    return values[0]


def bias_rows(bias):
    high = bias.astype(BF16).astype(F32)
    line = lax.broadcasted_iota(jnp.int32, (BIAS_ROWS, bias.shape[1]), 0)
    return jnp.where(line == 0, high, jnp.where(line == 1, bias - high, 0.0))


def row_place(row, n_chip):
    return jnp.where(row % 2 == core_index(), 0, n_chip) + row // 2


def dense_kernel(
    count_ref, row_hbm, col_hbm, tiles_hbm, bias_hbm, dense_ref, bias_ref,
    row_ref, col_ref, tiles_ref, sum_ref, sems, tile_sems,
):
    slots, tile = tiles_ref.shape[0], tiles_ref.shape[1]
    n_chip = sum_ref.shape[0] // (2 * tile)
    chunks = tile_sems.shape[0]
    size = slots // chunks
    small = [
        pltpu.make_async_copy(row_hbm, row_ref, sems.at[0]),
        pltpu.make_async_copy(col_hbm, col_ref, sems.at[1]),
        pltpu.make_async_copy(bias_hbm, bias_ref, sems.at[2]),
    ]
    large = []
    for k in range(chunks):
        part = pl.ds(k * size, size)
        large.append(
            pltpu.make_async_copy(tiles_hbm.at[0, 0, part], tiles_ref.at[part], tile_sems.at[k])
        )
    for copy in small + large:
        copy.start()
    sum_ref[...] = jnp.zeros_like(sum_ref)
    for copy in small:
        copy.wait()
    count = count_ref[0, 0]

    def body(slot, carry):
        rows = block_at(row_place(row_ref[0, 0, slot], n_chip), tile)
        cols = block_at(col_ref[0, 0, slot], tile)
        sum_ref[rows, cols] += tiles_ref[slot].astype(F32)
        return carry

    for k, copy in enumerate(large):
        copy.wait()
        lax.fori_loop(k * size, jnp.minimum(count, (k + 1) * size), body, 0)
    dense_ref[...] = sum_ref[...].astype(BF16)


def turn_kernel(dense_ref, after_ref, turned_ref):
    rows = dense_ref.shape[0]
    step = 256 if rows % 256 == 0 else rows
    for first in range(0, rows, step):
        turned_ref[:, first : first + step] = dense_ref[first : first + step, :].T


def dense_dot(left, right):
    return jnp.dot(left, right, preferred_element_type=F32)


def gather_sources(sources, source_ref, index, order):
    tile = sources[0].shape[0]
    for k, ref in zip(order(len(sources)), sources):
        source_ref[block_at(partner(index, k, len(sources)), tile), :] = ref[...]


def slot_product(refs, source_ref, acc_ref, turned):
    count_ref, row_ref, col_ref, tiles_ref = refs
    tile = tiles_ref.shape[1]
    n_chip = (source_ref if turned else acc_ref).shape[0] // (2 * tile)
    contract = 0 if turned else 1
    acc_ref[...] = jnp.zeros_like(acc_ref)

    def body(slot, carry):
        places = [row_place(row_ref[slot], n_chip), col_ref[slot]]
        source, target = places if turned else places[::-1]
        acc_ref[block_at(target, tile), :] += lax.dot_general(
            tiles_ref[slot],
            source_ref[block_at(source, tile), :],
            (((contract,), (0,)), ((), ())),
            preferred_element_type=F32,
        )
        return carry

    lax.fori_loop(0, count_ref[0], body, 0)


def forward_other_kernel(dense_ref, *refs):
    sources, (other_ref, source_ref) = refs[:-2], refs[-2:]
    gather_sources(sources, source_ref, row_index(), half_first)
    half = other_ref.shape[0]
    other_ref[...] = dense_dot(dense_ref[half:, :], source_ref[...]).astype(BF16)


def forward_own_kernel(dense_ref, source_ref, own_ref):
    own_ref[...] = dense_dot(dense_ref[: own_ref.shape[0], :], source_ref[...]).astype(BF16)


def slot_forward_kernel(count_ref, row_ref, col_ref, tiles_ref, *refs):
    sources, (other_ref, own_ref, source_ref, acc_ref) = refs[:-4], refs[-4:]
    gather_sources(sources, source_ref, row_index(), half_first)
    slot_product((count_ref, row_ref, col_ref, tiles_ref), source_ref, acc_ref, False)
    half = own_ref.shape[0]
    own_ref[...] = acc_ref[:half, :].astype(BF16)
    other_ref[...] = acc_ref[half:, :].astype(BF16)


def chip_kernel(own_ref, other_ref, *refs, k, n_chip):
    out_ref = refs[-1]
    rows = block_at(partner(chip_index(), k, n_chip), out_ref.shape[0])
    out_ref[...] = (own_ref[rows, :].astype(F32) + other_ref[rows, :].astype(F32)).astype(BF16)


def middle_kernel(weight_ref, bias_ref, cot_ref, *refs):
    parts, (hidden_ref, grad_ref, agg_ref) = refs[:-3], refs[-3:]
    aggregated = summed(parts).astype(BF16)
    agg_ref[...] = aggregated
    v = dense_dot(aggregated, weight_ref[...]) + bias_ref[...]
    square = v * v
    t = jnp.tanh(ROOT_2_OVER_PI * (v + CUBIC * (square * v)))
    half = 0.5 * (1.0 + t)
    hidden_ref[...] = (v * half).astype(BF16)
    slope = half + 0.5 * v * (1.0 - t * t) * (ROOT_2_OVER_PI * (1.0 + 3.0 * CUBIC * square))
    grad_ref[...] = (cot_ref[...].astype(F32) * slope).astype(BF16)


def copy_kernel(in_ref, out_ref):
    out_ref[...] = in_ref[...]


def term_kernel(agg_ref, grad_ref, out_ref, *, own):
    half = agg_ref.shape[1] // 2
    core = core_index() if own else 1 - core_index()
    grad = grad_ref[...]
    out_ref[:half, :] = lax.dot_general(
        agg_ref[:, block_at(core, half)],
        grad,
        (((0,), (0,)), ((), ())),
        preferred_element_type=F32,
    ).astype(BF16)
    out_ref[half:, :] = bias_rows(jnp.sum(grad.astype(F32), axis=0, keepdims=True)).astype(BF16)


def add_terms_kernel(*refs, n_terms):
    total = summed(refs[:n_terms])
    out_ref = refs[-1]
    half = total.shape[0] - BIAS_ROWS
    out_ref[:half, :] = total[:half].astype(BF16)
    out_ref[half:, :] = bias_rows(total[half : half + 1] + total[half + 1 : half + 2]).astype(BF16)


def scale_kernel(after_ref, *refs, factor):
    parts, (half_ref, bias_ref) = refs[:-2], refs[-2:]
    total = summed(parts) * factor
    half = half_ref.shape[0]
    half_ref[...] = total[:half]
    bias_ref[...] = total[half : half + 1] + total[half + 1 : half + 2]


def gather_kernel(after_ref, *refs):
    gather_sources(refs[:-1], refs[-1], chip_index(), far_first)


def back_own_kernel(turned_ref, source_ref, out_ref):
    out_ref[...] = dense_dot(turned_ref[:, : source_ref.shape[0]], source_ref[...])


def back_pieces_kernel(turned_ref, own_ref, source_ref, *outs):
    tile = outs[0].shape[0]
    for k, out_ref in zip(half_first(len(outs)), outs):
        rows = block_at(partner(row_index(), k, len(outs)), tile)
        rest = dense_dot(turned_ref[rows, source_ref.shape[0] :], source_ref[...])
        out_ref[...] = (own_ref[rows, :] + rest).astype(BF16)


def slot_back_kernel(count_ref, row_ref, col_ref, tiles_ref, own_ref, other_ref, *refs):
    outs, (source_ref, acc_ref) = refs[:-2], refs[-2:]
    half = own_ref.shape[0]
    source_ref[:half, :] = own_ref[...]
    source_ref[half:, :] = other_ref[...]
    slot_product((count_ref, row_ref, col_ref, tiles_ref), source_ref, acc_ref, True)
    tile = outs[0].shape[0]
    for k, out_ref in zip(half_first(len(outs)), outs):
        rows = block_at(partner(row_index(), k, len(outs)), tile)
        out_ref[...] = acc_ref[rows, :].astype(BF16)


def back_sum_kernel(*refs):
    total = refs[0][...].astype(F32)
    for ref in refs[1:-1]:
        total += ref[...].astype(F32)
    refs[-1][...] = total


def features_kernel(weight_ref, most_ref, last_ref, out_ref):
    out_ref[...] = lax.dot_general(
        (most_ref[...] + last_ref[...].astype(F32)).astype(BF16),
        weight_ref[...],
        (((1,), (1,)), ((), ())),
        preferred_element_type=F32,
    ).astype(BF16)


def write_kernel(
    features_ref, own_ref, other_ref, bias_ref, features_hbm, grad_hbm, bias_hbm, sems
):
    half = own_ref.shape[0]
    copies = [
        pltpu.make_async_copy(own_ref, grad_hbm.at[block_at(core_index(), half)], sems.at[0]),
        pltpu.make_async_copy(other_ref, grad_hbm.at[block_at(1 - core_index(), half)], sems.at[1]),
        pltpu.make_async_copy(features_ref, features_hbm, sems.at[2]),
        pltpu.make_async_copy(bias_ref, bias_hbm, sems.at[3]),
    ]
    for copy in copies:
        copy.start()
    for copy in copies:
        copy.wait()


def in_turn(count, make):
    made, before = {}, []
    for k in far_first(count):
        made[k] = make(k, before)
        before = [made[k]]
    return made


def local(features, weight, bias_term, cotangent, tile_values, tile_row, tile_col, tile_count):
    n_row = lax.axis_size("row")
    n_col = lax.axis_size("col")
    n_chip = n_col // 2
    tile, width = features.shape
    hidden = weight.shape[1]
    slots = tile_values.shape[2]
    row_nodes, col_nodes = n_col * tile, n_row * tile
    bias_row = bias_term.reshape(1, hidden)
    half = width // 2
    matrix = 2 * tile * width * hidden
    block_bytes = 2 * tile * width

    def like(rows, columns, dtype=BF16):
        return jax.ShapeDtypeStruct((rows, columns), dtype)

    near = 1
    own_nodes = n_chip * tile

    def add(terms, flops=0, after=()):
        return call(
            functools.partial(add_terms_kernel, n_terms=len(terms)),
            like(half + BIAS_ROWS, hidden),
            [VMEM_SPEC] * (len(terms) + len(after)),
            [],
            flops or len(terms) * half * hidden,
            len(terms) * half * hidden * 2,
        )(*terms, *after)

    is_dense = n_row * n_col <= 2 * slots
    if is_dense:
        chunks = 4 if slots % 4 == 0 else 1
        dense, bias_row = call(
            dense_kernel,
            (like(row_nodes, col_nodes), like(1, hidden, F32)),
            [SMEM_SPEC] + [HBM_SPEC] * 4,
            [
                pltpu.SMEM((1, 1, slots), jnp.int32),
                pltpu.SMEM((1, 1, slots), jnp.int32),
                pltpu.VMEM((slots, tile, tile), BF16),
                pltpu.VMEM((row_nodes, col_nodes), F32),
                pltpu.SemaphoreType.DMA((3,)),
                pltpu.SemaphoreType.DMA((chunks,)),
            ],
            0,
            12 * row_nodes * col_nodes,
        )(tile_count, *(
            pltpu.with_memory_space_constraint(array, pltpu.HBM)
            for array in (tile_row, tile_col, tile_values, bias_row)
        ))
    else:
        slot_args = (
            tile_count.reshape(1),
            tile_row.reshape(slots),
            tile_col.reshape(slots),
            tile_values.reshape(slots, tile, tile),
        )
        slot_specs = [SMEM_SPEC] * 3 + [VMEM_SPEC]

    sources = exchange([features] * n_row, "row", n_row, order=half_first)
    if is_dense:
        other, source = call(
            forward_other_kernel,
            (like(own_nodes, width), like(col_nodes, width)),
            [VMEM_SPEC] * (1 + n_row),
            [],
            slots * matrix // 2,
            row_nodes * width * 8,
        )(dense, *sources)
        own = call(
            forward_own_kernel,
            like(own_nodes, width),
            [VMEM_SPEC] * 2,
            [],
            slots * matrix // 2,
            row_nodes * width * 8,
        )(dense, source)
    else:
        other, own = call(
            slot_forward_kernel,
            (like(own_nodes, width), like(own_nodes, width)),
            slot_specs + [VMEM_SPEC] * n_row,
            [pltpu.VMEM((col_nodes, width), BF16), pltpu.VMEM((row_nodes, width), F32)],
            slots * matrix // 2,
            row_nodes * width * 8,
        )(*slot_args, *sources)
    swapped = swap_cores(other, n_col)

    def chip_piece(k, before):
        return call(
            functools.partial(chip_kernel, k=k, n_chip=n_chip),
            like(tile, width),
            [VMEM_SPEC] * (2 + len(before)),
            [],
            tile * width,
            3 * block_bytes,
        )(own, swapped, *before)

    pieces = in_turn(n_chip, chip_piece)
    parts = exchange(pieces, "col", n_col, 2)
    if is_dense:
        turned = call(
            turn_kernel,
            like(col_nodes, row_nodes),
            [VMEM_SPEC] * 2,
            [],
            0,
            4 * row_nodes * col_nodes,
        )(dense, pieces[0])
    hidden_own, grad, aggregated = call(
        middle_kernel,
        [like(tile, hidden), like(tile, hidden), like(tile, width)],
        [VMEM_SPEC] * (3 + n_chip),
        [],
        matrix,
        n_chip * block_bytes,
    )(weight, bias_row, cotangent, *parts)
    grads = exchange([grad] * n_chip, "col", n_col, 2)
    hidden_out = call(copy_kernel, like(tile, hidden), [VMEM_SPEC], [], 0, 2 * block_bytes)(hidden_own)
    mine, theirs = (
        call(
            functools.partial(term_kernel, own=own),
            like(half + BIAS_ROWS, hidden),
            [VMEM_SPEC] * 2,
            [],
            matrix // 2,
            4 * block_bytes,
        )(aggregated, grad)
        for own in (True, False)
    )
    chip_term = add([swap_cores(theirs, n_col), mine])
    add_late = functools.partial(add, flops=ROW_SUM_WEIGHT * matrix)
    row_terms = total_over(chip_term, add, "row", n_row)

    own_grads = call(
        gather_kernel,
        like(own_nodes, hidden),
        [VMEM_SPEC] * (1 + n_chip),
        [],
        0,
        own_nodes * hidden * 4,
    )(chip_term, *grads)
    other_grads = swap_cores(own_grads, n_col)
    if is_dense:
        back_own = call(
            back_own_kernel,
            like(col_nodes, hidden, F32),
            [VMEM_SPEC] * 2,
            [],
            slots * matrix // 2,
            row_nodes * hidden * 8,
        )(turned, own_grads)
        row_term = add_late(row_terms, after=[back_own])
        back_pieces = call(
            back_pieces_kernel,
            [like(tile, hidden)] * n_row,
            [VMEM_SPEC] * 3,
            [],
            slots * matrix // 2,
            row_nodes * hidden * 8,
        )(turned, back_own, other_grads)
    else:
        row_term = add_late(row_terms)
        back_pieces = call(
            slot_back_kernel,
            [like(tile, hidden)] * n_row,
            slot_specs + [VMEM_SPEC] * 2,
            [pltpu.VMEM((row_nodes, hidden), BF16), pltpu.VMEM((col_nodes, hidden), F32)],
            slots * matrix // 2,
            row_nodes * hidden * 8,
        )(*slot_args, own_grads, other_grads)
    by_partner = dict(zip(half_first(n_row), back_pieces))
    backs = exchange(by_partner, "row", n_row, order=half_first)
    most = call(
        back_sum_kernel,
        like(tile, hidden, F32),
        [VMEM_SPEC] * (n_row - 1),
        [],
        BACK_SUM_WEIGHT * matrix,
        n_row * block_bytes,
    )(*backs[:-2], backs[-1])
    own_features = call(
        features_kernel,
        like(tile, width),
        [VMEM_SPEC] * 3,
        [],
        FEATURES_WEIGHT * matrix,
        n_row * block_bytes,
    )(weight, most, backs[-2])
    all_terms = total_over(row_term, add, "col", n_col, 2)
    factor = (tile * n_row * n_col) ** (-0.5)
    own_half, bias_grad = call(
        functools.partial(scale_kernel, factor=factor),
        (like(half, hidden, F32), like(1, hidden, F32)),
        [VMEM_SPEC] * (1 + len(all_terms)),
        [],
        len(all_terms) * half * hidden,
        len(all_terms) * half * hidden * 2,
    )(most, *all_terms)
    grad_features, grad_weight, grad_bias = call(
        write_kernel,
        (like(tile, width), like(width, hidden, F32), like(1, hidden, F32)),
        [VMEM_SPEC] * 4,
        [pltpu.SemaphoreType.DMA((4,))],
        0,
        width * hidden * 8,
        HBM_SPEC,
    )(own_features, own_half, swap_cores(own_half, n_col), bias_grad)
    return hidden_out, grad_features, grad_weight, grad_bias.reshape(hidden)


def solution(mesh):
    return jax.shard_map(
        local,
        mesh=mesh,
        in_specs=(
            P(("col", "row"), None),
            P(),
            P(),
            P(("row", "col"), None),
            P("row", "col", None, None, None),
            P("row", "col", None),
            P("row", "col", None),
            P("row", "col"),
        ),
        out_specs=(P(("row", "col"), None), P(("col", "row"), None), P(), P()),
        check_vma=False,
    )
```

```python
import functools

import jax
import jax.numpy as jnp
from jax import lax
from jax.experimental import pallas as pl
from jax.experimental.pallas import tpu as pltpu
from jax.sharding import PartitionSpec as P

F32 = jnp.float32
BF16 = jnp.bfloat16
ROOT_2_OVER_PI = 0.7978845608028654
CUBIC = 0.044715
VMEM_LIMIT = 48 * 1024 * 1024
BIAS_ROWS = 16
BACK_SUM_WEIGHT = 30
ROW_SUM_WEIGHT = 120
FEATURES_WEIGHT = 100

VMEM_SPEC = pl.BlockSpec(memory_space=pltpu.VMEM)
HBM_SPEC = pl.BlockSpec(memory_space=pltpu.HBM)
SMEM_SPEC = pl.BlockSpec(memory_space=pltpu.SMEM)


def call(kernel, out_shape, in_specs, scratch, flops, moved, out_spec=VMEM_SPEC):
    return pl.pallas_call(
        kernel,
        out_shape=out_shape,
        in_specs=in_specs,
        out_specs=jax.tree.map(lambda _: out_spec, out_shape),
        scratch_shapes=scratch,
        compiler_params=pltpu.CompilerParams(vmem_limit_bytes=VMEM_LIMIT),
        cost_estimate=pl.CostEstimate(flops=flops, bytes_accessed=moved, transcendentals=0),
    )


def partner(index, k, count):
    if count & (count - 1) == 0:
        return index ^ k
    return (k - index) % count


def order(count):
    return [count // 2] + [k for k in range(count - 1, -1, -1) if k != count // 2]


def pairs_of(k, size, cores):
    return [(i, partner(i // cores, k, size // cores) * cores + i % cores) for i in range(size)]


def exchange(blocks, axis, size, cores=1):
    received = []
    for k in order(size // cores):
        pairs = pairs_of(k, size, cores)
        moves = any(i != j for i, j in pairs)
        received.append(lax.ppermute(blocks[k], axis, pairs) if moves else blocks[k])
    return received


def swap_cores(block, size):
    return lax.ppermute(block, "col", [(i, i ^ 1) for i in range(size)])


def total_over(block, add, axis, size, cores=1):
    count = size // cores
    if count & (count - 1):
        return exchange([block] * count, axis, size, cores)
    terms, step = [block], 1
    while step < count:
        block = add(terms) if len(terms) > 1 else block
        terms = [lax.ppermute(block, axis, pairs_of(step, size, cores)), block]
        step *= 2
    return terms


def block_at(index, size):
    return pl.ds(pl.multiple_of(index * size, size), size)


def row_index():
    return lax.axis_index("row")


def chip_index():
    return lax.axis_index("col") // 2


def core_index():
    return lax.axis_index("col") % 2


def summed(refs):
    by_partner = dict(zip(order(len(refs)), refs))
    values = [by_partner[k][...].astype(F32) for k in sorted(by_partner)]
    while len(values) > 1:
        values = [sum(values[i + 1 : i + 2], values[i]) for i in range(0, len(values), 2)]
    return values[0]


def bias_rows(bias):
    high = bias.astype(BF16).astype(F32)
    line = lax.broadcasted_iota(jnp.int32, (BIAS_ROWS, bias.shape[1]), 0)
    return jnp.where(line == 0, high, jnp.where(line == 1, bias - high, 0.0))


def row_place(row, n_chip):
    return jnp.where(row % 2 == core_index(), 0, n_chip) + row // 2


def dense_kernel(
    count_ref, row_hbm, col_hbm, tiles_hbm, bias_hbm, dense_ref, bias_ref,
    row_ref, col_ref, tiles_ref, sum_ref, sems, tile_sems,
):
    slots, tile = tiles_ref.shape[0], tiles_ref.shape[1]
    n_chip = sum_ref.shape[0] // (2 * tile)
    chunks = tile_sems.shape[0]
    size = slots // chunks
    small = [
        pltpu.make_async_copy(row_hbm, row_ref, sems.at[0]),
        pltpu.make_async_copy(col_hbm, col_ref, sems.at[1]),
        pltpu.make_async_copy(bias_hbm, bias_ref, sems.at[2]),
    ]
    large = []
    for k in range(chunks):
        part = pl.ds(k * size, size)
        large.append(
            pltpu.make_async_copy(tiles_hbm.at[0, 0, part], tiles_ref.at[part], tile_sems.at[k])
        )
    for copy in small + large:
        copy.start()
    sum_ref[...] = jnp.zeros_like(sum_ref)
    for copy in small:
        copy.wait()
    count = count_ref[0, 0]

    def body(slot, carry):
        rows = block_at(row_place(row_ref[0, 0, slot], n_chip), tile)
        cols = block_at(col_ref[0, 0, slot], tile)
        sum_ref[rows, cols] += tiles_ref[slot].astype(F32)
        return carry

    for k, copy in enumerate(large):
        copy.wait()
        lax.fori_loop(k * size, jnp.minimum(count, (k + 1) * size), body, 0)
    dense_ref[...] = sum_ref[...].astype(BF16)


def turn_kernel(dense_ref, after_ref, turned_ref):
    rows = dense_ref.shape[0]
    step = 256 if rows % 256 == 0 else rows
    for first in range(0, rows, step):
        turned_ref[:, first : first + step] = dense_ref[first : first + step, :].T


def dense_dot(left, right):
    return jnp.dot(left, right, preferred_element_type=F32)


def gather_sources(sources, source_ref, index):
    tile = sources[0].shape[0]
    for k, ref in zip(order(len(sources)), sources):
        source_ref[block_at(partner(index, k, len(sources)), tile), :] = ref[...]


def slot_product(refs, source_ref, acc_ref, turned):
    count_ref, row_ref, col_ref, tiles_ref = refs
    tile = tiles_ref.shape[1]
    n_chip = (source_ref if turned else acc_ref).shape[0] // (2 * tile)
    contract = 0 if turned else 1
    acc_ref[...] = jnp.zeros_like(acc_ref)

    def body(slot, carry):
        places = [row_place(row_ref[slot], n_chip), col_ref[slot]]
        source, target = places if turned else places[::-1]
        acc_ref[block_at(target, tile), :] += lax.dot_general(
            tiles_ref[slot],
            source_ref[block_at(source, tile), :],
            (((contract,), (0,)), ((), ())),
            preferred_element_type=F32,
        )
        return carry

    lax.fori_loop(0, count_ref[0], body, 0)


def forward_other_kernel(dense_ref, *refs):
    sources, (other_ref, source_ref) = refs[:-2], refs[-2:]
    gather_sources(sources, source_ref, row_index())
    half = other_ref.shape[0]
    other_ref[...] = dense_dot(dense_ref[half:, :], source_ref[...]).astype(BF16)


def forward_own_kernel(dense_ref, source_ref, own_ref):
    own_ref[...] = dense_dot(dense_ref[: own_ref.shape[0], :], source_ref[...]).astype(BF16)


def slot_forward_kernel(count_ref, row_ref, col_ref, tiles_ref, *refs):
    sources, (other_ref, own_ref, source_ref, acc_ref) = refs[:-4], refs[-4:]
    gather_sources(sources, source_ref, row_index())
    slot_product((count_ref, row_ref, col_ref, tiles_ref), source_ref, acc_ref, False)
    half = own_ref.shape[0]
    own_ref[...] = acc_ref[:half, :].astype(BF16)
    other_ref[...] = acc_ref[half:, :].astype(BF16)


def chip_kernel(own_ref, other_ref, *refs, k, n_chip):
    out_ref = refs[-1]
    rows = block_at(partner(chip_index(), k, n_chip), out_ref.shape[0])
    out_ref[...] = (own_ref[rows, :].astype(F32) + other_ref[rows, :].astype(F32)).astype(BF16)


def middle_kernel(weight_ref, bias_ref, cot_ref, *refs):
    parts, (hidden_ref, grad_ref, agg_ref) = refs[:-3], refs[-3:]
    aggregated = summed(parts).astype(BF16)
    agg_ref[...] = aggregated
    v = dense_dot(aggregated, weight_ref[...]) + bias_ref[...]
    square = v * v
    t = jnp.tanh(ROOT_2_OVER_PI * (v + CUBIC * (square * v)))
    half = 0.5 * (1.0 + t)
    hidden_ref[...] = (v * half).astype(BF16)
    slope = half + 0.5 * v * (1.0 - t * t) * (ROOT_2_OVER_PI * (1.0 + 3.0 * CUBIC * square))
    grad_ref[...] = (cot_ref[...].astype(F32) * slope).astype(BF16)


def copy_kernel(in_ref, out_ref):
    out_ref[...] = in_ref[...]


def term_kernel(agg_ref, grad_ref, out_ref, *, own):
    half = agg_ref.shape[1] // 2
    core = core_index() if own else 1 - core_index()
    grad = grad_ref[...]
    out_ref[:half, :] = lax.dot_general(
        agg_ref[:, block_at(core, half)],
        grad,
        (((0,), (0,)), ((), ())),
        preferred_element_type=F32,
    ).astype(BF16)
    out_ref[half:, :] = bias_rows(jnp.sum(grad.astype(F32), axis=0, keepdims=True)).astype(BF16)


def add_terms_kernel(*refs, n_terms):
    total = summed(refs[:n_terms])
    out_ref = refs[-1]
    half = total.shape[0] - BIAS_ROWS
    out_ref[:half, :] = total[:half].astype(BF16)
    out_ref[half:, :] = bias_rows(total[half : half + 1] + total[half + 1 : half + 2]).astype(BF16)


def scale_kernel(after_ref, *refs, factor):
    parts, (half_ref, bias_ref) = refs[:-2], refs[-2:]
    total = summed(parts) * factor
    half = half_ref.shape[0]
    half_ref[...] = total[:half]
    bias_ref[...] = total[half : half + 1] + total[half + 1 : half + 2]


def gather_kernel(after_ref, *refs):
    gather_sources(refs[:-1], refs[-1], chip_index())


def back_own_kernel(turned_ref, source_ref, out_ref):
    out_ref[...] = dense_dot(turned_ref[:, : source_ref.shape[0]], source_ref[...])


def back_pieces_kernel(turned_ref, own_ref, source_ref, *outs):
    tile = outs[0].shape[0]
    for k, out_ref in zip(order(len(outs)), outs):
        rows = block_at(partner(row_index(), k, len(outs)), tile)
        rest = dense_dot(turned_ref[rows, source_ref.shape[0] :], source_ref[...])
        out_ref[...] = (own_ref[rows, :] + rest).astype(BF16)


def slot_back_kernel(count_ref, row_ref, col_ref, tiles_ref, own_ref, other_ref, *refs):
    outs, (source_ref, acc_ref) = refs[:-2], refs[-2:]
    half = own_ref.shape[0]
    source_ref[:half, :] = own_ref[...]
    source_ref[half:, :] = other_ref[...]
    slot_product((count_ref, row_ref, col_ref, tiles_ref), source_ref, acc_ref, True)
    tile = outs[0].shape[0]
    for k, out_ref in zip(order(len(outs)), outs):
        rows = block_at(partner(row_index(), k, len(outs)), tile)
        out_ref[...] = acc_ref[rows, :].astype(BF16)


def back_sum_kernel(*refs):
    total = refs[0][...].astype(F32)
    for ref in refs[1:-1]:
        total += ref[...].astype(F32)
    refs[-1][...] = total


def features_kernel(weight_ref, most_ref, last_ref, out_ref):
    out_ref[...] = lax.dot_general(
        (most_ref[...] + last_ref[...].astype(F32)).astype(BF16),
        weight_ref[...],
        (((1,), (1,)), ((), ())),
        preferred_element_type=F32,
    ).astype(BF16)


def write_kernel(
    features_ref, own_ref, other_ref, bias_ref, features_hbm, grad_hbm, bias_hbm, sems
):
    half = own_ref.shape[0]
    copies = [
        pltpu.make_async_copy(own_ref, grad_hbm.at[block_at(core_index(), half)], sems.at[0]),
        pltpu.make_async_copy(other_ref, grad_hbm.at[block_at(1 - core_index(), half)], sems.at[1]),
        pltpu.make_async_copy(features_ref, features_hbm, sems.at[2]),
        pltpu.make_async_copy(bias_ref, bias_hbm, sems.at[3]),
    ]
    for copy in copies:
        copy.start()
    for copy in copies:
        copy.wait()


def in_turn(count, make):
    made, before = {}, []
    for k in order(count):
        made[k] = make(k, before)
        before = [made[k]]
    return made


def local(features, weight, bias_term, cotangent, tile_values, tile_row, tile_col, tile_count):
    n_row = lax.axis_size("row")
    n_col = lax.axis_size("col")
    n_chip = n_col // 2
    tile, width = features.shape
    hidden = weight.shape[1]
    slots = tile_values.shape[2]
    row_nodes, col_nodes = n_col * tile, n_row * tile
    bias_row = bias_term.reshape(1, hidden)
    half = width // 2
    matrix = 2 * tile * width * hidden
    block_bytes = 2 * tile * width

    def like(rows, columns, dtype=BF16):
        return jax.ShapeDtypeStruct((rows, columns), dtype)

    near = 1
    own_nodes = n_chip * tile

    def add(terms, flops=0, after=()):
        return call(
            functools.partial(add_terms_kernel, n_terms=len(terms)),
            like(half + BIAS_ROWS, hidden),
            [VMEM_SPEC] * (len(terms) + len(after)),
            [],
            flops or len(terms) * half * hidden,
            len(terms) * half * hidden * 2,
        )(*terms, *after)

    is_dense = n_row * n_col <= 2 * slots
    if is_dense:
        chunks = 4 if slots % 4 == 0 else 1
        dense, bias_row = call(
            dense_kernel,
            (like(row_nodes, col_nodes), like(1, hidden, F32)),
            [SMEM_SPEC] + [HBM_SPEC] * 4,
            [
                pltpu.SMEM((1, 1, slots), jnp.int32),
                pltpu.SMEM((1, 1, slots), jnp.int32),
                pltpu.VMEM((slots, tile, tile), BF16),
                pltpu.VMEM((row_nodes, col_nodes), F32),
                pltpu.SemaphoreType.DMA((3,)),
                pltpu.SemaphoreType.DMA((chunks,)),
            ],
            0,
            12 * row_nodes * col_nodes,
        )(tile_count, *(
            pltpu.with_memory_space_constraint(array, pltpu.HBM)
            for array in (tile_row, tile_col, tile_values, bias_row)
        ))
    else:
        slot_args = (
            tile_count.reshape(1),
            tile_row.reshape(slots),
            tile_col.reshape(slots),
            tile_values.reshape(slots, tile, tile),
        )
        slot_specs = [SMEM_SPEC] * 3 + [VMEM_SPEC]

    sources = exchange([features] * n_row, "row", n_row)
    if is_dense:
        other, source = call(
            forward_other_kernel,
            (like(own_nodes, width), like(col_nodes, width)),
            [VMEM_SPEC] * (1 + n_row),
            [],
            slots * matrix // 2,
            row_nodes * width * 8,
        )(dense, *sources)
        own = call(
            forward_own_kernel,
            like(own_nodes, width),
            [VMEM_SPEC] * 2,
            [],
            slots * matrix // 2,
            row_nodes * width * 8,
        )(dense, source)
    else:
        other, own = call(
            slot_forward_kernel,
            (like(own_nodes, width), like(own_nodes, width)),
            slot_specs + [VMEM_SPEC] * n_row,
            [pltpu.VMEM((col_nodes, width), BF16), pltpu.VMEM((row_nodes, width), F32)],
            slots * matrix // 2,
            row_nodes * width * 8,
        )(*slot_args, *sources)
    swapped = swap_cores(other, n_col)

    def chip_piece(k, before):
        return call(
            functools.partial(chip_kernel, k=k, n_chip=n_chip),
            like(tile, width),
            [VMEM_SPEC] * (2 + len(before)),
            [],
            tile * width,
            3 * block_bytes,
        )(own, swapped, *before)

    pieces = in_turn(n_chip, chip_piece)
    parts = exchange(pieces, "col", n_col, 2)
    if is_dense:
        turned = call(
            turn_kernel,
            like(col_nodes, row_nodes),
            [VMEM_SPEC] * 2,
            [],
            0,
            4 * row_nodes * col_nodes,
        )(dense, pieces[0])
    hidden_own, grad, aggregated = call(
        middle_kernel,
        [like(tile, hidden), like(tile, hidden), like(tile, width)],
        [VMEM_SPEC] * (3 + n_chip),
        [],
        matrix,
        n_chip * block_bytes,
    )(weight, bias_row, cotangent, *parts)
    grads = exchange([grad] * n_chip, "col", n_col, 2)
    hidden_out = call(copy_kernel, like(tile, hidden), [VMEM_SPEC], [], 0, 2 * block_bytes)(hidden_own)
    mine, theirs = (
        call(
            functools.partial(term_kernel, own=own),
            like(half + BIAS_ROWS, hidden),
            [VMEM_SPEC] * 2,
            [],
            matrix // 2,
            4 * block_bytes,
        )(aggregated, grad)
        for own in (True, False)
    )
    chip_term = add([swap_cores(theirs, n_col), mine])
    add_late = functools.partial(add, flops=ROW_SUM_WEIGHT * matrix)
    row_terms = total_over(chip_term, add, "row", n_row)

    own_grads = call(
        gather_kernel,
        like(own_nodes, hidden),
        [VMEM_SPEC] * (1 + n_chip),
        [],
        0,
        own_nodes * hidden * 4,
    )(chip_term, *grads)
    other_grads = swap_cores(own_grads, n_col)
    if is_dense:
        back_own = call(
            back_own_kernel,
            like(col_nodes, hidden, F32),
            [VMEM_SPEC] * 2,
            [],
            slots * matrix // 2,
            row_nodes * hidden * 8,
        )(turned, own_grads)
        row_term = add_late(row_terms, after=[back_own])
        back_pieces = call(
            back_pieces_kernel,
            [like(tile, hidden)] * n_row,
            [VMEM_SPEC] * 3,
            [],
            slots * matrix // 2,
            row_nodes * hidden * 8,
        )(turned, back_own, other_grads)
    else:
        row_term = add_late(row_terms)
        back_pieces = call(
            slot_back_kernel,
            [like(tile, hidden)] * n_row,
            slot_specs + [VMEM_SPEC] * 2,
            [pltpu.VMEM((row_nodes, hidden), BF16), pltpu.VMEM((col_nodes, hidden), F32)],
            slots * matrix // 2,
            row_nodes * hidden * 8,
        )(*slot_args, own_grads, other_grads)
    by_partner = dict(zip(order(n_row), back_pieces))
    backs = exchange(by_partner, "row", n_row)
    most = call(
        back_sum_kernel,
        like(tile, hidden, F32),
        [VMEM_SPEC] * (n_row - 1),
        [],
        BACK_SUM_WEIGHT * matrix,
        n_row * block_bytes,
    )(*backs[:-2], backs[-1])
    own_features = call(
        features_kernel,
        like(tile, width),
        [VMEM_SPEC] * 3,
        [],
        FEATURES_WEIGHT * matrix,
        n_row * block_bytes,
    )(weight, most, backs[-2])
    all_terms = total_over(row_term, add, "col", n_col, 2)
    factor = (tile * n_row * n_col) ** (-0.5)
    own_half, bias_grad = call(
        functools.partial(scale_kernel, factor=factor),
        (like(half, hidden, F32), like(1, hidden, F32)),
        [VMEM_SPEC] * (1 + len(all_terms)),
        [],
        len(all_terms) * half * hidden,
        len(all_terms) * half * hidden * 2,
    )(most, *all_terms)
    grad_features, grad_weight, grad_bias = call(
        write_kernel,
        (like(tile, width), like(width, hidden, F32), like(1, hidden, F32)),
        [VMEM_SPEC] * 4,
        [pltpu.SemaphoreType.DMA((4,))],
        0,
        width * hidden * 8,
        HBM_SPEC,
    )(own_features, own_half, swap_cores(own_half, n_col), bias_grad)
    return hidden_out, grad_features, grad_weight, grad_bias.reshape(hidden)


def solution(mesh):
    return jax.shard_map(
        local,
        mesh=mesh,
        in_specs=(
            P(("col", "row"), None),
            P(),
            P(),
            P(("row", "col"), None),
            P("row", "col", None, None, None),
            P("row", "col", None),
            P("row", "col", None),
            P("row", "col"),
        ),
        out_specs=(P(("row", "col"), None), P(("col", "row"), None), P(), P()),
        check_vma=False,
    )
```

```python
import functools

import jax
import jax.numpy as jnp
from jax import lax
from jax.experimental import pallas as pl
from jax.experimental.pallas import tpu as pltpu
from jax.sharding import PartitionSpec as P

F32 = jnp.float32
BF16 = jnp.bfloat16
ROOT_2_OVER_PI = 0.7978845608028654
CUBIC = 0.044715
VMEM_LIMIT = 48 * 1024 * 1024
BIAS_ROWS = 16
BACK_SUM_WEIGHT = 30
EARLY_WEIGHT = 40
ROW_SUM_WEIGHT = 140
FEATURES_WEIGHT = 100

VMEM_SPEC = pl.BlockSpec(memory_space=pltpu.VMEM)
HBM_SPEC = pl.BlockSpec(memory_space=pltpu.HBM)
SMEM_SPEC = pl.BlockSpec(memory_space=pltpu.SMEM)


def call(kernel, out_shape, in_specs, scratch, flops, moved, out_spec=VMEM_SPEC):
    return pl.pallas_call(
        kernel,
        out_shape=out_shape,
        in_specs=in_specs,
        out_specs=jax.tree.map(lambda _: out_spec, out_shape),
        scratch_shapes=scratch,
        compiler_params=pltpu.CompilerParams(vmem_limit_bytes=VMEM_LIMIT),
        cost_estimate=pl.CostEstimate(flops=flops, bytes_accessed=moved, transcendentals=0),
    )


def partner(index, k, count):
    if count & (count - 1) == 0:
        return index ^ k
    return (k - index) % count


def far_first(count):
    return list(range(count - 1, -1, -1))


def pairs_of(k, size, cores):
    return [(i, partner(i // cores, k, size // cores) * cores + i % cores) for i in range(size)]


def half_first(count):
    return [count // 2] + [k for k in far_first(count) if k != count // 2]


def exchange(blocks, axis, size, cores=1, order=far_first):
    received = []
    for k in order(size // cores):
        pairs = pairs_of(k, size, cores)
        moves = any(i != j for i, j in pairs)
        received.append(lax.ppermute(blocks[k], axis, pairs) if moves else blocks[k])
    return received


def swap_cores(block, size):
    return lax.ppermute(block, "col", [(i, i ^ 1) for i in range(size)])


def total_over(block, add, axis, size, cores=1):
    count = size // cores
    if count & (count - 1):
        return exchange([block] * count, axis, size, cores)
    terms, step = [block], 1
    while step < count:
        block = add(terms) if len(terms) > 1 else block
        terms = [lax.ppermute(block, axis, pairs_of(step, size, cores)), block]
        step *= 2
    return terms


def block_at(index, size):
    return pl.ds(pl.multiple_of(index * size, size), size)


def row_index():
    return lax.axis_index("row")


def chip_index():
    return lax.axis_index("col") // 2


def core_index():
    return lax.axis_index("col") % 2


def summed(refs):
    by_partner = dict(zip(far_first(len(refs)), refs))
    values = [by_partner[k][...].astype(F32) for k in sorted(by_partner)]
    while len(values) > 1:
        values = [sum(values[i + 1 : i + 2], values[i]) for i in range(0, len(values), 2)]
    return values[0]


def bias_rows(bias):
    high = bias.astype(BF16).astype(F32)
    line = lax.broadcasted_iota(jnp.int32, (BIAS_ROWS, bias.shape[1]), 0)
    return jnp.where(line == 0, high, jnp.where(line == 1, bias - high, 0.0))


def row_place(row, n_chip):
    return jnp.where(row % 2 == core_index(), 0, n_chip) + row // 2


def dense_kernel(
    count_ref, row_hbm, col_hbm, tiles_hbm, bias_hbm, dense_ref, bias_ref,
    row_ref, col_ref, tiles_ref, sum_ref, sems, tile_sems,
):
    slots, tile = tiles_ref.shape[0], tiles_ref.shape[1]
    n_chip = sum_ref.shape[0] // (2 * tile)
    chunks = tile_sems.shape[0]
    size = slots // chunks
    small = [
        pltpu.make_async_copy(row_hbm, row_ref, sems.at[0]),
        pltpu.make_async_copy(col_hbm, col_ref, sems.at[1]),
        pltpu.make_async_copy(bias_hbm, bias_ref, sems.at[2]),
    ]
    large = []
    for k in range(chunks):
        part = pl.ds(k * size, size)
        large.append(
            pltpu.make_async_copy(tiles_hbm.at[0, 0, part], tiles_ref.at[part], tile_sems.at[k])
        )
    for copy in small + large:
        copy.start()
    sum_ref[...] = jnp.zeros_like(sum_ref)
    for copy in small:
        copy.wait()
    count = count_ref[0, 0]

    def body(slot, carry):
        rows = block_at(row_place(row_ref[0, 0, slot], n_chip), tile)
        cols = block_at(col_ref[0, 0, slot], tile)
        sum_ref[rows, cols] += tiles_ref[slot].astype(F32)
        return carry

    for k, copy in enumerate(large):
        copy.wait()
        lax.fori_loop(k * size, jnp.minimum(count, (k + 1) * size), body, 0)
    dense_ref[...] = sum_ref[...].astype(BF16)


def turn_kernel(dense_ref, after_ref, turned_ref):
    rows = dense_ref.shape[0]
    step = 256 if rows % 256 == 0 else rows
    for first in range(0, rows, step):
        turned_ref[:, first : first + step] = dense_ref[first : first + step, :].T


def dense_dot(left, right):
    return jnp.dot(left, right, preferred_element_type=F32)


def gather_sources(sources, source_ref, index, order):
    tile = sources[0].shape[0]
    for k, ref in zip(order(len(sources)), sources):
        source_ref[block_at(partner(index, k, len(sources)), tile), :] = ref[...]


def slot_product(refs, source_ref, acc_ref, turned):
    count_ref, row_ref, col_ref, tiles_ref = refs
    tile = tiles_ref.shape[1]
    n_chip = (source_ref if turned else acc_ref).shape[0] // (2 * tile)
    contract = 0 if turned else 1
    acc_ref[...] = jnp.zeros_like(acc_ref)

    def body(slot, carry):
        places = [row_place(row_ref[slot], n_chip), col_ref[slot]]
        source, target = places if turned else places[::-1]
        acc_ref[block_at(target, tile), :] += lax.dot_general(
            tiles_ref[slot],
            source_ref[block_at(source, tile), :],
            (((contract,), (0,)), ((), ())),
            preferred_element_type=F32,
        )
        return carry

    lax.fori_loop(0, count_ref[0], body, 0)


def forward_other_kernel(dense_ref, *refs):
    sources, (other_ref, source_ref) = refs[:-2], refs[-2:]
    gather_sources(sources, source_ref, row_index(), half_first)
    half = other_ref.shape[0]
    other_ref[...] = dense_dot(dense_ref[half:, :], source_ref[...]).astype(BF16)


def forward_own_kernel(dense_ref, source_ref, own_ref):
    own_ref[...] = dense_dot(dense_ref[: own_ref.shape[0], :], source_ref[...]).astype(BF16)


def slot_forward_kernel(count_ref, row_ref, col_ref, tiles_ref, *refs):
    sources, (other_ref, own_ref, source_ref, acc_ref) = refs[:-4], refs[-4:]
    gather_sources(sources, source_ref, row_index(), half_first)
    slot_product((count_ref, row_ref, col_ref, tiles_ref), source_ref, acc_ref, False)
    half = own_ref.shape[0]
    own_ref[...] = acc_ref[:half, :].astype(BF16)
    other_ref[...] = acc_ref[half:, :].astype(BF16)


def chip_kernel(own_ref, other_ref, *refs, k, n_chip):
    out_ref = refs[-1]
    rows = block_at(partner(chip_index(), k, n_chip), out_ref.shape[0])
    out_ref[...] = (own_ref[rows, :].astype(F32) + other_ref[rows, :].astype(F32)).astype(BF16)


def middle_kernel(weight_ref, bias_ref, cot_ref, *refs):
    parts, (hidden_ref, grad_ref, agg_ref) = refs[:-3], refs[-3:]
    aggregated = summed(parts).astype(BF16)
    agg_ref[...] = aggregated
    v = dense_dot(aggregated, weight_ref[...]) + bias_ref[...]
    square = v * v
    t = jnp.tanh(ROOT_2_OVER_PI * (v + CUBIC * (square * v)))
    half = 0.5 * (1.0 + t)
    hidden_ref[...] = (v * half).astype(BF16)
    slope = half + 0.5 * v * (1.0 - t * t) * (ROOT_2_OVER_PI * (1.0 + 3.0 * CUBIC * square))
    grad_ref[...] = (cot_ref[...].astype(F32) * slope).astype(BF16)


def copy_kernel(in_ref, out_ref):
    out_ref[...] = in_ref[...]


def term_kernel(agg_ref, grad_ref, out_ref, *, own):
    half = agg_ref.shape[1] // 2
    core = core_index() if own else 1 - core_index()
    grad = grad_ref[...]
    out_ref[:half, :] = lax.dot_general(
        agg_ref[:, block_at(core, half)],
        grad,
        (((0,), (0,)), ((), ())),
        preferred_element_type=F32,
    ).astype(BF16)
    out_ref[half:, :] = bias_rows(jnp.sum(grad.astype(F32), axis=0, keepdims=True)).astype(BF16)


def add_terms_kernel(*refs, n_terms):
    total = summed(refs[:n_terms])
    out_ref = refs[-1]
    half = total.shape[0] - BIAS_ROWS
    out_ref[:half, :] = total[:half].astype(BF16)
    out_ref[half:, :] = bias_rows(total[half : half + 1] + total[half + 1 : half + 2]).astype(BF16)


def scale_kernel(after_ref, *refs, factor):
    parts, (half_ref, bias_ref) = refs[:-2], refs[-2:]
    total = summed(parts) * factor
    half = half_ref.shape[0]
    half_ref[...] = total[:half]
    bias_ref[...] = total[half : half + 1] + total[half + 1 : half + 2]


def gather_kernel(after_ref, *refs):
    gather_sources(refs[:-1], refs[-1], chip_index(), far_first)


def back_own_kernel(turned_ref, source_ref, out_ref):
    out_ref[...] = dense_dot(turned_ref[:, : source_ref.shape[0]], source_ref[...])


def back_pieces_kernel(turned_ref, own_ref, source_ref, *outs):
    tile = outs[0].shape[0]
    for k, out_ref in zip(half_first(len(outs)), outs):
        rows = block_at(partner(row_index(), k, len(outs)), tile)
        rest = dense_dot(turned_ref[rows, source_ref.shape[0] :], source_ref[...])
        out_ref[...] = (own_ref[rows, :] + rest).astype(BF16)


def slot_back_kernel(count_ref, row_ref, col_ref, tiles_ref, own_ref, other_ref, *refs):
    outs, (source_ref, acc_ref) = refs[:-2], refs[-2:]
    half = own_ref.shape[0]
    source_ref[:half, :] = own_ref[...]
    source_ref[half:, :] = other_ref[...]
    slot_product((count_ref, row_ref, col_ref, tiles_ref), source_ref, acc_ref, True)
    tile = outs[0].shape[0]
    for k, out_ref in zip(half_first(len(outs)), outs):
        rows = block_at(partner(row_index(), k, len(outs)), tile)
        out_ref[...] = acc_ref[rows, :].astype(BF16)


def back_sum_kernel(*refs):
    total = refs[0][...].astype(F32)
    for ref in refs[1:-1]:
        total += ref[...].astype(F32)
    refs[-1][...] = total


def features_kernel(weight_ref, most_ref, last_ref, out_ref):
    out_ref[...] = lax.dot_general(
        (most_ref[...] + last_ref[...].astype(F32)).astype(BF16),
        weight_ref[...],
        (((1,), (1,)), ((), ())),
        preferred_element_type=F32,
    ).astype(BF16)


def write_kernel(
    features_ref, own_ref, other_ref, bias_ref, features_hbm, grad_hbm, bias_hbm, sems
):
    half = own_ref.shape[0]
    copies = [
        pltpu.make_async_copy(own_ref, grad_hbm.at[block_at(core_index(), half)], sems.at[0]),
        pltpu.make_async_copy(other_ref, grad_hbm.at[block_at(1 - core_index(), half)], sems.at[1]),
        pltpu.make_async_copy(features_ref, features_hbm, sems.at[2]),
        pltpu.make_async_copy(bias_ref, bias_hbm, sems.at[3]),
    ]
    for copy in copies:
        copy.start()
    for copy in copies:
        copy.wait()


def in_turn(count, make):
    made, before = {}, []
    for k in far_first(count):
        made[k] = make(k, before)
        before = [made[k]]
    return made


def local(features, weight, bias_term, cotangent, tile_values, tile_row, tile_col, tile_count):
    n_row = lax.axis_size("row")
    n_col = lax.axis_size("col")
    n_chip = n_col // 2
    tile, width = features.shape
    hidden = weight.shape[1]
    slots = tile_values.shape[2]
    row_nodes, col_nodes = n_col * tile, n_row * tile
    bias_row = bias_term.reshape(1, hidden)
    half = width // 2
    matrix = 2 * tile * width * hidden
    block_bytes = 2 * tile * width

    def like(rows, columns, dtype=BF16):
        return jax.ShapeDtypeStruct((rows, columns), dtype)

    near = 1
    own_nodes = n_chip * tile

    def add(terms, flops=0, after=()):
        return call(
            functools.partial(add_terms_kernel, n_terms=len(terms)),
            like(half + BIAS_ROWS, hidden),
            [VMEM_SPEC] * (len(terms) + len(after)),
            [],
            flops or len(terms) * half * hidden,
            len(terms) * half * hidden * 2,
        )(*terms, *after)

    is_dense = n_row * n_col <= 2 * slots
    if is_dense:
        chunks = 4 if slots % 4 == 0 else 1
        dense, bias_row = call(
            dense_kernel,
            (like(row_nodes, col_nodes), like(1, hidden, F32)),
            [SMEM_SPEC] + [HBM_SPEC] * 4,
            [
                pltpu.SMEM((1, 1, slots), jnp.int32),
                pltpu.SMEM((1, 1, slots), jnp.int32),
                pltpu.VMEM((slots, tile, tile), BF16),
                pltpu.VMEM((row_nodes, col_nodes), F32),
                pltpu.SemaphoreType.DMA((3,)),
                pltpu.SemaphoreType.DMA((chunks,)),
            ],
            0,
            12 * row_nodes * col_nodes,
        )(tile_count, *(
            pltpu.with_memory_space_constraint(array, pltpu.HBM)
            for array in (tile_row, tile_col, tile_values, bias_row)
        ))
    else:
        slot_args = (
            tile_count.reshape(1),
            tile_row.reshape(slots),
            tile_col.reshape(slots),
            tile_values.reshape(slots, tile, tile),
        )
        slot_specs = [SMEM_SPEC] * 3 + [VMEM_SPEC]

    sources = exchange([features] * n_row, "row", n_row, order=half_first)
    if is_dense:
        other, source = call(
            forward_other_kernel,
            (like(own_nodes, width), like(col_nodes, width)),
            [VMEM_SPEC] * (1 + n_row),
            [],
            slots * matrix // 2,
            row_nodes * width * 8,
        )(dense, *sources)
        own = call(
            forward_own_kernel,
            like(own_nodes, width),
            [VMEM_SPEC] * 2,
            [],
            slots * matrix // 2,
            row_nodes * width * 8,
        )(dense, source)
    else:
        other, own = call(
            slot_forward_kernel,
            (like(own_nodes, width), like(own_nodes, width)),
            slot_specs + [VMEM_SPEC] * n_row,
            [pltpu.VMEM((col_nodes, width), BF16), pltpu.VMEM((row_nodes, width), F32)],
            slots * matrix // 2,
            row_nodes * width * 8,
        )(*slot_args, *sources)
    swapped = swap_cores(other, n_col)

    def chip_piece(k, before):
        return call(
            functools.partial(chip_kernel, k=k, n_chip=n_chip),
            like(tile, width),
            [VMEM_SPEC] * (2 + len(before)),
            [],
            tile * width,
            3 * block_bytes,
        )(own, swapped, *before)

    pieces = in_turn(n_chip, chip_piece)
    parts = exchange(pieces, "col", n_col, 2)
    if is_dense:
        turned = call(
            turn_kernel,
            like(col_nodes, row_nodes),
            [VMEM_SPEC] * 2,
            [],
            0,
            4 * row_nodes * col_nodes,
        )(dense, pieces[0])
    hidden_own, grad, aggregated = call(
        middle_kernel,
        [like(tile, hidden), like(tile, hidden), like(tile, width)],
        [VMEM_SPEC] * (3 + n_chip),
        [],
        matrix,
        n_chip * block_bytes,
    )(weight, bias_row, cotangent, *parts)
    grads = exchange([grad] * n_chip, "col", n_col, 2)
    hidden_out = call(copy_kernel, like(tile, hidden), [VMEM_SPEC], [], 0, 2 * block_bytes)(hidden_own)
    mine, theirs = (
        call(
            functools.partial(term_kernel, own=own),
            like(half + BIAS_ROWS, hidden),
            [VMEM_SPEC] * 2,
            [],
            matrix // 2,
            4 * block_bytes,
        )(aggregated, grad)
        for own in (True, False)
    )
    chip_term = add([swap_cores(theirs, n_col), mine])
    add_late = functools.partial(add, flops=ROW_SUM_WEIGHT * matrix)
    row_terms = total_over(chip_term, add, "row", n_row)

    early = [
        call(copy_kernel, like(tile, hidden), [VMEM_SPEC], [], EARLY_WEIGHT * matrix, 2 * block_bytes)(
            received
        )
        for received in grads[:-2]
    ]
    own_grads = call(
        gather_kernel,
        like(own_nodes, hidden),
        [VMEM_SPEC] * (1 + n_chip),
        [],
        0,
        own_nodes * hidden * 4,
    )(chip_term, *early, *grads[-2:])
    other_grads = swap_cores(own_grads, n_col)
    if is_dense:
        back_own = call(
            back_own_kernel,
            like(col_nodes, hidden, F32),
            [VMEM_SPEC] * 2,
            [],
            slots * matrix // 2,
            row_nodes * hidden * 8,
        )(turned, own_grads)
        row_term = add_late(row_terms, after=[back_own])
        back_pieces = call(
            back_pieces_kernel,
            [like(tile, hidden)] * n_row,
            [VMEM_SPEC] * 3,
            [],
            slots * matrix // 2,
            row_nodes * hidden * 8,
        )(turned, back_own, other_grads)
    else:
        row_term = add_late(row_terms)
        back_pieces = call(
            slot_back_kernel,
            [like(tile, hidden)] * n_row,
            slot_specs + [VMEM_SPEC] * 2,
            [pltpu.VMEM((row_nodes, hidden), BF16), pltpu.VMEM((col_nodes, hidden), F32)],
            slots * matrix // 2,
            row_nodes * hidden * 8,
        )(*slot_args, own_grads, other_grads)
    by_partner = dict(zip(half_first(n_row), back_pieces))
    backs = exchange(by_partner, "row", n_row, order=half_first)
    most = call(
        back_sum_kernel,
        like(tile, hidden, F32),
        [VMEM_SPEC] * (n_row - 1),
        [],
        BACK_SUM_WEIGHT * matrix,
        n_row * block_bytes,
    )(*backs[:-2], backs[-1])
    own_features = call(
        features_kernel,
        like(tile, width),
        [VMEM_SPEC] * 3,
        [],
        FEATURES_WEIGHT * matrix,
        n_row * block_bytes,
    )(weight, most, backs[-2])
    all_terms = total_over(row_term, add, "col", n_col, 2)
    factor = (tile * n_row * n_col) ** (-0.5)
    own_half, bias_grad = call(
        functools.partial(scale_kernel, factor=factor),
        (like(half, hidden, F32), like(1, hidden, F32)),
        [VMEM_SPEC] * (1 + len(all_terms)),
        [],
        len(all_terms) * half * hidden,
        len(all_terms) * half * hidden * 2,
    )(most, *all_terms)
    grad_features, grad_weight, grad_bias = call(
        write_kernel,
        (like(tile, width), like(width, hidden, F32), like(1, hidden, F32)),
        [VMEM_SPEC] * 4,
        [pltpu.SemaphoreType.DMA((4,))],
        0,
        width * hidden * 8,
        HBM_SPEC,
    )(own_features, own_half, swap_cores(own_half, n_col), bias_grad)
    return hidden_out, grad_features, grad_weight, grad_bias.reshape(hidden)


def solution(mesh):
    return jax.shard_map(
        local,
        mesh=mesh,
        in_specs=(
            P(("col", "row"), None),
            P(),
            P(),
            P(("row", "col"), None),
            P("row", "col", None, None, None),
            P("row", "col", None),
            P("row", "col", None),
            P("row", "col"),
        ),
        out_specs=(P(("row", "col"), None), P(("col", "row"), None), P(), P()),
        check_vma=False,
    )
```

```python
import functools

import jax
import jax.numpy as jnp
from jax import lax
from jax.experimental import pallas as pl
from jax.experimental.pallas import tpu as pltpu
from jax.sharding import PartitionSpec as P

F32 = jnp.float32
BF16 = jnp.bfloat16
ROOT_2_OVER_PI = 0.7978845608028654
CUBIC = 0.044715
VMEM_LIMIT = 48 * 1024 * 1024
BIAS_ROWS = 16
BACK_SUM_WEIGHT = 30
ROW_SUM_WEIGHT = 120
FEATURES_WEIGHT = 100

VMEM_SPEC = pl.BlockSpec(memory_space=pltpu.VMEM)
HBM_SPEC = pl.BlockSpec(memory_space=pltpu.HBM)
SMEM_SPEC = pl.BlockSpec(memory_space=pltpu.SMEM)


def call(kernel, out_shape, in_specs, scratch, flops, moved, out_spec=VMEM_SPEC):
    return pl.pallas_call(
        kernel,
        out_shape=out_shape,
        in_specs=in_specs,
        out_specs=jax.tree.map(lambda _: out_spec, out_shape),
        scratch_shapes=scratch,
        compiler_params=pltpu.CompilerParams(vmem_limit_bytes=VMEM_LIMIT),
        cost_estimate=pl.CostEstimate(flops=flops, bytes_accessed=moved, transcendentals=0),
    )


def partner(index, k, count):
    if count & (count - 1) == 0:
        return index ^ k
    return (k - index) % count


def far_first(count):
    return list(range(count - 1, -1, -1))


def pairs_of(k, size, cores):
    return [(i, partner(i // cores, k, size // cores) * cores + i % cores) for i in range(size)]


def half_first(count):
    return [count // 2] + [k for k in far_first(count) if k != count // 2]


def exchange(blocks, axis, size, cores=1, order=far_first):
    received = []
    for k in order(size // cores):
        pairs = pairs_of(k, size, cores)
        moves = any(i != j for i, j in pairs)
        received.append(lax.ppermute(blocks[k], axis, pairs) if moves else blocks[k])
    return received


def swap_cores(block, size):
    return lax.ppermute(block, "col", [(i, i ^ 1) for i in range(size)])


def total_over(block, add, axis, size, cores=1):
    count = size // cores
    if count & (count - 1):
        return exchange([block] * count, axis, size, cores)
    terms, step = [block], 1
    while step < count:
        block = add(terms) if len(terms) > 1 else block
        terms = [lax.ppermute(block, axis, pairs_of(step, size, cores)), block]
        step *= 2
    return terms


def block_at(index, size):
    return pl.ds(pl.multiple_of(index * size, size), size)


def row_index():
    return lax.axis_index("row")


def chip_index():
    return lax.axis_index("col") // 2


def core_index():
    return lax.axis_index("col") % 2


def summed(refs):
    by_partner = dict(zip(far_first(len(refs)), refs))
    values = [by_partner[k][...].astype(F32) for k in sorted(by_partner)]
    while len(values) > 1:
        values = [sum(values[i + 1 : i + 2], values[i]) for i in range(0, len(values), 2)]
    return values[0]


def bias_rows(bias):
    high = bias.astype(BF16).astype(F32)
    line = lax.broadcasted_iota(jnp.int32, (BIAS_ROWS, bias.shape[1]), 0)
    return jnp.where(line == 0, high, jnp.where(line == 1, bias - high, 0.0))


def row_place(row, n_chip):
    return jnp.where(row % 2 == core_index(), 0, n_chip) + row // 2


def dense_kernel(
    count_ref, row_hbm, col_hbm, tiles_hbm, bias_hbm, dense_ref, bias_ref,
    row_ref, col_ref, tiles_ref, sum_ref, sems, tile_sems,
):
    slots, tile = tiles_ref.shape[0], tiles_ref.shape[1]
    n_chip = sum_ref.shape[0] // (2 * tile)
    chunks = tile_sems.shape[0]
    size = slots // chunks
    small = [
        pltpu.make_async_copy(row_hbm, row_ref, sems.at[0]),
        pltpu.make_async_copy(col_hbm, col_ref, sems.at[1]),
        pltpu.make_async_copy(bias_hbm, bias_ref, sems.at[2]),
    ]
    large = []
    for k in range(chunks):
        part = pl.ds(k * size, size)
        large.append(
            pltpu.make_async_copy(tiles_hbm.at[0, 0, part], tiles_ref.at[part], tile_sems.at[k])
        )
    for copy in small + large:
        copy.start()
    sum_ref[...] = jnp.zeros_like(sum_ref)
    for copy in small:
        copy.wait()
    count = count_ref[0, 0]

    def body(slot, carry):
        rows = block_at(row_place(row_ref[0, 0, slot], n_chip), tile)
        cols = block_at(col_ref[0, 0, slot], tile)
        sum_ref[rows, cols] += tiles_ref[slot].astype(F32)
        return carry

    for k, copy in enumerate(large):
        copy.wait()
        lax.fori_loop(k * size, jnp.minimum(count, (k + 1) * size), body, 0)
    dense_ref[...] = sum_ref[...].astype(BF16)


def turn_kernel(dense_ref, after_ref, turned_ref):
    rows = dense_ref.shape[0]
    step = 256 if rows % 256 == 0 else rows
    for first in range(0, rows, step):
        turned_ref[:, first : first + step] = dense_ref[first : first + step, :].T


def dense_dot(left, right):
    return jnp.dot(left, right, preferred_element_type=F32)


def gather_sources(sources, source_ref, index, order):
    tile = sources[0].shape[0]
    for k, ref in zip(order(len(sources)), sources):
        source_ref[block_at(partner(index, k, len(sources)), tile), :] = ref[...]


def slot_product(refs, source_ref, acc_ref, turned):
    count_ref, row_ref, col_ref, tiles_ref = refs
    tile = tiles_ref.shape[1]
    n_chip = (source_ref if turned else acc_ref).shape[0] // (2 * tile)
    contract = 0 if turned else 1
    acc_ref[...] = jnp.zeros_like(acc_ref)

    def body(slot, carry):
        places = [row_place(row_ref[slot], n_chip), col_ref[slot]]
        source, target = places if turned else places[::-1]
        acc_ref[block_at(target, tile), :] += lax.dot_general(
            tiles_ref[slot],
            source_ref[block_at(source, tile), :],
            (((contract,), (0,)), ((), ())),
            preferred_element_type=F32,
        )
        return carry

    lax.fori_loop(0, count_ref[0], body, 0)


def forward_other_kernel(dense_ref, *refs):
    sources, (other_ref, source_ref) = refs[:-2], refs[-2:]
    gather_sources(sources, source_ref, row_index(), half_first)
    half = other_ref.shape[0]
    other_ref[...] = dense_dot(dense_ref[half:, :], source_ref[...]).astype(BF16)


def forward_own_kernel(dense_ref, source_ref, own_ref):
    own_ref[...] = dense_dot(dense_ref[: own_ref.shape[0], :], source_ref[...]).astype(BF16)


def slot_forward_kernel(count_ref, row_ref, col_ref, tiles_ref, *refs):
    sources, (other_ref, own_ref, source_ref, acc_ref) = refs[:-4], refs[-4:]
    gather_sources(sources, source_ref, row_index(), half_first)
    slot_product((count_ref, row_ref, col_ref, tiles_ref), source_ref, acc_ref, False)
    half = own_ref.shape[0]
    own_ref[...] = acc_ref[:half, :].astype(BF16)
    other_ref[...] = acc_ref[half:, :].astype(BF16)


def chip_kernel(own_ref, other_ref, *refs, k, n_chip):
    out_ref = refs[-1]
    rows = block_at(partner(chip_index(), k, n_chip), out_ref.shape[0])
    out_ref[...] = (own_ref[rows, :].astype(F32) + other_ref[rows, :].astype(F32)).astype(BF16)


def middle_kernel(weight_ref, bias_ref, cot_ref, *refs):
    parts, (hidden_ref, grad_ref, agg_ref) = refs[:-3], refs[-3:]
    aggregated = summed(parts).astype(BF16)
    agg_ref[...] = aggregated
    v = dense_dot(aggregated, weight_ref[...]) + bias_ref[...]
    square = v * v
    t = jnp.tanh(ROOT_2_OVER_PI * (v + CUBIC * (square * v)))
    half = 0.5 * (1.0 + t)
    hidden_ref[...] = (v * half).astype(BF16)
    slope = half + 0.5 * v * (1.0 - t * t) * (ROOT_2_OVER_PI * (1.0 + 3.0 * CUBIC * square))
    grad_ref[...] = (cot_ref[...].astype(F32) * slope).astype(BF16)


def copy_kernel(in_ref, out_ref):
    out_ref[...] = in_ref[...]


def term_kernel(agg_ref, grad_ref, out_ref, *, own):
    half = agg_ref.shape[1] // 2
    core = core_index() if own else 1 - core_index()
    grad = grad_ref[...]
    out_ref[:half, :] = lax.dot_general(
        agg_ref[:, block_at(core, half)],
        grad,
        (((0,), (0,)), ((), ())),
        preferred_element_type=F32,
    ).astype(BF16)
    out_ref[half:, :] = bias_rows(jnp.sum(grad.astype(F32), axis=0, keepdims=True)).astype(BF16)


def add_terms_kernel(*refs, n_terms):
    total = summed(refs[:n_terms])
    out_ref = refs[-1]
    half = total.shape[0] - BIAS_ROWS
    out_ref[:half, :] = total[:half].astype(BF16)
    out_ref[half:, :] = bias_rows(total[half : half + 1] + total[half + 1 : half + 2]).astype(BF16)


def scale_kernel(after_ref, *refs, factor):
    parts, (half_ref, bias_ref) = refs[:-2], refs[-2:]
    total = summed(parts) * factor
    half = half_ref.shape[0]
    half_ref[...] = total[:half]
    bias_ref[...] = total[half : half + 1] + total[half + 1 : half + 2]


def gather_kernel(after_ref, *refs):
    gather_sources(refs[:-1], refs[-1], chip_index(), far_first)


def back_own_kernel(turned_ref, source_ref, out_ref):
    out_ref[...] = dense_dot(turned_ref[:, : source_ref.shape[0]], source_ref[...])


def back_pieces_kernel(turned_ref, own_ref, source_ref, *outs, partners, n_row):
    tile = outs[0].shape[0]
    for k, out_ref in zip(partners, outs):
        rows = block_at(partner(row_index(), k, n_row), tile)
        rest = dense_dot(turned_ref[rows, source_ref.shape[0] :], source_ref[...])
        out_ref[...] = (own_ref[rows, :] + rest).astype(BF16)


def slot_back_kernel(count_ref, row_ref, col_ref, tiles_ref, own_ref, other_ref, *refs):
    outs, (source_ref, acc_ref) = refs[:-2], refs[-2:]
    half = own_ref.shape[0]
    source_ref[:half, :] = own_ref[...]
    source_ref[half:, :] = other_ref[...]
    slot_product((count_ref, row_ref, col_ref, tiles_ref), source_ref, acc_ref, True)
    tile = outs[0].shape[0]
    for k, out_ref in zip(half_first(len(outs)), outs):
        rows = block_at(partner(row_index(), k, len(outs)), tile)
        out_ref[...] = acc_ref[rows, :].astype(BF16)


def back_sum_kernel(*refs):
    total = refs[0][...].astype(F32)
    for ref in refs[1:-1]:
        total += ref[...].astype(F32)
    refs[-1][...] = total


def features_kernel(weight_ref, most_ref, last_ref, out_ref):
    out_ref[...] = lax.dot_general(
        (most_ref[...] + last_ref[...].astype(F32)).astype(BF16),
        weight_ref[...],
        (((1,), (1,)), ((), ())),
        preferred_element_type=F32,
    ).astype(BF16)


def write_kernel(
    features_ref, own_ref, other_ref, bias_ref, features_hbm, grad_hbm, bias_hbm, sems
):
    half = own_ref.shape[0]
    copies = [
        pltpu.make_async_copy(own_ref, grad_hbm.at[block_at(core_index(), half)], sems.at[0]),
        pltpu.make_async_copy(other_ref, grad_hbm.at[block_at(1 - core_index(), half)], sems.at[1]),
        pltpu.make_async_copy(features_ref, features_hbm, sems.at[2]),
        pltpu.make_async_copy(bias_ref, bias_hbm, sems.at[3]),
    ]
    for copy in copies:
        copy.start()
    for copy in copies:
        copy.wait()


def in_turn(count, make):
    made, before = {}, []
    for k in far_first(count):
        made[k] = make(k, before)
        before = [made[k]]
    return made


def local(features, weight, bias_term, cotangent, tile_values, tile_row, tile_col, tile_count):
    n_row = lax.axis_size("row")
    n_col = lax.axis_size("col")
    n_chip = n_col // 2
    tile, width = features.shape
    hidden = weight.shape[1]
    slots = tile_values.shape[2]
    row_nodes, col_nodes = n_col * tile, n_row * tile
    bias_row = bias_term.reshape(1, hidden)
    half = width // 2
    matrix = 2 * tile * width * hidden
    block_bytes = 2 * tile * width

    def like(rows, columns, dtype=BF16):
        return jax.ShapeDtypeStruct((rows, columns), dtype)

    near = 1
    own_nodes = n_chip * tile

    def add(terms, flops=0, after=()):
        return call(
            functools.partial(add_terms_kernel, n_terms=len(terms)),
            like(half + BIAS_ROWS, hidden),
            [VMEM_SPEC] * (len(terms) + len(after)),
            [],
            flops or len(terms) * half * hidden,
            len(terms) * half * hidden * 2,
        )(*terms, *after)

    is_dense = n_row * n_col <= 2 * slots
    if is_dense:
        chunks = 4 if slots % 4 == 0 else 1
        dense, bias_row = call(
            dense_kernel,
            (like(row_nodes, col_nodes), like(1, hidden, F32)),
            [SMEM_SPEC] + [HBM_SPEC] * 4,
            [
                pltpu.SMEM((1, 1, slots), jnp.int32),
                pltpu.SMEM((1, 1, slots), jnp.int32),
                pltpu.VMEM((slots, tile, tile), BF16),
                pltpu.VMEM((row_nodes, col_nodes), F32),
                pltpu.SemaphoreType.DMA((3,)),
                pltpu.SemaphoreType.DMA((chunks,)),
            ],
            0,
            12 * row_nodes * col_nodes,
        )(tile_count, *(
            pltpu.with_memory_space_constraint(array, pltpu.HBM)
            for array in (tile_row, tile_col, tile_values, bias_row)
        ))
    else:
        slot_args = (
            tile_count.reshape(1),
            tile_row.reshape(slots),
            tile_col.reshape(slots),
            tile_values.reshape(slots, tile, tile),
        )
        slot_specs = [SMEM_SPEC] * 3 + [VMEM_SPEC]

    sources = exchange([features] * n_row, "row", n_row, order=half_first)
    if is_dense:
        other, source = call(
            forward_other_kernel,
            (like(own_nodes, width), like(col_nodes, width)),
            [VMEM_SPEC] * (1 + n_row),
            [],
            slots * matrix // 2,
            row_nodes * width * 8,
        )(dense, *sources)
        own = call(
            forward_own_kernel,
            like(own_nodes, width),
            [VMEM_SPEC] * 2,
            [],
            slots * matrix // 2,
            row_nodes * width * 8,
        )(dense, source)
    else:
        other, own = call(
            slot_forward_kernel,
            (like(own_nodes, width), like(own_nodes, width)),
            slot_specs + [VMEM_SPEC] * n_row,
            [pltpu.VMEM((col_nodes, width), BF16), pltpu.VMEM((row_nodes, width), F32)],
            slots * matrix // 2,
            row_nodes * width * 8,
        )(*slot_args, *sources)
    swapped = swap_cores(other, n_col)

    def chip_piece(k, before):
        return call(
            functools.partial(chip_kernel, k=k, n_chip=n_chip),
            like(tile, width),
            [VMEM_SPEC] * (2 + len(before)),
            [],
            tile * width,
            3 * block_bytes,
        )(own, swapped, *before)

    pieces = in_turn(n_chip, chip_piece)
    parts = exchange(pieces, "col", n_col, 2)
    if is_dense:
        turned = call(
            turn_kernel,
            like(col_nodes, row_nodes),
            [VMEM_SPEC] * 2,
            [],
            0,
            4 * row_nodes * col_nodes,
        )(dense, pieces[0])
    hidden_own, grad, aggregated = call(
        middle_kernel,
        [like(tile, hidden), like(tile, hidden), like(tile, width)],
        [VMEM_SPEC] * (3 + n_chip),
        [],
        matrix,
        n_chip * block_bytes,
    )(weight, bias_row, cotangent, *parts)
    grads = exchange([grad] * n_chip, "col", n_col, 2)
    hidden_out = call(copy_kernel, like(tile, hidden), [VMEM_SPEC], [], 0, 2 * block_bytes)(hidden_own)
    mine, theirs = (
        call(
            functools.partial(term_kernel, own=own),
            like(half + BIAS_ROWS, hidden),
            [VMEM_SPEC] * 2,
            [],
            matrix // 2,
            4 * block_bytes,
        )(aggregated, grad)
        for own in (True, False)
    )
    chip_term = add([swap_cores(theirs, n_col), mine])
    add_late = functools.partial(add, flops=ROW_SUM_WEIGHT * matrix)
    row_terms = total_over(chip_term, add, "row", n_row)

    own_grads = call(
        gather_kernel,
        like(own_nodes, hidden),
        [VMEM_SPEC] * (1 + n_chip),
        [],
        0,
        own_nodes * hidden * 4,
    )(chip_term, *grads)
    other_grads = swap_cores(own_grads, n_col)
    if is_dense:
        back_own = call(
            back_own_kernel,
            like(col_nodes, hidden, F32),
            [VMEM_SPEC] * 2,
            [],
            slots * matrix // 2,
            row_nodes * hidden * 8,
        )(turned, own_grads)
        row_term = add_late(row_terms, after=[back_own])
        back_pieces = []
        for partners in (half_first(n_row)[:1], half_first(n_row)[1:]):
            back_pieces += call(
                functools.partial(back_pieces_kernel, partners=partners, n_row=n_row),
                [like(tile, hidden)] * len(partners),
                [VMEM_SPEC] * 3,
                [],
                len(partners) * n_chip * matrix,
                row_nodes * hidden * 2,
            )(turned, back_own, other_grads)
    else:
        row_term = add_late(row_terms)
        back_pieces = call(
            slot_back_kernel,
            [like(tile, hidden)] * n_row,
            slot_specs + [VMEM_SPEC] * 2,
            [pltpu.VMEM((row_nodes, hidden), BF16), pltpu.VMEM((col_nodes, hidden), F32)],
            slots * matrix // 2,
            row_nodes * hidden * 8,
        )(*slot_args, own_grads, other_grads)
    by_partner = dict(zip(half_first(n_row), back_pieces))
    backs = exchange(by_partner, "row", n_row, order=half_first)
    most = call(
        back_sum_kernel,
        like(tile, hidden, F32),
        [VMEM_SPEC] * (n_row - 1),
        [],
        BACK_SUM_WEIGHT * matrix,
        n_row * block_bytes,
    )(*backs[:-2], backs[-1])
    own_features = call(
        features_kernel,
        like(tile, width),
        [VMEM_SPEC] * 3,
        [],
        FEATURES_WEIGHT * matrix,
        n_row * block_bytes,
    )(weight, most, backs[-2])
    all_terms = total_over(row_term, add, "col", n_col, 2)
    factor = (tile * n_row * n_col) ** (-0.5)
    own_half, bias_grad = call(
        functools.partial(scale_kernel, factor=factor),
        (like(half, hidden, F32), like(1, hidden, F32)),
        [VMEM_SPEC] * (1 + len(all_terms)),
        [],
        len(all_terms) * half * hidden,
        len(all_terms) * half * hidden * 2,
    )(most, *all_terms)
    grad_features, grad_weight, grad_bias = call(
        write_kernel,
        (like(tile, width), like(width, hidden, F32), like(1, hidden, F32)),
        [VMEM_SPEC] * 4,
        [pltpu.SemaphoreType.DMA((4,))],
        0,
        width * hidden * 8,
        HBM_SPEC,
    )(own_features, own_half, swap_cores(own_half, n_col), bias_grad)
    return hidden_out, grad_features, grad_weight, grad_bias.reshape(hidden)


def solution(mesh):
    return jax.shard_map(
        local,
        mesh=mesh,
        in_specs=(
            P(("col", "row"), None),
            P(),
            P(),
            P(("row", "col"), None),
            P("row", "col", None, None, None),
            P("row", "col", None),
            P("row", "col", None),
            P("row", "col"),
        ),
        out_specs=(P(("row", "col"), None), P(("col", "row"), None), P(), P()),
        check_vma=False,
    )
```

```python
import functools

import jax
import jax.numpy as jnp
from jax import lax
from jax.experimental import pallas as pl
from jax.experimental.pallas import tpu as pltpu
from jax.sharding import PartitionSpec as P

F32 = jnp.float32
BF16 = jnp.bfloat16
ROOT_2_OVER_PI = 0.7978845608028654
CUBIC = 0.044715
VMEM_LIMIT = 48 * 1024 * 1024
BIAS_ROWS = 16
BACK_SUM_WEIGHT = 30
ROW_SUM_WEIGHT = 120
FEATURES_WEIGHT = 100

VMEM_SPEC = pl.BlockSpec(memory_space=pltpu.VMEM)
HBM_SPEC = pl.BlockSpec(memory_space=pltpu.HBM)
SMEM_SPEC = pl.BlockSpec(memory_space=pltpu.SMEM)


def call(kernel, out_shape, in_specs, scratch, flops, moved, out_spec=VMEM_SPEC):
    return pl.pallas_call(
        kernel,
        out_shape=out_shape,
        in_specs=in_specs,
        out_specs=jax.tree.map(lambda _: out_spec, out_shape),
        scratch_shapes=scratch,
        compiler_params=pltpu.CompilerParams(vmem_limit_bytes=VMEM_LIMIT),
        cost_estimate=pl.CostEstimate(flops=flops, bytes_accessed=moved, transcendentals=0),
    )


def partner(index, k, count):
    if count & (count - 1) == 0:
        return index ^ k
    return (k - index) % count


def far_first(count):
    return list(dict.fromkeys([count - 1, *range(1, count), 0]))


def pairs_of(k, size, cores):
    return [(i, partner(i // cores, k, size // cores) * cores + i % cores) for i in range(size)]


def half_first(count):
    return [count // 2] + [k for k in range(count - 1, -1, -1) if k != count // 2]


def exchange(blocks, axis, size, cores=1, order=far_first):
    received = []
    for k in order(size // cores):
        pairs = pairs_of(k, size, cores)
        moves = any(i != j for i, j in pairs)
        received.append(lax.ppermute(blocks[k], axis, pairs) if moves else blocks[k])
    return received


def swap_cores(block, size):
    return lax.ppermute(block, "col", [(i, i ^ 1) for i in range(size)])


def total_over(block, add, axis, size, cores=1):
    count = size // cores
    if count & (count - 1):
        return exchange([block] * count, axis, size, cores)
    terms, step = [block], 1
    while step < count:
        block = add(terms) if len(terms) > 1 else block
        terms = [lax.ppermute(block, axis, pairs_of(step, size, cores)), block]
        step *= 2
    return terms


def block_at(index, size):
    return pl.ds(pl.multiple_of(index * size, size), size)


def row_index():
    return lax.axis_index("row")


def chip_index():
    return lax.axis_index("col") // 2


def core_index():
    return lax.axis_index("col") % 2


def summed(refs):
    by_partner = dict(zip(far_first(len(refs)), refs))
    values = [by_partner[k][...].astype(F32) for k in sorted(by_partner)]
    while len(values) > 1:
        values = [sum(values[i + 1 : i + 2], values[i]) for i in range(0, len(values), 2)]
    return values[0]


def bias_rows(bias):
    high = bias.astype(BF16).astype(F32)
    line = lax.broadcasted_iota(jnp.int32, (BIAS_ROWS, bias.shape[1]), 0)
    return jnp.where(line == 0, high, jnp.where(line == 1, bias - high, 0.0))


def row_place(row, n_chip):
    return jnp.where(row % 2 == core_index(), 0, n_chip) + row // 2


def dense_kernel(
    count_ref, row_hbm, col_hbm, tiles_hbm, bias_hbm, dense_ref, bias_ref,
    row_ref, col_ref, tiles_ref, sum_ref, sems, tile_sems,
):
    slots, tile = tiles_ref.shape[0], tiles_ref.shape[1]
    n_chip = sum_ref.shape[0] // (2 * tile)
    chunks = tile_sems.shape[0]
    size = slots // chunks
    small = [
        pltpu.make_async_copy(row_hbm, row_ref, sems.at[0]),
        pltpu.make_async_copy(col_hbm, col_ref, sems.at[1]),
        pltpu.make_async_copy(bias_hbm, bias_ref, sems.at[2]),
    ]
    large = []
    for k in range(chunks):
        part = pl.ds(k * size, size)
        large.append(
            pltpu.make_async_copy(tiles_hbm.at[0, 0, part], tiles_ref.at[part], tile_sems.at[k])
        )
    for copy in small + large:
        copy.start()
    sum_ref[...] = jnp.zeros_like(sum_ref)
    for copy in small:
        copy.wait()
    count = count_ref[0, 0]

    def body(slot, carry):
        rows = block_at(row_place(row_ref[0, 0, slot], n_chip), tile)
        cols = block_at(col_ref[0, 0, slot], tile)
        sum_ref[rows, cols] += tiles_ref[slot].astype(F32)
        return carry

    for k, copy in enumerate(large):
        copy.wait()
        lax.fori_loop(k * size, jnp.minimum(count, (k + 1) * size), body, 0)
    dense_ref[...] = sum_ref[...].astype(BF16)


def turn_kernel(dense_ref, after_ref, turned_ref):
    rows = dense_ref.shape[0]
    step = 256 if rows % 256 == 0 else rows
    for first in range(0, rows, step):
        turned_ref[:, first : first + step] = dense_ref[first : first + step, :].T


def dense_dot(left, right):
    return jnp.dot(left, right, preferred_element_type=F32)


def gather_sources(sources, source_ref, index, order):
    tile = sources[0].shape[0]
    for k, ref in zip(order(len(sources)), sources):
        source_ref[block_at(partner(index, k, len(sources)), tile), :] = ref[...]


def slot_product(refs, source_ref, acc_ref, turned):
    count_ref, row_ref, col_ref, tiles_ref = refs
    tile = tiles_ref.shape[1]
    n_chip = (source_ref if turned else acc_ref).shape[0] // (2 * tile)
    contract = 0 if turned else 1
    acc_ref[...] = jnp.zeros_like(acc_ref)

    def body(slot, carry):
        places = [row_place(row_ref[slot], n_chip), col_ref[slot]]
        source, target = places if turned else places[::-1]
        acc_ref[block_at(target, tile), :] += lax.dot_general(
            tiles_ref[slot],
            source_ref[block_at(source, tile), :],
            (((contract,), (0,)), ((), ())),
            preferred_element_type=F32,
        )
        return carry

    lax.fori_loop(0, count_ref[0], body, 0)


def forward_other_kernel(dense_ref, *refs):
    sources, (other_ref, source_ref) = refs[:-2], refs[-2:]
    gather_sources(sources, source_ref, row_index(), half_first)
    half = other_ref.shape[0]
    other_ref[...] = dense_dot(dense_ref[half:, :], source_ref[...]).astype(BF16)


def forward_own_kernel(dense_ref, source_ref, own_ref):
    own_ref[...] = dense_dot(dense_ref[: own_ref.shape[0], :], source_ref[...]).astype(BF16)


def slot_forward_kernel(count_ref, row_ref, col_ref, tiles_ref, *refs):
    sources, (other_ref, own_ref, source_ref, acc_ref) = refs[:-4], refs[-4:]
    gather_sources(sources, source_ref, row_index(), half_first)
    slot_product((count_ref, row_ref, col_ref, tiles_ref), source_ref, acc_ref, False)
    half = own_ref.shape[0]
    own_ref[...] = acc_ref[:half, :].astype(BF16)
    other_ref[...] = acc_ref[half:, :].astype(BF16)


def chip_kernel(own_ref, other_ref, *refs, k, n_chip):
    out_ref = refs[-1]
    rows = block_at(partner(chip_index(), k, n_chip), out_ref.shape[0])
    out_ref[...] = (own_ref[rows, :].astype(F32) + other_ref[rows, :].astype(F32)).astype(BF16)


def middle_kernel(weight_ref, bias_ref, cot_ref, *refs):
    parts, (hidden_ref, grad_ref, agg_ref) = refs[:-3], refs[-3:]
    aggregated = summed(parts).astype(BF16)
    agg_ref[...] = aggregated
    v = dense_dot(aggregated, weight_ref[...]) + bias_ref[...]
    square = v * v
    t = jnp.tanh(ROOT_2_OVER_PI * (v + CUBIC * (square * v)))
    half = 0.5 * (1.0 + t)
    hidden_ref[...] = (v * half).astype(BF16)
    slope = half + 0.5 * v * (1.0 - t * t) * (ROOT_2_OVER_PI * (1.0 + 3.0 * CUBIC * square))
    grad_ref[...] = (cot_ref[...].astype(F32) * slope).astype(BF16)


def copy_kernel(in_ref, out_ref):
    out_ref[...] = in_ref[...]


def term_kernel(agg_ref, grad_ref, out_ref, *, own):
    half = agg_ref.shape[1] // 2
    core = core_index() if own else 1 - core_index()
    grad = grad_ref[...]
    out_ref[:half, :] = lax.dot_general(
        agg_ref[:, block_at(core, half)],
        grad,
        (((0,), (0,)), ((), ())),
        preferred_element_type=F32,
    ).astype(BF16)
    out_ref[half:, :] = bias_rows(jnp.sum(grad.astype(F32), axis=0, keepdims=True)).astype(BF16)


def add_terms_kernel(*refs, n_terms):
    total = summed(refs[:n_terms])
    out_ref = refs[-1]
    half = total.shape[0] - BIAS_ROWS
    out_ref[:half, :] = total[:half].astype(BF16)
    out_ref[half:, :] = bias_rows(total[half : half + 1] + total[half + 1 : half + 2]).astype(BF16)


def scale_kernel(after_ref, *refs, factor):
    parts, (half_ref, bias_ref) = refs[:-2], refs[-2:]
    total = summed(parts) * factor
    half = half_ref.shape[0]
    half_ref[...] = total[:half]
    bias_ref[...] = total[half : half + 1] + total[half + 1 : half + 2]


def gather_kernel(after_ref, *refs):
    gather_sources(refs[:-1], refs[-1], chip_index(), far_first)


def back_own_kernel(turned_ref, source_ref, out_ref):
    out_ref[...] = dense_dot(turned_ref[:, : source_ref.shape[0]], source_ref[...])


def back_pieces_kernel(turned_ref, own_ref, source_ref, *outs):
    tile = outs[0].shape[0]
    for k, out_ref in zip(half_first(len(outs)), outs):
        rows = block_at(partner(row_index(), k, len(outs)), tile)
        rest = dense_dot(turned_ref[rows, source_ref.shape[0] :], source_ref[...])
        out_ref[...] = (own_ref[rows, :] + rest).astype(BF16)


def slot_back_kernel(count_ref, row_ref, col_ref, tiles_ref, own_ref, other_ref, *refs):
    outs, (source_ref, acc_ref) = refs[:-2], refs[-2:]
    half = own_ref.shape[0]
    source_ref[:half, :] = own_ref[...]
    source_ref[half:, :] = other_ref[...]
    slot_product((count_ref, row_ref, col_ref, tiles_ref), source_ref, acc_ref, True)
    tile = outs[0].shape[0]
    for k, out_ref in zip(half_first(len(outs)), outs):
        rows = block_at(partner(row_index(), k, len(outs)), tile)
        out_ref[...] = acc_ref[rows, :].astype(BF16)


def back_sum_kernel(*refs):
    total = refs[0][...].astype(F32)
    for ref in refs[1:-1]:
        total += ref[...].astype(F32)
    refs[-1][...] = total


def features_kernel(weight_ref, most_ref, last_ref, out_ref):
    out_ref[...] = lax.dot_general(
        (most_ref[...] + last_ref[...].astype(F32)).astype(BF16),
        weight_ref[...],
        (((1,), (1,)), ((), ())),
        preferred_element_type=F32,
    ).astype(BF16)


def write_kernel(
    features_ref, own_ref, other_ref, bias_ref, features_hbm, grad_hbm, bias_hbm, sems
):
    half = own_ref.shape[0]
    copies = [
        pltpu.make_async_copy(own_ref, grad_hbm.at[block_at(core_index(), half)], sems.at[0]),
        pltpu.make_async_copy(other_ref, grad_hbm.at[block_at(1 - core_index(), half)], sems.at[1]),
        pltpu.make_async_copy(features_ref, features_hbm, sems.at[2]),
        pltpu.make_async_copy(bias_ref, bias_hbm, sems.at[3]),
    ]
    for copy in copies:
        copy.start()
    for copy in copies:
        copy.wait()


def in_turn(count, make):
    made, before = {}, []
    for k in far_first(count):
        made[k] = make(k, before)
        before = [made[k]]
    return made


def local(features, weight, bias_term, cotangent, tile_values, tile_row, tile_col, tile_count):
    n_row = lax.axis_size("row")
    n_col = lax.axis_size("col")
    n_chip = n_col // 2
    tile, width = features.shape
    hidden = weight.shape[1]
    slots = tile_values.shape[2]
    row_nodes, col_nodes = n_col * tile, n_row * tile
    bias_row = bias_term.reshape(1, hidden)
    half = width // 2
    matrix = 2 * tile * width * hidden
    block_bytes = 2 * tile * width

    def like(rows, columns, dtype=BF16):
        return jax.ShapeDtypeStruct((rows, columns), dtype)

    near = 1
    own_nodes = n_chip * tile

    def add(terms, flops=0, after=()):
        return call(
            functools.partial(add_terms_kernel, n_terms=len(terms)),
            like(half + BIAS_ROWS, hidden),
            [VMEM_SPEC] * (len(terms) + len(after)),
            [],
            flops or len(terms) * half * hidden,
            len(terms) * half * hidden * 2,
        )(*terms, *after)

    is_dense = n_row * n_col <= 2 * slots
    if is_dense:
        chunks = 4 if slots % 4 == 0 else 1
        dense, bias_row = call(
            dense_kernel,
            (like(row_nodes, col_nodes), like(1, hidden, F32)),
            [SMEM_SPEC] + [HBM_SPEC] * 4,
            [
                pltpu.SMEM((1, 1, slots), jnp.int32),
                pltpu.SMEM((1, 1, slots), jnp.int32),
                pltpu.VMEM((slots, tile, tile), BF16),
                pltpu.VMEM((row_nodes, col_nodes), F32),
                pltpu.SemaphoreType.DMA((3,)),
                pltpu.SemaphoreType.DMA((chunks,)),
            ],
            0,
            12 * row_nodes * col_nodes,
        )(tile_count, *(
            pltpu.with_memory_space_constraint(array, pltpu.HBM)
            for array in (tile_row, tile_col, tile_values, bias_row)
        ))
    else:
        slot_args = (
            tile_count.reshape(1),
            tile_row.reshape(slots),
            tile_col.reshape(slots),
            tile_values.reshape(slots, tile, tile),
        )
        slot_specs = [SMEM_SPEC] * 3 + [VMEM_SPEC]

    sources = exchange([features] * n_row, "row", n_row, order=half_first)
    if is_dense:
        other, source = call(
            forward_other_kernel,
            (like(own_nodes, width), like(col_nodes, width)),
            [VMEM_SPEC] * (1 + n_row),
            [],
            slots * matrix // 2,
            row_nodes * width * 8,
        )(dense, *sources)
        own = call(
            forward_own_kernel,
            like(own_nodes, width),
            [VMEM_SPEC] * 2,
            [],
            slots * matrix // 2,
            row_nodes * width * 8,
        )(dense, source)
    else:
        other, own = call(
            slot_forward_kernel,
            (like(own_nodes, width), like(own_nodes, width)),
            slot_specs + [VMEM_SPEC] * n_row,
            [pltpu.VMEM((col_nodes, width), BF16), pltpu.VMEM((row_nodes, width), F32)],
            slots * matrix // 2,
            row_nodes * width * 8,
        )(*slot_args, *sources)
    swapped = swap_cores(other, n_col)

    def chip_piece(k, before):
        return call(
            functools.partial(chip_kernel, k=k, n_chip=n_chip),
            like(tile, width),
            [VMEM_SPEC] * (2 + len(before)),
            [],
            tile * width,
            3 * block_bytes,
        )(own, swapped, *before)

    pieces = in_turn(n_chip, chip_piece)
    parts = exchange(pieces, "col", n_col, 2)
    if is_dense:
        turned = call(
            turn_kernel,
            like(col_nodes, row_nodes),
            [VMEM_SPEC] * 2,
            [],
            0,
            4 * row_nodes * col_nodes,
        )(dense, pieces[0])
    hidden_own, grad, aggregated = call(
        middle_kernel,
        [like(tile, hidden), like(tile, hidden), like(tile, width)],
        [VMEM_SPEC] * (3 + n_chip),
        [],
        matrix,
        n_chip * block_bytes,
    )(weight, bias_row, cotangent, *parts)
    grads = exchange([grad] * n_chip, "col", n_col, 2)
    hidden_out = call(copy_kernel, like(tile, hidden), [VMEM_SPEC], [], 0, 2 * block_bytes)(hidden_own)
    mine, theirs = (
        call(
            functools.partial(term_kernel, own=own),
            like(half + BIAS_ROWS, hidden),
            [VMEM_SPEC] * 2,
            [],
            matrix // 2,
            4 * block_bytes,
        )(aggregated, grad)
        for own in (True, False)
    )
    chip_term = add([swap_cores(theirs, n_col), mine])
    add_late = functools.partial(add, flops=ROW_SUM_WEIGHT * matrix)
    row_terms = total_over(chip_term, add, "row", n_row)

    own_grads = call(
        gather_kernel,
        like(own_nodes, hidden),
        [VMEM_SPEC] * (1 + n_chip),
        [],
        0,
        own_nodes * hidden * 4,
    )(chip_term, *grads)
    other_grads = swap_cores(own_grads, n_col)
    if is_dense:
        back_own = call(
            back_own_kernel,
            like(col_nodes, hidden, F32),
            [VMEM_SPEC] * 2,
            [],
            slots * matrix // 2,
            row_nodes * hidden * 8,
        )(turned, own_grads)
        row_term = add_late(row_terms, after=[back_own])
        back_pieces = call(
            back_pieces_kernel,
            [like(tile, hidden)] * n_row,
            [VMEM_SPEC] * 3,
            [],
            slots * matrix // 2,
            row_nodes * hidden * 8,
        )(turned, back_own, other_grads)
    else:
        row_term = add_late(row_terms)
        back_pieces = call(
            slot_back_kernel,
            [like(tile, hidden)] * n_row,
            slot_specs + [VMEM_SPEC] * 2,
            [pltpu.VMEM((row_nodes, hidden), BF16), pltpu.VMEM((col_nodes, hidden), F32)],
            slots * matrix // 2,
            row_nodes * hidden * 8,
        )(*slot_args, own_grads, other_grads)
    by_partner = dict(zip(half_first(n_row), back_pieces))
    backs = exchange(by_partner, "row", n_row, order=half_first)
    most = call(
        back_sum_kernel,
        like(tile, hidden, F32),
        [VMEM_SPEC] * (n_row - 1),
        [],
        BACK_SUM_WEIGHT * matrix,
        n_row * block_bytes,
    )(*backs[:-2], backs[-1])
    own_features = call(
        features_kernel,
        like(tile, width),
        [VMEM_SPEC] * 3,
        [],
        FEATURES_WEIGHT * matrix,
        n_row * block_bytes,
    )(weight, most, backs[-2])
    all_terms = total_over(row_term, add, "col", n_col, 2)
    factor = (tile * n_row * n_col) ** (-0.5)
    own_half, bias_grad = call(
        functools.partial(scale_kernel, factor=factor),
        (like(half, hidden, F32), like(1, hidden, F32)),
        [VMEM_SPEC] * (1 + len(all_terms)),
        [],
        len(all_terms) * half * hidden,
        len(all_terms) * half * hidden * 2,
    )(most, *all_terms)
    grad_features, grad_weight, grad_bias = call(
        write_kernel,
        (like(tile, width), like(width, hidden, F32), like(1, hidden, F32)),
        [VMEM_SPEC] * 4,
        [pltpu.SemaphoreType.DMA((4,))],
        0,
        width * hidden * 8,
        HBM_SPEC,
    )(own_features, own_half, swap_cores(own_half, n_col), bias_grad)
    return hidden_out, grad_features, grad_weight, grad_bias.reshape(hidden)


def solution(mesh):
    return jax.shard_map(
        local,
        mesh=mesh,
        in_specs=(
            P(("col", "row"), None),
            P(),
            P(),
            P(("row", "col"), None),
            P("row", "col", None, None, None),
            P("row", "col", None),
            P("row", "col", None),
            P("row", "col"),
        ),
        out_specs=(P(("row", "col"), None), P(("col", "row"), None), P(), P()),
        check_vma=False,
    )
```

```python
import functools

import jax
import jax.numpy as jnp
from jax import lax
from jax.experimental import pallas as pl
from jax.experimental.pallas import tpu as pltpu
from jax.sharding import PartitionSpec as P

F32 = jnp.float32
BF16 = jnp.bfloat16
ROOT_2_OVER_PI = 0.7978845608028654
CUBIC = 0.044715
VMEM_LIMIT = 48 * 1024 * 1024
BIAS_ROWS = 16
BACK_SUM_WEIGHT = 30
ROW_SUM_WEIGHT = 120
FEATURES_WEIGHT = 100

VMEM_SPEC = pl.BlockSpec(memory_space=pltpu.VMEM)
HBM_SPEC = pl.BlockSpec(memory_space=pltpu.HBM)
SMEM_SPEC = pl.BlockSpec(memory_space=pltpu.SMEM)


def call(kernel, out_shape, in_specs, scratch, flops, moved, out_spec=VMEM_SPEC):
    return pl.pallas_call(
        kernel,
        out_shape=out_shape,
        in_specs=in_specs,
        out_specs=jax.tree.map(lambda _: out_spec, out_shape),
        scratch_shapes=scratch,
        compiler_params=pltpu.CompilerParams(vmem_limit_bytes=VMEM_LIMIT),
        cost_estimate=pl.CostEstimate(flops=flops, bytes_accessed=moved, transcendentals=0),
    )


def partner(index, k, count):
    if count & (count - 1) == 0:
        return index ^ k
    return (k - index) % count


def far_first(count):
    return list(range(count - 1, -1, -1))


def pairs_of(k, size, cores):
    return [(i, partner(i // cores, k, size // cores) * cores + i % cores) for i in range(size)]


def half_first(count):
    return [count // 2] + [k for k in far_first(count) if k != count // 2]


def exchange(blocks, axis, size, cores=1, order=far_first):
    received = []
    for k in order(size // cores):
        pairs = pairs_of(k, size, cores)
        moves = any(i != j for i, j in pairs)
        received.append(lax.ppermute(blocks[k], axis, pairs) if moves else blocks[k])
    return received


def swap_cores(block, size):
    return lax.ppermute(block, "col", [(i, i ^ 1) for i in range(size)])


def total_over(block, add, axis, size, cores=1):
    count = size // cores
    if count & (count - 1):
        return exchange([block] * count, axis, size, cores)
    terms, step = [block], 1
    while step < count:
        block = add(terms) if len(terms) > 1 else block
        terms = [lax.ppermute(block, axis, pairs_of(step, size, cores)), block]
        step *= 2
    return terms


def block_at(index, size):
    return pl.ds(pl.multiple_of(index * size, size), size)


def row_index():
    return lax.axis_index("row")


def chip_index():
    return lax.axis_index("col") // 2


def core_index():
    return lax.axis_index("col") % 2


def summed(refs):
    by_partner = dict(zip(far_first(len(refs)), refs))
    values = [by_partner[k][...].astype(F32) for k in sorted(by_partner)]
    while len(values) > 1:
        values = [sum(values[i + 1 : i + 2], values[i]) for i in range(0, len(values), 2)]
    return values[0]


def bias_rows(bias):
    high = bias.astype(BF16).astype(F32)
    line = lax.broadcasted_iota(jnp.int32, (BIAS_ROWS, bias.shape[1]), 0)
    return jnp.where(line == 0, high, jnp.where(line == 1, bias - high, 0.0))


def row_place(row, n_chip):
    return jnp.where(row % 2 == core_index(), 0, n_chip) + row // 2


def dense_kernel(
    count_ref, row_hbm, col_hbm, tiles_hbm, bias_hbm, dense_ref, bias_ref,
    row_ref, col_ref, tiles_ref, sum_ref, sems, tile_sems,
):
    slots, tile = tiles_ref.shape[0], tiles_ref.shape[1]
    n_chip = sum_ref.shape[0] // (2 * tile)
    chunks = tile_sems.shape[0]
    size = slots // chunks
    small = [
        pltpu.make_async_copy(row_hbm, row_ref, sems.at[0]),
        pltpu.make_async_copy(col_hbm, col_ref, sems.at[1]),
        pltpu.make_async_copy(bias_hbm, bias_ref, sems.at[2]),
    ]
    large = []
    for k in range(chunks):
        part = pl.ds(k * size, size)
        large.append(
            pltpu.make_async_copy(tiles_hbm.at[0, 0, part], tiles_ref.at[part], tile_sems.at[k])
        )
    for copy in small + large:
        copy.start()
    sum_ref[...] = jnp.zeros_like(sum_ref)
    for copy in small:
        copy.wait()
    count = count_ref[0, 0]

    def body(slot, carry):
        rows = block_at(row_place(row_ref[0, 0, slot], n_chip), tile)
        cols = block_at(col_ref[0, 0, slot], tile)
        sum_ref[rows, cols] += tiles_ref[slot].astype(F32)
        return carry

    for k, copy in enumerate(large):
        copy.wait()
        lax.fori_loop(k * size, jnp.minimum(count, (k + 1) * size), body, 0)
    dense_ref[...] = sum_ref[...].astype(BF16)


def turn_kernel(dense_ref, after_ref, turned_ref):
    rows = dense_ref.shape[0]
    step = 256 if rows % 256 == 0 else rows
    for first in range(0, rows, step):
        turned_ref[:, first : first + step] = dense_ref[first : first + step, :].T


def dense_dot(left, right):
    return jnp.dot(left, right, preferred_element_type=F32)


def gather_sources(sources, source_ref, index, order):
    tile = sources[0].shape[0]
    for k, ref in zip(order(len(sources)), sources):
        source_ref[block_at(partner(index, k, len(sources)), tile), :] = ref[...]


def slot_product(refs, source_ref, acc_ref, turned):
    count_ref, row_ref, col_ref, tiles_ref = refs
    tile = tiles_ref.shape[1]
    n_chip = (source_ref if turned else acc_ref).shape[0] // (2 * tile)
    contract = 0 if turned else 1
    acc_ref[...] = jnp.zeros_like(acc_ref)

    def body(slot, carry):
        places = [row_place(row_ref[slot], n_chip), col_ref[slot]]
        source, target = places if turned else places[::-1]
        acc_ref[block_at(target, tile), :] += lax.dot_general(
            tiles_ref[slot],
            source_ref[block_at(source, tile), :],
            (((contract,), (0,)), ((), ())),
            preferred_element_type=F32,
        )
        return carry

    lax.fori_loop(0, count_ref[0], body, 0)


def forward_other_kernel(dense_ref, *refs):
    sources, (other_ref, source_ref) = refs[:-2], refs[-2:]
    gather_sources(sources, source_ref, row_index(), far_first)
    half = other_ref.shape[0]
    other_ref[...] = dense_dot(dense_ref[half:, :], source_ref[...]).astype(BF16)


def forward_own_kernel(dense_ref, source_ref, own_ref):
    own_ref[...] = dense_dot(dense_ref[: own_ref.shape[0], :], source_ref[...]).astype(BF16)


def slot_forward_kernel(count_ref, row_ref, col_ref, tiles_ref, *refs):
    sources, (other_ref, own_ref, source_ref, acc_ref) = refs[:-4], refs[-4:]
    gather_sources(sources, source_ref, row_index(), far_first)
    slot_product((count_ref, row_ref, col_ref, tiles_ref), source_ref, acc_ref, False)
    half = own_ref.shape[0]
    own_ref[...] = acc_ref[:half, :].astype(BF16)
    other_ref[...] = acc_ref[half:, :].astype(BF16)


def chip_kernel(own_ref, other_ref, *refs, k, n_chip):
    out_ref = refs[-1]
    rows = block_at(partner(chip_index(), k, n_chip), out_ref.shape[0])
    out_ref[...] = (own_ref[rows, :].astype(F32) + other_ref[rows, :].astype(F32)).astype(BF16)


def middle_kernel(weight_ref, bias_ref, cot_ref, *refs):
    parts, (hidden_ref, grad_ref, agg_ref) = refs[:-3], refs[-3:]
    aggregated = summed(parts).astype(BF16)
    agg_ref[...] = aggregated
    v = dense_dot(aggregated, weight_ref[...]) + bias_ref[...]
    square = v * v
    t = jnp.tanh(ROOT_2_OVER_PI * (v + CUBIC * (square * v)))
    half = 0.5 * (1.0 + t)
    hidden_ref[...] = (v * half).astype(BF16)
    slope = half + 0.5 * v * (1.0 - t * t) * (ROOT_2_OVER_PI * (1.0 + 3.0 * CUBIC * square))
    grad_ref[...] = (cot_ref[...].astype(F32) * slope).astype(BF16)


def copy_kernel(in_ref, out_ref):
    out_ref[...] = in_ref[...]


def term_kernel(agg_ref, grad_ref, out_ref, *, own):
    half = agg_ref.shape[1] // 2
    core = core_index() if own else 1 - core_index()
    grad = grad_ref[...]
    out_ref[:half, :] = lax.dot_general(
        agg_ref[:, block_at(core, half)],
        grad,
        (((0,), (0,)), ((), ())),
        preferred_element_type=F32,
    ).astype(BF16)
    out_ref[half:, :] = bias_rows(jnp.sum(grad.astype(F32), axis=0, keepdims=True)).astype(BF16)


def add_terms_kernel(*refs, n_terms):
    total = summed(refs[:n_terms])
    out_ref = refs[-1]
    half = total.shape[0] - BIAS_ROWS
    out_ref[:half, :] = total[:half].astype(BF16)
    out_ref[half:, :] = bias_rows(total[half : half + 1] + total[half + 1 : half + 2]).astype(BF16)


def scale_kernel(after_ref, *refs, factor):
    parts, (half_ref, bias_ref) = refs[:-2], refs[-2:]
    total = summed(parts) * factor
    half = half_ref.shape[0]
    half_ref[...] = total[:half]
    bias_ref[...] = total[half : half + 1] + total[half + 1 : half + 2]


def gather_kernel(after_ref, *refs):
    gather_sources(refs[:-1], refs[-1], chip_index(), far_first)


def back_own_kernel(turned_ref, source_ref, out_ref):
    out_ref[...] = dense_dot(turned_ref[:, : source_ref.shape[0]], source_ref[...])


def back_pieces_kernel(turned_ref, own_ref, source_ref, *outs):
    tile = outs[0].shape[0]
    for k, out_ref in zip(half_first(len(outs)), outs):
        rows = block_at(partner(row_index(), k, len(outs)), tile)
        rest = dense_dot(turned_ref[rows, source_ref.shape[0] :], source_ref[...])
        out_ref[...] = (own_ref[rows, :] + rest).astype(BF16)


def slot_back_kernel(count_ref, row_ref, col_ref, tiles_ref, own_ref, other_ref, *refs):
    outs, (source_ref, acc_ref) = refs[:-2], refs[-2:]
    half = own_ref.shape[0]
    source_ref[:half, :] = own_ref[...]
    source_ref[half:, :] = other_ref[...]
    slot_product((count_ref, row_ref, col_ref, tiles_ref), source_ref, acc_ref, True)
    tile = outs[0].shape[0]
    for k, out_ref in zip(half_first(len(outs)), outs):
        rows = block_at(partner(row_index(), k, len(outs)), tile)
        out_ref[...] = acc_ref[rows, :].astype(BF16)


def back_sum_kernel(*refs):
    total = refs[0][...].astype(F32)
    for ref in refs[1:-1]:
        total += ref[...].astype(F32)
    refs[-1][...] = total


def features_kernel(weight_ref, most_ref, last_ref, out_ref):
    out_ref[...] = lax.dot_general(
        (most_ref[...] + last_ref[...].astype(F32)).astype(BF16),
        weight_ref[...],
        (((1,), (1,)), ((), ())),
        preferred_element_type=F32,
    ).astype(BF16)


def write_kernel(
    features_ref, own_ref, other_ref, bias_ref, features_hbm, grad_hbm, bias_hbm, sems
):
    half = own_ref.shape[0]
    copies = [
        pltpu.make_async_copy(own_ref, grad_hbm.at[block_at(core_index(), half)], sems.at[0]),
        pltpu.make_async_copy(other_ref, grad_hbm.at[block_at(1 - core_index(), half)], sems.at[1]),
        pltpu.make_async_copy(features_ref, features_hbm, sems.at[2]),
        pltpu.make_async_copy(bias_ref, bias_hbm, sems.at[3]),
    ]
    for copy in copies:
        copy.start()
    for copy in copies:
        copy.wait()


def in_turn(count, make):
    made, before = {}, []
    for k in far_first(count):
        made[k] = make(k, before)
        before = [made[k]]
    return made


def local(features, weight, bias_term, cotangent, tile_values, tile_row, tile_col, tile_count):
    n_row = lax.axis_size("row")
    n_col = lax.axis_size("col")
    n_chip = n_col // 2
    tile, width = features.shape
    hidden = weight.shape[1]
    slots = tile_values.shape[2]
    row_nodes, col_nodes = n_col * tile, n_row * tile
    bias_row = bias_term.reshape(1, hidden)
    half = width // 2
    matrix = 2 * tile * width * hidden
    block_bytes = 2 * tile * width

    def like(rows, columns, dtype=BF16):
        return jax.ShapeDtypeStruct((rows, columns), dtype)

    near = 1
    own_nodes = n_chip * tile

    def add(terms, flops=0, after=()):
        return call(
            functools.partial(add_terms_kernel, n_terms=len(terms)),
            like(half + BIAS_ROWS, hidden),
            [VMEM_SPEC] * (len(terms) + len(after)),
            [],
            flops or len(terms) * half * hidden,
            len(terms) * half * hidden * 2,
        )(*terms, *after)

    is_dense = n_row * n_col <= 2 * slots
    if is_dense:
        chunks = 4 if slots % 4 == 0 else 1
        dense, bias_row = call(
            dense_kernel,
            (like(row_nodes, col_nodes), like(1, hidden, F32)),
            [SMEM_SPEC] + [HBM_SPEC] * 4,
            [
                pltpu.SMEM((1, 1, slots), jnp.int32),
                pltpu.SMEM((1, 1, slots), jnp.int32),
                pltpu.VMEM((slots, tile, tile), BF16),
                pltpu.VMEM((row_nodes, col_nodes), F32),
                pltpu.SemaphoreType.DMA((3,)),
                pltpu.SemaphoreType.DMA((chunks,)),
            ],
            0,
            12 * row_nodes * col_nodes,
        )(tile_count, *(
            pltpu.with_memory_space_constraint(array, pltpu.HBM)
            for array in (tile_row, tile_col, tile_values, bias_row)
        ))
    else:
        slot_args = (
            tile_count.reshape(1),
            tile_row.reshape(slots),
            tile_col.reshape(slots),
            tile_values.reshape(slots, tile, tile),
        )
        slot_specs = [SMEM_SPEC] * 3 + [VMEM_SPEC]

    sources = exchange([features] * n_row, "row", n_row)
    if is_dense:
        other, source = call(
            forward_other_kernel,
            (like(own_nodes, width), like(col_nodes, width)),
            [VMEM_SPEC] * (1 + n_row),
            [],
            slots * matrix // 2,
            row_nodes * width * 8,
        )(dense, *sources)
        own = call(
            forward_own_kernel,
            like(own_nodes, width),
            [VMEM_SPEC] * 2,
            [],
            slots * matrix // 2,
            row_nodes * width * 8,
        )(dense, source)
    else:
        other, own = call(
            slot_forward_kernel,
            (like(own_nodes, width), like(own_nodes, width)),
            slot_specs + [VMEM_SPEC] * n_row,
            [pltpu.VMEM((col_nodes, width), BF16), pltpu.VMEM((row_nodes, width), F32)],
            slots * matrix // 2,
            row_nodes * width * 8,
        )(*slot_args, *sources)
    swapped = swap_cores(other, n_col)

    def chip_piece(k, before):
        return call(
            functools.partial(chip_kernel, k=k, n_chip=n_chip),
            like(tile, width),
            [VMEM_SPEC] * (2 + len(before)),
            [],
            tile * width,
            3 * block_bytes,
        )(own, swapped, *before)

    pieces = in_turn(n_chip, chip_piece)
    parts = exchange(pieces, "col", n_col, 2)
    if is_dense:
        turned = call(
            turn_kernel,
            like(col_nodes, row_nodes),
            [VMEM_SPEC] * 2,
            [],
            0,
            4 * row_nodes * col_nodes,
        )(dense, pieces[0])
    hidden_own, grad, aggregated = call(
        middle_kernel,
        [like(tile, hidden), like(tile, hidden), like(tile, width)],
        [VMEM_SPEC] * (3 + n_chip),
        [],
        matrix,
        n_chip * block_bytes,
    )(weight, bias_row, cotangent, *parts)
    grads = exchange([grad] * n_chip, "col", n_col, 2)
    hidden_out = call(copy_kernel, like(tile, hidden), [VMEM_SPEC], [], 0, 2 * block_bytes)(hidden_own)
    mine, theirs = (
        call(
            functools.partial(term_kernel, own=own),
            like(half + BIAS_ROWS, hidden),
            [VMEM_SPEC] * 2,
            [],
            matrix // 2,
            4 * block_bytes,
        )(aggregated, grad)
        for own in (True, False)
    )
    chip_term = add([swap_cores(theirs, n_col), mine])
    add_late = functools.partial(add, flops=ROW_SUM_WEIGHT * matrix)
    row_terms = total_over(chip_term, add, "row", n_row)

    own_grads = call(
        gather_kernel,
        like(own_nodes, hidden),
        [VMEM_SPEC] * (1 + n_chip),
        [],
        0,
        own_nodes * hidden * 4,
    )(chip_term, *grads)
    other_grads = swap_cores(own_grads, n_col)
    if is_dense:
        back_own = call(
            back_own_kernel,
            like(col_nodes, hidden, F32),
            [VMEM_SPEC] * 2,
            [],
            slots * matrix // 2,
            row_nodes * hidden * 8,
        )(turned, own_grads)
        row_term = add_late(row_terms, after=[back_own])
        back_pieces = call(
            back_pieces_kernel,
            [like(tile, hidden)] * n_row,
            [VMEM_SPEC] * 3,
            [],
            slots * matrix // 2,
            row_nodes * hidden * 8,
        )(turned, back_own, other_grads)
    else:
        row_term = add_late(row_terms)
        back_pieces = call(
            slot_back_kernel,
            [like(tile, hidden)] * n_row,
            slot_specs + [VMEM_SPEC] * 2,
            [pltpu.VMEM((row_nodes, hidden), BF16), pltpu.VMEM((col_nodes, hidden), F32)],
            slots * matrix // 2,
            row_nodes * hidden * 8,
        )(*slot_args, own_grads, other_grads)
    by_partner = dict(zip(half_first(n_row), back_pieces))
    backs = exchange(by_partner, "row", n_row, order=half_first)
    most = call(
        back_sum_kernel,
        like(tile, hidden, F32),
        [VMEM_SPEC] * (n_row - 1),
        [],
        BACK_SUM_WEIGHT * matrix,
        n_row * block_bytes,
    )(*backs[:-2], backs[-1])
    own_features = call(
        features_kernel,
        like(tile, width),
        [VMEM_SPEC] * 3,
        [],
        FEATURES_WEIGHT * matrix,
        n_row * block_bytes,
    )(weight, most, backs[-2])
    all_terms = total_over(row_term, add, "col", n_col, 2)
    factor = (tile * n_row * n_col) ** (-0.5)
    own_half, bias_grad = call(
        functools.partial(scale_kernel, factor=factor),
        (like(half, hidden, F32), like(1, hidden, F32)),
        [VMEM_SPEC] * (1 + len(all_terms)),
        [],
        len(all_terms) * half * hidden,
        len(all_terms) * half * hidden * 2,
    )(most, *all_terms)
    grad_features, grad_weight, grad_bias = call(
        write_kernel,
        (like(tile, width), like(width, hidden, F32), like(1, hidden, F32)),
        [VMEM_SPEC] * 4,
        [pltpu.SemaphoreType.DMA((4,))],
        0,
        width * hidden * 8,
        HBM_SPEC,
    )(own_features, own_half, swap_cores(own_half, n_col), bias_grad)
    return hidden_out, grad_features, grad_weight, grad_bias.reshape(hidden)


def solution(mesh):
    return jax.shard_map(
        local,
        mesh=mesh,
        in_specs=(
            P(("col", "row"), None),
            P(),
            P(),
            P(("row", "col"), None),
            P("row", "col", None, None, None),
            P("row", "col", None),
            P("row", "col", None),
            P("row", "col"),
        ),
        out_specs=(P(("row", "col"), None), P(("col", "row"), None), P(), P()),
        check_vma=False,
    )
```
